32 devices in a mesh: leaf: 8 (over y, x, core), grp: 4 (over z).
Axes of the slice: x: 2, y: 2, z: 4, core: 2. Of those that a mesh axis runs over, the one named last changes fastest.
Arguments:
- rhs_local: float32 [8, 4, 1024, 128], P('leaf', None, 'grp'), may hold values from -6 to 6
- diag_inv_local: float32 [8, 4, 1024, 1024], P('leaf', None, 'grp'), may hold values from -0.1875 to 0.1875
- sub_local: float32 [8, 3, 1024, 1024], P('leaf', None, 'grp'), may hold values from -0.1875 to 0.1875
- tiles: float32 [8, 4, 3, 128, 1024], P('leaf', 'grp'), may hold values from -0.046875 to 0.046875
- tile_block: int32 [8, 4, 3], P('leaf', 'grp'), may hold values from 0 to 15
- tile_source: int32 [8, 4, 3], P('leaf', 'grp'), may hold values from 0 to 3
- tile_count: int32 [8, 4], P('leaf', 'grp'), may hold values from 1 to 3, as said below
- rhs_anc: float32 [2, 1024, 128], P(None, 'grp', 'leaf'), may hold values from -6 to 6
- diag_inv_anc: float32 [2, 1024, 1024], P(None, 'grp'), may hold values from -0.1875 to 0.1875
- sub_anc: float32 [1, 1024, 1024], P(None, 'grp'), may hold values from -0.1875 to 0.1875
Outputs:
- solution_local: float32 [8, 4, 1024, 128], P('leaf', None, 'grp')
- solution_anc: float32 [2, 1024, 128], P(None, 'grp', 'leaf')
The draws below stay inside these ranges and needn't reach their ends.
Inputs may be any that keep to these rules, and one draw needn't show every extreme that they name: `tile_count`: some device holds exactly 3 live tiles.
All inputs are finite; a program needn't handle non-finite values.
Results may differ from the reference program's by a relative error of at most 0.0003.
Values sent between devices are 32-bit elements; how exact they have to be, the bound alone decides.
No kernel may reach another device: no remote copies, remote signals or barrier semaphores. Data moves between devices by JAX's collectives and lax.ppermute only.
A program may use at most 64 MiB of HBM per device.

```python
import math
import jax
import jax.numpy as jnp
import numpy as np
from jax import lax

NS = 1024
RHS = 128
TILE = 128
CHAIN = 4
ANC = 2
MAXT = 3
GROUPS = 8
MEMBERS = 4
BLOCKS = 16


def draw_tile_count(key, part):
    first, second = jax.random.split(key)
    total = GROUPS * MEMBERS
    heavy = jax.random.randint(first, (total,), 0, 4) == 3
    counts = jnp.where(heavy, MAXT, 1)
    forced = jax.random.randint(second, (), 0, total)
    counts = jnp.where(jnp.arange(total, dtype=jnp.int32) == forced, MAXT, counts)
    return counts.reshape(GROUPS, MEMBERS).astype(jnp.int32)


def set_ends(result, rng, low, high):
    shape = result.shape
    index_at = [jax.random.randint(jax.random.fold_in(rng, axis), (), 0, shape[axis]) for axis in range(len(shape))]
    result = result.at[tuple(index_at)].set(low)
    longest = shape.index(max(shape))
    index_at[longest] = (index_at[longest] + 1) % shape[longest]
    return result.at[tuple(index_at)].set(high)


def block_levels(stream_key, shape, pieces, smallest, top_value):
    loudness = 1.0
    for dim, shards_of in pieces:
        heights = jax.random.uniform(jax.random.fold_in(jax.random.fold_in(stream_key, 6), dim), (shards_of,), jnp.float32, smallest / len(pieces), top_value / len(pieces))
        loudness = loudness * jnp.repeat(jnp.exp(heights), shape[dim] // shards_of).reshape((-1,) + (1,) * (len(shape) - 1 - dim))
    return loudness


def rank_table(number_of, skew):
    loads = [(1 << 20) // math.isqrt(rank ** skew) + 1 for rank in range(1, number_of + 1)]
    width = 1 + sum(loads) // (1 << 30)
    return np.cumsum(np.array([max(1, weight // width) for weight in loads]))


def skewed_ids(key, dims, number_of, skew):
    table = rank_table(number_of, skew)
    lot = jax.random.randint(jax.random.fold_in(key, 1), dims, 0, int(table[number_of - 1]))
    rank = jnp.searchsorted(jnp.asarray(table, jnp.int32), lot, side="right")
    return jax.random.permutation(jax.random.fold_in(key, 2), number_of)[rank].astype(jnp.int32)


def normal_values(own_key, shape, spread, reach, pieces=(), kind=jnp.bfloat16):
    factor_of = block_levels(own_key, shape, pieces, -0.22, 0.18) if pieces else 1.0
    entries = jax.random.normal(own_key, shape, jnp.float32) * spread * factor_of
    return jnp.minimum(jnp.maximum(entries, -reach), reach).astype(kind)


def setup_inputs(seed: int = 0) -> dict:
    arg_keys = jax.random.split(jax.random.key(seed), 11)
    return {
        "rhs_local": normal_values(arg_keys[0], (GROUPS, CHAIN, NS, RHS), 1.0, 6.0, ((0, 8), (2, 4)), jnp.float32),
        "diag_inv_local": normal_values(arg_keys[1], (GROUPS, CHAIN, NS, NS), NS ** -0.5, 0.1875, ((0, 8), (2, 4)), jnp.float32),
        "sub_local": normal_values(arg_keys[2], (GROUPS, CHAIN - 1, NS, NS), NS ** -0.5, 0.1875, ((0, 8), (2, 4)), jnp.float32),
        "tiles": normal_values(arg_keys[3], (GROUPS, MEMBERS, MAXT, TILE, NS), (NS * 16) ** -0.5, 0.046875, ((0, 8), (1, 4)), jnp.float32),
        "tile_block": set_ends(skewed_ids(arg_keys[4], (GROUPS, MEMBERS, MAXT), BLOCKS, 2), jax.random.fold_in(arg_keys[4], 3), 0, BLOCKS - 1).astype(jnp.int32),
        "tile_source": set_ends(jax.random.randint(arg_keys[5], (GROUPS, MEMBERS, MAXT), 0, CHAIN), jax.random.fold_in(arg_keys[5], 1), 0, CHAIN - 1).astype(jnp.int32),
        "tile_count": draw_tile_count(jax.random.fold_in(arg_keys[10], 71), 0),
        "rhs_anc": normal_values(arg_keys[7], (ANC, NS, RHS), 1.0, 6.0, ((1, 4), (2, 8)), jnp.float32),
        "diag_inv_anc": normal_values(arg_keys[8], (ANC, NS, NS), NS ** -0.5, 0.1875, ((1, 4),), jnp.float32),
        "sub_anc": normal_values(arg_keys[9], (ANC - 1, NS, NS), NS ** -0.5, 0.1875, ((1, 4),), jnp.float32),
    }


highest = lax.Precision.HIGHEST


def product(left, right):
    return jnp.dot(left, right, precision=highest, preferred_element_type=jnp.float32)


def reference(rhs_local, diag_inv_local, sub_local, tiles, tile_block, tile_source, tile_count, rhs_anc, diag_inv_anc, sub_anc):
    def solve_group(inputs):
        rhs_group, inverse_group, below_group = inputs
        solved = []
        update = jnp.zeros_like(rhs_group[0])
        for current in range(CHAIN):
            residual = rhs_group[current] - update
            solution = product(inverse_group[current], residual)
            solved.append(solution)
            if current + 1 < CHAIN:
                update = product(below_group[current], solution)
        return jnp.stack(solved)

    solution_local = lax.map(solve_group, (rhs_local, diag_inv_local, sub_local))

    def add_group(running, inputs):
        tiles_group, block_group, source_group, count_group, solved_group = inputs
        chosen = solved_group[source_group]
        tile_terms = jnp.einsum("gmtk,gmkr->gmtr", tiles_group, chosen, precision=highest, preferred_element_type=jnp.float32)
        active = (jnp.arange(MAXT, dtype=jnp.int32)[None, :] < count_group[:, None]).astype(jnp.float32)
        onehot = (block_group[:, :, None] == jnp.arange(BLOCKS, dtype=jnp.int32)[None, None, :]).astype(jnp.float32)
        onehot = onehot * active[:, :, None]
        added = jnp.einsum("gmb,gmtr->btr", onehot, tile_terms, precision=highest, preferred_element_type=jnp.float32)
        return running + added, None

    initial = jnp.zeros((BLOCKS, TILE, RHS), jnp.float32)
    summed, unused = lax.scan(add_group, initial, (tiles, tile_block, tile_source, tile_count, solution_local))
    partial_value = summed.reshape(ANC, NS, RHS)
    ancestors_solved = []
    update = jnp.zeros_like(rhs_anc[0])
    for ancestor in range(ANC):
        residual = rhs_anc[ancestor] - partial_value[ancestor] - update
        solution = product(diag_inv_anc[ancestor], residual)
        ancestors_solved.append(solution)
        if ancestor + 1 < ANC:
            update = product(sub_anc[ancestor], solution)
    return solution_local, jnp.stack(ancestors_solved)
```

```python
import jax
import jax.numpy as jnp
from jax import lax
from jax.sharding import PartitionSpec as P

high = lax.Precision.HIGH


def product(left, right):
    return jnp.dot(left, right, precision=high, preferred_element_type=jnp.float32)


def contract_last(left, right):
    return lax.dot_general(
        left,
        right,
        (((left.ndim - 1,), (right.ndim - 1,)), ((), ())),
        precision=high,
        preferred_element_type=jnp.float32,
    )


def send(value, axis, shift):
    count = lax.axis_size(axis)
    return lax.ppermute(value, axis, [(i, (i + shift) % count) for i in range(count)])


def gather_pieces(value):
    members = lax.axis_size("grp")
    return [value] + [send(value, "grp", shift) for shift in range(1, members)]


def column_block(matrix, shift, width):
    members = lax.axis_size("grp")
    owner = lax.rem(lax.axis_index("grp") - shift + members, members)
    return lax.dynamic_slice_in_dim(matrix, owner * width, width, 1)


def apply_rows(matrix, pieces):
    total = None
    for shift, piece in enumerate(pieces):
        term = product(column_block(matrix, shift, piece.shape[0]), piece)
        total = term if total is None else total + term
    return total


def in_order(pieces):
    members = lax.axis_size("grp")
    me = lax.axis_index("grp")
    stacked = jnp.stack(pieces)
    owners = lax.rem(me - jnp.arange(members, dtype=jnp.int32) + members, members)
    return stacked[owners].reshape(-1, pieces[0].shape[-1])


def on_device(
    rhs_local,
    diag_inv_local,
    sub_local,
    tiles,
    tile_block,
    tile_source,
    tile_count,
    rhs_anc,
    diag_inv_anc,
    sub_anc,
):
    rhs_group = rhs_local[0]
    inverse_group = diag_inv_local[0]
    below_group = sub_local[0]
    supernodes = rhs_group.shape[0]
    order = inverse_group.shape[-1]
    rhs_count = rhs_group.shape[-1]
    members = lax.axis_size("grp")
    groups = lax.axis_size("leaf")
    me = lax.axis_index("grp")
    leaf = lax.axis_index("leaf")
    rows = order // members

    wide = order // groups
    sub_columns = lax.dynamic_slice_in_dim(sub_anc[0], leaf * wide, wide, 1)
    inverse_columns = lax.dynamic_slice_in_dim(diag_inv_anc[0], leaf * wide, wide, 1)
    half = apply_rows(diag_inv_anc[1], gather_pieces(sub_columns))
    half = lax.all_gather(half, "leaf", axis=1, tiled=True)
    coupled = apply_rows(half, gather_pieces(inverse_columns))
    coupled = lax.all_gather(coupled, "leaf", axis=1, tiled=True)

    tiles_mine = tiles[0, 0]
    slots, tile_rows = tiles_mine.shape[:2]
    blocks_mine = jnp.where(
        jnp.arange(slots, dtype=jnp.int32) < tile_count[0, 0], tile_block[0, 0], -1
    )
    blocks_all = lax.all_gather(blocks_mine.astype(jnp.float32), "leaf", axis=0, tiled=True)

    solved = []
    gathered = []
    residual = rhs_group[0]
    for current in range(supernodes):
        owned = apply_rows(inverse_group[current], gather_pieces(residual))
        solved.append(owned)
        pieces = gather_pieces(owned)
        gathered.append(in_order(pieces))
        if current + 1 < supernodes:
            residual = rhs_group[current + 1] - apply_rows(below_group[current], pieces)

    chosen = jnp.stack(gathered)[tile_source[0, 0]]
    terms = jnp.einsum(
        "mtk,mkr->rmt", tiles_mine, chosen, precision=high, preferred_element_type=jnp.float32
    )
    received = lax.all_to_all(terms, "leaf", split_axis=0, concat_axis=0, tiled=True)
    part = rhs_count // groups
    received = received.reshape(groups, part, slots, tile_rows)
    ancestors = rhs_anc.shape[0]
    block_count = ancestors * order // tile_rows
    onehot = (
        blocks_all[:, None] == jnp.arange(block_count, dtype=jnp.float32)[None, :]
    ).astype(jnp.float32)
    summed = jnp.einsum(
        "gmq,grmt->rqt",
        onehot.reshape(groups, slots, block_count),
        received,
        precision=high,
        preferred_element_type=jnp.float32,
    ).reshape(part, ancestors, order)
    own = jnp.zeros((part, ancestors, order), jnp.float32)
    own = lax.dynamic_update_slice(own, jnp.transpose(rhs_anc, (2, 0, 1)), (0, 0, me * rows))
    total = sum(gather_pieces(own - summed))
    first = contract_last(diag_inv_anc[0], total[:, 0])
    second = contract_last(diag_inv_anc[1], total[:, 1]) - contract_last(coupled, total[:, 0])
    return (jnp.stack(solved)[None], jnp.stack([first, second]))


def solution(mesh):
    return jax.shard_map(
        on_device,
        mesh=mesh,
        in_specs=(
            P("leaf", None, "grp", None),
            P("leaf", None, "grp", None),
            P("leaf", None, "grp", None),
            P("leaf", "grp", None, None, None),
            P("leaf", "grp", None),
            P("leaf", "grp", None),
            P("leaf", "grp"),
            P(None, "grp", "leaf"),
            P(None, "grp", None),
            P(None, "grp", None),
        ),
        out_specs=(P("leaf", None, "grp", None), P(None, "grp", "leaf")),
        check_vma=False,
    )
```

```python
import jax
import jax.numpy as jnp
from jax import lax
from jax.sharding import PartitionSpec as P

high = lax.Precision.HIGH


def product(left, right):
    return jnp.dot(left, right, precision=high, preferred_element_type=jnp.float32)


def contract_last(left, right):
    return lax.dot_general(
        left,
        right,
        (((left.ndim - 1,), (right.ndim - 1,)), ((), ())),
        precision=high,
        preferred_element_type=jnp.float32,
    )


def ring_member(place, members):
    if place == 0:
        return 0
    return 2 * place - 1 if place <= members // 2 else 2 * (members - place)


def ring_place_of(member, members):
    return jnp.where(
        member % 2 == 1, (member + 1) // 2, jnp.where(member == 0, 0, members - member // 2)
    )


def ring_member_of(place, members):
    return jnp.where(place <= members // 2, jnp.maximum(2 * place - 1, 0), 2 * (members - place))


def ring_send(value, step):
    members = lax.axis_size("grp")
    pairs = [
        (ring_member(p, members), ring_member((p + step) % members, members))
        for p in range(members)
    ]
    return lax.ppermute(value, "grp", pairs)


def ring_owner(distance):
    members = lax.axis_size("grp")
    place = ring_place_of(lax.axis_index("grp"), members)
    return ring_member_of(lax.rem(place - distance + members, members), members)


def ring_gather(value):
    members = lax.axis_size("grp")
    rows = value.shape[0]
    half = rows // 2
    low, high_part = value[:half], value[half:]
    pieces = [(lax.axis_index("grp") * rows, value)]
    forward = [low, high_part]
    backward = [low, high_part]
    for distance in range(1, members // 2 + 1):
        last = 2 * distance == members
        ahead = ring_owner(distance) * rows
        behind = ring_owner(-distance) * rows
        if last:
            forward[0] = ring_send(forward[0], 1)
            backward[1] = ring_send(backward[1], -1)
            pieces.append((ahead, forward[0]))
            pieces.append((behind + half, backward[1]))
        else:
            forward[0] = ring_send(forward[0], 1)
            backward[1] = ring_send(backward[1], -1)
            forward[1] = ring_send(forward[1], 1)
            backward[0] = ring_send(backward[0], -1)
            pieces.append((ahead, forward[0]))
            pieces.append((behind + half, backward[1]))
            pieces.append((ahead + half, forward[1]))
            pieces.append((behind, backward[0]))
    return pieces


def apply_rows(matrix, pieces):
    total = None
    for offset, piece in pieces:
        columns = lax.dynamic_slice_in_dim(matrix, offset, piece.shape[0], 1)
        term = product(columns, piece)
        total = term if total is None else total + term
    return total


def send(value, axis, shift):
    count = lax.axis_size(axis)
    return lax.ppermute(value, axis, [(i, (i + shift) % count) for i in range(count)])


def apply_wide(matrix, portion):
    members = lax.axis_size("grp")
    me = lax.axis_index("grp")
    rows = portion.shape[-1]
    total = None
    for shift in range(members):
        piece = portion if shift == 0 else send(portion, "grp", shift)
        owner = lax.rem(me - shift + members, members)
        columns = lax.dynamic_slice_in_dim(matrix, owner * rows, rows, 1)
        term = contract_last(piece, columns)
        total = term if total is None else total + term
    return total


def assemble(pieces, order):
    whole = jnp.zeros((order, pieces[0][1].shape[1]), jnp.float32)
    for offset, piece in pieces:
        whole = lax.dynamic_update_slice_in_dim(whole, piece, offset, 0)
    return whole


def on_device(
    rhs_local,
    diag_inv_local,
    sub_local,
    tiles,
    tile_block,
    tile_source,
    tile_count,
    rhs_anc,
    diag_inv_anc,
    sub_anc,
):
    rhs_group = rhs_local[0]
    inverse_group = diag_inv_local[0]
    below_group = sub_local[0]
    supernodes = rhs_group.shape[0]
    order = inverse_group.shape[-1]
    rhs_count = rhs_group.shape[-1]
    members = lax.axis_size("grp")
    groups = lax.axis_size("leaf")
    me = lax.axis_index("grp")
    leaf = lax.axis_index("leaf")
    rows = order // members
    part = rhs_count // groups

    tiles_mine = tiles[0, 0]
    slots, tile_rows = tiles_mine.shape[:2]
    blocks = jnp.where(
        jnp.arange(slots, dtype=jnp.int32) < tile_count[0, 0], tile_block[0, 0], -1
    ).astype(jnp.float32)
    sources = tile_source[0, 0]

    solved = []
    residual = rhs_group[0]
    chosen = jnp.zeros((slots, order, rhs_count), jnp.float32)
    for current in range(supernodes):
        owned = apply_rows(inverse_group[current], ring_gather(residual))
        solved.append(owned)
        pieces = ring_gather(owned)
        if current + 1 < supernodes:
            residual = rhs_group[current + 1] - apply_rows(below_group[current], pieces)
            whole = assemble(pieces, order)
            chosen = jnp.where((sources == current)[:, None, None], whole[None], chosen)

    early = jnp.einsum(
        "mtk,mkr->rmt", tiles_mine, chosen, precision=high, preferred_element_type=jnp.float32
    ).reshape(rhs_count, slots * tile_rows)
    flat_tiles = tiles_mine.reshape(slots * tile_rows, order)
    late = None
    for offset, piece in pieces:
        columns = lax.dynamic_slice_in_dim(flat_tiles, offset, piece.shape[0], 1)
        term = lax.dot_general(
            piece,
            columns,
            (((0,), (1,)), ((), ())),
            precision=high,
            preferred_element_type=jnp.float32,
        )
        late = term if late is None else late + term
    is_late = jnp.repeat(sources == supernodes - 1, tile_rows)
    terms = jnp.where(is_late[None, :], late, early)
    tag = jnp.zeros((tile_rows,), jnp.float32).at[:slots].set(blocks)
    terms = jnp.concatenate(
        [terms, jnp.broadcast_to(tag[None, :], (rhs_count, tile_rows))], axis=1
    )

    received = [lax.dynamic_slice_in_dim(terms, leaf * part, part, 0)]
    for shift in range(1, groups):
        target = lax.rem(leaf + shift, groups)
        received.append(
            send(lax.dynamic_slice_in_dim(terms, target * part, part, 0), "leaf", shift)
        )
    received = jnp.stack(received)
    ancestors = rhs_anc.shape[0]
    block_count = ancestors * order // tile_rows
    width = slots * tile_rows
    onehot = (
        received[:, 0, width : width + slots, None]
        == jnp.arange(block_count, dtype=jnp.float32)[None, None, :]
    ).astype(jnp.float32)
    summed = jnp.einsum(
        "gmq,grmt->rqt",
        onehot,
        received[:, :, :width].reshape(groups, part, slots, tile_rows),
        precision=high,
        preferred_element_type=jnp.float32,
    ).reshape(part, ancestors, order)
    own = jnp.zeros((part, ancestors, order), jnp.float32)
    own = lax.dynamic_update_slice(own, jnp.transpose(rhs_anc, (2, 0, 1)), (0, 0, me * rows))
    share = own - summed

    first_share = share[:, 0]
    total = None
    for shift in range(members):
        target = lax.rem(me + shift, members)
        payload = [first_share] + [
            lax.dynamic_slice_in_dim(share[:, a], target * rows, rows, 1)
            for a in range(1, ancestors)
        ]
        payload = jnp.concatenate(payload, axis=1)
        payload = payload if shift == 0 else send(payload, "grp", shift)
        total = payload if total is None else total + payload
    solutions = [contract_last(total[:, :order], diag_inv_anc[0])]
    for ancestor in range(1, ancestors):
        begin = order + (ancestor - 1) * rows
        residual = total[:, begin : begin + rows] - apply_wide(sub_anc[ancestor - 1], solutions[-1])
        solutions.append(apply_wide(diag_inv_anc[ancestor], residual))
    solutions = jnp.stack([jnp.transpose(s) for s in solutions])
    return (jnp.stack(solved)[None], solutions)


def solution(mesh):
    return jax.shard_map(
        on_device,
        mesh=mesh,
        in_specs=(
            P("leaf", None, "grp", None),
            P("leaf", None, "grp", None),
            P("leaf", None, "grp", None),
            P("leaf", "grp", None, None, None),
            P("leaf", "grp", None),
            P("leaf", "grp", None),
            P("leaf", "grp"),
            P(None, "grp", "leaf"),
            P(None, "grp", None),
            P(None, "grp", None),
        ),
        out_specs=(P("leaf", None, "grp", None), P(None, "grp", "leaf")),
        check_vma=False,
    )
```

```python
import jax
import jax.numpy as jnp
from jax import lax
from jax.sharding import PartitionSpec as P

high = lax.Precision.HIGH


def product(left, right):
    return jnp.dot(left, right, precision=high, preferred_element_type=jnp.float32)


def contract_last(left, right):
    return lax.dot_general(
        left,
        right,
        (((left.ndim - 1,), (right.ndim - 1,)), ((), ())),
        precision=high,
        preferred_element_type=jnp.float32,
    )


def ring_member(place, members):
    if place == 0:
        return 0
    return 2 * place - 1 if place <= members // 2 else 2 * (members - place)


def ring_place_of(member, members):
    return jnp.where(
        member % 2 == 1, (member + 1) // 2, jnp.where(member == 0, 0, members - member // 2)
    )


def ring_member_of(place, members):
    return jnp.where(place <= members // 2, jnp.maximum(2 * place - 1, 0), 2 * (members - place))


def ring_send(value, step):
    members = lax.axis_size("grp")
    pairs = [
        (ring_member(p, members), ring_member((p + step) % members, members))
        for p in range(members)
    ]
    return lax.ppermute(value, "grp", pairs)


def ring_owner(distance):
    members = lax.axis_size("grp")
    place = ring_place_of(lax.axis_index("grp"), members)
    return ring_member_of(lax.rem(place - distance + members, members), members)


def ring_gather(value):
    members = lax.axis_size("grp")
    rows = value.shape[0]
    pieces = [(lax.axis_index("grp") * rows, value)]
    ahead = behind = value
    for distance in range(1, members // 2 + 1):
        ahead = ring_send(ahead, 1)
        pieces.append((ring_owner(distance) * rows, ahead))
        if 2 * distance < members:
            behind = ring_send(behind, -1)
            pieces.append((ring_owner(-distance) * rows, behind))
    return pieces


def columns_of(factor, index, offset, width):
    lead = factor.ndim - 3
    begin = (0,) * lead + (index, 0, offset)
    size = (1,) * (lead + 1) + (factor.shape[-2], width)
    return lax.dynamic_slice(factor, begin, size).reshape(factor.shape[-2], width)


def apply_rows(factor, index, pieces):
    total = None
    for offset, piece in pieces:
        term = product(columns_of(factor, index, offset, piece.shape[0]), piece)
        total = term if total is None else total + term
    return total


def send(value, axis, shift):
    count = lax.axis_size(axis)
    return lax.ppermute(value, axis, [(i, (i + shift) % count) for i in range(count)])


def swap(value, axis, distance, block):
    count = lax.axis_size(axis)
    outer = count // block
    if outer & (outer - 1):
        pairs = [(i, (i // block + distance) % outer * block + i % block) for i in range(count)]
    else:
        pairs = [(i, (i // block ^ distance) * block + i % block) for i in range(count)]
    return lax.ppermute(value, axis, pairs)


def leaf_exchange(terms):
    groups = lax.axis_size("leaf")
    leaf = lax.axis_index("leaf")
    inner = 2 if groups % 2 == 0 else 1
    outer = groups // inner
    width = terms.shape[1]
    part = terms.shape[0] // groups
    terms = terms.reshape(outer, inner, part, width)
    inside = leaf % inner
    held = [lax.dynamic_index_in_dim(terms, inside, 1, keepdims=False)]
    if inner == 2:
        away = lax.dynamic_index_in_dim(terms, 1 - inside, 1, keepdims=False)
        pairs = [(i, i ^ 1) for i in range(groups)]
        held.append(lax.ppermute(away, "leaf", pairs))
    held = jnp.stack(held, axis=1)
    outside = leaf // inner
    parts = [lax.dynamic_index_in_dim(held, outside, 0, keepdims=False)]
    for distance in range(1, outer):
        if outer & (outer - 1):
            target = lax.rem(outside + distance, outer)
        else:
            target = outside ^ distance
        portion = lax.dynamic_index_in_dim(held, target, 0, keepdims=False)
        parts.append(swap(portion, "leaf", distance, inner))
    return jnp.concatenate(parts, axis=0)


def apply_wide(factor, index, portion):
    members = lax.axis_size("grp")
    me = lax.axis_index("grp")
    rows = portion.shape[-1]
    total = None
    for shift in range(members):
        piece = portion if shift == 0 else send(portion, "grp", shift)
        owner = lax.rem(me - shift + members, members)
        term = contract_last(piece, columns_of(factor, index, owner * rows, rows))
        total = term if total is None else total + term
    return total


def assemble(pieces, order):
    whole = jnp.zeros((order, pieces[0][1].shape[1]), jnp.float32)
    for offset, piece in pieces:
        whole = lax.dynamic_update_slice_in_dim(whole, piece, offset, 0)
    return whole


def on_device(
    rhs_local,
    diag_inv_local,
    sub_local,
    tiles,
    tile_block,
    tile_source,
    tile_count,
    rhs_anc,
    diag_inv_anc,
    sub_anc,
):
    rhs_group = rhs_local[0]
    supernodes = rhs_group.shape[0]
    order = diag_inv_local.shape[-1]
    rhs_count = rhs_group.shape[-1]
    members = lax.axis_size("grp")
    groups = lax.axis_size("leaf")
    me = lax.axis_index("grp")
    leaf = lax.axis_index("leaf")
    rows = order // members
    part = rhs_count // groups

    tiles_mine = tiles[0, 0]
    slots, tile_rows = tiles_mine.shape[:2]
    blocks = jnp.where(
        jnp.arange(slots, dtype=jnp.int32) < tile_count[0, 0], tile_block[0, 0], -1
    ).astype(jnp.float32)
    sources = tile_source[0, 0]

    solved = []
    residual = rhs_group[0]
    chosen = jnp.zeros((slots, order, rhs_count), jnp.float32)
    for current in range(supernodes):
        owned = apply_rows(diag_inv_local, current, ring_gather(residual))
        solved.append(owned)
        pieces = ring_gather(owned)
        if current + 1 < supernodes:
            residual = rhs_group[current + 1] - apply_rows(sub_local, current, pieces)
            whole = assemble(pieces, order)
            chosen = jnp.where((sources == current)[:, None, None], whole[None], chosen)

    early = jnp.einsum(
        "mtk,mkr->rmt", tiles_mine, chosen, precision=high, preferred_element_type=jnp.float32
    ).reshape(rhs_count, slots * tile_rows)
    flat_tiles = tiles_mine.reshape(slots * tile_rows, order)
    late = None
    for offset, piece in pieces:
        columns = lax.dynamic_slice_in_dim(flat_tiles, offset, piece.shape[0], 1)
        term = lax.dot_general(
            piece,
            columns,
            (((0,), (1,)), ((), ())),
            precision=high,
            preferred_element_type=jnp.float32,
        )
        late = term if late is None else late + term
    is_late = jnp.repeat(sources == supernodes - 1, tile_rows)
    terms = jnp.where(is_late[None, :], late, early)
    tag = jnp.zeros((tile_rows,), jnp.float32).at[:slots].set(blocks)
    terms = jnp.concatenate(
        [terms, jnp.broadcast_to(tag[None, :], (rhs_count, tile_rows))], axis=1
    )

    received = leaf_exchange(terms)
    ancestors = rhs_anc.shape[0]
    block_count = ancestors * order // tile_rows
    width = slots * tile_rows
    onehot = (
        received[:, 0, width : width + slots, None]
        == jnp.arange(block_count, dtype=jnp.float32)[None, None, :]
    ).astype(jnp.float32)
    summed = jnp.einsum(
        "gmq,grmt->rqt",
        onehot,
        received[:, :, :width].reshape(groups, part, slots, tile_rows),
        precision=high,
        preferred_element_type=jnp.float32,
    ).reshape(part, ancestors, order)
    own = jnp.zeros((part, ancestors, order), jnp.float32)
    own = lax.dynamic_update_slice(own, jnp.transpose(rhs_anc, (2, 0, 1)), (0, 0, me * rows))
    share = own - summed

    first_share = share[:, 0]
    total = None
    for shift in range(members):
        target = lax.rem(me + shift, members)
        payload = [first_share] + [
            lax.dynamic_slice_in_dim(share[:, a], target * rows, rows, 1)
            for a in range(1, ancestors)
        ]
        payload = jnp.concatenate(payload, axis=1)
        payload = payload if shift == 0 else send(payload, "grp", shift)
        total = payload if total is None else total + payload
    solutions = [contract_last(total[:, :order], diag_inv_anc[0])]
    for ancestor in range(1, ancestors):
        begin = order + (ancestor - 1) * rows
        residual = total[:, begin : begin + rows] - apply_wide(sub_anc, ancestor - 1, solutions[-1])
        solutions.append(apply_wide(diag_inv_anc, ancestor, residual))
    solutions = jnp.stack([jnp.transpose(s) for s in solutions])
    return (jnp.stack(solved)[None], solutions)


def solution(mesh):
    return jax.shard_map(
        on_device,
        mesh=mesh,
        in_specs=(
            P("leaf", None, "grp", None),
            P("leaf", None, "grp", None),
            P("leaf", None, "grp", None),
            P("leaf", "grp", None, None, None),
            P("leaf", "grp", None),
            P("leaf", "grp", None),
            P("leaf", "grp"),
            P(None, "grp", "leaf"),
            P(None, "grp", None),
            P(None, "grp", None),
        ),
        out_specs=(P("leaf", None, "grp", None), P(None, "grp", "leaf")),
        check_vma=False,
    )
```

```python
import jax
import jax.numpy as jnp
from jax import lax
from jax.sharding import PartitionSpec as P

high = lax.Precision.HIGH


def product(left, right):
    return jnp.dot(left, right, precision=high, preferred_element_type=jnp.float32)


def contract_last(left, right):
    return lax.dot_general(
        left,
        right,
        (((left.ndim - 1,), (right.ndim - 1,)), ((), ())),
        precision=high,
        preferred_element_type=jnp.float32,
    )


def send(value, axis, shift):
    count = lax.axis_size(axis)
    return lax.ppermute(value, axis, [(i, (i + shift) % count) for i in range(count)])


def gather_rows(value):
    members = lax.axis_size("grp")
    me = lax.axis_index("grp")
    rows = value.shape[0]
    pieces = [(me * rows, value)]
    for shift in range(1, members):
        owner = lax.rem(me - shift + members, members)
        pieces.append((owner * rows, send(value, "grp", shift)))
    return pieces


def columns_of(factor, index, offset, width):
    lead = factor.ndim - 3
    begin = (0,) * lead + (index, 0, offset)
    size = (1,) * (lead + 1) + (factor.shape[-2], width)
    return lax.dynamic_slice(factor, begin, size).reshape(factor.shape[-2], width)


def apply_rows(factor, index, pieces):
    total = None
    for offset, piece in pieces:
        term = product(columns_of(factor, index, offset, piece.shape[0]), piece)
        total = term if total is None else total + term
    return total


def swap(value, axis, distance, block):
    count = lax.axis_size(axis)
    outer = count // block
    if outer & (outer - 1):
        pairs = [(i, (i // block + distance) % outer * block + i % block) for i in range(count)]
    else:
        pairs = [(i, (i // block ^ distance) * block + i % block) for i in range(count)]
    return lax.ppermute(value, axis, pairs)


def leaf_exchange(terms):
    groups = lax.axis_size("leaf")
    leaf = lax.axis_index("leaf")
    inner = 2 if groups % 2 == 0 else 1
    outer = groups // inner
    width = terms.shape[1]
    part = terms.shape[0] // groups
    terms = terms.reshape(outer, inner, part, width)
    inside = leaf % inner
    held = [lax.dynamic_index_in_dim(terms, inside, 1, keepdims=False)]
    if inner == 2:
        away = lax.dynamic_index_in_dim(terms, 1 - inside, 1, keepdims=False)
        pairs = [(i, i ^ 1) for i in range(groups)]
        held.append(lax.ppermute(away, "leaf", pairs))
    held = jnp.stack(held, axis=1)
    outside = leaf // inner
    parts = [lax.dynamic_index_in_dim(held, outside, 0, keepdims=False)]
    for distance in range(1, outer):
        if outer & (outer - 1):
            target = lax.rem(outside + distance, outer)
        else:
            target = outside ^ distance
        portion = lax.dynamic_index_in_dim(held, target, 0, keepdims=False)
        parts.append(swap(portion, "leaf", distance, inner))
    return jnp.concatenate(parts, axis=0)


def apply_wide(factor, index, portion):
    members = lax.axis_size("grp")
    me = lax.axis_index("grp")
    rows = portion.shape[-1]
    total = None
    for shift in range(members):
        piece = portion if shift == 0 else send(portion, "grp", shift)
        owner = lax.rem(me - shift + members, members)
        term = contract_last(piece, columns_of(factor, index, owner * rows, rows))
        total = term if total is None else total + term
    return total


def assemble(pieces, order):
    whole = jnp.zeros((order, pieces[0][1].shape[1]), jnp.float32)
    for offset, piece in pieces:
        whole = lax.dynamic_update_slice_in_dim(whole, piece, offset, 0)
    return whole


def on_device(
    rhs_local,
    diag_inv_local,
    sub_local,
    tiles,
    tile_block,
    tile_source,
    tile_count,
    rhs_anc,
    diag_inv_anc,
    sub_anc,
):
    rhs_group = rhs_local[0]
    supernodes = rhs_group.shape[0]
    order = diag_inv_local.shape[-1]
    rhs_count = rhs_group.shape[-1]
    members = lax.axis_size("grp")
    groups = lax.axis_size("leaf")
    me = lax.axis_index("grp")
    leaf = lax.axis_index("leaf")
    rows = order // members
    part = rhs_count // groups

    tiles_mine = tiles[0, 0]
    slots, tile_rows = tiles_mine.shape[:2]
    blocks = jnp.where(
        jnp.arange(slots, dtype=jnp.int32) < tile_count[0, 0], tile_block[0, 0], -1
    ).astype(jnp.float32)
    sources = tile_source[0, 0]

    solved = []
    residual = rhs_group[0]
    chosen = jnp.zeros((slots, order, rhs_count), jnp.float32)
    for current in range(supernodes):
        owned = apply_rows(diag_inv_local, current, gather_rows(residual))
        solved.append(owned)
        pieces = gather_rows(owned)
        if current + 1 < supernodes:
            residual = rhs_group[current + 1] - apply_rows(sub_local, current, pieces)
            whole = assemble(pieces, order)
            chosen = jnp.where((sources == current)[:, None, None], whole[None], chosen)

    early = jnp.einsum(
        "mtk,mkr->rmt", tiles_mine, chosen, precision=high, preferred_element_type=jnp.float32
    ).reshape(rhs_count, slots * tile_rows)
    flat_tiles = tiles_mine.reshape(slots * tile_rows, order)
    late = None
    for offset, piece in pieces:
        columns = lax.dynamic_slice_in_dim(flat_tiles, offset, piece.shape[0], 1)
        term = lax.dot_general(
            piece,
            columns,
            (((0,), (1,)), ((), ())),
            precision=high,
            preferred_element_type=jnp.float32,
        )
        late = term if late is None else late + term
    is_late = jnp.repeat(sources == supernodes - 1, tile_rows)
    terms = jnp.where(is_late[None, :], late, early)
    tag = jnp.zeros((tile_rows,), jnp.float32).at[:slots].set(blocks)
    terms = jnp.concatenate(
        [terms, jnp.broadcast_to(tag[None, :], (rhs_count, tile_rows))], axis=1
    )

    received = leaf_exchange(terms)
    ancestors = rhs_anc.shape[0]
    block_count = ancestors * order // tile_rows
    width = slots * tile_rows
    onehot = (
        received[:, 0, width : width + slots, None]
        == jnp.arange(block_count, dtype=jnp.float32)[None, None, :]
    ).astype(jnp.float32)
    summed = jnp.einsum(
        "gmq,grmt->rqt",
        onehot,
        received[:, :, :width].reshape(groups, part, slots, tile_rows),
        precision=high,
        preferred_element_type=jnp.float32,
    ).reshape(part, ancestors, order)
    own = jnp.zeros((part, ancestors, order), jnp.float32)
    own = lax.dynamic_update_slice(own, jnp.transpose(rhs_anc, (2, 0, 1)), (0, 0, me * rows))
    share = own - summed

    first_share = share[:, 0]
    total = None
    for shift in range(members):
        target = lax.rem(me + shift, members)
        payload = [first_share] + [
            lax.dynamic_slice_in_dim(share[:, a], target * rows, rows, 1)
            for a in range(1, ancestors)
        ]
        payload = jnp.concatenate(payload, axis=1)
        payload = payload if shift == 0 else send(payload, "grp", shift)
        total = payload if total is None else total + payload
    solutions = [contract_last(total[:, :order], diag_inv_anc[0])]
    for ancestor in range(1, ancestors):
        begin = order + (ancestor - 1) * rows
        residual = total[:, begin : begin + rows] - apply_wide(sub_anc, ancestor - 1, solutions[-1])
        solutions.append(apply_wide(diag_inv_anc, ancestor, residual))
    solutions = jnp.stack([jnp.transpose(s) for s in solutions])
    return (jnp.stack(solved)[None], solutions)


def solution(mesh):
    return jax.shard_map(
        on_device,
        mesh=mesh,
        in_specs=(
            P("leaf", None, "grp", None),
            P("leaf", None, "grp", None),
            P("leaf", None, "grp", None),
            P("leaf", "grp", None, None, None),
            P("leaf", "grp", None),
            P("leaf", "grp", None),
            P("leaf", "grp"),
            P(None, "grp", "leaf"),
            P(None, "grp", None),
            P(None, "grp", None),
        ),
        out_specs=(P("leaf", None, "grp", None), P(None, "grp", "leaf")),
        check_vma=False,
    )
```

```python
import jax
import jax.numpy as jnp
from jax import lax
from jax.sharding import PartitionSpec as P

high = lax.Precision.HIGH


def contract_last(left, right):
    return lax.dot_general(
        left,
        right,
        (((left.ndim - 1,), (right.ndim - 1,)), ((), ())),
        precision=high,
        preferred_element_type=jnp.float32,
    )


def send(value, axis, shift):
    count = lax.axis_size(axis)
    return lax.ppermute(value, axis, [(i, (i + shift) % count) for i in range(count)])


def gather_rows(value):
    members = lax.axis_size("grp")
    me = lax.axis_index("grp")
    rows = value.shape[1]
    pieces = [(me * rows, value)]
    for shift in range(1, members):
        owner = lax.rem(me - shift + members, members)
        pieces.append((owner * rows, send(value, "grp", shift)))
    return pieces


def columns_of(factor, index, offset, width):
    lead = factor.ndim - 3
    begin = (0,) * lead + (index, 0, offset)
    size = (1,) * (lead + 1) + (factor.shape[-2], width)
    return lax.dynamic_slice(factor, begin, size).reshape(factor.shape[-2], width)


def apply_rows(factor, index, pieces):
    total = None
    for offset, piece in pieces:
        term = contract_last(piece, columns_of(factor, index, offset, piece.shape[1]))
        total = term if total is None else total + term
    return total


def assemble(pieces, order):
    whole = jnp.zeros((pieces[0][1].shape[0], order), jnp.float32)
    for offset, piece in pieces:
        whole = lax.dynamic_update_slice_in_dim(whole, piece, offset, 1)
    return whole


def swap(value, axis, distance, block):
    count = lax.axis_size(axis)
    outer = count // block
    if outer & (outer - 1):
        pairs = [(i, (i // block + distance) % outer * block + i % block) for i in range(count)]
    else:
        pairs = [(i, (i // block ^ distance) * block + i % block) for i in range(count)]
    return lax.ppermute(value, axis, pairs)


def leaf_exchange(terms):
    groups = lax.axis_size("leaf")
    leaf = lax.axis_index("leaf")
    inner = 2 if groups % 2 == 0 else 1
    outer = groups // inner
    width = terms.shape[1]
    part = terms.shape[0] // groups
    terms = terms.reshape(outer, inner, part, width)
    inside = leaf % inner
    held = [lax.dynamic_index_in_dim(terms, inside, 1, keepdims=False)]
    if inner == 2:
        away = lax.dynamic_index_in_dim(terms, 1 - inside, 1, keepdims=False)
        pairs = [(i, i ^ 1) for i in range(groups)]
        held.append(lax.ppermute(away, "leaf", pairs))
    held = jnp.stack(held, axis=1)
    outside = leaf // inner
    parts = [lax.dynamic_index_in_dim(held, outside, 0, keepdims=False)]
    for distance in range(1, outer):
        if outer & (outer - 1):
            target = lax.rem(outside + distance, outer)
        else:
            target = outside ^ distance
        portion = lax.dynamic_index_in_dim(held, target, 0, keepdims=False)
        parts.append(swap(portion, "leaf", distance, inner))
    return jnp.concatenate(parts, axis=0)


def on_device(
    rhs_local,
    diag_inv_local,
    sub_local,
    tiles,
    tile_block,
    tile_source,
    tile_count,
    rhs_anc,
    diag_inv_anc,
    sub_anc,
):
    rhs_group = rhs_local[0]
    supernodes = rhs_group.shape[0]
    order = diag_inv_local.shape[-1]
    rhs_count = rhs_group.shape[-1]
    members = lax.axis_size("grp")
    groups = lax.axis_size("leaf")
    me = lax.axis_index("grp")
    leaf = lax.axis_index("leaf")
    rows = order // members
    part = rhs_count // groups

    tiles_mine = tiles[0, 0]
    slots, tile_rows = tiles_mine.shape[:2]
    blocks = jnp.where(
        jnp.arange(slots, dtype=jnp.int32) < tile_count[0, 0], tile_block[0, 0], -1
    ).astype(jnp.float32)
    sources = tile_source[0, 0]

    streams = 2 if rhs_count % 16 == 0 else 1
    depth = rhs_count // streams
    rhs_wide = jnp.swapaxes(rhs_group, 1, 2)
    split = [rhs_wide[:, i * depth : (i + 1) * depth] for i in range(streams)]
    solved = []
    residuals = [portion[0] for portion in split]
    chosen = [jnp.zeros((slots, depth, order), jnp.float32) for _ in range(streams)]
    for current in range(supernodes):
        owned = [apply_rows(diag_inv_local, current, gather_rows(r)) for r in residuals]
        solved.append(jnp.transpose(jnp.concatenate(owned, axis=0)))
        held = [gather_rows(value) for value in owned]
        if current + 1 < supernodes:
            residuals = [
                portion[current + 1] - apply_rows(sub_local, current, pieces)
                for portion, pieces in zip(split, held)
            ]
            chosen = [
                jnp.where((sources == current)[:, None, None], assemble(pieces, order)[None], old)
                for pieces, old in zip(held, chosen)
            ]

    flat_tiles = tiles_mine.reshape(slots * tile_rows, order)
    early = []
    late = []
    for pieces, picked in zip(held, chosen):
        early.append(
            jnp.concatenate(
                [contract_last(picked[m], tiles_mine[m]) for m in range(slots)], axis=1
            )
        )
        late.append(apply_rows(flat_tiles[None], 0, pieces))
    early = jnp.concatenate(early, axis=0)
    late = jnp.concatenate(late, axis=0)
    is_late = jnp.repeat(sources == supernodes - 1, tile_rows)
    terms = jnp.where(is_late[None, :], late, early)
    tag = jnp.zeros((tile_rows,), jnp.float32).at[:slots].set(blocks)
    terms = jnp.concatenate(
        [terms, jnp.broadcast_to(tag[None, :], (rhs_count, tile_rows))], axis=1
    )

    received = leaf_exchange(terms)
    ancestors = rhs_anc.shape[0]
    block_count = ancestors * order // tile_rows
    width = slots * tile_rows
    onehot = (
        received[:, 0, width : width + slots, None]
        == jnp.arange(block_count, dtype=jnp.float32)[None, None, :]
    ).astype(jnp.float32)
    summed = jnp.einsum(
        "gmq,grmt->rqt",
        onehot,
        received[:, :, :width].reshape(groups, part, slots, tile_rows),
        precision=high,
        preferred_element_type=jnp.float32,
    ).reshape(part, ancestors, order)
    own = jnp.zeros((part, ancestors, order), jnp.float32)
    own = lax.dynamic_update_slice(own, jnp.transpose(rhs_anc, (2, 0, 1)), (0, 0, me * rows))
    share = own - summed

    first_share = share[:, 0]
    total = None
    for shift in range(members):
        target = lax.rem(me + shift, members)
        payload = [first_share] + [
            lax.dynamic_slice_in_dim(share[:, a], target * rows, rows, 1)
            for a in range(1, ancestors)
        ]
        payload = jnp.concatenate(payload, axis=1)
        payload = payload if shift == 0 else send(payload, "grp", shift)
        total = payload if total is None else total + payload
    solutions = [contract_last(total[:, :order], diag_inv_anc[0])]
    for ancestor in range(1, ancestors):
        begin = order + (ancestor - 1) * rows
        residual = total[:, begin : begin + rows] - apply_rows(
            sub_anc, ancestor - 1, gather_rows(solutions[-1])
        )
        solutions.append(apply_rows(diag_inv_anc, ancestor, gather_rows(residual)))
    solutions = jnp.stack([jnp.transpose(s) for s in solutions])
    return (jnp.stack(solved)[None], solutions)


def solution(mesh):
    return jax.shard_map(
        on_device,
        mesh=mesh,
        in_specs=(
            P("leaf", None, "grp", None),
            P("leaf", None, "grp", None),
            P("leaf", None, "grp", None),
            P("leaf", "grp", None, None, None),
            P("leaf", "grp", None),
            P("leaf", "grp", None),
            P("leaf", "grp"),
            P(None, "grp", "leaf"),
            P(None, "grp", None),
            P(None, "grp", None),
        ),
        out_specs=(P("leaf", None, "grp", None), P(None, "grp", "leaf")),
        check_vma=False,
    )
```

```python
import jax
import jax.numpy as jnp
from jax import lax
from jax.sharding import PartitionSpec as P

high = lax.Precision.HIGH


def contract_last(left, right):
    return lax.dot_general(
        left,
        right,
        (((left.ndim - 1,), (right.ndim - 1,)), ((), ())),
        precision=high,
        preferred_element_type=jnp.float32,
    )


def send(value, axis, shift):
    count = lax.axis_size(axis)
    return lax.ppermute(value, axis, [(i, (i + shift) % count) for i in range(count)])


def gather_rows(value):
    members = lax.axis_size("grp")
    me = lax.axis_index("grp")
    rows = value.shape[1]
    pieces = [(me * rows, value)]
    if members == 4:
        beside = lax.ppermute(value, "grp", [(0, 1), (1, 0), (2, 3), (3, 2)])
        across = lax.ppermute(value, "grp", [(1, 2), (2, 1), (0, 3), (3, 0)])
        inward = lax.ppermute(beside, "grp", [(1, 2), (2, 1)])
        outward = lax.ppermute(across, "grp", [(1, 0), (2, 3)])
        pieces.append(((me ^ 1) * rows, beside))
        pieces.append(((me ^ 3) * rows, across))
        pieces.append(((me ^ 2) * rows, inward + outward))
        return pieces
    for shift in range(1, members):
        owner = lax.rem(me - shift + members, members)
        pieces.append((owner * rows, send(value, "grp", shift)))
    return pieces


def columns_of(factor, index, offset, width):
    lead = factor.ndim - 3
    begin = (0,) * lead + (index, 0, offset)
    size = (1,) * (lead + 1) + (factor.shape[-2], width)
    return lax.dynamic_slice(factor, begin, size).reshape(factor.shape[-2], width)


def apply_rows(factor, index, pieces):
    total = None
    for offset, piece in pieces:
        term = contract_last(piece, columns_of(factor, index, offset, piece.shape[1]))
        total = term if total is None else total + term
    return total


def assemble(pieces, order):
    whole = jnp.zeros((pieces[0][1].shape[0], order), jnp.float32)
    for offset, piece in pieces:
        whole = lax.dynamic_update_slice_in_dim(whole, piece, offset, 1)
    return whole


def swap(value, axis, distance, block):
    count = lax.axis_size(axis)
    outer = count // block
    if outer & (outer - 1):
        pairs = [(i, (i // block + distance) % outer * block + i % block) for i in range(count)]
    else:
        pairs = [(i, (i // block ^ distance) * block + i % block) for i in range(count)]
    return lax.ppermute(value, axis, pairs)


def leaf_exchange(terms):
    groups = lax.axis_size("leaf")
    leaf = lax.axis_index("leaf")
    inner = 2 if groups % 2 == 0 else 1
    outer = groups // inner
    width = terms.shape[1]
    part = terms.shape[0] // groups
    terms = terms.reshape(outer, inner, part, width)
    inside = leaf % inner
    held = [lax.dynamic_index_in_dim(terms, inside, 1, keepdims=False)]
    if inner == 2:
        away = lax.dynamic_index_in_dim(terms, 1 - inside, 1, keepdims=False)
        pairs = [(i, i ^ 1) for i in range(groups)]
        held.append(lax.ppermute(away, "leaf", pairs))
    held = jnp.stack(held, axis=1)
    outside = leaf // inner
    parts = [lax.dynamic_index_in_dim(held, outside, 0, keepdims=False)]
    for distance in range(1, outer):
        if outer & (outer - 1):
            target = lax.rem(outside + distance, outer)
        else:
            target = outside ^ distance
        portion = lax.dynamic_index_in_dim(held, target, 0, keepdims=False)
        parts.append(swap(portion, "leaf", distance, inner))
    return jnp.concatenate(parts, axis=0)


def on_device(
    rhs_local,
    diag_inv_local,
    sub_local,
    tiles,
    tile_block,
    tile_source,
    tile_count,
    rhs_anc,
    diag_inv_anc,
    sub_anc,
):
    rhs_group = rhs_local[0]
    supernodes = rhs_group.shape[0]
    order = diag_inv_local.shape[-1]
    rhs_count = rhs_group.shape[-1]
    members = lax.axis_size("grp")
    groups = lax.axis_size("leaf")
    me = lax.axis_index("grp")
    leaf = lax.axis_index("leaf")
    rows = order // members
    part = rhs_count // groups

    tiles_mine = tiles[0, 0]
    slots, tile_rows = tiles_mine.shape[:2]
    blocks = jnp.where(
        jnp.arange(slots, dtype=jnp.int32) < tile_count[0, 0], tile_block[0, 0], -1
    ).astype(jnp.float32)
    sources = tile_source[0, 0]

    streams = 2 if rhs_count % 16 == 0 else 1
    depth = rhs_count // streams
    rhs_wide = jnp.swapaxes(rhs_group, 1, 2)
    split = [rhs_wide[:, i * depth : (i + 1) * depth] for i in range(streams)]
    solved = []
    residuals = [portion[0] for portion in split]
    chosen = [jnp.zeros((slots, depth, order), jnp.float32) for _ in range(streams)]
    for current in range(supernodes):
        owned = [apply_rows(diag_inv_local, current, gather_rows(r)) for r in residuals]
        solved.append(jnp.transpose(jnp.concatenate(owned, axis=0)))
        held = [gather_rows(value) for value in owned]
        if current + 1 < supernodes:
            residuals = [
                portion[current + 1] - apply_rows(sub_local, current, pieces)
                for portion, pieces in zip(split, held)
            ]
            chosen = [
                jnp.where((sources == current)[:, None, None], assemble(pieces, order)[None], old)
                for pieces, old in zip(held, chosen)
            ]

    flat_tiles = tiles_mine.reshape(slots * tile_rows, order)
    early = []
    late = []
    for pieces, picked in zip(held, chosen):
        early.append(
            jnp.concatenate(
                [contract_last(picked[m], tiles_mine[m]) for m in range(slots)], axis=1
            )
        )
        late.append(apply_rows(flat_tiles[None], 0, pieces))
    early = jnp.concatenate(early, axis=0)
    late = jnp.concatenate(late, axis=0)
    is_late = jnp.repeat(sources == supernodes - 1, tile_rows)
    terms = jnp.where(is_late[None, :], late, early)
    tag = jnp.zeros((tile_rows,), jnp.float32).at[:slots].set(blocks)
    terms = jnp.concatenate(
        [terms, jnp.broadcast_to(tag[None, :], (rhs_count, tile_rows))], axis=1
    )

    received = leaf_exchange(terms)
    ancestors = rhs_anc.shape[0]
    block_count = ancestors * order // tile_rows
    width = slots * tile_rows
    onehot = (
        received[:, 0, width : width + slots, None]
        == jnp.arange(block_count, dtype=jnp.float32)[None, None, :]
    ).astype(jnp.float32)
    summed = jnp.einsum(
        "gmq,grmt->rqt",
        onehot,
        received[:, :, :width].reshape(groups, part, slots, tile_rows),
        precision=high,
        preferred_element_type=jnp.float32,
    ).reshape(part, ancestors, order)
    own = jnp.zeros((part, ancestors, order), jnp.float32)
    own = lax.dynamic_update_slice(own, jnp.transpose(rhs_anc, (2, 0, 1)), (0, 0, me * rows))
    share = own - summed

    first_share = share[:, 0]
    total = None
    for shift in range(members):
        target = lax.rem(me + shift, members)
        payload = [first_share] + [
            lax.dynamic_slice_in_dim(share[:, a], target * rows, rows, 1)
            for a in range(1, ancestors)
        ]
        payload = jnp.concatenate(payload, axis=1)
        payload = payload if shift == 0 else send(payload, "grp", shift)
        total = payload if total is None else total + payload
    solutions = [contract_last(total[:, :order], diag_inv_anc[0])]
    for ancestor in range(1, ancestors):
        begin = order + (ancestor - 1) * rows
        residual = total[:, begin : begin + rows] - apply_rows(
            sub_anc, ancestor - 1, gather_rows(solutions[-1])
        )
        solutions.append(apply_rows(diag_inv_anc, ancestor, gather_rows(residual)))
    solutions = jnp.stack([jnp.transpose(s) for s in solutions])
    return (jnp.stack(solved)[None], solutions)


def solution(mesh):
    return jax.shard_map(
        on_device,
        mesh=mesh,
        in_specs=(
            P("leaf", None, "grp", None),
            P("leaf", None, "grp", None),
            P("leaf", None, "grp", None),
            P("leaf", "grp", None, None, None),
            P("leaf", "grp", None),
            P("leaf", "grp", None),
            P("leaf", "grp"),
            P(None, "grp", "leaf"),
            P(None, "grp", None),
            P(None, "grp", None),
        ),
        out_specs=(P("leaf", None, "grp", None), P(None, "grp", "leaf")),
        check_vma=False,
    )
```

```python
import jax
import jax.numpy as jnp
from jax import lax
from jax.sharding import PartitionSpec as P

high = lax.Precision.HIGH


def contract_last(left, right):
    return lax.dot_general(
        left,
        right,
        (((left.ndim - 1,), (right.ndim - 1,)), ((), ())),
        precision=high,
        preferred_element_type=jnp.float32,
    )


def partner(index, distance, count):
    if count & (count - 1):
        return lax.rem(index - distance + 2 * count, count)
    return index ^ abs(distance)


def send(value, axis, distance):
    count = lax.axis_size(axis)
    if count & (count - 1):
        pairs = [(i, (i + distance) % count) for i in range(count)]
    else:
        pairs = [(i, i ^ distance) for i in range(count)]
    return lax.ppermute(value, axis, pairs)


def gather_rows(value):
    members = lax.axis_size("grp")
    me = lax.axis_index("grp")
    rows = value.shape[1]
    pieces = [(me * rows, value)]
    for distance in range(1, members):
        owner = partner(me, distance, members)
        pieces.append((owner * rows, send(value, "grp", distance)))
    return pieces


def columns_of(factor, index, offset, width):
    lead = factor.ndim - 3
    begin = (0,) * lead + (index, 0, offset)
    size = (1,) * (lead + 1) + (factor.shape[-2], width)
    return lax.dynamic_slice(factor, begin, size).reshape(factor.shape[-2], width)


def apply_rows(factor, index, pieces):
    total = None
    for offset, piece in pieces:
        term = contract_last(piece, columns_of(factor, index, offset, piece.shape[1]))
        total = term if total is None else total + term
    return total


def assemble(pieces, order):
    whole = jnp.zeros((pieces[0][1].shape[0], order), jnp.float32)
    for offset, piece in pieces:
        whole = lax.dynamic_update_slice_in_dim(whole, piece, offset, 1)
    return whole


def swap(value, axis, distance, block):
    count = lax.axis_size(axis)
    outer = count // block
    if outer & (outer - 1):
        pairs = [(i, (i // block + distance) % outer * block + i % block) for i in range(count)]
    else:
        pairs = [(i, (i // block ^ distance) * block + i % block) for i in range(count)]
    return lax.ppermute(value, axis, pairs)


def leaf_exchange(terms):
    groups = lax.axis_size("leaf")
    leaf = lax.axis_index("leaf")
    inner = 2 if groups % 2 == 0 else 1
    outer = groups // inner
    width = terms.shape[1]
    part = terms.shape[0] // groups
    terms = terms.reshape(outer, inner, part, width)
    inside = leaf % inner
    held = [lax.dynamic_index_in_dim(terms, inside, 1, keepdims=False)]
    if inner == 2:
        away = lax.dynamic_index_in_dim(terms, 1 - inside, 1, keepdims=False)
        pairs = [(i, i ^ 1) for i in range(groups)]
        held.append(lax.ppermute(away, "leaf", pairs))
    held = jnp.stack(held, axis=1)
    outside = leaf // inner
    parts = [lax.dynamic_index_in_dim(held, outside, 0, keepdims=False)]
    for distance in range(1, outer):
        if outer & (outer - 1):
            target = lax.rem(outside + distance, outer)
        else:
            target = outside ^ distance
        portion = lax.dynamic_index_in_dim(held, target, 0, keepdims=False)
        parts.append(swap(portion, "leaf", distance, inner))
    return jnp.concatenate(parts, axis=0)


def on_device(
    rhs_local,
    diag_inv_local,
    sub_local,
    tiles,
    tile_block,
    tile_source,
    tile_count,
    rhs_anc,
    diag_inv_anc,
    sub_anc,
):
    rhs_group = rhs_local[0]
    supernodes = rhs_group.shape[0]
    order = diag_inv_local.shape[-1]
    rhs_count = rhs_group.shape[-1]
    members = lax.axis_size("grp")
    groups = lax.axis_size("leaf")
    me = lax.axis_index("grp")
    leaf = lax.axis_index("leaf")
    rows = order // members
    part = rhs_count // groups

    tiles_mine = tiles[0, 0]
    slots, tile_rows = tiles_mine.shape[:2]
    blocks = jnp.where(
        jnp.arange(slots, dtype=jnp.int32) < tile_count[0, 0], tile_block[0, 0], -1
    ).astype(jnp.float32)
    sources = tile_source[0, 0]

    streams = 2 if rhs_count % 16 == 0 else 1
    depth = rhs_count // streams
    rhs_wide = jnp.swapaxes(rhs_group, 1, 2)
    split = [rhs_wide[:, i * depth : (i + 1) * depth] for i in range(streams)]
    solved = []
    residuals = [portion[0] for portion in split]
    chosen = [jnp.zeros((slots, depth, order), jnp.float32) for _ in range(streams)]
    for current in range(supernodes):
        owned = [apply_rows(diag_inv_local, current, gather_rows(r)) for r in residuals]
        solved.append(jnp.transpose(jnp.concatenate(owned, axis=0)))
        held = [gather_rows(value) for value in owned]
        if current + 1 < supernodes:
            residuals = [
                portion[current + 1] - apply_rows(sub_local, current, pieces)
                for portion, pieces in zip(split, held)
            ]
            chosen = [
                jnp.where((sources == current)[:, None, None], assemble(pieces, order)[None], old)
                for pieces, old in zip(held, chosen)
            ]

    flat_tiles = tiles_mine.reshape(slots * tile_rows, order)
    early = []
    late = []
    for pieces, picked in zip(held, chosen):
        early.append(
            jnp.concatenate(
                [contract_last(picked[m], tiles_mine[m]) for m in range(slots)], axis=1
            )
        )
        late.append(apply_rows(flat_tiles[None], 0, pieces))
    early = jnp.concatenate(early, axis=0)
    late = jnp.concatenate(late, axis=0)
    is_late = jnp.repeat(sources == supernodes - 1, tile_rows)
    terms = jnp.where(is_late[None, :], late, early)
    tag = jnp.zeros((tile_rows,), jnp.float32).at[:slots].set(blocks)
    terms = jnp.concatenate(
        [terms, jnp.broadcast_to(tag[None, :], (rhs_count, tile_rows))], axis=1
    )

    received = leaf_exchange(terms)
    ancestors = rhs_anc.shape[0]
    block_count = ancestors * order // tile_rows
    width = slots * tile_rows
    onehot = (
        received[:, 0, width : width + slots, None]
        == jnp.arange(block_count, dtype=jnp.float32)[None, None, :]
    ).astype(jnp.float32)
    summed = jnp.einsum(
        "gmq,grmt->rqt",
        onehot,
        received[:, :, :width].reshape(groups, part, slots, tile_rows),
        precision=high,
        preferred_element_type=jnp.float32,
    ).reshape(part, ancestors, order)
    own = jnp.zeros((part, ancestors, order), jnp.float32)
    own = lax.dynamic_update_slice(own, jnp.transpose(rhs_anc, (2, 0, 1)), (0, 0, me * rows))
    share = own - summed

    first_share = share[:, 0]
    total = None
    for distance in range(members):
        target = partner(me, -distance, members) if distance else me
        payload = [first_share] + [
            lax.dynamic_slice_in_dim(share[:, a], target * rows, rows, 1)
            for a in range(1, ancestors)
        ]
        payload = jnp.concatenate(payload, axis=1)
        payload = send(payload, "grp", distance) if distance else payload
        total = payload if total is None else total + payload
    solutions = [contract_last(total[:, :order], diag_inv_anc[0])]
    for ancestor in range(1, ancestors):
        begin = order + (ancestor - 1) * rows
        residual = total[:, begin : begin + rows] - apply_rows(
            sub_anc, ancestor - 1, gather_rows(solutions[-1])
        )
        solutions.append(apply_rows(diag_inv_anc, ancestor, gather_rows(residual)))
    solutions = jnp.stack([jnp.transpose(s) for s in solutions])
    return (jnp.stack(solved)[None], solutions)


def solution(mesh):
    return jax.shard_map(
        on_device,
        mesh=mesh,
        in_specs=(
            P("leaf", None, "grp", None),
            P("leaf", None, "grp", None),
            P("leaf", None, "grp", None),
            P("leaf", "grp", None, None, None),
            P("leaf", "grp", None),
            P("leaf", "grp", None),
            P("leaf", "grp"),
            P(None, "grp", "leaf"),
            P(None, "grp", None),
            P(None, "grp", None),
        ),
        out_specs=(P("leaf", None, "grp", None), P(None, "grp", "leaf")),
        check_vma=False,
    )
```

```python
import jax
import jax.numpy as jnp
from jax import lax
from jax.experimental import pallas as pl
from jax.experimental.pallas import tpu as pltpu
from jax.sharding import PartitionSpec as P

high = lax.Precision.HIGH


def contract_last(left, right):
    return lax.dot_general(
        left,
        right,
        (((left.ndim - 1,), (right.ndim - 1,)), ((), ())),
        precision=high,
        preferred_element_type=jnp.float32,
    )


def partner(index, distance, count):
    if count & (count - 1):
        return lax.rem(index - distance + 2 * count, count)
    return index ^ abs(distance)


def send(value, axis, distance):
    count = lax.axis_size(axis)
    if count & (count - 1):
        pairs = [(i, (i + distance) % count) for i in range(count)]
    else:
        pairs = [(i, i ^ distance) for i in range(count)]
    return lax.ppermute(value, axis, pairs)


def gather_rows(value):
    members = lax.axis_size("grp")
    me = lax.axis_index("grp")
    rows = value.shape[1]
    pieces = [(me * rows, value)]
    for distance in range(1, members):
        owner = partner(me, distance, members)
        pieces.append((owner * rows, send(value, "grp", distance)))
    return pieces


def columns_of(factor, index, offset, width):
    lead = factor.ndim - 3
    begin = (0,) * lead + (index, 0, offset)
    size = (1,) * (lead + 1) + (factor.shape[-2], width)
    return lax.dynamic_slice(factor, begin, size).reshape(factor.shape[-2], width)


def apply_rows(factor, index, pieces):
    total = None
    for offset, piece in pieces:
        term = contract_last(piece, columns_of(factor, index, offset, piece.shape[1]))
        total = term if total is None else total + term
    return total


def assemble(pieces, order):
    whole = jnp.zeros((pieces[0][1].shape[0], order), jnp.float32)
    for offset, piece in pieces:
        whole = lax.dynamic_update_slice_in_dim(whole, piece, offset, 1)
    return whole


def swap(value, axis, distance, block):
    count = lax.axis_size(axis)
    outer = count // block
    if outer & (outer - 1):
        pairs = [(i, (i // block + distance) % outer * block + i % block) for i in range(count)]
    else:
        pairs = [(i, (i // block ^ distance) * block + i % block) for i in range(count)]
    return lax.ppermute(value, axis, pairs)


VMEM = pl.BlockSpec(memory_space=pltpu.VMEM)
SMEM = pl.BlockSpec(memory_space=pltpu.SMEM)


def local_kernel(body, outs, operands, specs=None, flops=0, scratch=()):
    size = sum(o.size * o.dtype.itemsize for o in list(outs) + list(operands))
    return pl.pallas_call(
        body,
        out_shape=list(outs),
        in_specs=specs or [VMEM] * len(operands),
        out_specs=[VMEM] * len(outs),
        scratch_shapes=list(scratch),
        cost_estimate=pl.CostEstimate(flops=flops, bytes_accessed=size, transcendentals=0),
    )(*operands)


def float_array(*shape):
    return jax.ShapeDtypeStruct(shape, jnp.float32)


def high_low(value):
    top = value.astype(jnp.bfloat16)
    return top, (value - top.astype(jnp.float32)).astype(jnp.bfloat16)


def split_product(left, top, rest):
    def dot(x, y):
        return lax.dot_general(
            x, y, (((1,), (1,)), ((), ())), preferred_element_type=jnp.float32
        )

    left_top, left_rest = high_low(left)
    return dot(left_top, top) + (dot(left_top, rest) + dot(left_rest, top))


def leaf_shape():
    groups = lax.axis_size("leaf")
    inner = 2 if groups % 2 == 0 else 1
    return groups // inner, inner


def pack_terms(early, late, sources, blocks, count, last, tile_rows):
    outer, inner = leaf_shape()
    slots = sources.shape[-1]
    depth = early[0].shape[0]
    streams = len(early)
    part = depth * streams // (outer * inner)
    width = (slots + 1) * tile_rows

    def body(*refs):
        early_refs, late_refs = refs[:streams], refs[streams : 2 * streams]
        source_ref, block_ref, count_ref = refs[2 * streams : 2 * streams + 3]
        outs = refs[2 * streams + 3 : -1]
        terms = refs[-1]
        lanes = lax.broadcasted_iota(jnp.int32, (depth, tile_rows), 1)
        tag = jnp.full((depth, tile_rows), -1.0, jnp.float32)
        for m in range(slots):
            value = jnp.where(m < count_ref[0, 0], block_ref[0, 0, m], -1).astype(jnp.float32)
            tag = jnp.where(lanes == m, value, tag)
        for i in range(streams):
            rows = slice(i * depth, (i + 1) * depth)
            for m in range(slots):
                at = slice(m * tile_rows, (m + 1) * tile_rows)
                terms[rows, at] = jnp.where(
                    source_ref[0, 0, m] == last, late_refs[i][:, at], early_refs[i][:, at]
                )
            terms[rows, slots * tile_rows :] = tag
        inside = lax.rem(lax.axis_index("leaf"), inner)
        for o in range(outer):
            cut = [
                terms[(o * inner + i) * part : (o * inner + i + 1) * part, :]
                for i in range(inner)
            ]
            for i in range(inner):
                outs[i][o] = jnp.where(inside == 0, cut[i], cut[inner - 1 - i])

    return local_kernel(
        body,
        [float_array(outer, part, width)] * inner,
        [*early, *late, sources, blocks, count],
        [VMEM] * (2 * streams) + [SMEM] * 3,
        scratch=[pltpu.VMEM((streams * depth, width), jnp.float32)],
    )


def leaf_exchange(packed):
    outer, inner = leaf_shape()
    part, width = packed[0].shape[1:]
    held = [packed[0]]
    if inner == 2:
        pairs = [(i, i ^ 1) for i in range(outer * inner)]
        held.append(lax.ppermute(packed[1], "leaf", pairs))

    def body(*refs):
        outside = lax.div(lax.axis_index("leaf"), inner)
        for distance in range(outer):
            target = partner(outside, -distance, outer) if distance else outside
            for i in range(inner):
                refs[inner + distance][i] = refs[i][target]

    portions = local_kernel(body, [float_array(inner, part, width)] * outer, held)
    return [portions[0]] + [
        swap(portions[distance], "leaf", distance, inner) for distance in range(1, outer)
    ]


def share_out(received, rhs_turned, order, slots, tile_rows):
    members = lax.axis_size("grp")
    ancestors, part, rows = rhs_turned.shape
    inner = received[0].shape[0]
    block_count = ancestors * order // tile_rows
    width = order + (ancestors - 1) * rows

    def body(*refs):
        sources = refs[: len(received)]
        rhs_ref = refs[len(received)]
        outs = refs[len(received) + 1 : -1]
        share = refs[-1]
        me = lax.axis_index("grp")
        totals = [jnp.zeros((part, tile_rows), jnp.float32) for _ in range(block_count)]
        for source in sources:
            for i in range(inner):
                for m in range(slots):
                    tile = source[i, :, m * tile_rows : (m + 1) * tile_rows]
                    tag = source[i, :, slots * tile_rows + m : slots * tile_rows + m + 1]
                    tag = jnp.broadcast_to(tag, tile.shape)
                    for q in range(block_count):
                        totals[q] = totals[q] + jnp.where(tag == float(q), tile, 0.0)
        for q in range(block_count):
            share[:, q * tile_rows : (q + 1) * tile_rows] = -totals[q]
        for a in range(ancestors):
            for j in range(members):
                at = slice(a * order + j * rows, a * order + (j + 1) * rows)
                share[:, at] = share[:, at] + jnp.where(me == j, rhs_ref[a], 0.0)
        for distance in range(members):
            target = partner(me, -distance, members) if distance else me
            out = outs[distance]
            out[:, :order] = share[:, :order]
            for a in range(1, ancestors):
                value = jnp.zeros((part, rows), jnp.float32)
                for j in range(members):
                    at = slice(a * order + j * rows, a * order + (j + 1) * rows)
                    value = jnp.where(target == j, share[:, at], value)
                out[:, order + (a - 1) * rows : order + a * rows] = value

    return local_kernel(
        body,
        [float_array(part, width)] * members,
        [*received, rhs_turned],
        scratch=[pltpu.VMEM((part, ancestors * order), jnp.float32)],
    )


def split_factors(factors, after):
    count = len(factors)

    def body(*refs):
        for i in range(count):
            top, rest = high_low(refs[i][...])
            refs[count + 1 + 2 * i][...] = top
            refs[count + 2 + 2 * i][...] = rest

    outs = []
    for factor in factors:
        outs += [jax.ShapeDtypeStruct(factor.shape, jnp.bfloat16)] * 2
    return local_kernel(
        body,
        outs,
        [*factors, after],
        [VMEM] * count + [pl.BlockSpec(memory_space=pl.ANY)],
        flops=4 * sum(f.size for f in factors),
    )


def solve_first(payloads, top, rest):
    part, width = payloads[0].shape
    rows, order = top.shape[1:]

    def body(*refs):
        sums = refs[: len(payloads)]
        top_ref, rest_ref, out, left = refs[len(payloads) :]
        total = sums[0][...]
        for ref in sums[1:]:
            total = total + ref[...]
        out[...] = split_product(total[:, :order], top_ref[0], rest_ref[0])
        left[...] = total[:, order:]

    return local_kernel(
        body,
        [float_array(part, rows), float_array(part, width - order)],
        [*payloads, top, rest],
        flops=6 * part * rows * order,
    )


def apply_split(pieces, top, rest, index, base=None, begin=0):
    members = lax.axis_size("grp")
    part, width = pieces[0].shape
    rows, order = top.shape[1:]
    extra = [] if base is None else [base]

    def body(*refs):
        held = refs[:members]
        top_ref, rest_ref = refs[members : members + 2]
        out, whole = refs[-2:]
        me = lax.axis_index("grp")
        for j in range(members):
            value = jnp.zeros((part, width), jnp.float32)
            for distance in range(members):
                owner = partner(me, distance, members) if distance else me
                value = jnp.where(owner == j, held[distance][...], value)
            whole[:, j * width : (j + 1) * width] = value
        result = split_product(whole[...], top_ref[index], rest_ref[index])
        if extra:
            result = refs[members + 2][:, begin : begin + rows] - result
        out[...] = result

    return local_kernel(
        body,
        [float_array(part, rows)],
        [*pieces, top, rest, *extra],
        flops=6 * part * rows * order,
        scratch=[pltpu.VMEM((part, order), jnp.float32)],
    )[0]


def on_device(
    rhs_local,
    diag_inv_local,
    sub_local,
    tiles,
    tile_block,
    tile_source,
    tile_count,
    rhs_anc,
    diag_inv_anc,
    sub_anc,
):
    rhs_group = rhs_local[0]
    supernodes = rhs_group.shape[0]
    order = diag_inv_local.shape[-1]
    rhs_count = rhs_group.shape[-1]
    members = lax.axis_size("grp")
    rows = order // members

    tiles_mine = tiles[0, 0]
    slots, tile_rows = tiles_mine.shape[:2]
    sources = tile_source[0, 0]

    streams = 2 if rhs_count % 16 == 0 else 1
    depth = rhs_count // streams
    first_rhs = jnp.transpose(lax.optimization_barrier(rhs_group[0]))
    first_factor = lax.optimization_barrier(diag_inv_local[0, 0])
    rhs_wide = jnp.swapaxes(rhs_group[1:], 1, 2)
    split = [rhs_wide[:, i * depth : (i + 1) * depth] for i in range(streams)]
    solved = []
    residuals = [first_rhs[i * depth : (i + 1) * depth] for i in range(streams)]
    chosen = [jnp.zeros((slots, depth, order), jnp.float32) for _ in range(streams)]
    for current in range(supernodes):
        factor, index = (diag_inv_local, current) if current else (first_factor[None], 0)
        owned = [apply_rows(factor, index, gather_rows(r)) for r in residuals]
        solved.append(jnp.transpose(jnp.concatenate(owned, axis=0)))
        held = [gather_rows(value) for value in owned]
        if current + 1 < supernodes:
            residuals = [
                portion[current] - apply_rows(sub_local, current, pieces)
                for portion, pieces in zip(split, held)
            ]
            chosen = [
                jnp.where((sources == current)[:, None, None], assemble(pieces, order)[None], old)
                for pieces, old in zip(held, chosen)
            ]

    flat_tiles = tiles_mine.reshape(slots * tile_rows, order)
    early = []
    late = []
    for pieces, picked in zip(held, chosen):
        early.append(
            jnp.concatenate(
                [contract_last(picked[m], tiles_mine[m]) for m in range(slots)], axis=1
            )
        )
        late.append(apply_rows(flat_tiles[None], 0, pieces))
    packed = pack_terms(
        early, late, tile_source, tile_block, tile_count, supernodes - 1, tile_rows
    )
    received = leaf_exchange(packed)
    shares = share_out(received, jnp.swapaxes(rhs_anc, 1, 2), order, slots, tile_rows)
    payloads = [shares[0]] + [send(shares[d], "grp", d) for d in range(1, members)]
    inverse_top, inverse_rest, below_top, below_rest = split_factors(
        [diag_inv_anc, sub_anc], shares[0]
    )
    solution, left = solve_first(payloads, inverse_top, inverse_rest)
    solutions = [solution]
    for ancestor in range(1, rhs_anc.shape[0]):
        pieces = [piece for _, piece in gather_rows(solutions[-1])]
        residual = apply_split(
            pieces, below_top, below_rest, ancestor - 1, left, (ancestor - 1) * rows
        )
        pieces = [piece for _, piece in gather_rows(residual)]
        solutions.append(apply_split(pieces, inverse_top, inverse_rest, ancestor))
    solutions = jnp.swapaxes(jnp.stack(solutions), 1, 2)
    return (jnp.stack(solved)[None], solutions)


def solution(mesh):
    return jax.shard_map(
        on_device,
        mesh=mesh,
        in_specs=(
            P("leaf", None, "grp", None),
            P("leaf", None, "grp", None),
            P("leaf", None, "grp", None),
            P("leaf", "grp", None, None, None),
            P("leaf", "grp", None),
            P("leaf", "grp", None),
            P("leaf", "grp"),
            P(None, "grp", "leaf"),
            P(None, "grp", None),
            P(None, "grp", None),
        ),
        out_specs=(P("leaf", None, "grp", None), P(None, "grp", "leaf")),
        check_vma=False,
    )
```

```python
import jax
import jax.numpy as jnp
from jax import lax
from jax.experimental import pallas as pl
from jax.experimental.pallas import tpu as pltpu
from jax.sharding import PartitionSpec as P

high = lax.Precision.HIGH


def contract_last(left, right):
    return lax.dot_general(
        left,
        right,
        (((left.ndim - 1,), (right.ndim - 1,)), ((), ())),
        precision=high,
        preferred_element_type=jnp.float32,
    )


def partner(index, distance, count):
    if count & (count - 1):
        return lax.rem(index - distance + 2 * count, count)
    return index ^ abs(distance)


def send(value, axis, distance):
    count = lax.axis_size(axis)
    if count & (count - 1):
        pairs = [(i, (i + distance) % count) for i in range(count)]
    else:
        pairs = [(i, i ^ distance) for i in range(count)]
    return lax.ppermute(value, axis, pairs)


def gather_rows(value):
    members = lax.axis_size("grp")
    me = lax.axis_index("grp")
    rows = value.shape[1]
    pieces = [(me * rows, value)]
    for distance in range(1, members):
        owner = partner(me, distance, members)
        pieces.append((owner * rows, send(value, "grp", distance)))
    return pieces


def assemble(pieces, order):
    whole = jnp.zeros((pieces[0][1].shape[0], order), jnp.float32)
    for offset, piece in pieces:
        whole = lax.dynamic_update_slice_in_dim(whole, piece, offset, 1)
    return whole


def swap(value, axis, distance, block):
    count = lax.axis_size(axis)
    outer = count // block
    if outer & (outer - 1):
        pairs = [(i, (i // block + distance) % outer * block + i % block) for i in range(count)]
    else:
        pairs = [(i, (i // block ^ distance) * block + i % block) for i in range(count)]
    return lax.ppermute(value, axis, pairs)


VMEM = pl.BlockSpec(memory_space=pltpu.VMEM)
SMEM = pl.BlockSpec(memory_space=pltpu.SMEM)


def local_kernel(body, outs, operands, specs=None, flops=0, scratch=()):
    size = sum(o.size * o.dtype.itemsize for o in list(outs) + list(operands))
    return pl.pallas_call(
        body,
        out_shape=list(outs),
        in_specs=specs or [VMEM] * len(operands),
        out_specs=[VMEM] * len(outs),
        scratch_shapes=list(scratch),
        cost_estimate=pl.CostEstimate(flops=flops, bytes_accessed=size, transcendentals=0),
        compiler_params=pltpu.CompilerParams(vmem_limit_bytes=2 * size + 2**21),
    )(*operands)


def float_array(*shape):
    return jax.ShapeDtypeStruct(shape, jnp.float32)


def high_low(value):
    top = value.astype(jnp.bfloat16)
    return top, (value - top.astype(jnp.float32)).astype(jnp.bfloat16)


def split_product(left, top, rest):
    def dot(x, y):
        return lax.dot_general(
            x, y, (((1,), (1,)), ((), ())), preferred_element_type=jnp.float32
        )

    left_top, left_rest = high_low(left)
    return dot(left_top, top) + (dot(left_top, rest) + dot(left_rest, top))


def leaf_shape():
    groups = lax.axis_size("leaf")
    inner = 2 if groups % 2 == 0 else 1
    return groups // inner, inner


def select_terms(sources_ref, gathered, tile_refs, store):
    for m in range(tile_refs.shape[0]):
        chosen = gathered[0][...]
        for index in range(1, len(gathered)):
            chosen = jnp.where(sources_ref[0, 0, m] == index, gathered[index][...], chosen)
        top, rest = high_low(tile_refs[m])
        store(m, split_product(chosen, top, rest))


def tile_terms(gathered, tiles, sources):
    slots, tile_rows, order = tiles.shape
    depth = gathered[0].shape[0]
    count = len(gathered)

    def body(*refs):
        out = refs[-1]

        def store(m, term):
            out[:, m * tile_rows : (m + 1) * tile_rows] = term

        select_terms(refs[count + 1], refs[:count], refs[count], store)

    return local_kernel(
        body,
        [float_array(depth, slots * tile_rows)],
        [*gathered, tiles, sources],
        [VMEM] * (count + 1) + [SMEM],
        flops=6 * depth * slots * tile_rows * order,
    )[0]


def pack_terms(done, gathered, tiles, sources, blocks, live):
    outer, inner = leaf_shape()
    slots, tile_rows, order = tiles.shape
    depth = gathered[0].shape[0]
    streams = len(done) + 1
    part = depth * streams // (outer * inner)
    width = (slots + 1) * tile_rows
    count = len(gathered)
    base = len(done)

    def body(*refs):
        source_ref, block_ref, live_ref = refs[base + count + 1 : base + count + 4]
        outs = refs[base + count + 4 : -1]
        terms = refs[-1]
        lanes = lax.broadcasted_iota(jnp.int32, (streams * depth, tile_rows), 1)
        tag = jnp.full((streams * depth, tile_rows), -1.0, jnp.float32)
        for m in range(slots):
            value = jnp.where(m < live_ref[0, 0], block_ref[0, 0, m], -1).astype(jnp.float32)
            tag = jnp.where(lanes == m, value, tag)
        terms[:, slots * tile_rows :] = tag
        for i in range(base):
            terms[i * depth : (i + 1) * depth, : slots * tile_rows] = refs[i][...]

        def store(m, term):
            terms[base * depth :, m * tile_rows : (m + 1) * tile_rows] = term

        select_terms(source_ref, refs[base : base + count], refs[base + count], store)
        inside = lax.rem(lax.axis_index("leaf"), inner)
        for o in range(outer):
            cut = [
                terms[(o * inner + i) * part : (o * inner + i + 1) * part, :]
                for i in range(inner)
            ]
            for i in range(inner):
                outs[i][o] = jnp.where(inside == 0, cut[i], cut[inner - 1 - i])

    return local_kernel(
        body,
        [float_array(outer, part, width)] * inner,
        [*done, *gathered, tiles, sources, blocks, live],
        [VMEM] * (base + count + 1) + [SMEM] * 3,
        flops=6 * depth * slots * tile_rows * order,
        scratch=[pltpu.VMEM((streams * depth, width), jnp.float32)],
    )


def turn(rhs, first, last, streams):
    rows, count = rhs.shape[2:]
    depth = count // streams

    def body(rhs_ref, *outs):
        for index in range(first, last):
            wide = jnp.transpose(rhs_ref[0, index - first])
            for i in range(streams):
                outs[(index - first) * streams + i][...] = wide[i * depth : (i + 1) * depth]

    return local_kernel(
        body,
        [float_array(depth, rows)] * (streams * (last - first)),
        [rhs[:, first:last]],
    )


def turn_back(solved, after):
    flat = [value for streams in solved for value in streams]
    streams = len(solved[0])
    depth, rows = flat[0].shape

    def body(*refs):
        out = refs[-1]
        for index in range(len(solved)):
            wide = jnp.concatenate(
                [refs[index * streams + i][...] for i in range(streams)], axis=0
            )
            out[0, index] = jnp.transpose(wide)

    return local_kernel(
        body,
        [float_array(1, len(solved), rows, depth * streams)],
        [*flat, after],
        [VMEM] * len(flat) + [pl.BlockSpec(memory_space=pl.ANY)],
    )[0]


def leaf_exchange(packed):
    outer, inner = leaf_shape()
    part, width = packed[0].shape[1:]
    held = [packed[0]]
    if inner == 2:
        pairs = [(i, i ^ 1) for i in range(outer * inner)]
        held.append(lax.ppermute(packed[1], "leaf", pairs))

    def body(*refs):
        outside = lax.div(lax.axis_index("leaf"), inner)
        for distance in range(outer):
            target = partner(outside, -distance, outer) if distance else outside
            for i in range(inner):
                refs[inner + distance][i] = refs[i][target]

    portions = local_kernel(body, [float_array(inner, part, width)] * outer, held)
    return [portions[0]] + [
        swap(portions[distance], "leaf", distance, inner) for distance in range(1, outer)
    ]


def share_out(received, rhs_turned, order, slots, tile_rows, after):
    members = lax.axis_size("grp")
    ancestors, part, rows = rhs_turned.shape
    inner = received[0].shape[0]
    block_count = ancestors * order // tile_rows
    width = order + (ancestors - 1) * rows

    def body(*refs):
        sources = refs[: len(received)]
        rhs_ref = refs[len(received)]
        outs = refs[len(received) + 2 : -1]
        share = refs[-1]
        me = lax.axis_index("grp")
        totals = [jnp.zeros((part, tile_rows), jnp.float32) for _ in range(block_count)]
        for source in sources:
            for i in range(inner):
                for m in range(slots):
                    tile = source[i, :, m * tile_rows : (m + 1) * tile_rows]
                    tag = source[i, :, slots * tile_rows + m : slots * tile_rows + m + 1]
                    tag = jnp.broadcast_to(tag, tile.shape)
                    for q in range(block_count):
                        totals[q] = totals[q] + jnp.where(tag == float(q), tile, 0.0)
        for q in range(block_count):
            share[:, q * tile_rows : (q + 1) * tile_rows] = -totals[q]
        for a in range(ancestors):
            for j in range(members):
                at = slice(a * order + j * rows, a * order + (j + 1) * rows)
                share[:, at] = share[:, at] + jnp.where(me == j, rhs_ref[a], 0.0)
        for distance in range(members):
            target = partner(me, -distance, members) if distance else me
            out = outs[distance]
            out[:, :order] = share[:, :order]
            for a in range(1, ancestors):
                value = jnp.zeros((part, rows), jnp.float32)
                for j in range(members):
                    at = slice(a * order + j * rows, a * order + (j + 1) * rows)
                    value = jnp.where(target == j, share[:, at], value)
                out[:, order + (a - 1) * rows : order + a * rows] = value

    return local_kernel(
        body,
        [float_array(part, width)] * members,
        [*received, rhs_turned, after],
        [VMEM] * (len(received) + 1) + [pl.BlockSpec(memory_space=pl.ANY)],
        scratch=[pltpu.VMEM((part, ancestors * order), jnp.float32)],
    )


def split_factors(factors, after):
    count = len(factors)

    def body(*refs):
        for i in range(count):
            top, rest = high_low(refs[i][...])
            refs[count + 1 + 2 * i][...] = top
            refs[count + 2 + 2 * i][...] = rest

    outs = []
    for factor in factors:
        outs += [jax.ShapeDtypeStruct(factor.shape, jnp.bfloat16)] * 2
    return local_kernel(
        body,
        outs,
        [*factors, after],
        [VMEM] * count + [pl.BlockSpec(memory_space=pl.ANY)],
        flops=4 * sum(f.size for f in factors),
    )


def solve_first(payloads, top, rest):
    part, width = payloads[0].shape
    rows, order = top.shape[1:]

    def body(*refs):
        sums = refs[: len(payloads)]
        top_ref, rest_ref, out, left = refs[len(payloads) :]
        total = sums[0][...]
        for ref in sums[1:]:
            total = total + ref[...]
        out[...] = split_product(total[:, :order], top_ref[0], rest_ref[0])
        left[...] = total[:, order:]

    return local_kernel(
        body,
        [float_array(part, rows), float_array(part, width - order)],
        [*payloads, top, rest],
        flops=6 * part * rows * order,
    )


def apply_split(pieces, top, rest, index, base=None, begin=0):
    members = lax.axis_size("grp")
    part, width = pieces[0].shape
    rows, order = top.shape[1:]
    extra = [] if base is None else [base]

    def body(*refs):
        held = refs[:members]
        top_ref, rest_ref = refs[members : members + 2]
        out, whole = refs[-2:]
        me = lax.axis_index("grp")
        for j in range(members):
            value = jnp.zeros((part, width), jnp.float32)
            for distance in range(members):
                owner = partner(me, distance, members) if distance else me
                value = jnp.where(owner == j, held[distance][...], value)
            whole[:, j * width : (j + 1) * width] = value
        result = split_product(whole[...], top_ref[index], rest_ref[index])
        if extra:
            result = refs[members + 2][:, begin : begin + rows] - result
        out[...] = result

    return local_kernel(
        body,
        [float_array(part, rows)],
        [*pieces, top, rest, *extra],
        flops=6 * part * rows * order,
        scratch=[pltpu.VMEM((part, order), jnp.float32)],
    )[0]


def on_device(
    rhs_local,
    diag_inv_local,
    sub_local,
    tiles,
    tile_block,
    tile_source,
    tile_count,
    rhs_anc,
    diag_inv_anc,
    sub_anc,
):
    supernodes, _, order = diag_inv_local.shape[1:]
    rhs_count = rhs_local.shape[-1]
    members = lax.axis_size("grp")
    rows = order // members
    slots, tile_rows = tiles.shape[2:4]

    streams = 2 if rhs_count % 16 == 0 else 1
    residuals = turn(rhs_local, 0, 1, streams)
    later = turn(rhs_local, 1, supernodes, streams)
    solved = []
    gathered = []
    for current in range(supernodes):
        owned = []
        for residual in residuals:
            whole = assemble(gather_rows(residual), order)
            owned.append(contract_last(whole, diag_inv_local[0, current]))
        solved.append(owned)
        gathered.append([assemble(gather_rows(value), order) for value in owned])
        if current + 1 < supernodes:
            residuals = [
                later[current * streams + i] - contract_last(whole, sub_local[0, current])
                for i, whole in enumerate(gathered[-1])
            ]

    by_stream = [[values[i] for values in gathered] for i in range(streams)]
    done = [tile_terms(values, tiles[0, 0], tile_source) for values in by_stream[:-1]]
    packed = pack_terms(done, by_stream[-1], tiles[0, 0], tile_source, tile_block, tile_count)
    received = leaf_exchange(packed)
    solution_local = turn_back(solved, packed[0])
    shares = share_out(
        received, jnp.swapaxes(rhs_anc, 1, 2), order, slots, tile_rows, solution_local
    )
    payloads = [shares[0]] + [send(shares[d], "grp", d) for d in range(1, members)]
    inverse_top, inverse_rest, below_top, below_rest = split_factors(
        [diag_inv_anc, sub_anc], shares[0]
    )
    solution, left = solve_first(payloads, inverse_top, inverse_rest)
    solutions = [solution]
    for ancestor in range(1, rhs_anc.shape[0]):
        pieces = [piece for _, piece in gather_rows(solutions[-1])]
        residual = apply_split(
            pieces, below_top, below_rest, ancestor - 1, left, (ancestor - 1) * rows
        )
        pieces = [piece for _, piece in gather_rows(residual)]
        solutions.append(apply_split(pieces, inverse_top, inverse_rest, ancestor))
    solutions = jnp.swapaxes(jnp.stack(solutions), 1, 2)
    return (solution_local, solutions)


def solution(mesh):
    return jax.shard_map(
        on_device,
        mesh=mesh,
        in_specs=(
            P("leaf", None, "grp", None),
            P("leaf", None, "grp", None),
            P("leaf", None, "grp", None),
            P("leaf", "grp", None, None, None),
            P("leaf", "grp", None),
            P("leaf", "grp", None),
            P("leaf", "grp"),
            P(None, "grp", "leaf"),
            P(None, "grp", None),
            P(None, "grp", None),
        ),
        out_specs=(P("leaf", None, "grp", None), P(None, "grp", "leaf")),
        check_vma=False,
    )
```

```python
import jax
import jax.numpy as jnp
from jax import lax
from jax.experimental import pallas as pl
from jax.experimental.pallas import tpu as pltpu
from jax.sharding import PartitionSpec as P

high = lax.Precision.HIGH


def contract_last(left, right):
    return lax.dot_general(
        left,
        right,
        (((left.ndim - 1,), (right.ndim - 1,)), ((), ())),
        precision=high,
        preferred_element_type=jnp.float32,
    )


def partner(index, distance, count):
    if count & (count - 1):
        return lax.rem(index - distance + 2 * count, count)
    return index ^ abs(distance)


def send(value, axis, distance):
    count = lax.axis_size(axis)
    if count & (count - 1):
        pairs = [(i, (i + distance) % count) for i in range(count)]
    else:
        pairs = [(i, i ^ distance) for i in range(count)]
    return lax.ppermute(value, axis, pairs)


def gather_rows(value):
    members = lax.axis_size("grp")
    me = lax.axis_index("grp")
    rows = value.shape[1]
    pieces = [(me * rows, value)]
    for distance in range(1, members):
        owner = partner(me, distance, members)
        pieces.append((owner * rows, send(value, "grp", distance)))
    return pieces


def assemble(pieces, order):
    whole = jnp.zeros((pieces[0][1].shape[0], order), jnp.float32)
    for offset, piece in pieces:
        whole = lax.dynamic_update_slice_in_dim(whole, piece, offset, 1)
    return whole


def apply_pieces(factor, index, pieces):
    total = None
    for offset, piece in pieces:
        size = (1, 1, factor.shape[2], piece.shape[1])
        columns = lax.dynamic_slice(factor, (0, index, 0, offset), size)[0, 0]
        term = contract_last(piece, columns)
        total = term if total is None else total + term
    return total


def swap(value, axis, distance, block):
    count = lax.axis_size(axis)
    outer = count // block
    if outer & (outer - 1):
        pairs = [(i, (i // block + distance) % outer * block + i % block) for i in range(count)]
    else:
        pairs = [(i, (i // block ^ distance) * block + i % block) for i in range(count)]
    return lax.ppermute(value, axis, pairs)


VMEM = pl.BlockSpec(memory_space=pltpu.VMEM)
SMEM = pl.BlockSpec(memory_space=pltpu.SMEM)


def local_kernel(body, outs, operands, specs=None, flops=0, scratch=()):
    size = sum(o.size * o.dtype.itemsize for o in list(outs) + list(operands))
    return pl.pallas_call(
        body,
        out_shape=list(outs),
        in_specs=specs or [VMEM] * len(operands),
        out_specs=[VMEM] * len(outs),
        scratch_shapes=list(scratch),
        cost_estimate=pl.CostEstimate(flops=flops, bytes_accessed=size, transcendentals=0),
        compiler_params=pltpu.CompilerParams(vmem_limit_bytes=2 * size + 2**21),
    )(*operands)


def float_array(*shape):
    return jax.ShapeDtypeStruct(shape, jnp.float32)


def high_low(value):
    top = value.astype(jnp.bfloat16)
    return top, (value - top.astype(jnp.float32)).astype(jnp.bfloat16)


def split_product(left, top, rest):
    def dot(x, y):
        return lax.dot_general(
            x, y, (((1,), (1,)), ((), ())), preferred_element_type=jnp.float32
        )

    left_top, left_rest = high_low(left)
    return dot(left_top, top) + (dot(left_top, rest) + dot(left_rest, top))


def leaf_shape():
    groups = lax.axis_size("leaf")
    inner = 2 if groups % 2 == 0 else 1
    return groups // inner, inner


def select_terms(sources_ref, gathered, tile_refs, store):
    for m in range(tile_refs.shape[0]):
        chosen = gathered[0][...]
        for index in range(1, len(gathered)):
            chosen = jnp.where(sources_ref[0, 0, m] == index, gathered[index][...], chosen)
        top, rest = high_low(tile_refs[m])
        store(m, split_product(chosen, top, rest))


def tile_terms(gathered, tiles, sources):
    slots, tile_rows, order = tiles.shape
    depth = gathered[0].shape[0]
    count = len(gathered)

    def body(*refs):
        out = refs[-1]

        def store(m, term):
            out[:, m * tile_rows : (m + 1) * tile_rows] = term

        select_terms(refs[count + 1], refs[:count], refs[count], store)

    return local_kernel(
        body,
        [float_array(depth, slots * tile_rows)],
        [*gathered, tiles, sources],
        [VMEM] * (count + 1) + [SMEM],
        flops=6 * depth * slots * tile_rows * order,
    )[0]


def pack_terms(done, gathered, tiles, sources, blocks, live):
    outer, inner = leaf_shape()
    slots, tile_rows, order = tiles.shape
    depth = gathered[0].shape[0]
    streams = len(done) + 1
    part = depth * streams // (outer * inner)
    width = (slots + 1) * tile_rows
    count = len(gathered)
    base = len(done)

    def body(*refs):
        source_ref, block_ref, live_ref = refs[base + count + 1 : base + count + 4]
        outs = refs[base + count + 4 : -1]
        terms = refs[-1]
        lanes = lax.broadcasted_iota(jnp.int32, (streams * depth, tile_rows), 1)
        tag = jnp.full((streams * depth, tile_rows), -1.0, jnp.float32)
        for m in range(slots):
            value = jnp.where(m < live_ref[0, 0], block_ref[0, 0, m], -1).astype(jnp.float32)
            tag = jnp.where(lanes == m, value, tag)
        terms[:, slots * tile_rows :] = tag
        for i in range(base):
            terms[i * depth : (i + 1) * depth, : slots * tile_rows] = refs[i][...]

        def store(m, term):
            terms[base * depth :, m * tile_rows : (m + 1) * tile_rows] = term

        select_terms(source_ref, refs[base : base + count], refs[base + count], store)
        inside = lax.rem(lax.axis_index("leaf"), inner)
        for o in range(outer):
            cut = [
                terms[(o * inner + i) * part : (o * inner + i + 1) * part, :]
                for i in range(inner)
            ]
            for i in range(inner):
                outs[i][o] = jnp.where(inside == 0, cut[i], cut[inner - 1 - i])

    return local_kernel(
        body,
        [float_array(outer, part, width)] * inner,
        [*done, *gathered, tiles, sources, blocks, live],
        [VMEM] * (base + count + 1) + [SMEM] * 3,
        flops=6 * depth * slots * tile_rows * order,
        scratch=[pltpu.VMEM((streams * depth, width), jnp.float32)],
    )


def turn(rhs, first, last, streams):
    rows, count = rhs.shape[2:]
    depth = count // streams

    def body(rhs_ref, *outs):
        for index in range(first, last):
            wide = jnp.transpose(rhs_ref[0, index - first])
            for i in range(streams):
                outs[(index - first) * streams + i][...] = wide[i * depth : (i + 1) * depth]

    return local_kernel(
        body,
        [float_array(depth, rows)] * (streams * (last - first)),
        [rhs[:, first:last]],
    )


def turn_back(solved, after):
    flat = [value for streams in solved for value in streams]
    streams = len(solved[0])
    depth, rows = flat[0].shape

    def body(*refs):
        out = refs[-1]
        for index in range(len(solved)):
            wide = jnp.concatenate(
                [refs[index * streams + i][...] for i in range(streams)], axis=0
            )
            out[0, index] = jnp.transpose(wide)

    return local_kernel(
        body,
        [float_array(1, len(solved), rows, depth * streams)],
        [*flat, after],
        [VMEM] * len(flat) + [pl.BlockSpec(memory_space=pl.ANY)],
    )[0]


def leaf_exchange(packed):
    outer, inner = leaf_shape()
    part, width = packed[0].shape[1:]
    held = [packed[0]]
    if inner == 2:
        pairs = [(i, i ^ 1) for i in range(outer * inner)]
        held.append(lax.ppermute(packed[1], "leaf", pairs))

    def body(*refs):
        outside = lax.div(lax.axis_index("leaf"), inner)
        for distance in range(outer):
            target = partner(outside, -distance, outer) if distance else outside
            for i in range(inner):
                refs[inner + distance][i] = refs[i][target]

    portions = local_kernel(body, [float_array(inner, part, width)] * outer, held)
    return [portions[0]] + [
        swap(portions[distance], "leaf", distance, inner) for distance in range(1, outer)
    ]


def share_out(received, rhs_turned, order, slots, tile_rows, after):
    members = lax.axis_size("grp")
    ancestors, part, rows = rhs_turned.shape
    inner = received[0].shape[0]
    block_count = ancestors * order // tile_rows
    width = order + (ancestors - 1) * rows

    def body(*refs):
        sources = refs[: len(received)]
        rhs_ref = refs[len(received)]
        outs = refs[len(received) + 2 : -1]
        share = refs[-1]
        me = lax.axis_index("grp")
        totals = [jnp.zeros((part, tile_rows), jnp.float32) for _ in range(block_count)]
        for source in sources:
            for i in range(inner):
                for m in range(slots):
                    tile = source[i, :, m * tile_rows : (m + 1) * tile_rows]
                    tag = source[i, :, slots * tile_rows + m : slots * tile_rows + m + 1]
                    tag = jnp.broadcast_to(tag, tile.shape)
                    for q in range(block_count):
                        totals[q] = totals[q] + jnp.where(tag == float(q), tile, 0.0)
        for q in range(block_count):
            share[:, q * tile_rows : (q + 1) * tile_rows] = -totals[q]
        for a in range(ancestors):
            for j in range(members):
                at = slice(a * order + j * rows, a * order + (j + 1) * rows)
                share[:, at] = share[:, at] + jnp.where(me == j, rhs_ref[a], 0.0)
        for distance in range(members):
            target = partner(me, -distance, members) if distance else me
            out = outs[distance]
            out[:, :order] = share[:, :order]
            for a in range(1, ancestors):
                value = jnp.zeros((part, rows), jnp.float32)
                for j in range(members):
                    at = slice(a * order + j * rows, a * order + (j + 1) * rows)
                    value = jnp.where(target == j, share[:, at], value)
                out[:, order + (a - 1) * rows : order + a * rows] = value

    return local_kernel(
        body,
        [float_array(part, width)] * members,
        [*received, rhs_turned, after],
        [VMEM] * (len(received) + 1) + [pl.BlockSpec(memory_space=pl.ANY)],
        scratch=[pltpu.VMEM((part, ancestors * order), jnp.float32)],
    )


def split_factors(factors, after):
    count = len(factors)

    def body(*refs):
        for i in range(count):
            top, rest = high_low(refs[i][...])
            refs[count + 1 + 2 * i][...] = top
            refs[count + 2 + 2 * i][...] = rest

    outs = []
    for factor in factors:
        outs += [jax.ShapeDtypeStruct(factor.shape, jnp.bfloat16)] * 2
    return local_kernel(
        body,
        outs,
        [*factors, after],
        [VMEM] * count + [pl.BlockSpec(memory_space=pl.ANY)],
        flops=4 * sum(f.size for f in factors),
    )


def solve_first(payloads, top, rest):
    part, width = payloads[0].shape
    rows, order = top.shape[1:]

    def body(*refs):
        sums = refs[: len(payloads)]
        top_ref, rest_ref, out, left = refs[len(payloads) :]
        total = sums[0][...]
        for ref in sums[1:]:
            total = total + ref[...]
        out[...] = split_product(total[:, :order], top_ref[0], rest_ref[0])
        left[...] = total[:, order:]

    return local_kernel(
        body,
        [float_array(part, rows), float_array(part, width - order)],
        [*payloads, top, rest],
        flops=6 * part * rows * order,
    )


def apply_split(pieces, top, rest, index, base=None, begin=0):
    members = lax.axis_size("grp")
    part, width = pieces[0].shape
    rows, order = top.shape[1:]
    extra = [] if base is None else [base]

    def body(*refs):
        held = refs[:members]
        top_ref, rest_ref = refs[members : members + 2]
        out, whole = refs[-2:]
        me = lax.axis_index("grp")
        for j in range(members):
            value = jnp.zeros((part, width), jnp.float32)
            for distance in range(members):
                owner = partner(me, distance, members) if distance else me
                value = jnp.where(owner == j, held[distance][...], value)
            whole[:, j * width : (j + 1) * width] = value
        result = split_product(whole[...], top_ref[index], rest_ref[index])
        if extra:
            result = refs[members + 2][:, begin : begin + rows] - result
        out[...] = result

    return local_kernel(
        body,
        [float_array(part, rows)],
        [*pieces, top, rest, *extra],
        flops=6 * part * rows * order,
        scratch=[pltpu.VMEM((part, order), jnp.float32)],
    )[0]


def on_device(
    rhs_local,
    diag_inv_local,
    sub_local,
    tiles,
    tile_block,
    tile_source,
    tile_count,
    rhs_anc,
    diag_inv_anc,
    sub_anc,
):
    supernodes, _, order = diag_inv_local.shape[1:]
    rhs_count = rhs_local.shape[-1]
    members = lax.axis_size("grp")
    rows = order // members
    slots, tile_rows = tiles.shape[2:4]

    streams = 2 if rhs_count % 16 == 0 else 1
    residuals = turn(rhs_local, 0, 1, streams)
    later = turn(rhs_local, 1, supernodes, streams)
    solved = []
    gathered = []
    for current in range(supernodes):
        owned = []
        for residual in residuals:
            pieces = gather_rows(residual)
            if current:
                owned.append(apply_pieces(diag_inv_local, current, pieces))
            else:
                whole = assemble(pieces, order)
                owned.append(contract_last(whole, diag_inv_local[0, current]))
        solved.append(owned)
        held = [gather_rows(value) for value in owned]
        gathered.append([assemble(pieces, order) for pieces in held])
        if current + 1 < supernodes:
            residuals = [
                later[current * streams + i] - apply_pieces(sub_local, current, pieces)
                for i, pieces in enumerate(held)
            ]

    by_stream = [[values[i] for values in gathered] for i in range(streams)]
    done = [tile_terms(values, tiles[0, 0], tile_source) for values in by_stream[:-1]]
    packed = pack_terms(done, by_stream[-1], tiles[0, 0], tile_source, tile_block, tile_count)
    received = leaf_exchange(packed)
    solution_local = turn_back(solved, packed[0])
    shares = share_out(
        received, jnp.swapaxes(rhs_anc, 1, 2), order, slots, tile_rows, solution_local
    )
    payloads = [shares[0]] + [send(shares[d], "grp", d) for d in range(1, members)]
    inverse_top, inverse_rest, below_top, below_rest = split_factors(
        [diag_inv_anc, sub_anc], shares[0]
    )
    solution, left = solve_first(payloads, inverse_top, inverse_rest)
    solutions = [solution]
    for ancestor in range(1, rhs_anc.shape[0]):
        pieces = [piece for _, piece in gather_rows(solutions[-1])]
        residual = apply_split(
            pieces, below_top, below_rest, ancestor - 1, left, (ancestor - 1) * rows
        )
        pieces = [piece for _, piece in gather_rows(residual)]
        solutions.append(apply_split(pieces, inverse_top, inverse_rest, ancestor))
    solutions = jnp.swapaxes(jnp.stack(solutions), 1, 2)
    return (solution_local, solutions)


def solution(mesh):
    return jax.shard_map(
        on_device,
        mesh=mesh,
        in_specs=(
            P("leaf", None, "grp", None),
            P("leaf", None, "grp", None),
            P("leaf", None, "grp", None),
            P("leaf", "grp", None, None, None),
            P("leaf", "grp", None),
            P("leaf", "grp", None),
            P("leaf", "grp"),
            P(None, "grp", "leaf"),
            P(None, "grp", None),
            P(None, "grp", None),
        ),
        out_specs=(P("leaf", None, "grp", None), P(None, "grp", "leaf")),
        check_vma=False,
    )
```

```python
import jax
import jax.numpy as jnp
from jax import lax
from jax.experimental import pallas as pl
from jax.experimental.pallas import tpu as pltpu
from jax.sharding import PartitionSpec as P

high = lax.Precision.HIGH


def contract_last(left, right):
    return lax.dot_general(
        left,
        right,
        (((left.ndim - 1,), (right.ndim - 1,)), ((), ())),
        precision=high,
        preferred_element_type=jnp.float32,
    )


def partner(index, distance, count):
    if count & (count - 1):
        return lax.rem(index - distance + 2 * count, count)
    return index ^ abs(distance)


def send(value, axis, distance):
    count = lax.axis_size(axis)
    if count & (count - 1):
        pairs = [(i, (i + distance) % count) for i in range(count)]
    else:
        pairs = [(i, i ^ distance) for i in range(count)]
    return lax.ppermute(value, axis, pairs)


def gather_rows(value, stream=0):
    members = lax.axis_size("grp")
    me = lax.axis_index("grp")
    rows = value.shape[1]
    pieces = [(me * rows, value)]
    distances = list(range(members - 1, 0, -1))
    if stream % 2:
        distances[:2] = distances[1::-1]
    for distance in distances:
        owner = partner(me, distance, members)
        pieces.append((owner * rows, send(value, "grp", distance)))
    return pieces


def gather_small(value):
    members = lax.axis_size("grp")
    if members & (members - 1):
        return [value] + [send(value, "grp", d) for d in range(1, members)]
    held = value[None]
    distance = 1
    while distance < members:
        held = jnp.concatenate([held, send(held, "grp", distance)], axis=0)
        distance *= 2
    return [held]


def assemble(pieces, order):
    whole = jnp.zeros((pieces[0][1].shape[0], order), jnp.float32)
    for offset, piece in pieces:
        whole = lax.dynamic_update_slice_in_dim(whole, piece, offset, 1)
    return whole


def apply_pieces(factor, index, pieces):
    total = None
    for offset, piece in pieces:
        size = (1, 1, factor.shape[2], piece.shape[1])
        columns = lax.dynamic_slice(factor, (0, index, 0, offset), size)[0, 0]
        term = contract_last(piece, columns)
        total = term if total is None else total + term
    return total


def swap(value, axis, distance, block):
    count = lax.axis_size(axis)
    outer = count // block
    if outer & (outer - 1):
        pairs = [(i, (i // block + distance) % outer * block + i % block) for i in range(count)]
    else:
        pairs = [(i, (i // block ^ distance) * block + i % block) for i in range(count)]
    return lax.ppermute(value, axis, pairs)


VMEM = pl.BlockSpec(memory_space=pltpu.VMEM)
SMEM = pl.BlockSpec(memory_space=pltpu.SMEM)


def local_kernel(body, outs, operands, specs=None, flops=0, scratch=(), limit=None):
    size = sum(o.size * o.dtype.itemsize for o in list(outs) + list(operands))
    return pl.pallas_call(
        body,
        out_shape=list(outs),
        in_specs=specs or [VMEM] * len(operands),
        out_specs=[VMEM] * len(outs),
        scratch_shapes=list(scratch),
        cost_estimate=pl.CostEstimate(flops=flops, bytes_accessed=size, transcendentals=0),
        compiler_params=pltpu.CompilerParams(vmem_limit_bytes=limit or 2 * size + 2**21),
    )(*operands)


def float_array(*shape):
    return jax.ShapeDtypeStruct(shape, jnp.float32)


def high_low(value):
    top = value.astype(jnp.bfloat16)
    return top, (value - top.astype(jnp.float32)).astype(jnp.bfloat16)


def split_product(left, top, rest):
    def dot(x, y):
        return lax.dot_general(
            x, y, (((1,), (1,)), ((), ())), preferred_element_type=jnp.float32
        )

    left_top, left_rest = high_low(left)
    return dot(left_top, top) + (dot(left_top, rest) + dot(left_rest, top))


def leaf_shape():
    groups = lax.axis_size("leaf")
    inner = 2 if groups % 2 == 0 else 1
    return groups // inner, inner


def select_terms(sources_ref, gathered, tile_refs, store):
    for m in range(tile_refs.shape[0]):
        chosen = gathered[0][...]
        for index in range(1, len(gathered)):
            chosen = jnp.where(sources_ref[0, 0, m] == index, gathered[index][...], chosen)
        top, rest = high_low(tile_refs[m])
        store(m, split_product(chosen, top, rest))


def tile_terms(gathered, tiles, sources):
    slots, tile_rows, order = tiles.shape
    depth = gathered[0].shape[0]
    count = len(gathered)

    def body(*refs):
        out = refs[-1]

        def store(m, term):
            out[:, m * tile_rows : (m + 1) * tile_rows] = term

        select_terms(refs[count + 1], refs[:count], refs[count], store)

    return local_kernel(
        body,
        [float_array(depth, slots * tile_rows)],
        [*gathered, tiles, sources],
        [VMEM] * (count + 1) + [SMEM],
        flops=6 * depth * slots * tile_rows * order,
    )[0]


def pack_terms(done, gathered, tiles, sources, blocks, live):
    outer, inner = leaf_shape()
    slots, tile_rows, order = tiles.shape
    depth = gathered[0].shape[0]
    streams = len(done) + 1
    part = depth * streams // (outer * inner)
    width = (slots + 1) * tile_rows
    count = len(gathered)
    base = len(done)

    def body(*refs):
        source_ref, block_ref, live_ref = refs[base + count + 1 : base + count + 4]
        outs = refs[base + count + 4 : -1]
        terms = refs[-1]
        lanes = lax.broadcasted_iota(jnp.int32, (streams * depth, tile_rows), 1)
        tag = jnp.full((streams * depth, tile_rows), -1.0, jnp.float32)
        for m in range(slots):
            value = jnp.where(m < live_ref[0, 0], block_ref[0, 0, m], -1).astype(jnp.float32)
            tag = jnp.where(lanes == m, value, tag)
        terms[:, slots * tile_rows :] = tag
        for i in range(base):
            terms[i * depth : (i + 1) * depth, : slots * tile_rows] = refs[i][...]

        def store(m, term):
            terms[base * depth :, m * tile_rows : (m + 1) * tile_rows] = term

        select_terms(source_ref, refs[base : base + count], refs[base + count], store)
        inside = lax.rem(lax.axis_index("leaf"), inner)
        for o in range(outer):
            cut = [
                terms[(o * inner + i) * part : (o * inner + i + 1) * part, :]
                for i in range(inner)
            ]
            for i in range(inner):
                outs[i][o] = jnp.where(inside == 0, cut[i], cut[inner - 1 - i])

    return local_kernel(
        body,
        [float_array(outer, part, width)] * inner,
        [*done, *gathered, tiles, sources, blocks, live],
        [VMEM] * (base + count + 1) + [SMEM] * 3,
        flops=6 * depth * slots * tile_rows * order,
        scratch=[pltpu.VMEM((streams * depth, width), jnp.float32)],
    )


def turn(rhs, first, last, streams):
    rows, count = rhs.shape[2:]
    depth = count // streams

    def body(rhs_ref, *refs):
        outs, (held, sem) = refs[:-2], refs[-2:]
        copy = pltpu.make_async_copy(rhs_ref.at[0, first:last], held, sem)
        copy.start()
        copy.wait()
        for index in range(last - first):
            wide = jnp.transpose(held[index])
            for i in range(streams):
                outs[index * streams + i][...] = wide[i * depth : (i + 1) * depth]

    return local_kernel(
        body,
        [float_array(depth, rows)] * (streams * (last - first)),
        [rhs],
        [pl.BlockSpec(memory_space=pl.ANY)],
        scratch=[
            pltpu.VMEM((last - first, rows, count), jnp.float32),
            pltpu.SemaphoreType.DMA(()),
        ],
    )


def turn_back(solved, after):
    flat = [value for streams in solved for value in streams]
    streams = len(solved[0])
    depth, rows = flat[0].shape

    def body(*refs):
        out, tie = refs[-2:]
        for index in range(len(solved)):
            wide = jnp.concatenate(
                [refs[index * streams + i][...] for i in range(streams)], axis=0
            )
            out[0, index] = jnp.transpose(wide)
        tie[...] = jnp.zeros(tie.shape, jnp.float32)

    return local_kernel(
        body,
        [float_array(1, len(solved), rows, depth * streams), float_array(8, 128)],
        [*flat, after],
        [VMEM] * len(flat) + [pl.BlockSpec(memory_space=pl.ANY)],
    )


def leaf_exchange(packed):
    outer, inner = leaf_shape()
    part, width = packed[0].shape[1:]
    held = [packed[0]]
    if inner == 2:
        pairs = [(i, i ^ 1) for i in range(outer * inner)]
        held.append(lax.ppermute(packed[1], "leaf", pairs))

    def body(*refs):
        outside = lax.div(lax.axis_index("leaf"), inner)
        for distance in range(outer):
            target = partner(outside, -distance, outer) if distance else outside
            for i in range(inner):
                refs[inner + distance][i] = refs[i][target]

    portions = local_kernel(body, [float_array(inner, part, width)] * outer, held)
    return [portions[0]] + [
        swap(portions[distance], "leaf", distance, inner) for distance in range(1, outer)
    ]


def share_out(received, rhs_turned, order, slots, tile_rows, after):
    members = lax.axis_size("grp")
    ancestors, part, rows = rhs_turned.shape
    inner = received[0].shape[0]
    block_count = ancestors * order // tile_rows
    width = order + (ancestors - 1) * rows

    def body(*refs):
        sources = refs[: len(received)]
        rhs_ref = refs[len(received)]
        outs = refs[len(received) + 2 : -1]
        share = refs[-1]
        me = lax.axis_index("grp")
        totals = [jnp.zeros((part, tile_rows), jnp.float32) for _ in range(block_count)]
        for source in sources:
            for i in range(inner):
                for m in range(slots):
                    tile = source[i, :, m * tile_rows : (m + 1) * tile_rows]
                    tag = source[i, :, slots * tile_rows + m : slots * tile_rows + m + 1]
                    tag = jnp.broadcast_to(tag, tile.shape)
                    for q in range(block_count):
                        totals[q] = totals[q] + jnp.where(tag == float(q), tile, 0.0)
        for q in range(block_count):
            share[:, q * tile_rows : (q + 1) * tile_rows] = -totals[q]
        for a in range(ancestors):
            for j in range(members):
                at = slice(a * order + j * rows, a * order + (j + 1) * rows)
                share[:, at] = share[:, at] + jnp.where(me == j, rhs_ref[a], 0.0)
        for distance in range(members):
            target = partner(me, -distance, members) if distance else me
            out = outs[distance]
            out[:, :order] = share[:, :order]
            for a in range(1, ancestors):
                value = jnp.zeros((part, rows), jnp.float32)
                for j in range(members):
                    at = slice(a * order + j * rows, a * order + (j + 1) * rows)
                    value = jnp.where(target == j, share[:, at], value)
                out[:, order + (a - 1) * rows : order + a * rows] = value

    return local_kernel(
        body,
        [float_array(part, width)] * members,
        [*received, rhs_turned, after],
        [VMEM] * (len(received) + 1) + [pl.BlockSpec(memory_space=pl.ANY)],
        scratch=[pltpu.VMEM((part, ancestors * order), jnp.float32)],
    )


def split_factors(factors, after):
    count = len(factors)

    def body(*refs):
        for i in range(count):
            top, rest = high_low(refs[i][...])
            refs[count + 1 + 2 * i][...] = top
            refs[count + 2 + 2 * i][...] = rest

    outs = []
    for factor in factors:
        outs += [jax.ShapeDtypeStruct(factor.shape, jnp.bfloat16)] * 2
    return local_kernel(
        body,
        outs,
        [*factors, after],
        [VMEM] * count + [pl.BlockSpec(memory_space=pl.ANY)],
        flops=4 * sum(f.size for f in factors),
    )


def solve_first(payloads, top, rest):
    part, width = payloads[0].shape
    rows, order = top.shape[1:]

    def body(*refs):
        sums = refs[: len(payloads)]
        top_ref, rest_ref, out, left = refs[len(payloads) :]
        total = sums[0][...]
        for ref in sums[1:]:
            total = total + ref[...]
        out[...] = split_product(total[:, :order], top_ref[0], rest_ref[0])
        left[...] = total[:, order:]

    return local_kernel(
        body,
        [float_array(part, rows), float_array(part, width - order)],
        [*payloads, top, rest],
        flops=6 * part * rows * order,
    )


def put_in_order(held, whole):
    me = lax.axis_index("grp")
    members = len(held)
    width = held[0].shape[1]
    for j in range(members):
        value = jnp.zeros(held[0].shape, jnp.float32)
        for distance in range(members):
            owner = partner(me, distance, members) if distance else me
            value = jnp.where(owner == j, held[distance], value)
        whole[:, j * width : (j + 1) * width] = value


def apply_first(value, stream, factor):
    members = lax.axis_size("grp")
    depth, width = value.shape
    rows, order = factor.shape[2:]
    order_of = list(range(members - 1, 0, -1))
    if stream % 2:
        order_of[:2] = order_of[1::-1]
    held = {0: value}
    for distance in order_of:
        held[distance] = send(value, "grp", distance)

    def body(*refs):
        factor_ref, out, whole, matrix, sem = refs[members:]
        copy = pltpu.make_async_copy(factor_ref.at[0, 0], matrix, sem)
        copy.start()
        put_in_order([refs[d][...] for d in range(members)], whole)
        copy.wait()
        top, rest = high_low(matrix[...])
        out[...] = split_product(whole[...], top, rest)

    return local_kernel(
        body,
        [float_array(depth, rows)],
        [held[d] for d in range(members)] + [factor],
        [VMEM] * members + [pl.BlockSpec(memory_space=pl.ANY)],
        flops=6 * depth * rows * order,
        scratch=[
            pltpu.VMEM((depth, order), jnp.float32),
            pltpu.VMEM((rows, order), jnp.float32),
            pltpu.SemaphoreType.DMA(()),
        ],
        limit=2**24,
    )[0]


def apply_split(pieces, top, rest, index, base=None, begin=0):
    members = lax.axis_size("grp")
    part, width = pieces[0].shape[-2:]
    rows, order = top.shape[1:]
    extra = [] if base is None else [base]
    count = len(pieces)

    def body(*refs):
        top_ref, rest_ref = refs[count : count + 2]
        out, whole = refs[-2:]
        if count == 1:
            held = [refs[0][d] for d in range(members)]
        else:
            held = [refs[d][...] for d in range(members)]
        put_in_order(held, whole)
        result = split_product(whole[...], top_ref[index], rest_ref[index])
        if extra:
            result = refs[count + 2][:, begin : begin + rows] - result
        out[...] = result

    return local_kernel(
        body,
        [float_array(part, rows)],
        [*pieces, top, rest, *extra],
        flops=6 * part * rows * order,
        scratch=[pltpu.VMEM((part, order), jnp.float32)],
    )[0]


def on_device(
    rhs_local,
    diag_inv_local,
    sub_local,
    tiles,
    tile_block,
    tile_source,
    tile_count,
    rhs_anc,
    diag_inv_anc,
    sub_anc,
):
    supernodes, _, order = diag_inv_local.shape[1:]
    rhs_count = rhs_local.shape[-1]
    members = lax.axis_size("grp")
    rows = order // members
    slots, tile_rows = tiles.shape[2:4]

    streams = 2 if rhs_count % 16 == 0 else 1
    residuals = turn(rhs_local, 0, 1, streams)
    later = turn(rhs_local, 1, supernodes, streams)
    solved = []
    gathered = []
    for current in range(supernodes):
        owned = []
        for residual in residuals:
            if current:
                pieces = gather_rows(residual, len(owned))
                owned.append(apply_pieces(diag_inv_local, current, pieces))
            else:
                owned.append(apply_first(residual, len(owned), diag_inv_local))
        solved.append(owned)
        held = [gather_rows(value, i) for i, value in enumerate(owned)]
        gathered.append([assemble(pieces, order) for pieces in held])
        if current + 1 < supernodes:
            residuals = [
                later[current * streams + i] - apply_pieces(sub_local, current, pieces)
                for i, pieces in enumerate(held)
            ]

    by_stream = [[values[i] for values in gathered] for i in range(streams)]
    done = [tile_terms(values, tiles[0, 0], tile_source) for values in by_stream[:-1]]
    packed = pack_terms(done, by_stream[-1], tiles[0, 0], tile_source, tile_block, tile_count)
    received = leaf_exchange(packed)
    solution_local, tie = turn_back(solved, packed[0])
    shares = share_out(
        received, jnp.swapaxes(rhs_anc, 1, 2), order, slots, tile_rows, tie
    )
    payloads = [shares[0]] + [send(shares[d], "grp", d) for d in range(1, members)]
    inverse_top, inverse_rest, below_top, below_rest = split_factors(
        [diag_inv_anc, sub_anc], shares[0]
    )
    solution, left = solve_first(payloads, inverse_top, inverse_rest)
    solutions = [solution]
    for ancestor in range(1, rhs_anc.shape[0]):
        pieces = gather_small(solutions[-1])
        residual = apply_split(
            pieces, below_top, below_rest, ancestor - 1, left, (ancestor - 1) * rows
        )
        pieces = gather_small(residual)
        solutions.append(apply_split(pieces, inverse_top, inverse_rest, ancestor))
    solutions = jnp.swapaxes(jnp.stack(solutions), 1, 2)
    return (solution_local, solutions)


def solution(mesh):
    return jax.shard_map(
        on_device,
        mesh=mesh,
        in_specs=(
            P("leaf", None, "grp", None),
            P("leaf", None, "grp", None),
            P("leaf", None, "grp", None),
            P("leaf", "grp", None, None, None),
            P("leaf", "grp", None),
            P("leaf", "grp", None),
            P("leaf", "grp"),
            P(None, "grp", "leaf"),
            P(None, "grp", None),
            P(None, "grp", None),
        ),
        out_specs=(P("leaf", None, "grp", None), P(None, "grp", "leaf")),
        check_vma=False,
    )
```

```python
import jax
import jax.numpy as jnp
from jax import lax
from jax.experimental import pallas as pl
from jax.experimental.pallas import tpu as pltpu
from jax.sharding import PartitionSpec as P

high = lax.Precision.HIGH


def contract_last(left, right):
    return lax.dot_general(
        left,
        right,
        (((left.ndim - 1,), (right.ndim - 1,)), ((), ())),
        precision=high,
        preferred_element_type=jnp.float32,
    )


def partner(index, distance, count):
    if count & (count - 1):
        return lax.rem(index - distance + 2 * count, count)
    return index ^ abs(distance)


def send(value, axis, distance):
    count = lax.axis_size(axis)
    if count & (count - 1):
        pairs = [(i, (i + distance) % count) for i in range(count)]
    else:
        pairs = [(i, i ^ distance) for i in range(count)]
    return lax.ppermute(value, axis, pairs)


def gather_rows(value):
    members = lax.axis_size("grp")
    me = lax.axis_index("grp")
    rows = value.shape[1]
    pieces = [(me * rows, value)]
    for distance in range(1, members):
        owner = partner(me, distance, members)
        pieces.append((owner * rows, send(value, "grp", distance)))
    return pieces


def assemble(pieces, order):
    whole = jnp.zeros((pieces[0][1].shape[0], order), jnp.float32)
    for offset, piece in pieces:
        whole = lax.dynamic_update_slice_in_dim(whole, piece, offset, 1)
    return whole


def apply_pieces(factor, index, pieces):
    total = None
    for offset, piece in pieces:
        size = (1, 1, factor.shape[2], piece.shape[1])
        columns = lax.dynamic_slice(factor, (0, index, 0, offset), size)[0, 0]
        term = contract_last(piece, columns)
        total = term if total is None else total + term
    return total


def swap(value, axis, distance, block):
    count = lax.axis_size(axis)
    outer = count // block
    if outer & (outer - 1):
        pairs = [(i, (i // block + distance) % outer * block + i % block) for i in range(count)]
    else:
        pairs = [(i, (i // block ^ distance) * block + i % block) for i in range(count)]
    return lax.ppermute(value, axis, pairs)


VMEM = pl.BlockSpec(memory_space=pltpu.VMEM)
SMEM = pl.BlockSpec(memory_space=pltpu.SMEM)


def local_kernel(body, outs, operands, specs=None, flops=0, scratch=(), limit=None):
    size = sum(o.size * o.dtype.itemsize for o in list(outs) + list(operands))
    return pl.pallas_call(
        body,
        out_shape=list(outs),
        in_specs=specs or [VMEM] * len(operands),
        out_specs=[VMEM] * len(outs),
        scratch_shapes=list(scratch),
        cost_estimate=pl.CostEstimate(flops=flops, bytes_accessed=size, transcendentals=0),
        compiler_params=pltpu.CompilerParams(vmem_limit_bytes=limit or 2 * size + 2**21),
    )(*operands)


def float_array(*shape):
    return jax.ShapeDtypeStruct(shape, jnp.float32)


def high_low(value):
    top = value.astype(jnp.bfloat16)
    return top, (value - top.astype(jnp.float32)).astype(jnp.bfloat16)


def split_product(left, top, rest):
    def dot(x, y):
        return lax.dot_general(
            x, y, (((1,), (1,)), ((), ())), preferred_element_type=jnp.float32
        )

    left_top, left_rest = high_low(left)
    return dot(left_top, top) + (dot(left_top, rest) + dot(left_rest, top))


def leaf_shape():
    groups = lax.axis_size("leaf")
    inner = 2 if groups % 2 == 0 else 1
    return groups // inner, inner


def select_terms(sources_ref, gathered, tile_refs, store):
    for m in range(tile_refs.shape[0]):
        chosen = gathered[0][...]
        for index in range(1, len(gathered)):
            chosen = jnp.where(sources_ref[0, 0, m] == index, gathered[index][...], chosen)
        top, rest = high_low(tile_refs[m])
        store(m, split_product(chosen, top, rest))


def tile_terms(gathered, tiles, sources):
    slots, tile_rows, order = tiles.shape
    depth = gathered[0].shape[0]
    count = len(gathered)

    def body(*refs):
        out = refs[-1]

        def store(m, term):
            out[:, m * tile_rows : (m + 1) * tile_rows] = term

        select_terms(refs[count + 1], refs[:count], refs[count], store)

    return local_kernel(
        body,
        [float_array(depth, slots * tile_rows)],
        [*gathered, tiles, sources],
        [VMEM] * (count + 1) + [SMEM],
        flops=6 * depth * slots * tile_rows * order,
    )[0]


def pack_terms(done, gathered, tiles, sources, blocks, live):
    outer, inner = leaf_shape()
    slots, tile_rows, order = tiles.shape
    depth = gathered[0].shape[0]
    streams = len(done) + 1
    part = depth * streams // (outer * inner)
    width = (slots + 1) * tile_rows
    count = len(gathered)
    base = len(done)

    def body(*refs):
        source_ref, block_ref, live_ref = refs[base + count + 1 : base + count + 4]
        outs = refs[base + count + 4 : -1]
        terms = refs[-1]
        lanes = lax.broadcasted_iota(jnp.int32, (streams * depth, tile_rows), 1)
        tag = jnp.full((streams * depth, tile_rows), -1.0, jnp.float32)
        for m in range(slots):
            value = jnp.where(m < live_ref[0, 0], block_ref[0, 0, m], -1).astype(jnp.float32)
            tag = jnp.where(lanes == m, value, tag)
        terms[:, slots * tile_rows :] = tag
        for i in range(base):
            terms[i * depth : (i + 1) * depth, : slots * tile_rows] = refs[i][...]

        def store(m, term):
            terms[base * depth :, m * tile_rows : (m + 1) * tile_rows] = term

        select_terms(source_ref, refs[base : base + count], refs[base + count], store)
        inside = lax.rem(lax.axis_index("leaf"), inner)
        for o in range(outer):
            cut = [
                terms[(o * inner + i) * part : (o * inner + i + 1) * part, :]
                for i in range(inner)
            ]
            for i in range(inner):
                outs[i][o] = jnp.where(inside == 0, cut[i], cut[inner - 1 - i])

    return local_kernel(
        body,
        [float_array(outer, part, width)] * inner,
        [*done, *gathered, tiles, sources, blocks, live],
        [VMEM] * (base + count + 1) + [SMEM] * 3,
        flops=6 * depth * slots * tile_rows * order,
        scratch=[pltpu.VMEM((streams * depth, width), jnp.float32)],
    )


def turn(rhs, first, last, streams):
    rows, count = rhs.shape[2:]
    depth = count // streams

    def body(rhs_ref, *refs):
        outs, (held, sem) = refs[:-2], refs[-2:]
        copy = pltpu.make_async_copy(rhs_ref.at[0, first:last], held, sem)
        copy.start()
        copy.wait()
        for index in range(last - first):
            wide = jnp.transpose(held[index])
            for i in range(streams):
                outs[index * streams + i][...] = wide[i * depth : (i + 1) * depth]

    return local_kernel(
        body,
        [float_array(depth, rows)] * (streams * (last - first)),
        [rhs],
        [pl.BlockSpec(memory_space=pl.ANY)],
        scratch=[
            pltpu.VMEM((last - first, rows, count), jnp.float32),
            pltpu.SemaphoreType.DMA(()),
        ],
    )


def turn_back(solved, after):
    flat = [value for streams in solved for value in streams]
    streams = len(solved[0])
    depth, rows = flat[0].shape

    def body(*refs):
        out, tie = refs[-2:]
        for index in range(len(solved)):
            wide = jnp.concatenate(
                [refs[index * streams + i][...] for i in range(streams)], axis=0
            )
            out[0, index] = jnp.transpose(wide)
        tie[...] = jnp.zeros(tie.shape, jnp.float32)

    return local_kernel(
        body,
        [float_array(1, len(solved), rows, depth * streams), float_array(8, 128)],
        [*flat, after],
        [VMEM] * len(flat) + [pl.BlockSpec(memory_space=pl.ANY)],
    )


def leaf_exchange(packed):
    outer, inner = leaf_shape()
    part, width = packed[0].shape[1:]
    held = [packed[0]]
    if inner == 2:
        pairs = [(i, i ^ 1) for i in range(outer * inner)]
        held.append(lax.ppermute(packed[1], "leaf", pairs))

    def body(*refs):
        outside = lax.div(lax.axis_index("leaf"), inner)
        for distance in range(outer):
            target = partner(outside, -distance, outer) if distance else outside
            for i in range(inner):
                refs[inner + distance][i] = refs[i][target]

    portions = local_kernel(body, [float_array(inner, part, width)] * outer, held)
    return [portions[0]] + [
        swap(portions[distance], "leaf", distance, inner) for distance in range(1, outer)
    ]


def share_out(received, rhs_turned, order, slots, tile_rows, after):
    members = lax.axis_size("grp")
    ancestors, part, rows = rhs_turned.shape
    inner = received[0].shape[0]
    block_count = ancestors * order // tile_rows
    width = order + (ancestors - 1) * rows

    def body(*refs):
        sources = refs[: len(received)]
        rhs_ref = refs[len(received)]
        outs = refs[len(received) + 2 : -1]
        share = refs[-1]
        me = lax.axis_index("grp")
        totals = [jnp.zeros((part, tile_rows), jnp.float32) for _ in range(block_count)]
        for source in sources:
            for i in range(inner):
                for m in range(slots):
                    tile = source[i, :, m * tile_rows : (m + 1) * tile_rows]
                    tag = source[i, :, slots * tile_rows + m : slots * tile_rows + m + 1]
                    tag = jnp.broadcast_to(tag, tile.shape)
                    for q in range(block_count):
                        totals[q] = totals[q] + jnp.where(tag == float(q), tile, 0.0)
        for q in range(block_count):
            share[:, q * tile_rows : (q + 1) * tile_rows] = -totals[q]
        for a in range(ancestors):
            for j in range(members):
                at = slice(a * order + j * rows, a * order + (j + 1) * rows)
                share[:, at] = share[:, at] + jnp.where(me == j, rhs_ref[a], 0.0)
        for distance in range(members):
            target = partner(me, -distance, members) if distance else me
            out = outs[distance]
            out[:, :order] = share[:, :order]
            for a in range(1, ancestors):
                value = jnp.zeros((part, rows), jnp.float32)
                for j in range(members):
                    at = slice(a * order + j * rows, a * order + (j + 1) * rows)
                    value = jnp.where(target == j, share[:, at], value)
                out[:, order + (a - 1) * rows : order + a * rows] = value

    return local_kernel(
        body,
        [float_array(part, width)] * members,
        [*received, rhs_turned, after],
        [VMEM] * (len(received) + 1) + [pl.BlockSpec(memory_space=pl.ANY)],
        scratch=[pltpu.VMEM((part, ancestors * order), jnp.float32)],
    )


def split_factors(factors, after):
    count = len(factors)

    def body(*refs):
        for i in range(count):
            top, rest = high_low(refs[i][...])
            refs[count + 1 + 2 * i][...] = top
            refs[count + 2 + 2 * i][...] = rest

    outs = []
    for factor in factors:
        outs += [jax.ShapeDtypeStruct(factor.shape, jnp.bfloat16)] * 2
    return local_kernel(
        body,
        outs,
        [*factors, after],
        [VMEM] * count + [pl.BlockSpec(memory_space=pl.ANY)],
        flops=4 * sum(f.size for f in factors),
    )


def solve_first(payloads, top, rest):
    part, width = payloads[0].shape
    rows, order = top.shape[1:]

    def body(*refs):
        sums = refs[: len(payloads)]
        top_ref, rest_ref, out, left = refs[len(payloads) :]
        total = sums[0][...]
        for ref in sums[1:]:
            total = total + ref[...]
        out[...] = split_product(total[:, :order], top_ref[0], rest_ref[0])
        left[...] = total[:, order:]

    return local_kernel(
        body,
        [float_array(part, rows), float_array(part, width - order)],
        [*payloads, top, rest],
        flops=6 * part * rows * order,
    )


def put_in_order(held, whole):
    me = lax.axis_index("grp")
    members = len(held)
    width = held[0].shape[1]
    for j in range(members):
        value = jnp.zeros(held[0].shape, jnp.float32)
        for distance in range(members):
            owner = partner(me, distance, members) if distance else me
            value = jnp.where(owner == j, held[distance], value)
        whole[:, j * width : (j + 1) * width] = value


def apply_first(value, factor):
    members = lax.axis_size("grp")
    depth, width = value.shape
    rows, order = factor.shape[2:]
    held = [value] + [send(value, "grp", distance) for distance in range(1, members)]

    def body(*refs):
        factor_ref, out, whole, matrix, sem = refs[members:]
        copy = pltpu.make_async_copy(factor_ref.at[0, 0], matrix, sem)
        copy.start()
        put_in_order([refs[d][...] for d in range(members)], whole)
        copy.wait()
        top, rest = high_low(matrix[...])
        out[...] = split_product(whole[...], top, rest)

    return local_kernel(
        body,
        [float_array(depth, rows)],
        [*held, factor],
        [VMEM] * members + [pl.BlockSpec(memory_space=pl.ANY)],
        flops=6 * depth * rows * order,
        scratch=[
            pltpu.VMEM((depth, order), jnp.float32),
            pltpu.VMEM((rows, order), jnp.float32),
            pltpu.SemaphoreType.DMA(()),
        ],
        limit=2**24,
    )[0]


def apply_split(pieces, top, rest, index, base=None, begin=0):
    members = lax.axis_size("grp")
    part, width = pieces[0].shape
    rows, order = top.shape[1:]
    extra = [] if base is None else [base]

    def body(*refs):
        top_ref, rest_ref = refs[members : members + 2]
        out, whole = refs[-2:]
        put_in_order([refs[d][...] for d in range(members)], whole)
        result = split_product(whole[...], top_ref[index], rest_ref[index])
        if extra:
            result = refs[members + 2][:, begin : begin + rows] - result
        out[...] = result

    return local_kernel(
        body,
        [float_array(part, rows)],
        [*pieces, top, rest, *extra],
        flops=6 * part * rows * order,
        scratch=[pltpu.VMEM((part, order), jnp.float32)],
    )[0]


def on_device(
    rhs_local,
    diag_inv_local,
    sub_local,
    tiles,
    tile_block,
    tile_source,
    tile_count,
    rhs_anc,
    diag_inv_anc,
    sub_anc,
):
    supernodes, _, order = diag_inv_local.shape[1:]
    rhs_count = rhs_local.shape[-1]
    members = lax.axis_size("grp")
    rows = order // members
    slots, tile_rows = tiles.shape[2:4]

    streams = 2 if rhs_count % 16 == 0 else 1
    residuals = turn(rhs_local, 0, 1, streams)
    later = turn(rhs_local, 1, supernodes, streams)
    solved = []
    gathered = []
    for current in range(supernodes):
        owned = []
        for residual in residuals:
            if current:
                pieces = gather_rows(residual)
                owned.append(apply_pieces(diag_inv_local, current, pieces))
            else:
                owned.append(apply_first(residual, diag_inv_local))
        solved.append(owned)
        held = [gather_rows(value) for value in owned]
        gathered.append([assemble(pieces, order) for pieces in held])
        if current + 1 < supernodes:
            residuals = [
                later[current * streams + i] - apply_pieces(sub_local, current, pieces)
                for i, pieces in enumerate(held)
            ]

    by_stream = [[values[i] for values in gathered] for i in range(streams)]
    done = [tile_terms(values, tiles[0, 0], tile_source) for values in by_stream[:-1]]
    packed = pack_terms(done, by_stream[-1], tiles[0, 0], tile_source, tile_block, tile_count)
    received = leaf_exchange(packed)
    solution_local, tie = turn_back(solved, packed[0])
    shares = share_out(
        received, jnp.swapaxes(rhs_anc, 1, 2), order, slots, tile_rows, tie
    )
    payloads = [shares[0]] + [send(shares[d], "grp", d) for d in range(1, members)]
    inverse_top, inverse_rest, below_top, below_rest = split_factors(
        [diag_inv_anc, sub_anc], shares[0]
    )
    solution, left = solve_first(payloads, inverse_top, inverse_rest)
    solutions = [solution]
    for ancestor in range(1, rhs_anc.shape[0]):
        pieces = [piece for _, piece in gather_rows(solutions[-1])]
        residual = apply_split(
            pieces, below_top, below_rest, ancestor - 1, left, (ancestor - 1) * rows
        )
        pieces = [piece for _, piece in gather_rows(residual)]
        solutions.append(apply_split(pieces, inverse_top, inverse_rest, ancestor))
    solutions = jnp.swapaxes(jnp.stack(solutions), 1, 2)
    return (solution_local, solutions)


def solution(mesh):
    return jax.shard_map(
        on_device,
        mesh=mesh,
        in_specs=(
            P("leaf", None, "grp", None),
            P("leaf", None, "grp", None),
            P("leaf", None, "grp", None),
            P("leaf", "grp", None, None, None),
            P("leaf", "grp", None),
            P("leaf", "grp", None),
            P("leaf", "grp"),
            P(None, "grp", "leaf"),
            P(None, "grp", None),
            P(None, "grp", None),
        ),
        out_specs=(P("leaf", None, "grp", None), P(None, "grp", "leaf")),
        check_vma=False,
    )
```

```python
import jax
import jax.numpy as jnp
from jax import lax
from jax.experimental import pallas as pl
from jax.experimental.pallas import tpu as pltpu
from jax.sharding import PartitionSpec as P

high = lax.Precision.HIGH


def contract_last(left, right):
    return lax.dot_general(
        left,
        right,
        (((left.ndim - 1,), (right.ndim - 1,)), ((), ())),
        precision=high,
        preferred_element_type=jnp.float32,
    )


def partner(index, distance, count):
    if count & (count - 1):
        return lax.rem(index - distance + 2 * count, count)
    return index ^ abs(distance)


def send(value, axis, distance):
    count = lax.axis_size(axis)
    if count & (count - 1):
        pairs = [(i, (i + distance) % count) for i in range(count)]
    else:
        pairs = [(i, i ^ distance) for i in range(count)]
    return lax.ppermute(value, axis, pairs)


def gather_rows(value):
    members = lax.axis_size("grp")
    me = lax.axis_index("grp")
    rows = value.shape[1]
    pieces = [(me * rows, value)]
    for distance in range(1, members):
        owner = partner(me, distance, members)
        pieces.append((owner * rows, send(value, "grp", distance)))
    return pieces


def assemble(pieces, order):
    whole = jnp.zeros((pieces[0][1].shape[0], order), jnp.float32)
    for offset, piece in pieces:
        whole = lax.dynamic_update_slice_in_dim(whole, piece, offset, 1)
    return whole


def apply_pieces(factor, index, pieces):
    total = None
    for offset, piece in pieces:
        size = (1, 1, factor.shape[2], piece.shape[1])
        columns = lax.dynamic_slice(factor, (0, index, 0, offset), size)[0, 0]
        term = contract_last(piece, columns)
        total = term if total is None else total + term
    return total


def swap(value, axis, distance, block):
    count = lax.axis_size(axis)
    outer = count // block
    if outer & (outer - 1):
        pairs = [(i, (i // block + distance) % outer * block + i % block) for i in range(count)]
    else:
        pairs = [(i, (i // block ^ distance) * block + i % block) for i in range(count)]
    return lax.ppermute(value, axis, pairs)


VMEM = pl.BlockSpec(memory_space=pltpu.VMEM)
SMEM = pl.BlockSpec(memory_space=pltpu.SMEM)
HBM = pl.BlockSpec(memory_space=pltpu.HBM)
ANY = pl.BlockSpec(memory_space=pl.ANY)


def local_kernel(body, outs, operands, specs=None, flops=0, scratch=(), limit=None):
    size = sum(o.size * o.dtype.itemsize for o in list(outs) + list(operands))
    return pl.pallas_call(
        body,
        out_shape=list(outs),
        in_specs=specs or [VMEM] * len(operands),
        out_specs=[VMEM] * len(outs),
        scratch_shapes=list(scratch),
        cost_estimate=pl.CostEstimate(flops=flops, bytes_accessed=size, transcendentals=0),
        compiler_params=pltpu.CompilerParams(vmem_limit_bytes=limit or 2 * size + 2**21),
    )(*operands)


def float_array(*shape):
    return jax.ShapeDtypeStruct(shape, jnp.float32)


def high_low(value):
    top = value.astype(jnp.bfloat16)
    return top, (value - top.astype(jnp.float32)).astype(jnp.bfloat16)


def split_product(left, top, rest):
    def dot(x, y):
        return lax.dot_general(
            x, y, (((1,), (1,)), ((), ())), preferred_element_type=jnp.float32
        )

    count = left.shape[0]
    left_top, left_rest = high_low(left)
    both = dot(jnp.concatenate([left_top, left_rest], axis=0), top)
    return both[:count] + (dot(left_top, rest) + both[count:])


def leaf_shape():
    groups = lax.axis_size("leaf")
    inner = 2 if groups % 2 == 0 else 1
    return groups // inner, inner


def select_terms(sources_ref, gathered, tile_refs, store):
    for m in range(tile_refs.shape[0]):
        chosen = gathered[0][...]
        for index in range(1, len(gathered)):
            chosen = jnp.where(sources_ref[0, 0, m] == index, gathered[index][...], chosen)
        top, rest = high_low(tile_refs[m])
        store(m, split_product(chosen, top, rest))


def tile_terms(gathered, tiles, sources):
    slots, tile_rows, order = tiles.shape
    depth = gathered[0].shape[0]
    count = len(gathered)

    def body(*refs):
        out = refs[-1]

        def store(m, term):
            out[:, m * tile_rows : (m + 1) * tile_rows] = term

        select_terms(refs[count + 1], refs[:count], refs[count], store)

    return local_kernel(
        body,
        [float_array(depth, slots * tile_rows)],
        [*gathered, tiles, sources],
        [VMEM] * (count + 1) + [SMEM],
        flops=6 * depth * slots * tile_rows * order,
    )[0]


def pack_terms(done, gathered, tiles, sources, blocks, live):
    outer, inner = leaf_shape()
    slots, tile_rows, order = tiles.shape
    depth = gathered[0].shape[0]
    streams = len(done) + 1
    part = depth * streams // (outer * inner)
    width = (slots + 1) * tile_rows
    count = len(gathered)
    base = len(done)

    def body(*refs):
        source_ref, block_ref, live_ref = refs[base + count + 1 : base + count + 4]
        outs = refs[base + count + 4 : -1]
        terms = refs[-1]
        lanes = lax.broadcasted_iota(jnp.int32, (streams * depth, tile_rows), 1)
        tag = jnp.full((streams * depth, tile_rows), -1.0, jnp.float32)
        for m in range(slots):
            value = jnp.where(m < live_ref[0, 0], block_ref[0, 0, m], -1).astype(jnp.float32)
            tag = jnp.where(lanes == m, value, tag)
        terms[:, slots * tile_rows :] = tag
        for i in range(base):
            terms[i * depth : (i + 1) * depth, : slots * tile_rows] = refs[i][...]

        def store(m, term):
            terms[base * depth :, m * tile_rows : (m + 1) * tile_rows] = term

        select_terms(source_ref, refs[base : base + count], refs[base + count], store)
        inside = lax.rem(lax.axis_index("leaf"), inner)
        for o in range(outer):
            cut = [
                terms[(o * inner + i) * part : (o * inner + i + 1) * part, :]
                for i in range(inner)
            ]
            for i in range(inner):
                outs[i][o] = jnp.where(inside == 0, cut[i], cut[inner - 1 - i])

    return local_kernel(
        body,
        [float_array(outer, part, width)] * inner,
        [*done, *gathered, tiles, sources, blocks, live],
        [VMEM] * (base + count + 1) + [SMEM] * 3,
        flops=6 * depth * slots * tile_rows * order,
        scratch=[pltpu.VMEM((streams * depth, width), jnp.float32)],
    )


def turn(rhs, index, streams, after=None):
    rows, count = rhs.shape[2:]
    depth = count // streams
    extra = [] if after is None else [after]

    def body(rhs_ref, *refs):
        outs, (held, sem) = refs[len(extra) : -2], refs[-2:]
        copy = pltpu.make_async_copy(rhs_ref.at[0, index], held, sem)
        copy.start()
        copy.wait()
        wide = jnp.transpose(held[...])
        for i in range(streams):
            outs[i][...] = wide[i * depth : (i + 1) * depth]

    return local_kernel(
        body,
        [float_array(depth, rows)] * streams,
        [rhs, *extra],
        [HBM] + [ANY] * len(extra),
        scratch=[pltpu.VMEM((rows, count), jnp.float32), pltpu.SemaphoreType.DMA(())],
    )


def turn_back(solved, after):
    flat = [value for streams in solved for value in streams]
    streams = len(solved[0])
    depth, rows = flat[0].shape

    def body(*refs):
        out, tie = refs[-2:]
        for index in range(len(solved)):
            wide = jnp.concatenate(
                [refs[index * streams + i][...] for i in range(streams)], axis=0
            )
            out[0, index] = jnp.transpose(wide)
        tie[...] = jnp.zeros(tie.shape, jnp.float32)

    return local_kernel(
        body,
        [float_array(1, len(solved), rows, depth * streams), float_array(8, 128)],
        [*flat, after],
        [VMEM] * len(flat) + [ANY],
    )


def leaf_exchange(packed):
    outer, inner = leaf_shape()
    part, width = packed[0].shape[1:]
    held = [packed[0]]
    if inner == 2:
        pairs = [(i, i ^ 1) for i in range(outer * inner)]
        held.append(lax.ppermute(packed[1], "leaf", pairs))

    def body(*refs):
        outside = lax.div(lax.axis_index("leaf"), inner)
        for distance in range(outer):
            target = partner(outside, -distance, outer) if distance else outside
            for i in range(inner):
                refs[inner + distance][i] = refs[i][target]

    portions = local_kernel(body, [float_array(inner, part, width)] * outer, held)
    return [portions[0]] + [
        swap(portions[distance], "leaf", distance, inner) for distance in range(1, outer)
    ]


def share_out(received, rhs_turned, order, slots, tile_rows, after):
    members = lax.axis_size("grp")
    ancestors, part, rows = rhs_turned.shape
    inner = received[0].shape[0]
    block_count = ancestors * order // tile_rows
    width = order + (ancestors - 1) * rows

    def body(*refs):
        sources = refs[: len(received)]
        rhs_ref = refs[len(received)]
        outs = refs[len(received) + 2 : -1]
        share = refs[-1]
        me = lax.axis_index("grp")
        totals = [jnp.zeros((part, tile_rows), jnp.float32) for _ in range(block_count)]
        for source in sources:
            for i in range(inner):
                for m in range(slots):
                    tile = source[i, :, m * tile_rows : (m + 1) * tile_rows]
                    tag = source[i, :, slots * tile_rows + m : slots * tile_rows + m + 1]
                    tag = jnp.broadcast_to(tag, tile.shape)
                    for q in range(block_count):
                        totals[q] = totals[q] + jnp.where(tag == float(q), tile, 0.0)
        for q in range(block_count):
            share[:, q * tile_rows : (q + 1) * tile_rows] = -totals[q]
        for a in range(ancestors):
            for j in range(members):
                at = slice(a * order + j * rows, a * order + (j + 1) * rows)
                share[:, at] = share[:, at] + jnp.where(me == j, rhs_ref[a], 0.0)
        for distance in range(members):
            target = partner(me, -distance, members) if distance else me
            out = outs[distance]
            out[:, :order] = share[:, :order]
            for a in range(1, ancestors):
                value = jnp.zeros((part, rows), jnp.float32)
                for j in range(members):
                    at = slice(a * order + j * rows, a * order + (j + 1) * rows)
                    value = jnp.where(target == j, share[:, at], value)
                out[:, order + (a - 1) * rows : order + a * rows] = value

    return local_kernel(
        body,
        [float_array(part, width)] * members,
        [*received, rhs_turned, after],
        [VMEM] * (len(received) + 1) + [ANY],
        scratch=[pltpu.VMEM((part, ancestors * order), jnp.float32)],
    )


def split_factors(factors, after):
    count = len(factors)

    def body(*refs):
        for i in range(count):
            top, rest = high_low(refs[i][...])
            refs[count + 1 + 2 * i][...] = top
            refs[count + 2 + 2 * i][...] = rest

    outs = []
    for factor in factors:
        outs += [jax.ShapeDtypeStruct(factor.shape, jnp.bfloat16)] * 2
    return local_kernel(
        body,
        outs,
        [*factors, after],
        [VMEM] * count + [ANY],
        flops=4 * sum(f.size for f in factors),
    )


def solve_first(payloads, top, rest):
    part, width = payloads[0].shape
    rows, order = top.shape[1:]

    def body(*refs):
        sums = refs[: len(payloads)]
        top_ref, rest_ref, out, left = refs[len(payloads) :]
        total = sums[0][...]
        for ref in sums[1:]:
            total = total + ref[...]
        out[...] = split_product(total[:, :order], top_ref[0], rest_ref[0])
        left[...] = total[:, order:]

    return local_kernel(
        body,
        [float_array(part, rows), float_array(part, width - order)],
        [*payloads, top, rest],
        flops=6 * part * rows * order,
    )


def put_in_order(held, whole):
    me = lax.axis_index("grp")
    members = len(held)
    width = held[0].shape[1]
    for j in range(members):
        value = jnp.zeros(held[0].shape, jnp.float32)
        for distance in range(members):
            owner = partner(me, distance, members) if distance else me
            value = jnp.where(owner == j, held[distance], value)
        whole[:, j * width : (j + 1) * width] = value


def apply_first(value, factor):
    members = lax.axis_size("grp")
    depth, width = value.shape
    rows, order = factor.shape[2:]
    held = [value] + [send(value, "grp", distance) for distance in range(1, members)]

    def body(*refs):
        factor_ref, out, whole, matrix, sem = refs[members:]
        copy = pltpu.make_async_copy(factor_ref.at[0, 0], matrix, sem)
        copy.start()
        put_in_order([refs[d][...] for d in range(members)], whole)
        copy.wait()
        top, rest = high_low(matrix[...])
        out[...] = split_product(whole[...], top, rest)

    return local_kernel(
        body,
        [float_array(depth, rows)],
        [*held, factor],
        [VMEM] * members + [HBM],
        flops=6 * depth * rows * order,
        scratch=[
            pltpu.VMEM((depth, order), jnp.float32),
            pltpu.VMEM((rows, order), jnp.float32),
            pltpu.SemaphoreType.DMA(()),
        ],
        limit=2**24,
    )[0]


def apply_split(pieces, top, rest, index, base=None, begin=0, others=None):
    members = lax.axis_size("grp")
    part, width = pieces[0].shape
    rows, order = top.shape[1:]
    extra = list(others or []) if base is None else [base]

    def body(*refs):
        top_ref, rest_ref = refs[members : members + 2]
        out, whole = refs[-2:]
        put_in_order([refs[d][...] for d in range(members)], whole)
        result = split_product(whole[...], top_ref[index], rest_ref[index])
        if others is not None:
            for i in range(len(others)):
                out[i] = refs[members + 2 + i][...]
            out[len(others)] = result
            return
        if base is not None:
            result = refs[members + 2][:, begin : begin + rows] - result
        out[...] = result

    shape = (part, rows) if others is None else (len(others) + 1, part, rows)
    return local_kernel(
        body,
        [float_array(*shape)],
        [*pieces, top, rest, *extra],
        flops=6 * part * rows * order,
        scratch=[pltpu.VMEM((part, order), jnp.float32)],
    )[0]


def on_device(
    rhs_local,
    diag_inv_local,
    sub_local,
    tiles,
    tile_block,
    tile_source,
    tile_count,
    rhs_anc,
    diag_inv_anc,
    sub_anc,
):
    supernodes, _, order = diag_inv_local.shape[1:]
    rhs_count = rhs_local.shape[-1]
    members = lax.axis_size("grp")
    rows = order // members
    slots, tile_rows = tiles.shape[2:4]

    streams = 2 if rhs_count % 16 == 0 else 1
    residuals = turn(rhs_local, 0, streams)
    solved = []
    gathered = []
    for current in range(supernodes):
        owned = []
        for residual in residuals:
            if current:
                pieces = gather_rows(residual)
                owned.append(apply_pieces(diag_inv_local, current, pieces))
            else:
                owned.append(apply_first(residual, diag_inv_local))
        solved.append(owned)
        held = [gather_rows(value) for value in owned]
        gathered.append([assemble(pieces, order) for pieces in held])
        if current + 1 < supernodes:
            turned = turn(rhs_local, current + 1, streams, owned[0])
            residuals = [
                turned[i] - apply_pieces(sub_local, current, pieces)
                for i, pieces in enumerate(held)
            ]

    by_stream = [[values[i] for values in gathered] for i in range(streams)]
    done = [tile_terms(values, tiles[0, 0], tile_source) for values in by_stream[:-1]]
    packed = pack_terms(done, by_stream[-1], tiles[0, 0], tile_source, tile_block, tile_count)
    received = leaf_exchange(packed)
    solution_local, tie = turn_back(solved, packed[0])
    shares = share_out(
        received, jnp.swapaxes(rhs_anc, 1, 2), order, slots, tile_rows, tie
    )
    payloads = [shares[0]] + [send(shares[d], "grp", d) for d in range(1, members)]
    inverse_top, inverse_rest, below_top, below_rest = split_factors(
        [diag_inv_anc, sub_anc], shares[0]
    )
    solution, left = solve_first(payloads, inverse_top, inverse_rest)
    solutions = [solution]
    ancestors = rhs_anc.shape[0]
    for ancestor in range(1, ancestors):
        pieces = [piece for _, piece in gather_rows(solutions[-1])]
        residual = apply_split(
            pieces, below_top, below_rest, ancestor - 1, left, (ancestor - 1) * rows
        )
        pieces = [piece for _, piece in gather_rows(residual)]
        others = solutions if ancestor + 1 == ancestors else None
        solved_now = apply_split(pieces, inverse_top, inverse_rest, ancestor, others=others)
        solutions.append(solved_now)
    solutions = solutions[-1] if ancestors > 1 else solutions[0][None]
    solutions = jnp.swapaxes(solutions, 1, 2)
    return (solution_local, solutions)


def solution(mesh):
    return jax.shard_map(
        on_device,
        mesh=mesh,
        in_specs=(
            P("leaf", None, "grp", None),
            P("leaf", None, "grp", None),
            P("leaf", None, "grp", None),
            P("leaf", "grp", None, None, None),
            P("leaf", "grp", None),
            P("leaf", "grp", None),
            P("leaf", "grp"),
            P(None, "grp", "leaf"),
            P(None, "grp", None),
            P(None, "grp", None),
        ),
        out_specs=(P("leaf", None, "grp", None), P(None, "grp", "leaf")),
        check_vma=False,
    )
```

```python
import jax
import jax.numpy as jnp
from jax import lax
from jax.experimental import pallas as pl
from jax.experimental.pallas import tpu as pltpu
from jax.sharding import PartitionSpec as P

high = lax.Precision.HIGH


def contract_last(left, right):
    return lax.dot_general(
        left,
        right,
        (((left.ndim - 1,), (right.ndim - 1,)), ((), ())),
        precision=high,
        preferred_element_type=jnp.float32,
    )


def partner(index, distance, count):
    if count & (count - 1):
        return lax.rem(index - distance + 2 * count, count)
    return index ^ abs(distance)


def send(value, axis, distance):
    count = lax.axis_size(axis)
    if count & (count - 1):
        pairs = [(i, (i + distance) % count) for i in range(count)]
    else:
        pairs = [(i, i ^ distance) for i in range(count)]
    return lax.ppermute(value, axis, pairs)


def gather_rows(value):
    members = lax.axis_size("grp")
    me = lax.axis_index("grp")
    rows = value.shape[1]
    pieces = [(me * rows, value)]
    for distance in range(1, members):
        owner = partner(me, distance, members)
        pieces.append((owner * rows, send(value, "grp", distance)))
    return pieces


def assemble(pieces, order):
    whole = jnp.zeros((pieces[0][1].shape[0], order), jnp.float32)
    for offset, piece in pieces:
        whole = lax.dynamic_update_slice_in_dim(whole, piece, offset, 1)
    return whole


def apply_pieces(factor, index, pieces):
    total = None
    for offset, piece in pieces:
        size = (1, 1, factor.shape[2], piece.shape[1])
        columns = lax.dynamic_slice(factor, (0, index, 0, offset), size)[0, 0]
        term = contract_last(piece, columns)
        total = term if total is None else total + term
    return total


def swap(value, axis, distance, block):
    count = lax.axis_size(axis)
    outer = count // block
    if outer & (outer - 1):
        pairs = [(i, (i // block + distance) % outer * block + i % block) for i in range(count)]
    else:
        pairs = [(i, (i // block ^ distance) * block + i % block) for i in range(count)]
    return lax.ppermute(value, axis, pairs)


VMEM = pl.BlockSpec(memory_space=pltpu.VMEM)
SMEM = pl.BlockSpec(memory_space=pltpu.SMEM)
ANY = pl.BlockSpec(memory_space=pl.ANY)


def local_kernel(body, outs, operands, specs=None, flops=0, scratch=(), limit=None):
    size = sum(o.size * o.dtype.itemsize for o in list(outs) + list(operands))
    return pl.pallas_call(
        body,
        out_shape=list(outs),
        in_specs=specs or [VMEM] * len(operands),
        out_specs=[VMEM] * len(outs),
        scratch_shapes=list(scratch),
        cost_estimate=pl.CostEstimate(flops=flops, bytes_accessed=size, transcendentals=0),
        compiler_params=pltpu.CompilerParams(vmem_limit_bytes=limit or 2 * size + 2**21),
    )(*operands)


def float_array(*shape):
    return jax.ShapeDtypeStruct(shape, jnp.float32)


def high_low(value):
    top = value.astype(jnp.bfloat16)
    return top, (value - top.astype(jnp.float32)).astype(jnp.bfloat16)


def split_product(left, top, rest):
    def dot(x, y):
        return lax.dot_general(
            x, y, (((1,), (1,)), ((), ())), preferred_element_type=jnp.float32
        )

    count = left.shape[0]
    left_top, left_rest = high_low(left)
    both = dot(jnp.concatenate([left_top, left_rest], axis=0), top)
    return both[:count] + (dot(left_top, rest) + both[count:])


def leaf_shape():
    groups = lax.axis_size("leaf")
    inner = 2 if groups % 2 == 0 else 1
    return groups // inner, inner


def select_terms(sources_ref, gathered, tile_refs, store):
    for m in range(tile_refs.shape[0]):
        chosen = gathered[0][...]
        for index in range(1, len(gathered)):
            chosen = jnp.where(sources_ref[0, 0, m] == index, gathered[index][...], chosen)
        top, rest = high_low(tile_refs[m])
        store(m, split_product(chosen, top, rest))


def tile_terms(gathered, tiles, sources):
    slots, tile_rows, order = tiles.shape
    depth = gathered[0].shape[0]
    count = len(gathered)

    def body(*refs):
        out = refs[-1]

        def store(m, term):
            out[:, m * tile_rows : (m + 1) * tile_rows] = term

        select_terms(refs[count + 1], refs[:count], refs[count], store)

    return local_kernel(
        body,
        [float_array(depth, slots * tile_rows)],
        [*gathered, tiles, sources],
        [VMEM] * (count + 1) + [SMEM],
        flops=6 * depth * slots * tile_rows * order,
    )[0]


def pack_terms(done, gathered, tiles, sources, blocks, live):
    outer, inner = leaf_shape()
    slots, tile_rows, order = tiles.shape
    depth = gathered[0].shape[0]
    streams = len(done) + 1
    part = depth * streams // (outer * inner)
    width = (slots + 1) * tile_rows
    count = len(gathered)
    base = len(done)

    def body(*refs):
        source_ref, block_ref, live_ref = refs[base + count + 1 : base + count + 4]
        outs = refs[base + count + 4 : -1]
        terms = refs[-1]
        lanes = lax.broadcasted_iota(jnp.int32, (streams * depth, tile_rows), 1)
        tag = jnp.full((streams * depth, tile_rows), -1.0, jnp.float32)
        for m in range(slots):
            value = jnp.where(m < live_ref[0, 0], block_ref[0, 0, m], -1).astype(jnp.float32)
            tag = jnp.where(lanes == m, value, tag)
        terms[:, slots * tile_rows :] = tag
        for i in range(base):
            terms[i * depth : (i + 1) * depth, : slots * tile_rows] = refs[i][...]

        def store(m, term):
            terms[base * depth :, m * tile_rows : (m + 1) * tile_rows] = term

        select_terms(source_ref, refs[base : base + count], refs[base + count], store)
        inside = lax.rem(lax.axis_index("leaf"), inner)
        for o in range(outer):
            cut = [
                terms[(o * inner + i) * part : (o * inner + i + 1) * part, :]
                for i in range(inner)
            ]
            for i in range(inner):
                outs[i][o] = jnp.where(inside == 0, cut[i], cut[inner - 1 - i])

    return local_kernel(
        body,
        [float_array(outer, part, width)] * inner,
        [*done, *gathered, tiles, sources, blocks, live],
        [VMEM] * (base + count + 1) + [SMEM] * 3,
        flops=6 * depth * slots * tile_rows * order,
        scratch=[pltpu.VMEM((streams * depth, width), jnp.float32)],
    )


def turn(rhs, first, last, streams):
    rows, count = rhs.shape[2:]
    depth = count // streams

    def body(rhs_ref, out, held, sem):
        copy = pltpu.make_async_copy(rhs_ref.at[0, first:last], held, sem)
        copy.start()
        copy.wait()
        for index in range(last - first):
            wide = jnp.transpose(held[index])
            for i in range(streams):
                out[index * streams + i] = wide[i * depth : (i + 1) * depth]

    return local_kernel(
        body,
        [float_array(streams * (last - first), depth, rows)],
        [rhs],
        [ANY],
        scratch=[
            pltpu.VMEM((last - first, rows, count), jnp.float32),
            pltpu.SemaphoreType.DMA(()),
        ],
    )[0]


def turn_first(rhs, streams):
    rows, count = rhs.shape[2:]
    depth = count // streams

    def body(rhs_ref, *refs):
        outs, (held, sem) = refs[:-2], refs[-2:]
        copy = pltpu.make_async_copy(rhs_ref.at[0, 0], held, sem)
        copy.start()
        copy.wait()
        wide = jnp.transpose(held[...])
        for i in range(streams):
            outs[i][...] = wide[i * depth : (i + 1) * depth]

    return local_kernel(
        body,
        [float_array(depth, rows)] * streams,
        [rhs],
        [ANY],
        scratch=[pltpu.VMEM((rows, count), jnp.float32), pltpu.SemaphoreType.DMA(())],
    )


def turn_back(solved, after):
    flat = [value for streams in solved for value in streams]
    streams = len(solved[0])
    depth, rows = flat[0].shape

    def body(*refs):
        out, tie = refs[-2:]
        for index in range(len(solved)):
            wide = jnp.concatenate(
                [refs[index * streams + i][...] for i in range(streams)], axis=0
            )
            out[0, index] = jnp.transpose(wide)
        tie[...] = jnp.zeros(tie.shape, jnp.float32)

    return local_kernel(
        body,
        [float_array(1, len(solved), rows, depth * streams), float_array(8, 128)],
        [*flat, after],
        [VMEM] * len(flat) + [ANY],
    )


def leaf_exchange(packed):
    outer, inner = leaf_shape()
    part, width = packed[0].shape[1:]
    held = [packed[0]]
    if inner == 2:
        pairs = [(i, i ^ 1) for i in range(outer * inner)]
        held.append(lax.ppermute(packed[1], "leaf", pairs))

    def body(*refs):
        outside = lax.div(lax.axis_index("leaf"), inner)
        for distance in range(outer):
            target = partner(outside, -distance, outer) if distance else outside
            for i in range(inner):
                refs[inner + distance][i] = refs[i][target]

    portions = local_kernel(body, [float_array(inner, part, width)] * outer, held)
    return [portions[0]] + [
        swap(portions[distance], "leaf", distance, inner) for distance in range(1, outer)
    ]


def share_out(received, rhs_turned, order, slots, tile_rows, after):
    members = lax.axis_size("grp")
    ancestors, part, rows = rhs_turned.shape
    inner = received[0].shape[0]
    block_count = ancestors * order // tile_rows
    width = order + (ancestors - 1) * rows

    def body(*refs):
        sources = refs[: len(received)]
        rhs_ref = refs[len(received)]
        outs = refs[len(received) + 2 : -1]
        share = refs[-1]
        me = lax.axis_index("grp")
        totals = [jnp.zeros((part, tile_rows), jnp.float32) for _ in range(block_count)]
        for source in sources:
            for i in range(inner):
                for m in range(slots):
                    tile = source[i, :, m * tile_rows : (m + 1) * tile_rows]
                    tag = source[i, :, slots * tile_rows + m : slots * tile_rows + m + 1]
                    tag = jnp.broadcast_to(tag, tile.shape)
                    for q in range(block_count):
                        totals[q] = totals[q] + jnp.where(tag == float(q), tile, 0.0)
        for q in range(block_count):
            share[:, q * tile_rows : (q + 1) * tile_rows] = -totals[q]
        for a in range(ancestors):
            for j in range(members):
                at = slice(a * order + j * rows, a * order + (j + 1) * rows)
                share[:, at] = share[:, at] + jnp.where(me == j, rhs_ref[a], 0.0)
        for distance in range(members):
            target = partner(me, -distance, members) if distance else me
            out = outs[distance]
            out[:, :order] = share[:, :order]
            for a in range(1, ancestors):
                value = jnp.zeros((part, rows), jnp.float32)
                for j in range(members):
                    at = slice(a * order + j * rows, a * order + (j + 1) * rows)
                    value = jnp.where(target == j, share[:, at], value)
                out[:, order + (a - 1) * rows : order + a * rows] = value

    return local_kernel(
        body,
        [float_array(part, width)] * members,
        [*received, rhs_turned, after],
        [VMEM] * (len(received) + 1) + [ANY],
        scratch=[pltpu.VMEM((part, ancestors * order), jnp.float32)],
    )


def split_factors(factors, after):
    count = len(factors)

    def body(*refs):
        for i in range(count):
            top, rest = high_low(refs[i][...])
            refs[count + 1 + 2 * i][...] = top
            refs[count + 2 + 2 * i][...] = rest

    outs = []
    for factor in factors:
        outs += [jax.ShapeDtypeStruct(factor.shape, jnp.bfloat16)] * 2
    return local_kernel(
        body,
        outs,
        [*factors, after],
        [VMEM] * count + [ANY],
        flops=4 * sum(f.size for f in factors),
    )


def solve_first(payloads, top, rest):
    part, width = payloads[0].shape
    rows, order = top.shape[1:]

    def body(*refs):
        sums = refs[: len(payloads)]
        top_ref, rest_ref, out, left = refs[len(payloads) :]
        total = sums[0][...]
        for ref in sums[1:]:
            total = total + ref[...]
        out[...] = split_product(total[:, :order], top_ref[0], rest_ref[0])
        left[...] = total[:, order:]

    return local_kernel(
        body,
        [float_array(part, rows), float_array(part, width - order)],
        [*payloads, top, rest],
        flops=6 * part * rows * order,
    )


def put_in_order(held, whole):
    me = lax.axis_index("grp")
    members = len(held)
    width = held[0].shape[1]
    for j in range(members):
        value = jnp.zeros(held[0].shape, jnp.float32)
        for distance in range(members):
            owner = partner(me, distance, members) if distance else me
            value = jnp.where(owner == j, held[distance], value)
        whole[:, j * width : (j + 1) * width] = value


def apply_first(value, factor):
    members = lax.axis_size("grp")
    depth, width = value.shape
    rows, order = factor.shape[2:]
    held = [value] + [send(value, "grp", distance) for distance in range(1, members)]

    def body(*refs):
        factor_ref, out, whole, matrix, sem = refs[members:]
        copy = pltpu.make_async_copy(factor_ref.at[0, 0], matrix, sem)
        copy.start()
        put_in_order([refs[d][...] for d in range(members)], whole)
        copy.wait()
        top, rest = high_low(matrix[...])
        out[...] = split_product(whole[...], top, rest)

    return local_kernel(
        body,
        [float_array(depth, rows)],
        [*held, factor],
        [VMEM] * members + [ANY],
        flops=6 * depth * rows * order,
        scratch=[
            pltpu.VMEM((depth, order), jnp.float32),
            pltpu.VMEM((rows, order), jnp.float32),
            pltpu.SemaphoreType.DMA(()),
        ],
        limit=56 * 2**20,
    )[0]


def apply_split(pieces, top, rest, index, base=None, begin=0, others=None):
    members = lax.axis_size("grp")
    part, width = pieces[0].shape
    rows, order = top.shape[1:]
    extra = list(others or []) if base is None else [base]

    def body(*refs):
        top_ref, rest_ref = refs[members : members + 2]
        out, whole = refs[-2:]
        put_in_order([refs[d][...] for d in range(members)], whole)
        result = split_product(whole[...], top_ref[index], rest_ref[index])
        if others is not None:
            for i in range(len(others)):
                out[i] = refs[members + 2 + i][...]
            out[len(others)] = result
            return
        if base is not None:
            result = refs[members + 2][:, begin : begin + rows] - result
        out[...] = result

    shape = (part, rows) if others is None else (len(others) + 1, part, rows)
    return local_kernel(
        body,
        [float_array(*shape)],
        [*pieces, top, rest, *extra],
        flops=6 * part * rows * order,
        scratch=[pltpu.VMEM((part, order), jnp.float32)],
    )[0]


def on_device(
    rhs_local,
    diag_inv_local,
    sub_local,
    tiles,
    tile_block,
    tile_source,
    tile_count,
    rhs_anc,
    diag_inv_anc,
    sub_anc,
):
    supernodes, _, order = diag_inv_local.shape[1:]
    rhs_count = rhs_local.shape[-1]
    members = lax.axis_size("grp")
    rows = order // members
    slots, tile_rows = tiles.shape[2:4]

    streams = 2 if rhs_count % 16 == 0 else 1
    residuals = turn_first(rhs_local, streams)
    later = turn(rhs_local, 1, supernodes, streams)
    solved = []
    gathered = []
    for current in range(supernodes):
        owned = []
        for residual in residuals:
            if current:
                pieces = gather_rows(residual)
                owned.append(apply_pieces(diag_inv_local, current, pieces))
            else:
                owned.append(apply_first(residual, diag_inv_local))
        solved.append(owned)
        held = [gather_rows(value) for value in owned]
        gathered.append([assemble(pieces, order) for pieces in held])
        if current + 1 < supernodes:
            residuals = [
                later[current * streams + i] - apply_pieces(sub_local, current, pieces)
                for i, pieces in enumerate(held)
            ]

    by_stream = [[values[i] for values in gathered] for i in range(streams)]
    done = [tile_terms(values, tiles[0, 0], tile_source) for values in by_stream[:-1]]
    packed = pack_terms(done, by_stream[-1], tiles[0, 0], tile_source, tile_block, tile_count)
    received = leaf_exchange(packed)
    solution_local, tie = turn_back(solved, packed[0])
    shares = share_out(
        received, jnp.swapaxes(rhs_anc, 1, 2), order, slots, tile_rows, tie
    )
    payloads = [shares[0]] + [send(shares[d], "grp", d) for d in range(1, members)]
    inverse_top, inverse_rest, below_top, below_rest = split_factors(
        [diag_inv_anc, sub_anc], shares[0]
    )
    solution, left = solve_first(payloads, inverse_top, inverse_rest)
    solutions = [solution]
    ancestors = rhs_anc.shape[0]
    for ancestor in range(1, ancestors):
        pieces = [piece for _, piece in gather_rows(solutions[-1])]
        residual = apply_split(
            pieces, below_top, below_rest, ancestor - 1, left, (ancestor - 1) * rows
        )
        pieces = [piece for _, piece in gather_rows(residual)]
        others = solutions if ancestor + 1 == ancestors else None
        solved_now = apply_split(pieces, inverse_top, inverse_rest, ancestor, others=others)
        solutions.append(solved_now)
    solutions = solutions[-1] if ancestors > 1 else solutions[0][None]
    solutions = jnp.swapaxes(solutions, 1, 2)
    return (solution_local, solutions)


def solution(mesh):
    return jax.shard_map(
        on_device,
        mesh=mesh,
        in_specs=(
            P("leaf", None, "grp", None),
            P("leaf", None, "grp", None),
            P("leaf", None, "grp", None),
            P("leaf", "grp", None, None, None),
            P("leaf", "grp", None),
            P("leaf", "grp", None),
            P("leaf", "grp"),
            P(None, "grp", "leaf"),
            P(None, "grp", None),
            P(None, "grp", None),
        ),
        out_specs=(P("leaf", None, "grp", None), P(None, "grp", "leaf")),
        check_vma=False,
    )
```

```python
import jax
import jax.numpy as jnp
from jax import lax
from jax.experimental import pallas as pl
from jax.experimental.pallas import tpu as pltpu
from jax.sharding import PartitionSpec as P

high = lax.Precision.HIGH


def contract_last(left, right):
    return lax.dot_general(
        left,
        right,
        (((left.ndim - 1,), (right.ndim - 1,)), ((), ())),
        precision=high,
        preferred_element_type=jnp.float32,
    )


def partner(index, distance, count):
    if count & (count - 1):
        return lax.rem(index - distance + 2 * count, count)
    return index ^ abs(distance)


def send(value, axis, distance):
    count = lax.axis_size(axis)
    if count & (count - 1):
        pairs = [(i, (i + distance) % count) for i in range(count)]
    else:
        pairs = [(i, i ^ distance) for i in range(count)]
    return lax.ppermute(value, axis, pairs)


def gather_rows(value):
    members = lax.axis_size("grp")
    me = lax.axis_index("grp")
    rows = value.shape[1]
    pieces = [(me * rows, value)]
    for distance in range(1, members):
        owner = partner(me, distance, members)
        pieces.append((owner * rows, send(value, "grp", distance)))
    return pieces


def assemble(pieces, order):
    whole = jnp.zeros((pieces[0][1].shape[0], order), jnp.float32)
    for offset, piece in pieces:
        whole = lax.dynamic_update_slice_in_dim(whole, piece, offset, 1)
    return whole


def pair_up(pieces):
    members = len(pieces)
    if members & (members - 1) or members == 1:
        return pieces
    pairs = []
    for at in range(0, members, 2):
        (first, left), (second, right) = pieces[at : at + 2]
        rows, width = left.shape
        both = jnp.zeros((rows, 2 * width), jnp.float32)
        begin = jnp.minimum(first, second)
        both = lax.dynamic_update_slice_in_dim(both, left, first - begin, 1)
        both = lax.dynamic_update_slice_in_dim(both, right, second - begin, 1)
        pairs.append((begin, both))
    return pairs


def apply_pieces(factor, index, pieces):
    total = None
    for offset, piece in pieces:
        size = (1, 1, factor.shape[2], piece.shape[1])
        columns = lax.dynamic_slice(factor, (0, index, 0, offset), size)[0, 0]
        term = contract_last(piece, columns)
        total = term if total is None else total + term
    return total


def swap(value, axis, distance, block):
    count = lax.axis_size(axis)
    outer = count // block
    if outer & (outer - 1):
        pairs = [(i, (i // block + distance) % outer * block + i % block) for i in range(count)]
    else:
        pairs = [(i, (i // block ^ distance) * block + i % block) for i in range(count)]
    return lax.ppermute(value, axis, pairs)


VMEM = pl.BlockSpec(memory_space=pltpu.VMEM)
SMEM = pl.BlockSpec(memory_space=pltpu.SMEM)
ANY = pl.BlockSpec(memory_space=pl.ANY)


def local_kernel(body, outs, operands, specs=None, flops=0, scratch=(), limit=None):
    size = sum(o.size * o.dtype.itemsize for o in list(outs) + list(operands))
    return pl.pallas_call(
        body,
        out_shape=list(outs),
        in_specs=specs or [VMEM] * len(operands),
        out_specs=[VMEM] * len(outs),
        scratch_shapes=list(scratch),
        cost_estimate=pl.CostEstimate(flops=flops, bytes_accessed=size, transcendentals=0),
        compiler_params=pltpu.CompilerParams(vmem_limit_bytes=limit or 2 * size + 2**21),
    )(*operands)


def float_array(*shape):
    return jax.ShapeDtypeStruct(shape, jnp.float32)


def high_low(value):
    top = value.astype(jnp.bfloat16)
    return top, (value - top.astype(jnp.float32)).astype(jnp.bfloat16)


def split_product(left, top, rest):
    def dot(x, y):
        return lax.dot_general(
            x, y, (((1,), (1,)), ((), ())), preferred_element_type=jnp.float32
        )

    count = left.shape[0]
    left_top, left_rest = high_low(left)
    both = dot(jnp.concatenate([left_top, left_rest], axis=0), top)
    return both[:count] + (dot(left_top, rest) + both[count:])


def leaf_shape():
    groups = lax.axis_size("leaf")
    inner = 2 if groups % 2 == 0 else 1
    return groups // inner, inner


def select_terms(sources_ref, gathered, tile_refs, store):
    for m in range(tile_refs.shape[0]):
        chosen = gathered[0][...]
        for index in range(1, len(gathered)):
            chosen = jnp.where(sources_ref[0, 0, m] == index, gathered[index][...], chosen)
        top, rest = high_low(tile_refs[m])
        store(m, split_product(chosen, top, rest))


def tile_terms(gathered, tiles, sources):
    slots, tile_rows, order = tiles.shape
    depth = gathered[0].shape[0]
    count = len(gathered)

    def body(*refs):
        out = refs[-1]

        def store(m, term):
            out[:, m * tile_rows : (m + 1) * tile_rows] = term

        select_terms(refs[count + 1], refs[:count], refs[count], store)

    return local_kernel(
        body,
        [float_array(depth, slots * tile_rows)],
        [*gathered, tiles, sources],
        [VMEM] * (count + 1) + [SMEM],
        flops=6 * depth * slots * tile_rows * order,
    )[0]


def pack_terms(done, gathered, tiles, sources, blocks, live):
    outer, inner = leaf_shape()
    slots, tile_rows, order = tiles.shape
    depth = gathered[0].shape[0]
    streams = len(done) + 1
    part = depth * streams // (outer * inner)
    width = (slots + 1) * tile_rows
    count = len(gathered)
    base = len(done)

    def body(*refs):
        source_ref, block_ref, live_ref = refs[base + count + 1 : base + count + 4]
        outs = refs[base + count + 4 : -1]
        terms = refs[-1]
        lanes = lax.broadcasted_iota(jnp.int32, (streams * depth, tile_rows), 1)
        tag = jnp.full((streams * depth, tile_rows), -1.0, jnp.float32)
        for m in range(slots):
            value = jnp.where(m < live_ref[0, 0], block_ref[0, 0, m], -1).astype(jnp.float32)
            tag = jnp.where(lanes == m, value, tag)
        terms[:, slots * tile_rows :] = tag
        for i in range(base):
            terms[i * depth : (i + 1) * depth, : slots * tile_rows] = refs[i][...]

        def store(m, term):
            terms[base * depth :, m * tile_rows : (m + 1) * tile_rows] = term

        select_terms(source_ref, refs[base : base + count], refs[base + count], store)
        inside = lax.rem(lax.axis_index("leaf"), inner)
        for o in range(outer):
            cut = [
                terms[(o * inner + i) * part : (o * inner + i + 1) * part, :]
                for i in range(inner)
            ]
            for i in range(inner):
                outs[i][o] = jnp.where(inside == 0, cut[i], cut[inner - 1 - i])

    return local_kernel(
        body,
        [float_array(outer, part, width)] * inner,
        [*done, *gathered, tiles, sources, blocks, live],
        [VMEM] * (base + count + 1) + [SMEM] * 3,
        flops=6 * depth * slots * tile_rows * order,
        scratch=[pltpu.VMEM((streams * depth, width), jnp.float32)],
    )


def turn(rhs, first, last, streams):
    rows, count = rhs.shape[2:]
    depth = count // streams

    def body(rhs_ref, out, held, sem):
        copy = pltpu.make_async_copy(rhs_ref.at[0, first:last], held, sem)
        copy.start()
        copy.wait()
        for index in range(last - first):
            wide = jnp.transpose(held[index])
            for i in range(streams):
                out[index * streams + i] = wide[i * depth : (i + 1) * depth]

    return local_kernel(
        body,
        [float_array(streams * (last - first), depth, rows)],
        [rhs],
        [ANY],
        scratch=[
            pltpu.VMEM((last - first, rows, count), jnp.float32),
            pltpu.SemaphoreType.DMA(()),
        ],
    )[0]


def turn_first(rhs, streams):
    rows, count = rhs.shape[2:]
    depth = count // streams

    def body(rhs_ref, *refs):
        outs, (held, sem) = refs[:-2], refs[-2:]
        copy = pltpu.make_async_copy(rhs_ref.at[0, 0], held, sem)
        copy.start()
        copy.wait()
        wide = jnp.transpose(held[...])
        for i in range(streams):
            outs[i][...] = wide[i * depth : (i + 1) * depth]

    return local_kernel(
        body,
        [float_array(depth, rows)] * streams,
        [rhs],
        [ANY],
        scratch=[pltpu.VMEM((rows, count), jnp.float32), pltpu.SemaphoreType.DMA(())],
    )


def turn_back(solved, after):
    flat = [value for streams in solved for value in streams]
    streams = len(solved[0])
    depth, rows = flat[0].shape

    def body(*refs):
        out, tie = refs[-2:]
        for index in range(len(solved)):
            wide = jnp.concatenate(
                [refs[index * streams + i][...] for i in range(streams)], axis=0
            )
            out[0, index] = jnp.transpose(wide)
        tie[...] = jnp.zeros(tie.shape, jnp.float32)

    return local_kernel(
        body,
        [float_array(1, len(solved), rows, depth * streams), float_array(8, 128)],
        [*flat, after],
        [VMEM] * len(flat) + [ANY],
    )


def leaf_exchange(packed):
    outer, inner = leaf_shape()
    part, width = packed[0].shape[1:]
    held = [packed[0]]
    if inner == 2:
        pairs = [(i, i ^ 1) for i in range(outer * inner)]
        held.append(lax.ppermute(packed[1], "leaf", pairs))

    def body(*refs):
        outside = lax.div(lax.axis_index("leaf"), inner)
        for distance in range(outer):
            target = partner(outside, -distance, outer) if distance else outside
            for i in range(inner):
                refs[inner + distance][i] = refs[i][target]

    portions = local_kernel(body, [float_array(inner, part, width)] * outer, held)
    return [portions[0]] + [
        swap(portions[distance], "leaf", distance, inner) for distance in range(1, outer)
    ]


def share_out(received, rhs_turned, order, slots, tile_rows, after):
    members = lax.axis_size("grp")
    ancestors, part, rows = rhs_turned.shape
    inner = received[0].shape[0]
    block_count = ancestors * order // tile_rows
    width = order + (ancestors - 1) * rows

    def body(*refs):
        sources = refs[: len(received)]
        rhs_ref = refs[len(received)]
        outs = refs[len(received) + 2 : -1]
        share = refs[-1]
        me = lax.axis_index("grp")
        totals = [jnp.zeros((part, tile_rows), jnp.float32) for _ in range(block_count)]
        for source in sources:
            for i in range(inner):
                for m in range(slots):
                    tile = source[i, :, m * tile_rows : (m + 1) * tile_rows]
                    tag = source[i, :, slots * tile_rows + m : slots * tile_rows + m + 1]
                    tag = jnp.broadcast_to(tag, tile.shape)
                    for q in range(block_count):
                        totals[q] = totals[q] + jnp.where(tag == float(q), tile, 0.0)
        for q in range(block_count):
            share[:, q * tile_rows : (q + 1) * tile_rows] = -totals[q]
        for a in range(ancestors):
            for j in range(members):
                at = slice(a * order + j * rows, a * order + (j + 1) * rows)
                share[:, at] = share[:, at] + jnp.where(me == j, rhs_ref[a], 0.0)
        for distance in range(members):
            target = partner(me, -distance, members) if distance else me
            out = outs[distance]
            out[:, :order] = share[:, :order]
            for a in range(1, ancestors):
                value = jnp.zeros((part, rows), jnp.float32)
                for j in range(members):
                    at = slice(a * order + j * rows, a * order + (j + 1) * rows)
                    value = jnp.where(target == j, share[:, at], value)
                out[:, order + (a - 1) * rows : order + a * rows] = value

    return local_kernel(
        body,
        [float_array(part, width)] * members,
        [*received, rhs_turned, after],
        [VMEM] * (len(received) + 1) + [ANY],
        scratch=[pltpu.VMEM((part, ancestors * order), jnp.float32)],
    )


def split_factors(factors, after):
    count = len(factors)

    def body(*refs):
        for i in range(count):
            top, rest = high_low(refs[i][...])
            refs[count + 1 + 2 * i][...] = top
            refs[count + 2 + 2 * i][...] = rest

    outs = []
    for factor in factors:
        outs += [jax.ShapeDtypeStruct(factor.shape, jnp.bfloat16)] * 2
    return local_kernel(
        body,
        outs,
        [*factors, after],
        [VMEM] * count + [ANY],
        flops=4 * sum(f.size for f in factors),
    )


def solve_first(payloads, top, rest):
    part, width = payloads[0].shape
    rows, order = top.shape[1:]

    def body(*refs):
        sums = refs[: len(payloads)]
        top_ref, rest_ref, out, left = refs[len(payloads) :]
        total = sums[0][...]
        for ref in sums[1:]:
            total = total + ref[...]
        out[...] = split_product(total[:, :order], top_ref[0], rest_ref[0])
        left[...] = total[:, order:]

    return local_kernel(
        body,
        [float_array(part, rows), float_array(part, width - order)],
        [*payloads, top, rest],
        flops=6 * part * rows * order,
    )


def put_in_order(held, whole):
    me = lax.axis_index("grp")
    members = len(held)
    width = held[0].shape[1]
    for j in range(members):
        value = jnp.zeros(held[0].shape, jnp.float32)
        for distance in range(members):
            owner = partner(me, distance, members) if distance else me
            value = jnp.where(owner == j, held[distance], value)
        whole[:, j * width : (j + 1) * width] = value


def apply_split(pieces, top, rest, index, base=None, begin=0, others=None):
    members = lax.axis_size("grp")
    part, width = pieces[0].shape
    rows, order = top.shape[1:]
    extra = list(others or []) if base is None else [base]

    def body(*refs):
        top_ref, rest_ref = refs[members : members + 2]
        out, whole = refs[-2:]
        put_in_order([refs[d][...] for d in range(members)], whole)
        result = split_product(whole[...], top_ref[index], rest_ref[index])
        if others is not None:
            for i in range(len(others)):
                out[i] = refs[members + 2 + i][...]
            out[len(others)] = result
            return
        if base is not None:
            result = refs[members + 2][:, begin : begin + rows] - result
        out[...] = result

    shape = (part, rows) if others is None else (len(others) + 1, part, rows)
    return local_kernel(
        body,
        [float_array(*shape)],
        [*pieces, top, rest, *extra],
        flops=6 * part * rows * order,
        scratch=[pltpu.VMEM((part, order), jnp.float32)],
    )[0]


def split_first(factor):
    rows, order = factor.shape[2:]

    def body(factor_ref, top, rest, matrix, sem):
        copy = pltpu.make_async_copy(factor_ref.at[0, 0], matrix, sem)
        copy.start()
        copy.wait()
        top[0], rest[0] = high_low(matrix[...])

    return local_kernel(
        body,
        [jax.ShapeDtypeStruct((1, rows, order), jnp.bfloat16)] * 2,
        [factor],
        [ANY],
        scratch=[pltpu.VMEM((rows, order), jnp.float32), pltpu.SemaphoreType.DMA(())],
        limit=56 * 2**20,
    )


def on_device(
    rhs_local,
    diag_inv_local,
    sub_local,
    tiles,
    tile_block,
    tile_source,
    tile_count,
    rhs_anc,
    diag_inv_anc,
    sub_anc,
):
    supernodes, _, order = diag_inv_local.shape[1:]
    rhs_count = rhs_local.shape[-1]
    members = lax.axis_size("grp")
    rows = order // members
    slots, tile_rows = tiles.shape[2:4]

    streams = 2 if rhs_count % 16 == 0 else 1
    residuals = turn_first(rhs_local, streams)
    later = turn(rhs_local, 1, supernodes, streams)
    first_top, first_rest = split_first(diag_inv_local)
    solved = []
    gathered = []
    for current in range(supernodes):
        owned = []
        for residual in residuals:
            pieces = gather_rows(residual)
            if current:
                owned.append(apply_pieces(diag_inv_local, current, pair_up(pieces)))
            else:
                values = [piece for _, piece in pieces]
                owned.append(apply_split(values, first_top, first_rest, 0))
        solved.append(owned)
        held = [pair_up(gather_rows(value)) for value in owned]
        gathered.append([assemble(pieces, order) for pieces in held])
        if current + 1 < supernodes:
            residuals = [
                later[current * streams + i] - apply_pieces(sub_local, current, pieces)
                for i, pieces in enumerate(held)
            ]

    by_stream = [[values[i] for values in gathered] for i in range(streams)]
    done = [tile_terms(values, tiles[0, 0], tile_source) for values in by_stream[:-1]]
    packed = pack_terms(done, by_stream[-1], tiles[0, 0], tile_source, tile_block, tile_count)
    received = leaf_exchange(packed)
    solution_local, tie = turn_back(solved, packed[0])
    shares = share_out(
        received, jnp.swapaxes(rhs_anc, 1, 2), order, slots, tile_rows, tie
    )
    payloads = [shares[0]] + [send(shares[d], "grp", d) for d in range(1, members)]
    inverse_top, inverse_rest, below_top, below_rest = split_factors(
        [diag_inv_anc, sub_anc], shares[0]
    )
    solution, left = solve_first(payloads, inverse_top, inverse_rest)
    solutions = [solution]
    ancestors = rhs_anc.shape[0]
    for ancestor in range(1, ancestors):
        pieces = [piece for _, piece in gather_rows(solutions[-1])]
        residual = apply_split(
            pieces, below_top, below_rest, ancestor - 1, left, (ancestor - 1) * rows
        )
        pieces = [piece for _, piece in gather_rows(residual)]
        others = solutions if ancestor + 1 == ancestors else None
        solved_now = apply_split(pieces, inverse_top, inverse_rest, ancestor, others=others)
        solutions.append(solved_now)
    solutions = solutions[-1] if ancestors > 1 else solutions[0][None]
    solutions = jnp.swapaxes(solutions, 1, 2)
    return (solution_local, solutions)


def solution(mesh):
    return jax.shard_map(
        on_device,
        mesh=mesh,
        in_specs=(
            P("leaf", None, "grp", None),
            P("leaf", None, "grp", None),
            P("leaf", None, "grp", None),
            P("leaf", "grp", None, None, None),
            P("leaf", "grp", None),
            P("leaf", "grp", None),
            P("leaf", "grp"),
            P(None, "grp", "leaf"),
            P(None, "grp", None),
            P(None, "grp", None),
        ),
        out_specs=(P("leaf", None, "grp", None), P(None, "grp", "leaf")),
        check_vma=False,
    )
```

```python
import jax
import jax.numpy as jnp
from jax import lax
from jax.experimental import pallas as pl
from jax.experimental.pallas import tpu as pltpu
from jax.sharding import PartitionSpec as P

high = lax.Precision.HIGH


def contract_last(left, right):
    return lax.dot_general(
        left,
        right,
        (((left.ndim - 1,), (right.ndim - 1,)), ((), ())),
        precision=high,
        preferred_element_type=jnp.float32,
    )


def partner(index, distance, count):
    if count & (count - 1):
        return lax.rem(index - distance + 2 * count, count)
    return index ^ abs(distance)


def send(value, axis, distance):
    count = lax.axis_size(axis)
    if count & (count - 1):
        pairs = [(i, (i + distance) % count) for i in range(count)]
    else:
        pairs = [(i, i ^ distance) for i in range(count)]
    return lax.ppermute(value, axis, pairs)


def gather_rows(value, ties=()):
    members = lax.axis_size("grp")
    me = lax.axis_index("grp")
    rows = value.shape[1]
    pieces = [(me * rows, value)]
    for distance in range(1, members):
        owner = partner(me, distance, members)
        tied = value
        if distance in dict(ties):
            tied = lax.optimization_barrier((value, dict(ties)[distance]))[0]
        pieces.append((owner * rows, send(tied, "grp", distance)))
    return pieces


def assemble(pieces, order):
    whole = jnp.zeros((pieces[0][1].shape[0], order), jnp.float32)
    for offset, piece in pieces:
        whole = lax.dynamic_update_slice_in_dim(whole, piece, offset, 1)
    return whole


def apply_pieces(factor, index, pieces):
    total = None
    for offset, piece in pieces:
        size = (1, 1, factor.shape[2], piece.shape[1])
        columns = lax.dynamic_slice(factor, (0, index, 0, offset), size)[0, 0]
        term = contract_last(piece, columns)
        total = term if total is None else total + term
    return total


def swap(value, axis, distance, block):
    count = lax.axis_size(axis)
    outer = count // block
    if outer & (outer - 1):
        pairs = [(i, (i // block + distance) % outer * block + i % block) for i in range(count)]
    else:
        pairs = [(i, (i // block ^ distance) * block + i % block) for i in range(count)]
    return lax.ppermute(value, axis, pairs)


VMEM = pl.BlockSpec(memory_space=pltpu.VMEM)
SMEM = pl.BlockSpec(memory_space=pltpu.SMEM)
ANY = pl.BlockSpec(memory_space=pl.ANY)


def local_kernel(body, outs, operands, specs=None, flops=0, scratch=(), limit=None):
    size = sum(o.size * o.dtype.itemsize for o in list(outs) + list(operands))
    return pl.pallas_call(
        body,
        out_shape=list(outs),
        in_specs=specs or [VMEM] * len(operands),
        out_specs=[VMEM] * len(outs),
        scratch_shapes=list(scratch),
        cost_estimate=pl.CostEstimate(flops=flops, bytes_accessed=size, transcendentals=0),
        compiler_params=pltpu.CompilerParams(vmem_limit_bytes=limit or 2 * size + 2**21),
    )(*operands)


def float_array(*shape):
    return jax.ShapeDtypeStruct(shape, jnp.float32)


def high_low(value):
    top = value.astype(jnp.bfloat16)
    return top, (value - top.astype(jnp.float32)).astype(jnp.bfloat16)


def split_product(left, top, rest):
    def dot(x, y):
        return lax.dot_general(
            x, y, (((1,), (1,)), ((), ())), preferred_element_type=jnp.float32
        )

    count = left.shape[0]
    left_top, left_rest = high_low(left)
    both = dot(jnp.concatenate([left_top, left_rest], axis=0), top)
    return both[:count] + (dot(left_top, rest) + both[count:])


def leaf_shape():
    groups = lax.axis_size("leaf")
    inner = 2 if groups % 2 == 0 else 1
    return groups // inner, inner


def select_terms(sources_ref, gathered, tile_refs, store):
    for m in range(tile_refs.shape[0]):
        chosen = gathered[0][...]
        for index in range(1, len(gathered)):
            chosen = jnp.where(sources_ref[0, 0, m] == index, gathered[index][...], chosen)
        top, rest = high_low(tile_refs[m])
        store(m, split_product(chosen, top, rest))


def tile_terms(gathered, tiles, sources):
    slots, tile_rows, order = tiles.shape
    depth = gathered[0].shape[0]
    count = len(gathered)

    def body(*refs):
        out = refs[-1]

        def store(m, term):
            out[:, m * tile_rows : (m + 1) * tile_rows] = term

        select_terms(refs[count + 1], refs[:count], refs[count], store)

    return local_kernel(
        body,
        [float_array(depth, slots * tile_rows)],
        [*gathered, tiles, sources],
        [VMEM] * (count + 1) + [SMEM],
        flops=6 * depth * slots * tile_rows * order,
    )[0]


def pack_terms(done, gathered, tiles, sources, blocks, live):
    outer, inner = leaf_shape()
    slots, tile_rows, order = tiles.shape
    depth = gathered[0].shape[0]
    streams = len(done) + 1
    part = depth * streams // (outer * inner)
    width = (slots + 1) * tile_rows
    count = len(gathered)
    base = len(done)

    def body(*refs):
        source_ref, block_ref, live_ref = refs[base + count + 1 : base + count + 4]
        outs = refs[base + count + 4 : -1]
        terms = refs[-1]
        lanes = lax.broadcasted_iota(jnp.int32, (streams * depth, tile_rows), 1)
        tag = jnp.full((streams * depth, tile_rows), -1.0, jnp.float32)
        for m in range(slots):
            value = jnp.where(m < live_ref[0, 0], block_ref[0, 0, m], -1).astype(jnp.float32)
            tag = jnp.where(lanes == m, value, tag)
        terms[:, slots * tile_rows :] = tag
        for i in range(base):
            terms[i * depth : (i + 1) * depth, : slots * tile_rows] = refs[i][...]

        def store(m, term):
            terms[base * depth :, m * tile_rows : (m + 1) * tile_rows] = term

        select_terms(source_ref, refs[base : base + count], refs[base + count], store)
        inside = lax.rem(lax.axis_index("leaf"), inner)
        for o in range(outer):
            cut = [
                terms[(o * inner + i) * part : (o * inner + i + 1) * part, :]
                for i in range(inner)
            ]
            for i in range(inner):
                outs[i][o] = jnp.where(inside == 0, cut[i], cut[inner - 1 - i])

    return local_kernel(
        body,
        [float_array(outer, part, width)] * inner,
        [*done, *gathered, tiles, sources, blocks, live],
        [VMEM] * (base + count + 1) + [SMEM] * 3,
        flops=6 * depth * slots * tile_rows * order,
        scratch=[pltpu.VMEM((streams * depth, width), jnp.float32)],
    )


def turn(rhs, first, last, streams):
    rows, count = rhs.shape[2:]
    depth = count // streams

    def body(rhs_ref, out, held, sem):
        copy = pltpu.make_async_copy(rhs_ref.at[0, first:last], held, sem)
        copy.start()
        copy.wait()
        for index in range(last - first):
            wide = jnp.transpose(held[index])
            for i in range(streams):
                out[index * streams + i] = wide[i * depth : (i + 1) * depth]

    return local_kernel(
        body,
        [float_array(streams * (last - first), depth, rows)],
        [rhs],
        [ANY],
        scratch=[
            pltpu.VMEM((last - first, rows, count), jnp.float32),
            pltpu.SemaphoreType.DMA(()),
        ],
    )[0]


def turn_first(rhs, streams):
    rows, count = rhs.shape[2:]
    depth = count // streams

    def body(rhs_ref, *refs):
        outs, (held, sem) = refs[:-2], refs[-2:]
        copy = pltpu.make_async_copy(rhs_ref.at[0, 0], held, sem)
        copy.start()
        copy.wait()
        wide = jnp.transpose(held[...])
        for i in range(streams):
            outs[i][...] = wide[i * depth : (i + 1) * depth]

    return local_kernel(
        body,
        [float_array(depth, rows)] * streams,
        [rhs],
        [ANY],
        scratch=[pltpu.VMEM((rows, count), jnp.float32), pltpu.SemaphoreType.DMA(())],
    )


def turn_back(solved, after):
    flat = [value for streams in solved for value in streams]
    streams = len(solved[0])
    depth, rows = flat[0].shape

    def body(*refs):
        out, tie = refs[-2:]
        for index in range(len(solved)):
            wide = jnp.concatenate(
                [refs[index * streams + i][...] for i in range(streams)], axis=0
            )
            out[0, index] = jnp.transpose(wide)
        tie[...] = jnp.zeros(tie.shape, jnp.float32)

    return local_kernel(
        body,
        [float_array(1, len(solved), rows, depth * streams), float_array(8, 128)],
        [*flat, after],
        [VMEM] * len(flat) + [ANY],
    )


def leaf_exchange(packed):
    outer, inner = leaf_shape()
    part, width = packed[0].shape[1:]
    held = [packed[0]]
    if inner == 2:
        pairs = [(i, i ^ 1) for i in range(outer * inner)]
        held.append(lax.ppermute(packed[1], "leaf", pairs))

    def body(*refs):
        outside = lax.div(lax.axis_index("leaf"), inner)
        for distance in range(outer):
            target = partner(outside, -distance, outer) if distance else outside
            for i in range(inner):
                refs[inner + distance][i] = refs[i][target]

    portions = local_kernel(body, [float_array(inner, part, width)] * outer, held)
    return [portions[0]] + [
        swap(portions[distance], "leaf", distance, inner) for distance in range(1, outer)
    ]


def share_out(received, rhs_turned, order, slots, tile_rows, after):
    members = lax.axis_size("grp")
    ancestors, part, rows = rhs_turned.shape
    inner = received[0].shape[0]
    block_count = ancestors * order // tile_rows
    width = order + (ancestors - 1) * rows

    def body(*refs):
        sources = refs[: len(received)]
        rhs_ref = refs[len(received)]
        outs = refs[len(received) + 2 : -1]
        share = refs[-1]
        me = lax.axis_index("grp")
        totals = [jnp.zeros((part, tile_rows), jnp.float32) for _ in range(block_count)]
        for source in sources:
            for i in range(inner):
                for m in range(slots):
                    tile = source[i, :, m * tile_rows : (m + 1) * tile_rows]
                    tag = source[i, :, slots * tile_rows + m : slots * tile_rows + m + 1]
                    tag = jnp.broadcast_to(tag, tile.shape)
                    for q in range(block_count):
                        totals[q] = totals[q] + jnp.where(tag == float(q), tile, 0.0)
        for q in range(block_count):
            share[:, q * tile_rows : (q + 1) * tile_rows] = -totals[q]
        for a in range(ancestors):
            for j in range(members):
                at = slice(a * order + j * rows, a * order + (j + 1) * rows)
                share[:, at] = share[:, at] + jnp.where(me == j, rhs_ref[a], 0.0)
        for distance in range(members):
            target = partner(me, -distance, members) if distance else me
            out = outs[distance]
            out[:, :order] = share[:, :order]
            for a in range(1, ancestors):
                value = jnp.zeros((part, rows), jnp.float32)
                for j in range(members):
                    at = slice(a * order + j * rows, a * order + (j + 1) * rows)
                    value = jnp.where(target == j, share[:, at], value)
                out[:, order + (a - 1) * rows : order + a * rows] = value

    return local_kernel(
        body,
        [float_array(part, width)] * members,
        [*received, rhs_turned, after],
        [VMEM] * (len(received) + 1) + [ANY],
        scratch=[pltpu.VMEM((part, ancestors * order), jnp.float32)],
    )


def split_factors(factors, after):
    count = len(factors)

    def body(*refs):
        for i in range(count):
            top, rest = high_low(refs[i][...])
            refs[count + 1 + 2 * i][...] = top
            refs[count + 2 + 2 * i][...] = rest

    outs = []
    for factor in factors:
        outs += [jax.ShapeDtypeStruct(factor.shape, jnp.bfloat16)] * 2
    return local_kernel(
        body,
        outs,
        [*factors, after],
        [VMEM] * count + [ANY],
        flops=4 * sum(f.size for f in factors),
    )


def solve_first(payloads, top, rest):
    part, width = payloads[0].shape
    rows, order = top.shape[1:]

    def body(*refs):
        sums = refs[: len(payloads)]
        top_ref, rest_ref, out, left = refs[len(payloads) :]
        total = sums[0][...]
        for ref in sums[1:]:
            total = total + ref[...]
        out[...] = split_product(total[:, :order], top_ref[0], rest_ref[0])
        left[...] = total[:, order:]

    return local_kernel(
        body,
        [float_array(part, rows), float_array(part, width - order)],
        [*payloads, top, rest],
        flops=6 * part * rows * order,
    )


def put_in_order(held, whole):
    me = lax.axis_index("grp")
    members = len(held)
    width = held[0].shape[1]
    for j in range(members):
        value = jnp.zeros(held[0].shape, jnp.float32)
        for distance in range(members):
            owner = partner(me, distance, members) if distance else me
            value = jnp.where(owner == j, held[distance], value)
        whole[:, j * width : (j + 1) * width] = value


def apply_split(pieces, top, rest, index, base=None, begin=0, others=None):
    members = lax.axis_size("grp")
    part, width = pieces[0].shape
    rows, order = top.shape[1:]
    extra = list(others or []) if base is None else [base]

    def body(*refs):
        top_ref, rest_ref = refs[members : members + 2]
        out, whole = refs[-2:]
        put_in_order([refs[d][...] for d in range(members)], whole)
        result = split_product(whole[...], top_ref[index], rest_ref[index])
        if others is not None:
            for i in range(len(others)):
                out[i] = refs[members + 2 + i][...]
            out[len(others)] = result
            return
        if base is not None:
            result = refs[members + 2][:, begin : begin + rows] - result
        out[...] = result

    shape = (part, rows) if others is None else (len(others) + 1, part, rows)
    return local_kernel(
        body,
        [float_array(*shape)],
        [*pieces, top, rest, *extra],
        flops=6 * part * rows * order,
        scratch=[pltpu.VMEM((part, order), jnp.float32)],
    )[0]


def on_device(
    rhs_local,
    diag_inv_local,
    sub_local,
    tiles,
    tile_block,
    tile_source,
    tile_count,
    rhs_anc,
    diag_inv_anc,
    sub_anc,
):
    supernodes, _, order = diag_inv_local.shape[1:]
    rhs_count = rhs_local.shape[-1]
    members = lax.axis_size("grp")
    rows = order // members
    slots, tile_rows = tiles.shape[2:4]

    streams = 2 if rhs_count % 16 == 0 else 1
    residuals = turn_first(rhs_local, streams)
    later = turn(rhs_local, 1, supernodes, streams)
    first = diag_inv_local[0, 0]
    rounded = lax.reduce_precision(first, 8, 7)
    first_top = rounded.astype(jnp.bfloat16)[None]
    first_rest = (first - rounded).astype(jnp.bfloat16)[None]
    solved = [[None] * streams for _ in range(supernodes)]
    gathered = [[None] * streams for _ in range(supernodes)]
    values = list(residuals)
    last = None
    for step in range(2 * supernodes):
        current = step // 2
        for i in range(streams):
            ties = [(1, last[1][1])] if last is not None else []
            pieces = gather_rows(values[i], ties)
            if step == 0:
                owned = apply_split([p for _, p in pieces], first_top, first_rest, 0)
            else:
                whole = assemble(pieces, order)
                if step % 2 == 0:
                    owned = contract_last(whole, diag_inv_local[0, current])
                elif current + 1 < supernodes:
                    owned = later[current * streams + i] - contract_last(whole, sub_local[0, current])
            if step % 2 == 0:
                solved[current][i] = owned
            else:
                gathered[current][i] = whole
            values[i] = owned
            last = pieces

    by_stream = [[values[i] for values in gathered] for i in range(streams)]
    done = [tile_terms(values, tiles[0, 0], tile_source) for values in by_stream[:-1]]
    packed = pack_terms(done, by_stream[-1], tiles[0, 0], tile_source, tile_block, tile_count)
    received = leaf_exchange(packed)
    solution_local, tie = turn_back(solved, packed[0])
    shares = share_out(
        received, jnp.swapaxes(rhs_anc, 1, 2), order, slots, tile_rows, tie
    )
    payloads = [shares[0]] + [send(shares[d], "grp", d) for d in range(1, members)]
    inverse_top, inverse_rest, below_top, below_rest = split_factors(
        [diag_inv_anc, sub_anc], shares[0]
    )
    solution, left = solve_first(payloads, inverse_top, inverse_rest)
    solutions = [solution]
    ancestors = rhs_anc.shape[0]
    for ancestor in range(1, ancestors):
        pieces = [piece for _, piece in gather_rows(solutions[-1])]
        residual = apply_split(
            pieces, below_top, below_rest, ancestor - 1, left, (ancestor - 1) * rows
        )
        pieces = [piece for _, piece in gather_rows(residual)]
        others = solutions if ancestor + 1 == ancestors else None
        solved_now = apply_split(pieces, inverse_top, inverse_rest, ancestor, others=others)
        solutions.append(solved_now)
    solutions = solutions[-1] if ancestors > 1 else solutions[0][None]
    solutions = jnp.swapaxes(solutions, 1, 2)
    return (solution_local, solutions)


def solution(mesh):
    return jax.shard_map(
        on_device,
        mesh=mesh,
        in_specs=(
            P("leaf", None, "grp", None),
            P("leaf", None, "grp", None),
            P("leaf", None, "grp", None),
            P("leaf", "grp", None, None, None),
            P("leaf", "grp", None),
            P("leaf", "grp", None),
            P("leaf", "grp"),
            P(None, "grp", "leaf"),
            P(None, "grp", None),
            P(None, "grp", None),
        ),
        out_specs=(P("leaf", None, "grp", None), P(None, "grp", "leaf")),
        check_vma=False,
    )
```

```python
import jax
import jax.numpy as jnp
from jax import lax
from jax.experimental import pallas as pl
from jax.experimental.pallas import tpu as pltpu
from jax.sharding import PartitionSpec as P

high = lax.Precision.HIGH


def contract_last(left, right):
    return lax.dot_general(
        left,
        right,
        (((left.ndim - 1,), (right.ndim - 1,)), ((), ())),
        precision=high,
        preferred_element_type=jnp.float32,
    )


def partner(index, distance, count):
    if count & (count - 1):
        return lax.rem(index - distance + 2 * count, count)
    return index ^ abs(distance)


def send(value, axis, distance):
    count = lax.axis_size(axis)
    if count & (count - 1):
        pairs = [(i, (i + distance) % count) for i in range(count)]
    else:
        pairs = [(i, i ^ distance) for i in range(count)]
    return lax.ppermute(value, axis, pairs)


def gather_rows(value, ties=()):
    members = lax.axis_size("grp")
    me = lax.axis_index("grp")
    rows = value.shape[1]
    pieces = [(me * rows, value)]
    for distance in range(1, members):
        owner = partner(me, distance, members)
        tied = value
        if distance in dict(ties):
            tied = lax.optimization_barrier((value, dict(ties)[distance]))[0]
        pieces.append((owner * rows, send(tied, "grp", distance)))
    return pieces


def assemble(pieces, order):
    whole = jnp.zeros((pieces[0][1].shape[0], order), jnp.float32)
    for offset, piece in pieces:
        whole = lax.dynamic_update_slice_in_dim(whole, piece, offset, 1)
    return whole


def apply_pieces(factor, index, pieces):
    total = None
    for offset, piece in pieces:
        size = (1, 1, factor.shape[2], piece.shape[1])
        columns = lax.dynamic_slice(factor, (0, index, 0, offset), size)[0, 0]
        term = contract_last(piece, columns)
        total = term if total is None else total + term
    return total


def swap(value, axis, distance, block):
    count = lax.axis_size(axis)
    outer = count // block
    if outer & (outer - 1):
        pairs = [(i, (i // block + distance) % outer * block + i % block) for i in range(count)]
    else:
        pairs = [(i, (i // block ^ distance) * block + i % block) for i in range(count)]
    return lax.ppermute(value, axis, pairs)


VMEM = pl.BlockSpec(memory_space=pltpu.VMEM)
SMEM = pl.BlockSpec(memory_space=pltpu.SMEM)
ANY = pl.BlockSpec(memory_space=pl.ANY)


def local_kernel(body, outs, operands, specs=None, flops=0, scratch=(), limit=None):
    size = sum(o.size * o.dtype.itemsize for o in list(outs) + list(operands))
    return pl.pallas_call(
        body,
        out_shape=list(outs),
        in_specs=specs or [VMEM] * len(operands),
        out_specs=[VMEM] * len(outs),
        scratch_shapes=list(scratch),
        cost_estimate=pl.CostEstimate(flops=flops, bytes_accessed=size, transcendentals=0),
        compiler_params=pltpu.CompilerParams(vmem_limit_bytes=limit or 2 * size + 2**21),
    )(*operands)


def float_array(*shape):
    return jax.ShapeDtypeStruct(shape, jnp.float32)


def high_low(value):
    top = value.astype(jnp.bfloat16)
    return top, (value - top.astype(jnp.float32)).astype(jnp.bfloat16)


def split_product(left, top, rest):
    def dot(x, y):
        return lax.dot_general(
            x, y, (((1,), (1,)), ((), ())), preferred_element_type=jnp.float32
        )

    count = left.shape[0]
    left_top, left_rest = high_low(left)
    both = dot(jnp.concatenate([left_top, left_rest], axis=0), top)
    return both[:count] + (dot(left_top, rest) + both[count:])


def leaf_shape():
    groups = lax.axis_size("leaf")
    inner = 2 if groups % 2 == 0 else 1
    return groups // inner, inner


def select_terms(sources_ref, gathered, tile_refs, store):
    for m in range(tile_refs.shape[0]):
        chosen = gathered[0][...]
        for index in range(1, len(gathered)):
            chosen = jnp.where(sources_ref[0, 0, m] == index, gathered[index][...], chosen)
        top, rest = high_low(tile_refs[m])
        store(m, split_product(chosen, top, rest))


def tile_terms(gathered, tiles, sources):
    slots, tile_rows, order = tiles.shape
    depth = gathered[0].shape[0]
    count = len(gathered)

    def body(*refs):
        out = refs[-1]

        def store(m, term):
            out[:, m * tile_rows : (m + 1) * tile_rows] = term

        select_terms(refs[count + 1], refs[:count], refs[count], store)

    return local_kernel(
        body,
        [float_array(depth, slots * tile_rows)],
        [*gathered, tiles, sources],
        [VMEM] * (count + 1) + [SMEM],
        flops=6 * depth * slots * tile_rows * order,
    )[0]


def pack_terms(done, gathered, tiles, sources, blocks, live):
    outer, inner = leaf_shape()
    slots, tile_rows, order = tiles.shape
    depth = gathered[0].shape[0]
    streams = len(done) + 1
    part = depth * streams // (outer * inner)
    width = (slots + 1) * tile_rows
    count = len(gathered)
    base = len(done)

    def body(*refs):
        source_ref, block_ref, live_ref = refs[base + count + 1 : base + count + 4]
        outs = refs[base + count + 4 : -1]
        terms = refs[-1]
        lanes = lax.broadcasted_iota(jnp.int32, (streams * depth, tile_rows), 1)
        tag = jnp.full((streams * depth, tile_rows), -1.0, jnp.float32)
        for m in range(slots):
            value = jnp.where(m < live_ref[0, 0], block_ref[0, 0, m], -1).astype(jnp.float32)
            tag = jnp.where(lanes == m, value, tag)
        terms[:, slots * tile_rows :] = tag
        for i in range(base):
            terms[i * depth : (i + 1) * depth, : slots * tile_rows] = refs[i][...]

        def store(m, term):
            terms[base * depth :, m * tile_rows : (m + 1) * tile_rows] = term

        select_terms(source_ref, refs[base : base + count], refs[base + count], store)
        inside = lax.rem(lax.axis_index("leaf"), inner)
        for o in range(outer):
            cut = [
                terms[(o * inner + i) * part : (o * inner + i + 1) * part, :]
                for i in range(inner)
            ]
            for i in range(inner):
                outs[i][o] = jnp.where(inside == 0, cut[i], cut[inner - 1 - i])

    return local_kernel(
        body,
        [float_array(outer, part, width)] * inner,
        [*done, *gathered, tiles, sources, blocks, live],
        [VMEM] * (base + count + 1) + [SMEM] * 3,
        flops=6 * depth * slots * tile_rows * order,
        scratch=[pltpu.VMEM((streams * depth, width), jnp.float32)],
    )


def turn(rhs, first, last, streams):
    rows, count = rhs.shape[2:]
    depth = count // streams

    def body(rhs_ref, out, held, sem):
        copy = pltpu.make_async_copy(rhs_ref.at[0, first:last], held, sem)
        copy.start()
        copy.wait()
        for index in range(last - first):
            wide = jnp.transpose(held[index])
            for i in range(streams):
                out[index * streams + i] = wide[i * depth : (i + 1) * depth]

    return local_kernel(
        body,
        [float_array(streams * (last - first), depth, rows)],
        [rhs],
        [ANY],
        scratch=[
            pltpu.VMEM((last - first, rows, count), jnp.float32),
            pltpu.SemaphoreType.DMA(()),
        ],
    )[0]


def turn_first(rhs, streams):
    rows, count = rhs.shape[2:]
    depth = count // streams

    def body(rhs_ref, *refs):
        outs, (held, sem) = refs[:-2], refs[-2:]
        copy = pltpu.make_async_copy(rhs_ref.at[0, 0], held, sem)
        copy.start()
        copy.wait()
        wide = jnp.transpose(held[...])
        for i in range(streams):
            outs[i][...] = wide[i * depth : (i + 1) * depth]

    return local_kernel(
        body,
        [float_array(depth, rows)] * streams,
        [rhs],
        [ANY],
        scratch=[pltpu.VMEM((rows, count), jnp.float32), pltpu.SemaphoreType.DMA(())],
    )


def turn_back(solved, after):
    flat = [value for streams in solved for value in streams]
    streams = len(solved[0])
    depth, rows = flat[0].shape

    def body(*refs):
        out, tie = refs[-2:]
        for index in range(len(solved)):
            wide = jnp.concatenate(
                [refs[index * streams + i][...] for i in range(streams)], axis=0
            )
            out[0, index] = jnp.transpose(wide)
        tie[...] = jnp.zeros(tie.shape, jnp.float32)

    return local_kernel(
        body,
        [float_array(1, len(solved), rows, depth * streams), float_array(8, 128)],
        [*flat, after],
        [VMEM] * len(flat) + [ANY],
    )


def leaf_exchange(packed):
    outer, inner = leaf_shape()
    part, width = packed[0].shape[1:]
    held = [packed[0]]
    if inner == 2:
        pairs = [(i, i ^ 1) for i in range(outer * inner)]
        held.append(lax.ppermute(packed[1], "leaf", pairs))

    def body(*refs):
        outside = lax.div(lax.axis_index("leaf"), inner)
        for distance in range(outer):
            target = partner(outside, -distance, outer) if distance else outside
            for i in range(inner):
                refs[inner + distance][i] = refs[i][target]

    portions = local_kernel(body, [float_array(inner, part, width)] * outer, held)
    return [portions[0]] + [
        swap(portions[distance], "leaf", distance, inner) for distance in range(1, outer)
    ]


def share_out(received, rhs_turned, order, slots, tile_rows, after):
    members = lax.axis_size("grp")
    ancestors, part, rows = rhs_turned.shape
    inner = received[0].shape[0]
    block_count = ancestors * order // tile_rows
    width = order + (ancestors - 1) * rows

    def body(*refs):
        sources = refs[: len(received)]
        rhs_ref = refs[len(received)]
        outs = refs[len(received) + 2 : -1]
        share = refs[-1]
        me = lax.axis_index("grp")
        totals = [jnp.zeros((part, tile_rows), jnp.float32) for _ in range(block_count)]
        for source in sources:
            for i in range(inner):
                for m in range(slots):
                    tile = source[i, :, m * tile_rows : (m + 1) * tile_rows]
                    tag = source[i, :, slots * tile_rows + m : slots * tile_rows + m + 1]
                    tag = jnp.broadcast_to(tag, tile.shape)
                    for q in range(block_count):
                        totals[q] = totals[q] + jnp.where(tag == float(q), tile, 0.0)
        for q in range(block_count):
            share[:, q * tile_rows : (q + 1) * tile_rows] = -totals[q]
        for a in range(ancestors):
            for j in range(members):
                at = slice(a * order + j * rows, a * order + (j + 1) * rows)
                share[:, at] = share[:, at] + jnp.where(me == j, rhs_ref[a], 0.0)
        for distance in range(members):
            target = partner(me, -distance, members) if distance else me
            out = outs[distance]
            out[:, :order] = share[:, :order]
            for a in range(1, ancestors):
                value = jnp.zeros((part, rows), jnp.float32)
                for j in range(members):
                    at = slice(a * order + j * rows, a * order + (j + 1) * rows)
                    value = jnp.where(target == j, share[:, at], value)
                out[:, order + (a - 1) * rows : order + a * rows] = value

    return local_kernel(
        body,
        [float_array(part, width)] * members,
        [*received, rhs_turned, after],
        [VMEM] * (len(received) + 1) + [ANY],
        scratch=[pltpu.VMEM((part, ancestors * order), jnp.float32)],
    )


def split_factors(factors, after):
    count = len(factors)

    def body(*refs):
        for i in range(count):
            top, rest = high_low(refs[i][...])
            refs[count + 1 + 2 * i][...] = top
            refs[count + 2 + 2 * i][...] = rest

    outs = []
    for factor in factors:
        outs += [jax.ShapeDtypeStruct(factor.shape, jnp.bfloat16)] * 2
    return local_kernel(
        body,
        outs,
        [*factors, after],
        [VMEM] * count + [ANY],
        flops=4 * sum(f.size for f in factors),
    )


def solve_first(payloads, top, rest):
    part, width = payloads[0].shape
    rows, order = top.shape[1:]

    def body(*refs):
        sums = refs[: len(payloads)]
        top_ref, rest_ref, out, left = refs[len(payloads) :]
        total = sums[0][...]
        for ref in sums[1:]:
            total = total + ref[...]
        out[...] = split_product(total[:, :order], top_ref[0], rest_ref[0])
        left[...] = total[:, order:]

    return local_kernel(
        body,
        [float_array(part, rows), float_array(part, width - order)],
        [*payloads, top, rest],
        flops=6 * part * rows * order,
    )


def put_in_order(held, whole):
    me = lax.axis_index("grp")
    members = len(held)
    width = held[0].shape[1]
    for j in range(members):
        value = jnp.zeros(held[0].shape, jnp.float32)
        for distance in range(members):
            owner = partner(me, distance, members) if distance else me
            value = jnp.where(owner == j, held[distance], value)
        whole[:, j * width : (j + 1) * width] = value


def apply_split(pieces, top, rest, index, base=None, begin=0, others=None):
    members = lax.axis_size("grp")
    part, width = pieces[0].shape
    rows, order = top.shape[1:]
    extra = list(others or []) if base is None else [base]

    def body(*refs):
        top_ref, rest_ref = refs[members : members + 2]
        out, whole = refs[-2:]
        put_in_order([refs[d][...] for d in range(members)], whole)
        result = split_product(whole[...], top_ref[index], rest_ref[index])
        if others is not None:
            for i in range(len(others)):
                out[i] = refs[members + 2 + i][...]
            out[len(others)] = result
            return
        if base is not None:
            result = refs[members + 2][:, begin : begin + rows] - result
        out[...] = result

    shape = (part, rows) if others is None else (len(others) + 1, part, rows)
    return local_kernel(
        body,
        [float_array(*shape)],
        [*pieces, top, rest, *extra],
        flops=6 * part * rows * order,
        scratch=[pltpu.VMEM((part, order), jnp.float32)],
    )[0]


def on_device(
    rhs_local,
    diag_inv_local,
    sub_local,
    tiles,
    tile_block,
    tile_source,
    tile_count,
    rhs_anc,
    diag_inv_anc,
    sub_anc,
):
    supernodes, _, order = diag_inv_local.shape[1:]
    rhs_count = rhs_local.shape[-1]
    members = lax.axis_size("grp")
    rows = order // members
    slots, tile_rows = tiles.shape[2:4]

    streams = 2 if rhs_count % 16 == 0 else 1
    residuals = turn_first(rhs_local, streams)
    later = turn(rhs_local, 1, supernodes, streams)
    first = diag_inv_local[0, 0]
    rounded = lax.reduce_precision(first, 8, 7)
    first_top = rounded.astype(jnp.bfloat16)[None]
    first_rest = (first - rounded).astype(jnp.bfloat16)[None]
    solved = [[None] * streams for _ in range(supernodes)]
    gathered = [[None] * streams for _ in range(supernodes)]
    values = list(residuals)
    last = None
    for step in range(2 * supernodes):
        current = step // 2
        for i in range(streams):
            turn_taken = step > 0 and last is not None
            ties = [(1, last[0][1][1])] if step * streams + i > streams else []
            pieces = gather_rows(values[i], ties)
            if turn_taken and True:
                offset, piece = pieces[1]
                pieces[1] = (offset, lax.optimization_barrier((piece, last[1]))[0])
            if step == 0:
                owned = apply_split([p for _, p in pieces], first_top, first_rest, 0)
            else:
                whole = assemble(pieces, order)
                if step % 2 == 0:
                    owned = contract_last(whole, diag_inv_local[0, current])
                elif current + 1 < supernodes:
                    owned = later[current * streams + i] - contract_last(whole, sub_local[0, current])
            if step % 2 == 0:
                solved[current][i] = owned
            else:
                gathered[current][i] = whole
            values[i] = owned
            last = (pieces, owned)

    by_stream = [[values[i] for values in gathered] for i in range(streams)]
    done = [tile_terms(values, tiles[0, 0], tile_source) for values in by_stream[:-1]]
    packed = pack_terms(done, by_stream[-1], tiles[0, 0], tile_source, tile_block, tile_count)
    received = leaf_exchange(packed)
    solution_local, tie = turn_back(solved, packed[0])
    shares = share_out(
        received, jnp.swapaxes(rhs_anc, 1, 2), order, slots, tile_rows, tie
    )
    payloads = [shares[0]] + [send(shares[d], "grp", d) for d in range(1, members)]
    inverse_top, inverse_rest, below_top, below_rest = split_factors(
        [diag_inv_anc, sub_anc], shares[0]
    )
    solution, left = solve_first(payloads, inverse_top, inverse_rest)
    solutions = [solution]
    ancestors = rhs_anc.shape[0]
    for ancestor in range(1, ancestors):
        pieces = [piece for _, piece in gather_rows(solutions[-1])]
        residual = apply_split(
            pieces, below_top, below_rest, ancestor - 1, left, (ancestor - 1) * rows
        )
        pieces = [piece for _, piece in gather_rows(residual)]
        others = solutions if ancestor + 1 == ancestors else None
        solved_now = apply_split(pieces, inverse_top, inverse_rest, ancestor, others=others)
        solutions.append(solved_now)
    solutions = solutions[-1] if ancestors > 1 else solutions[0][None]
    solutions = jnp.swapaxes(solutions, 1, 2)
    return (solution_local, solutions)


def solution(mesh):
    return jax.shard_map(
        on_device,
        mesh=mesh,
        in_specs=(
            P("leaf", None, "grp", None),
            P("leaf", None, "grp", None),
            P("leaf", None, "grp", None),
            P("leaf", "grp", None, None, None),
            P("leaf", "grp", None),
            P("leaf", "grp", None),
            P("leaf", "grp"),
            P(None, "grp", "leaf"),
            P(None, "grp", None),
            P(None, "grp", None),
        ),
        out_specs=(P("leaf", None, "grp", None), P(None, "grp", "leaf")),
        check_vma=False,
    )
```

```python
import jax
import jax.numpy as jnp
from jax import lax
from jax.experimental import pallas as pl
from jax.experimental.pallas import tpu as pltpu
from jax.sharding import PartitionSpec as P

high = lax.Precision.HIGH


def contract_last(left, right):
    return lax.dot_general(
        left,
        right,
        (((left.ndim - 1,), (right.ndim - 1,)), ((), ())),
        precision=high,
        preferred_element_type=jnp.float32,
    )


def partner(index, distance, count):
    if count & (count - 1):
        return lax.rem(index - distance + 2 * count, count)
    return index ^ abs(distance)


def send(value, axis, distance):
    count = lax.axis_size(axis)
    if count & (count - 1):
        pairs = [(i, (i + distance) % count) for i in range(count)]
    else:
        pairs = [(i, i ^ distance) for i in range(count)]
    return lax.ppermute(value, axis, pairs)


def gather_rows(value, ties=(), swapped=False, far_first=False):
    members = lax.axis_size("grp")
    me = lax.axis_index("grp")
    rows = value.shape[1]
    pieces = [(me * rows, value)]
    distances = list(range(1, members))
    if far_first:
        distances = distances[1:] + distances[:1]
    if swapped:
        distances[1:3] = distances[2:0:-1]
    for distance in distances:
        owner = partner(me, distance, members)
        tied = value
        if distance in dict(ties):
            tied = lax.optimization_barrier((value, dict(ties)[distance]))[0]
        pieces.append((owner * rows, send(tied, "grp", distance)))
    return pieces


def gather_far_first(value):
    return [piece for _, piece in gather_rows(value, far_first=True)]


def gather_sorted(pieces, swapped):
    if swapped:
        return pieces[:2] + pieces[3:1:-1] + pieces[4:]
    return pieces


def assemble(pieces, order):
    whole = jnp.zeros((pieces[0][1].shape[0], order), jnp.float32)
    for offset, piece in pieces:
        whole = lax.dynamic_update_slice_in_dim(whole, piece, offset, 1)
    return whole


def apply_pieces(factor, index, pieces):
    total = None
    for offset, piece in pieces:
        size = (1, 1, factor.shape[2], piece.shape[1])
        columns = lax.dynamic_slice(factor, (0, index, 0, offset), size)[0, 0]
        term = contract_last(piece, columns)
        total = term if total is None else total + term
    return total


def swap(value, axis, distance, block):
    count = lax.axis_size(axis)
    outer = count // block
    if outer & (outer - 1):
        pairs = [(i, (i // block + distance) % outer * block + i % block) for i in range(count)]
    else:
        pairs = [(i, (i // block ^ distance) * block + i % block) for i in range(count)]
    return lax.ppermute(value, axis, pairs)


VMEM = pl.BlockSpec(memory_space=pltpu.VMEM)
SMEM = pl.BlockSpec(memory_space=pltpu.SMEM)
ANY = pl.BlockSpec(memory_space=pl.ANY)


def local_kernel(body, outs, operands, specs=None, flops=0, scratch=(), limit=None):
    size = sum(o.size * o.dtype.itemsize for o in list(outs) + list(operands))
    return pl.pallas_call(
        body,
        out_shape=list(outs),
        in_specs=specs or [VMEM] * len(operands),
        out_specs=[VMEM] * len(outs),
        scratch_shapes=list(scratch),
        cost_estimate=pl.CostEstimate(flops=flops, bytes_accessed=size, transcendentals=0),
        compiler_params=pltpu.CompilerParams(vmem_limit_bytes=limit or 2 * size + 2**21),
    )(*operands)


def float_array(*shape):
    return jax.ShapeDtypeStruct(shape, jnp.float32)


def high_low(value):
    top = value.astype(jnp.bfloat16)
    return top, (value - top.astype(jnp.float32)).astype(jnp.bfloat16)


def split_product(left, top, rest):
    def dot(x, y):
        return lax.dot_general(
            x, y, (((1,), (1,)), ((), ())), preferred_element_type=jnp.float32
        )

    count = left.shape[0]
    left_top, left_rest = high_low(left)
    both = dot(jnp.concatenate([left_top, left_rest], axis=0), top)
    return both[:count] + (dot(left_top, rest) + both[count:])


def leaf_shape():
    groups = lax.axis_size("leaf")
    inner = 2 if groups % 2 == 0 else 1
    return groups // inner, inner


def select_terms(sources_ref, gathered, tile_refs, store):
    for m in range(tile_refs.shape[0]):
        chosen = gathered[0][...]
        for index in range(1, len(gathered)):
            chosen = jnp.where(sources_ref[0, 0, m] == index, gathered[index][...], chosen)
        top, rest = high_low(tile_refs[m])
        store(m, split_product(chosen, top, rest))


def tile_terms(gathered, tiles, sources):
    slots, tile_rows, order = tiles.shape
    depth = gathered[0].shape[0]
    count = len(gathered)

    def body(*refs):
        out = refs[-1]

        def store(m, term):
            out[:, m * tile_rows : (m + 1) * tile_rows] = term

        select_terms(refs[count + 1], refs[:count], refs[count], store)

    return local_kernel(
        body,
        [float_array(depth, slots * tile_rows)],
        [*gathered, tiles, sources],
        [VMEM] * (count + 1) + [SMEM],
        flops=6 * depth * slots * tile_rows * order,
    )[0]


def pack_terms(done, gathered, tiles, sources, blocks, live):
    outer, inner = leaf_shape()
    slots, tile_rows, order = tiles.shape
    depth = gathered[0].shape[0]
    streams = len(done) + 1
    part = depth * streams // (outer * inner)
    width = (slots + 1) * tile_rows
    count = len(gathered)
    base = len(done)

    def body(*refs):
        source_ref, block_ref, live_ref = refs[base + count + 1 : base + count + 4]
        outs = refs[base + count + 4 : -1]
        terms = refs[-1]
        lanes = lax.broadcasted_iota(jnp.int32, (streams * depth, tile_rows), 1)
        tag = jnp.full((streams * depth, tile_rows), -1.0, jnp.float32)
        for m in range(slots):
            value = jnp.where(m < live_ref[0, 0], block_ref[0, 0, m], -1).astype(jnp.float32)
            tag = jnp.where(lanes == m, value, tag)
        terms[:, slots * tile_rows :] = tag
        for i in range(base):
            terms[i * depth : (i + 1) * depth, : slots * tile_rows] = refs[i][...]

        def store(m, term):
            terms[base * depth :, m * tile_rows : (m + 1) * tile_rows] = term

        select_terms(source_ref, refs[base : base + count], refs[base + count], store)
        inside = lax.rem(lax.axis_index("leaf"), inner)
        for o in range(outer):
            cut = [
                terms[(o * inner + i) * part : (o * inner + i + 1) * part, :]
                for i in range(inner)
            ]
            for i in range(inner):
                outs[i][o] = jnp.where(inside == 0, cut[i], cut[inner - 1 - i])

    return local_kernel(
        body,
        [float_array(outer, part, width)] * inner,
        [*done, *gathered, tiles, sources, blocks, live],
        [VMEM] * (base + count + 1) + [SMEM] * 3,
        flops=6 * depth * slots * tile_rows * order,
        scratch=[pltpu.VMEM((streams * depth, width), jnp.float32)],
    )


def turn(rhs, first, last, streams, after):
    rows, count = rhs.shape[2:]
    depth = count // streams

    def body(rhs_ref, after_ref, out, held, sem):
        copy = pltpu.make_async_copy(rhs_ref.at[0, first:last], held, sem)
        copy.start()
        copy.wait()
        for index in range(last - first):
            wide = jnp.transpose(held[index])
            for i in range(streams):
                out[index * streams + i] = wide[i * depth : (i + 1) * depth]

    return local_kernel(
        body,
        [float_array(streams * (last - first), depth, rows)],
        [rhs, after],
        [ANY, ANY],
        scratch=[
            pltpu.VMEM((last - first, rows, count), jnp.float32),
            pltpu.SemaphoreType.DMA(()),
        ],
    )[0]


def turn_first(rhs, streams):
    rows, count = rhs.shape[2:]
    depth = count // streams

    def body(rhs_ref, *refs):
        outs, (held, sem) = refs[:-2], refs[-2:]
        copy = pltpu.make_async_copy(rhs_ref.at[0, 0], held, sem)
        copy.start()
        copy.wait()
        wide = jnp.transpose(held[...])
        for i in range(streams):
            outs[i][...] = wide[i * depth : (i + 1) * depth]

    return local_kernel(
        body,
        [float_array(depth, rows)] * streams,
        [rhs],
        [ANY],
        scratch=[pltpu.VMEM((rows, count), jnp.float32), pltpu.SemaphoreType.DMA(())],
    )


def turn_back(solved, after):
    flat = [value for streams in solved for value in streams]
    streams = len(solved[0])
    depth, rows = flat[0].shape

    def body(*refs):
        out, tie = refs[-2:]
        for index in range(len(solved)):
            wide = jnp.concatenate(
                [refs[index * streams + i][...] for i in range(streams)], axis=0
            )
            out[0, index] = jnp.transpose(wide)
        tie[...] = jnp.zeros(tie.shape, jnp.float32)

    return local_kernel(
        body,
        [float_array(1, len(solved), rows, depth * streams), float_array(8, 128)],
        [*flat, after],
        [VMEM] * len(flat) + [ANY],
    )


def leaf_exchange(packed):
    outer, inner = leaf_shape()
    part, width = packed[0].shape[1:]
    held = [packed[0]]
    if inner == 2:
        pairs = [(i, i ^ 1) for i in range(outer * inner)]
        held.append(lax.ppermute(packed[1], "leaf", pairs))

    def body(*refs):
        outside = lax.div(lax.axis_index("leaf"), inner)
        for distance in range(outer):
            target = partner(outside, -distance, outer) if distance else outside
            for i in range(inner):
                refs[inner + distance][i] = refs[i][target]

    portions = local_kernel(body, [float_array(inner, part, width)] * outer, held)
    return [portions[0]] + [
        swap(portions[distance], "leaf", distance, inner) for distance in range(outer - 1, 0, -1)
    ]


def share_out(received, rhs_turned, order, slots, tile_rows, after):
    members = lax.axis_size("grp")
    ancestors, part, rows = rhs_turned.shape
    inner = received[0].shape[0]
    block_count = ancestors * order // tile_rows
    width = order + (ancestors - 1) * rows

    def body(*refs):
        sources = refs[: len(received)]
        rhs_ref = refs[len(received)]
        outs = refs[len(received) + 2 : -1]
        share = refs[-1]
        me = lax.axis_index("grp")
        totals = [jnp.zeros((part, tile_rows), jnp.float32) for _ in range(block_count)]
        for source in sources:
            for i in range(inner):
                for m in range(slots):
                    tile = source[i, :, m * tile_rows : (m + 1) * tile_rows]
                    tag = source[i, :, slots * tile_rows + m : slots * tile_rows + m + 1]
                    tag = jnp.broadcast_to(tag, tile.shape)
                    for q in range(block_count):
                        totals[q] = totals[q] + jnp.where(tag == float(q), tile, 0.0)
        for q in range(block_count):
            share[:, q * tile_rows : (q + 1) * tile_rows] = -totals[q]
        for a in range(ancestors):
            for j in range(members):
                at = slice(a * order + j * rows, a * order + (j + 1) * rows)
                share[:, at] = share[:, at] + jnp.where(me == j, rhs_ref[a], 0.0)
        for distance in range(members):
            target = partner(me, -distance, members) if distance else me
            out = outs[distance]
            out[:, :order] = share[:, :order]
            for a in range(1, ancestors):
                value = jnp.zeros((part, rows), jnp.float32)
                for j in range(members):
                    at = slice(a * order + j * rows, a * order + (j + 1) * rows)
                    value = jnp.where(target == j, share[:, at], value)
                out[:, order + (a - 1) * rows : order + a * rows] = value

    return local_kernel(
        body,
        [float_array(part, width)] * members,
        [*received, rhs_turned, after],
        [VMEM] * (len(received) + 1) + [ANY],
        scratch=[pltpu.VMEM((part, ancestors * order), jnp.float32)],
    )


def split_factors(factors, after):
    count = len(factors)

    def body(*refs):
        for i in range(count):
            top, rest = high_low(refs[i][...])
            refs[count + 1 + 2 * i][...] = top
            refs[count + 2 + 2 * i][...] = rest

    outs = []
    for factor in factors:
        outs += [jax.ShapeDtypeStruct(factor.shape, jnp.bfloat16)] * 2
    return local_kernel(
        body,
        outs,
        [*factors, after],
        [VMEM] * count + [ANY],
        flops=4 * sum(f.size for f in factors),
    )


def solve_first(payloads, top, rest):
    part, width = payloads[0].shape
    rows, order = top.shape[1:]

    def body(*refs):
        sums = refs[: len(payloads)]
        top_ref, rest_ref, out, left = refs[len(payloads) :]
        total = sums[0][...]
        for ref in sums[1:]:
            total = total + ref[...]
        out[...] = split_product(total[:, :order], top_ref[0], rest_ref[0])
        left[...] = total[:, order:]

    return local_kernel(
        body,
        [float_array(part, rows), float_array(part, width - order)],
        [*payloads, top, rest],
        flops=6 * part * rows * order,
    )


def put_in_order(held, whole):
    me = lax.axis_index("grp")
    members = len(held)
    width = held[0].shape[1]
    for j in range(members):
        value = jnp.zeros(held[0].shape, jnp.float32)
        for distance in range(members):
            owner = partner(me, distance, members) if distance else me
            value = jnp.where(owner == j, held[distance], value)
        whole[:, j * width : (j + 1) * width] = value


def apply_split(pieces, top, rest, index, base=None, begin=0, others=None, far_first=True):
    members = lax.axis_size("grp")
    part, width = pieces[0].shape
    rows, order = top.shape[1:]
    extra = list(others or []) if base is None else [base]

    def body(*refs):
        top_ref, rest_ref = refs[members : members + 2]
        out, whole = refs[-2:]
        held = [refs[d][...] for d in range(members)]
        if far_first:
            held = held[:1] + held[-1:] + held[1:-1] if members > 2 else held
        put_in_order(held, whole)
        result = split_product(whole[...], top_ref[index], rest_ref[index])
        if others is not None:
            for i in range(len(others)):
                out[i] = refs[members + 2 + i][...]
            out[len(others)] = result
            return
        if base is not None:
            result = refs[members + 2][:, begin : begin + rows] - result
        out[...] = result

    shape = (part, rows) if others is None else (len(others) + 1, part, rows)
    return local_kernel(
        body,
        [float_array(*shape)],
        [*pieces, top, rest, *extra],
        flops=6 * part * rows * order,
        scratch=[pltpu.VMEM((part, order), jnp.float32)],
    )[0]


def on_device(
    rhs_local,
    diag_inv_local,
    sub_local,
    tiles,
    tile_block,
    tile_source,
    tile_count,
    rhs_anc,
    diag_inv_anc,
    sub_anc,
):
    supernodes, _, order = diag_inv_local.shape[1:]
    rhs_count = rhs_local.shape[-1]
    members = lax.axis_size("grp")
    rows = order // members
    slots, tile_rows = tiles.shape[2:4]

    streams = 2 if rhs_count % 16 == 0 else 1
    residuals = turn_first(rhs_local, streams)
    first = diag_inv_local[0, 0]
    rounded = lax.reduce_precision(first, 8, 7)
    first_top = rounded.astype(jnp.bfloat16)[None]
    first_rest = (first - rounded).astype(jnp.bfloat16)[None]
    solved = [[None] * streams for _ in range(supernodes)]
    gathered = [[None] * streams for _ in range(supernodes)]
    values = list(residuals)
    last = None
    for step in range(2 * supernodes):
        current = step // 2
        for i in range(streams):
            turn_taken = step > 0 and last is not None
            ties = [(1, last[0][1][1])] if step * streams + i > streams else []
            pieces = gather_rows(values[i], ties, i % 2 == 1)
            if step == 1 and i == 0:
                later = turn(rhs_local, 1, supernodes, streams, pieces[1][1])
            if turn_taken:
                offset, piece = pieces[1]
                pieces[1] = (offset, lax.optimization_barrier((piece, last[1]))[0])
            if step == 0:
                owned = apply_split(
                    [p for _, p in gather_sorted(pieces, i % 2 == 1)],
                    first_top,
                    first_rest,
                    0,
                    far_first=False,
                )
            else:
                whole = assemble(pieces, order)
                if step % 2 == 0:
                    owned = contract_last(whole, diag_inv_local[0, current])
                elif current + 1 < supernodes:
                    owned = later[current * streams + i] - contract_last(whole, sub_local[0, current])
            if step % 2 == 0:
                solved[current][i] = owned
            else:
                gathered[current][i] = whole
            values[i] = owned
            last = (pieces, owned)

    by_stream = [[values[i] for values in gathered] for i in range(streams)]
    done = [tile_terms(values, tiles[0, 0], tile_source) for values in by_stream[:-1]]
    packed = pack_terms(done, by_stream[-1], tiles[0, 0], tile_source, tile_block, tile_count)
    received = leaf_exchange(packed)
    solution_local, tie = turn_back(solved, packed[0])
    shares = share_out(
        received, jnp.swapaxes(rhs_anc, 1, 2), order, slots, tile_rows, tie
    )
    far_first = list(range(2, members)) + list(range(1, min(members, 2)))
    payloads = [shares[0]] + [send(shares[d], "grp", d) for d in far_first]
    inverse_top, inverse_rest, below_top, below_rest = split_factors(
        [diag_inv_anc, sub_anc], shares[0]
    )
    solution, left = solve_first(payloads, inverse_top, inverse_rest)
    solutions = [solution]
    ancestors = rhs_anc.shape[0]
    for ancestor in range(1, ancestors):
        pieces = gather_far_first(solutions[-1])
        residual = apply_split(
            pieces, below_top, below_rest, ancestor - 1, left, (ancestor - 1) * rows
        )
        pieces = gather_far_first(residual)
        others = solutions if ancestor + 1 == ancestors else None
        solved_now = apply_split(pieces, inverse_top, inverse_rest, ancestor, others=others)
        solutions.append(solved_now)
    solutions = solutions[-1] if ancestors > 1 else solutions[0][None]
    solutions = jnp.swapaxes(solutions, 1, 2)
    return (solution_local, solutions)


def solution(mesh):
    return jax.shard_map(
        on_device,
        mesh=mesh,
        in_specs=(
            P("leaf", None, "grp", None),
            P("leaf", None, "grp", None),
            P("leaf", None, "grp", None),
            P("leaf", "grp", None, None, None),
            P("leaf", "grp", None),
            P("leaf", "grp", None),
            P("leaf", "grp"),
            P(None, "grp", "leaf"),
            P(None, "grp", None),
            P(None, "grp", None),
        ),
        out_specs=(P("leaf", None, "grp", None), P(None, "grp", "leaf")),
        check_vma=False,
    )
```

```python
import jax
import jax.numpy as jnp
from jax import lax
from jax.experimental import pallas as pl
from jax.experimental.pallas import tpu as pltpu
from jax.sharding import PartitionSpec as P

high = lax.Precision.HIGH


def contract_last(left, right):
    return lax.dot_general(
        left,
        right,
        (((left.ndim - 1,), (right.ndim - 1,)), ((), ())),
        precision=high,
        preferred_element_type=jnp.float32,
    )


def partner(index, distance, count):
    if count & (count - 1):
        return lax.rem(index - distance + 2 * count, count)
    return index ^ abs(distance)


def send(value, axis, distance):
    count = lax.axis_size(axis)
    if count & (count - 1):
        pairs = [(i, (i + distance) % count) for i in range(count)]
    else:
        pairs = [(i, i ^ distance) for i in range(count)]
    return lax.ppermute(value, axis, pairs)


def gather_rows(value, ties=(), far_first=False):
    members = lax.axis_size("grp")
    me = lax.axis_index("grp")
    rows = value.shape[1]
    pieces = [(me * rows, value)]
    distances = list(range(1, members))
    if far_first:
        distances = distances[1:] + distances[:1]
    for distance in distances:
        owner = partner(me, distance, members)
        tied = value
        if distance in dict(ties):
            tied = lax.optimization_barrier((value, dict(ties)[distance]))[0]
        pieces.append((owner * rows, send(tied, "grp", distance)))
    return pieces


def gather_far_first(value):
    return [piece for _, piece in gather_rows(value, far_first=True)]


def assemble(pieces, order):
    whole = jnp.zeros((pieces[0][1].shape[0], order), jnp.float32)
    for offset, piece in pieces:
        whole = lax.dynamic_update_slice_in_dim(whole, piece, offset, 1)
    return whole


def apply_pieces(factor, index, pieces):
    total = None
    for offset, piece in pieces:
        size = (1, 1, factor.shape[2], piece.shape[1])
        columns = lax.dynamic_slice(factor, (0, index, 0, offset), size)[0, 0]
        term = contract_last(piece, columns)
        total = term if total is None else total + term
    return total


def swap(value, axis, distance, block):
    count = lax.axis_size(axis)
    outer = count // block
    if outer & (outer - 1):
        pairs = [(i, (i // block + distance) % outer * block + i % block) for i in range(count)]
    else:
        pairs = [(i, (i // block ^ distance) * block + i % block) for i in range(count)]
    return lax.ppermute(value, axis, pairs)


VMEM = pl.BlockSpec(memory_space=pltpu.VMEM)
SMEM = pl.BlockSpec(memory_space=pltpu.SMEM)
ANY = pl.BlockSpec(memory_space=pl.ANY)


def local_kernel(body, outs, operands, specs=None, flops=0, scratch=(), limit=None):
    size = sum(o.size * o.dtype.itemsize for o in list(outs) + list(operands))
    return pl.pallas_call(
        body,
        out_shape=list(outs),
        in_specs=specs or [VMEM] * len(operands),
        out_specs=[VMEM] * len(outs),
        scratch_shapes=list(scratch),
        cost_estimate=pl.CostEstimate(flops=flops, bytes_accessed=size, transcendentals=0),
        compiler_params=pltpu.CompilerParams(vmem_limit_bytes=limit or 2 * size + 2**21),
    )(*operands)


def float_array(*shape):
    return jax.ShapeDtypeStruct(shape, jnp.float32)


def high_low(value):
    top = value.astype(jnp.bfloat16)
    return top, (value - top.astype(jnp.float32)).astype(jnp.bfloat16)


def split_product(left, top, rest):
    def dot(x, y):
        return lax.dot_general(
            x, y, (((1,), (1,)), ((), ())), preferred_element_type=jnp.float32
        )

    count = left.shape[0]
    left_top, left_rest = high_low(left)
    both = dot(jnp.concatenate([left_top, left_rest], axis=0), top)
    return both[:count] + (dot(left_top, rest) + both[count:])


def leaf_shape():
    groups = lax.axis_size("leaf")
    inner = 2 if groups % 2 == 0 else 1
    return groups // inner, inner


def select_terms(sources_ref, gathered, tile_refs, store):
    for m in range(tile_refs.shape[0]):
        chosen = gathered[0][...]
        for index in range(1, len(gathered)):
            chosen = jnp.where(sources_ref[0, 0, m] == index, gathered[index][...], chosen)
        top, rest = high_low(tile_refs[m])
        store(m, split_product(chosen, top, rest))


def tile_terms(gathered, tiles, sources):
    slots, tile_rows, order = tiles.shape
    depth = gathered[0].shape[0]
    count = len(gathered)

    def body(*refs):
        out = refs[-1]

        def store(m, term):
            out[:, m * tile_rows : (m + 1) * tile_rows] = term

        select_terms(refs[count + 1], refs[:count], refs[count], store)

    return local_kernel(
        body,
        [float_array(depth, slots * tile_rows)],
        [*gathered, tiles, sources],
        [VMEM] * (count + 1) + [SMEM],
        flops=6 * depth * slots * tile_rows * order,
    )[0]


def pack_terms(done, gathered, tiles, sources, blocks, live):
    outer, inner = leaf_shape()
    slots, tile_rows, order = tiles.shape
    depth = gathered[0].shape[0]
    streams = len(done) + 1
    part = depth * streams // (outer * inner)
    width = (slots + 1) * tile_rows
    count = len(gathered)
    base = len(done)

    def body(*refs):
        source_ref, block_ref, live_ref = refs[base + count + 1 : base + count + 4]
        outs = refs[base + count + 4 : -1]
        terms = refs[-1]
        lanes = lax.broadcasted_iota(jnp.int32, (streams * depth, tile_rows), 1)
        tag = jnp.full((streams * depth, tile_rows), -1.0, jnp.float32)
        for m in range(slots):
            value = jnp.where(m < live_ref[0, 0], block_ref[0, 0, m], -1).astype(jnp.float32)
            tag = jnp.where(lanes == m, value, tag)
        terms[:, slots * tile_rows :] = tag
        for i in range(base):
            terms[i * depth : (i + 1) * depth, : slots * tile_rows] = refs[i][...]

        def store(m, term):
            terms[base * depth :, m * tile_rows : (m + 1) * tile_rows] = term

        select_terms(source_ref, refs[base : base + count], refs[base + count], store)
        inside = lax.rem(lax.axis_index("leaf"), inner)
        for o in range(outer):
            cut = [
                terms[(o * inner + i) * part : (o * inner + i + 1) * part, :]
                for i in range(inner)
            ]
            for i in range(inner):
                outs[i][o] = jnp.where(inside == 0, cut[i], cut[inner - 1 - i])

    return local_kernel(
        body,
        [float_array(outer, part, width)] * inner,
        [*done, *gathered, tiles, sources, blocks, live],
        [VMEM] * (base + count + 1) + [SMEM] * 3,
        flops=6 * depth * slots * tile_rows * order,
        scratch=[pltpu.VMEM((streams * depth, width), jnp.float32)],
    )


def turn(rhs, first, last, streams, after):
    rows, count = rhs.shape[2:]
    depth = count // streams

    def body(rhs_ref, after_ref, out, held, sem):
        copy = pltpu.make_async_copy(rhs_ref.at[0, first:last], held, sem)
        copy.start()
        copy.wait()
        for index in range(last - first):
            wide = jnp.transpose(held[index])
            for i in range(streams):
                out[index * streams + i] = wide[i * depth : (i + 1) * depth]

    return local_kernel(
        body,
        [float_array(streams * (last - first), depth, rows)],
        [rhs, after],
        [ANY, ANY],
        scratch=[
            pltpu.VMEM((last - first, rows, count), jnp.float32),
            pltpu.SemaphoreType.DMA(()),
        ],
    )[0]


def turn_first(rhs, streams):
    rows, count = rhs.shape[2:]
    depth = count // streams

    def body(rhs_ref, *refs):
        outs, (held, sem) = refs[:-2], refs[-2:]
        copy = pltpu.make_async_copy(rhs_ref.at[0, 0], held, sem)
        copy.start()
        copy.wait()
        wide = jnp.transpose(held[...])
        for i in range(streams):
            outs[i][...] = wide[i * depth : (i + 1) * depth]

    return local_kernel(
        body,
        [float_array(depth, rows)] * streams,
        [rhs],
        [ANY],
        scratch=[pltpu.VMEM((rows, count), jnp.float32), pltpu.SemaphoreType.DMA(())],
    )


def turn_back(solved, after):
    flat = [value for streams in solved for value in streams]
    streams = len(solved[0])
    depth, rows = flat[0].shape

    def body(*refs):
        out, tie = refs[-2:]
        for index in range(len(solved)):
            wide = jnp.concatenate(
                [refs[index * streams + i][...] for i in range(streams)], axis=0
            )
            out[0, index] = jnp.transpose(wide)
        tie[...] = jnp.zeros(tie.shape, jnp.float32)

    return local_kernel(
        body,
        [float_array(1, len(solved), rows, depth * streams), float_array(8, 128)],
        [*flat, after],
        [VMEM] * len(flat) + [ANY],
    )


def leaf_exchange(packed):
    outer, inner = leaf_shape()
    part, width = packed[0].shape[1:]
    held = [packed[0]]
    if inner == 2:
        pairs = [(i, i ^ 1) for i in range(outer * inner)]
        held.append(lax.ppermute(packed[1], "leaf", pairs))

    def body(*refs):
        outside = lax.div(lax.axis_index("leaf"), inner)
        for distance in range(outer):
            target = partner(outside, -distance, outer) if distance else outside
            for i in range(inner):
                refs[inner + distance][i] = refs[i][target]

    portions = local_kernel(body, [float_array(inner, part, width)] * outer, held)
    return [portions[0]] + [
        swap(portions[distance], "leaf", distance, inner) for distance in range(outer - 1, 0, -1)
    ]


def share_out(received, rhs_turned, order, slots, tile_rows, after):
    members = lax.axis_size("grp")
    ancestors, part, rows = rhs_turned.shape
    inner = received[0].shape[0]
    block_count = ancestors * order // tile_rows
    width = order + (ancestors - 1) * rows

    def body(*refs):
        sources = refs[: len(received)]
        rhs_ref = refs[len(received)]
        outs = refs[len(received) + 2 : -1]
        share = refs[-1]
        me = lax.axis_index("grp")
        totals = [jnp.zeros((part, tile_rows), jnp.float32) for _ in range(block_count)]
        for source in sources:
            for i in range(inner):
                for m in range(slots):
                    tile = source[i, :, m * tile_rows : (m + 1) * tile_rows]
                    tag = source[i, :, slots * tile_rows + m : slots * tile_rows + m + 1]
                    tag = jnp.broadcast_to(tag, tile.shape)
                    for q in range(block_count):
                        totals[q] = totals[q] + jnp.where(tag == float(q), tile, 0.0)
        for q in range(block_count):
            share[:, q * tile_rows : (q + 1) * tile_rows] = -totals[q]
        for a in range(ancestors):
            for j in range(members):
                at = slice(a * order + j * rows, a * order + (j + 1) * rows)
                share[:, at] = share[:, at] + jnp.where(me == j, rhs_ref[a], 0.0)
        for distance in range(members):
            target = partner(me, -distance, members) if distance else me
            out = outs[distance]
            out[:, :order] = share[:, :order]
            for a in range(1, ancestors):
                value = jnp.zeros((part, rows), jnp.float32)
                for j in range(members):
                    at = slice(a * order + j * rows, a * order + (j + 1) * rows)
                    value = jnp.where(target == j, share[:, at], value)
                out[:, order + (a - 1) * rows : order + a * rows] = value

    return local_kernel(
        body,
        [float_array(part, width)] * members,
        [*received, rhs_turned, after],
        [VMEM] * (len(received) + 1) + [ANY],
        scratch=[pltpu.VMEM((part, ancestors * order), jnp.float32)],
    )


def split_factors(factors, after):
    count = len(factors)

    def body(*refs):
        for i in range(count):
            top, rest = high_low(refs[i][...])
            refs[count + 1 + 2 * i][...] = top
            refs[count + 2 + 2 * i][...] = rest

    outs = []
    for factor in factors:
        outs += [jax.ShapeDtypeStruct(factor.shape, jnp.bfloat16)] * 2
    return local_kernel(
        body,
        outs,
        [*factors, after],
        [VMEM] * count + [ANY],
        flops=4 * sum(f.size for f in factors),
    )


def solve_first(payloads, top, rest):
    part, width = payloads[0].shape
    rows, order = top.shape[1:]

    def body(*refs):
        sums = refs[: len(payloads)]
        top_ref, rest_ref, out, left = refs[len(payloads) :]
        total = sums[0][...]
        for ref in sums[1:]:
            total = total + ref[...]
        out[...] = split_product(total[:, :order], top_ref[0], rest_ref[0])
        left[...] = total[:, order:]

    return local_kernel(
        body,
        [float_array(part, rows), float_array(part, width - order)],
        [*payloads, top, rest],
        flops=6 * part * rows * order,
    )


def put_in_order(held, whole):
    me = lax.axis_index("grp")
    members = len(held)
    width = held[0].shape[1]
    for j in range(members):
        value = jnp.zeros(held[0].shape, jnp.float32)
        for distance in range(members):
            owner = partner(me, distance, members) if distance else me
            value = jnp.where(owner == j, held[distance], value)
        whole[:, j * width : (j + 1) * width] = value


def apply_split(pieces, top, rest, index, base=None, begin=0, others=None, far_first=True):
    members = lax.axis_size("grp")
    part, width = pieces[0].shape
    rows, order = top.shape[1:]
    extra = list(others or []) if base is None else [base]

    def body(*refs):
        top_ref, rest_ref = refs[members : members + 2]
        out, whole = refs[-2:]
        held = [refs[d][...] for d in range(members)]
        if far_first:
            held = held[:1] + held[-1:] + held[1:-1] if members > 2 else held
        put_in_order(held, whole)
        result = split_product(whole[...], top_ref[index], rest_ref[index])
        if others is not None:
            for i in range(len(others)):
                out[i] = refs[members + 2 + i][...]
            out[len(others)] = result
            return
        if base is not None:
            result = refs[members + 2][:, begin : begin + rows] - result
        out[...] = result

    shape = (part, rows) if others is None else (len(others) + 1, part, rows)
    return local_kernel(
        body,
        [float_array(*shape)],
        [*pieces, top, rest, *extra],
        flops=6 * part * rows * order,
        scratch=[pltpu.VMEM((part, order), jnp.float32)],
    )[0]


def on_device(
    rhs_local,
    diag_inv_local,
    sub_local,
    tiles,
    tile_block,
    tile_source,
    tile_count,
    rhs_anc,
    diag_inv_anc,
    sub_anc,
):
    supernodes, _, order = diag_inv_local.shape[1:]
    rhs_count = rhs_local.shape[-1]
    members = lax.axis_size("grp")
    rows = order // members
    slots, tile_rows = tiles.shape[2:4]

    streams = 2 if rhs_count % 16 == 0 else 1
    residuals = turn_first(rhs_local, streams)
    first = diag_inv_local[0, 0]
    rounded = lax.reduce_precision(first, 8, 7)
    first_top = rounded.astype(jnp.bfloat16)[None]
    first_rest = (first - rounded).astype(jnp.bfloat16)[None]
    solved = [[None] * streams for _ in range(supernodes)]
    gathered = [[None] * streams for _ in range(supernodes)]
    values = list(residuals)
    last = None
    for step in range(2 * supernodes):
        current = step // 2
        for i in range(streams):
            turn_taken = step > 0 and last is not None
            ties = [(1, last[0][1][1])] if step * streams + i > streams else []
            pieces = gather_rows(values[i], ties)
            if step == 1 and i == 0:
                later = turn(rhs_local, 1, supernodes, streams, pieces[1][1])
            if turn_taken:
                offset, piece = pieces[1]
                pieces[1] = (offset, lax.optimization_barrier((piece, last[1]))[0])
            if step == 0:
                owned = apply_split(
                    [p for _, p in pieces],
                    first_top,
                    first_rest,
                    0,
                    far_first=False,
                )
            else:
                whole = assemble(pieces, order)
                if step % 2 == 0:
                    owned = contract_last(whole, diag_inv_local[0, current])
                elif current + 1 < supernodes:
                    owned = later[current * streams + i] - contract_last(whole, sub_local[0, current])
            if step % 2 == 0:
                solved[current][i] = owned
            else:
                gathered[current][i] = whole
            values[i] = owned
            last = (pieces, owned)

    by_stream = [[values[i] for values in gathered] for i in range(streams)]
    done = [tile_terms(values, tiles[0, 0], tile_source) for values in by_stream[:-1]]
    packed = pack_terms(done, by_stream[-1], tiles[0, 0], tile_source, tile_block, tile_count)
    received = leaf_exchange(packed)
    solution_local, tie = turn_back(solved, packed[0])
    shares = share_out(
        received, jnp.swapaxes(rhs_anc, 1, 2), order, slots, tile_rows, tie
    )
    far_first = list(range(2, members)) + list(range(1, min(members, 2)))
    payloads = [shares[0]] + [send(shares[d], "grp", d) for d in far_first]
    inverse_top, inverse_rest, below_top, below_rest = split_factors(
        [diag_inv_anc, sub_anc], shares[0]
    )
    solution, left = solve_first(payloads, inverse_top, inverse_rest)
    solutions = [solution]
    ancestors = rhs_anc.shape[0]
    for ancestor in range(1, ancestors):
        pieces = gather_far_first(solutions[-1])
        residual = apply_split(
            pieces, below_top, below_rest, ancestor - 1, left, (ancestor - 1) * rows
        )
        pieces = gather_far_first(residual)
        others = solutions if ancestor + 1 == ancestors else None
        solved_now = apply_split(pieces, inverse_top, inverse_rest, ancestor, others=others)
        solutions.append(solved_now)
    solutions = solutions[-1] if ancestors > 1 else solutions[0][None]
    solutions = jnp.swapaxes(solutions, 1, 2)
    return (solution_local, solutions)


def solution(mesh):
    return jax.shard_map(
        on_device,
        mesh=mesh,
        in_specs=(
            P("leaf", None, "grp", None),
            P("leaf", None, "grp", None),
            P("leaf", None, "grp", None),
            P("leaf", "grp", None, None, None),
            P("leaf", "grp", None),
            P("leaf", "grp", None),
            P("leaf", "grp"),
            P(None, "grp", "leaf"),
            P(None, "grp", None),
            P(None, "grp", None),
        ),
        out_specs=(P("leaf", None, "grp", None), P(None, "grp", "leaf")),
        check_vma=False,
    )
```

```python
import jax
import jax.numpy as jnp
from jax import lax
from jax.experimental import pallas as pl
from jax.experimental.pallas import tpu as pltpu
from jax.sharding import PartitionSpec as P

high = lax.Precision.HIGH


def contract_last(left, right):
    return lax.dot_general(
        left,
        right,
        (((left.ndim - 1,), (right.ndim - 1,)), ((), ())),
        precision=high,
        preferred_element_type=jnp.float32,
    )


def partner(index, distance, count):
    if count & (count - 1):
        return lax.rem(index - distance + 2 * count, count)
    return index ^ abs(distance)


def send(value, axis, distance):
    count = lax.axis_size(axis)
    if count & (count - 1):
        pairs = [(i, (i + distance) % count) for i in range(count)]
    else:
        pairs = [(i, i ^ distance) for i in range(count)]
    return lax.ppermute(value, axis, pairs)


def gather_rows(value, ties=(), far_first=False):
    members = lax.axis_size("grp")
    me = lax.axis_index("grp")
    rows = value.shape[1]
    pieces = [(me * rows, value)]
    distances = list(range(1, members))
    if far_first:
        distances = distances[1:] + distances[:1]
    for distance in distances:
        owner = partner(me, distance, members)
        tied = value
        if distance in dict(ties):
            tied = lax.optimization_barrier((value, dict(ties)[distance]))[0]
        pieces.append((owner * rows, send(tied, "grp", distance)))
    return pieces


def gather_far_first(value):
    return [piece for _, piece in gather_rows(value, far_first=True)]


def assemble(pieces, order):
    whole = jnp.zeros((pieces[0][1].shape[0], order), jnp.float32)
    for offset, piece in pieces:
        whole = lax.dynamic_update_slice_in_dim(whole, piece, offset, 1)
    return whole


def apply_pieces(factor, index, pieces):
    total = None
    for offset, piece in pieces:
        size = (1, 1, factor.shape[2], piece.shape[1])
        columns = lax.dynamic_slice(factor, (0, index, 0, offset), size)[0, 0]
        term = contract_last(piece, columns)
        total = term if total is None else total + term
    return total


def swap(value, axis, distance, block):
    count = lax.axis_size(axis)
    outer = count // block
    if outer & (outer - 1):
        pairs = [(i, (i // block + distance) % outer * block + i % block) for i in range(count)]
    else:
        pairs = [(i, (i // block ^ distance) * block + i % block) for i in range(count)]
    return lax.ppermute(value, axis, pairs)


VMEM = pl.BlockSpec(memory_space=pltpu.VMEM)
SMEM = pl.BlockSpec(memory_space=pltpu.SMEM)
ANY = pl.BlockSpec(memory_space=pl.ANY)


def local_kernel(body, outs, operands, specs=None, flops=0, scratch=(), limit=None):
    size = sum(o.size * o.dtype.itemsize for o in list(outs) + list(operands))
    return pl.pallas_call(
        body,
        out_shape=list(outs),
        in_specs=specs or [VMEM] * len(operands),
        out_specs=[VMEM] * len(outs),
        scratch_shapes=list(scratch),
        cost_estimate=pl.CostEstimate(flops=flops, bytes_accessed=size, transcendentals=0),
        compiler_params=pltpu.CompilerParams(vmem_limit_bytes=limit or 2 * size + 2**21),
    )(*operands)


def float_array(*shape):
    return jax.ShapeDtypeStruct(shape, jnp.float32)


def high_low(value):
    top = value.astype(jnp.bfloat16)
    return top, (value - top.astype(jnp.float32)).astype(jnp.bfloat16)


def split_product(left, top, rest):
    def dot(x, y):
        return lax.dot_general(
            x, y, (((1,), (1,)), ((), ())), preferred_element_type=jnp.float32
        )

    count = left.shape[0]
    left_top, left_rest = high_low(left)
    both = dot(jnp.concatenate([left_top, left_rest], axis=0), top)
    return both[:count] + (dot(left_top, rest) + both[count:])


def leaf_shape():
    groups = lax.axis_size("leaf")
    inner = 2 if groups % 2 == 0 else 1
    return groups // inner, inner


def select_terms(sources_ref, gathered, tile_refs, store):
    for m in range(tile_refs.shape[0]):
        chosen = gathered[0][...]
        for index in range(1, len(gathered)):
            chosen = jnp.where(sources_ref[0, 0, m] == index, gathered[index][...], chosen)
        top, rest = high_low(tile_refs[m])
        store(m, split_product(chosen, top, rest))


def tile_terms(gathered, tiles, sources):
    slots, tile_rows, order = tiles.shape
    depth = gathered[0].shape[0]
    count = len(gathered)

    def body(*refs):
        out = refs[-1]

        def store(m, term):
            out[:, m * tile_rows : (m + 1) * tile_rows] = term

        select_terms(refs[count + 1], refs[:count], refs[count], store)

    return local_kernel(
        body,
        [float_array(depth, slots * tile_rows)],
        [*gathered, tiles, sources],
        [VMEM] * (count + 1) + [SMEM],
        flops=6 * depth * slots * tile_rows * order,
    )[0]


def pack_terms(done, gathered, tiles, sources, blocks, live):
    outer, inner = leaf_shape()
    slots, tile_rows, order = tiles.shape
    depth = gathered[0].shape[0]
    streams = len(done) + 1
    part = depth * streams // (outer * inner)
    width = (slots + 1) * tile_rows
    count = len(gathered)
    base = len(done)

    def body(*refs):
        source_ref, block_ref, live_ref = refs[base + count + 1 : base + count + 4]
        outs = refs[base + count + 4 : -1]
        terms = refs[-1]
        lanes = lax.broadcasted_iota(jnp.int32, (streams * depth, tile_rows), 1)
        tag = jnp.full((streams * depth, tile_rows), -1.0, jnp.float32)
        for m in range(slots):
            value = jnp.where(m < live_ref[0, 0], block_ref[0, 0, m], -1).astype(jnp.float32)
            tag = jnp.where(lanes == m, value, tag)
        terms[:, slots * tile_rows :] = tag
        for i in range(base):
            terms[i * depth : (i + 1) * depth, : slots * tile_rows] = refs[i][...]

        def store(m, term):
            terms[base * depth :, m * tile_rows : (m + 1) * tile_rows] = term

        select_terms(source_ref, refs[base : base + count], refs[base + count], store)
        inside = lax.rem(lax.axis_index("leaf"), inner)
        for o in range(outer):
            cut = [
                terms[(o * inner + i) * part : (o * inner + i + 1) * part, :]
                for i in range(inner)
            ]
            for i in range(inner):
                outs[i][o] = jnp.where(inside == 0, cut[i], cut[inner - 1 - i])

    return local_kernel(
        body,
        [float_array(outer, part, width)] * inner,
        [*done, *gathered, tiles, sources, blocks, live],
        [VMEM] * (base + count + 1) + [SMEM] * 3,
        flops=6 * depth * slots * tile_rows * order,
        scratch=[pltpu.VMEM((streams * depth, width), jnp.float32)],
    )


def turn(rhs, first, last, streams, after):
    rows, count = rhs.shape[2:]
    depth = count // streams

    def body(rhs_ref, after_ref, out, held, sem):
        copy = pltpu.make_async_copy(rhs_ref.at[0, first:last], held, sem)
        copy.start()
        copy.wait()
        for index in range(last - first):
            wide = jnp.transpose(held[index])
            for i in range(streams):
                out[index * streams + i] = wide[i * depth : (i + 1) * depth]

    return local_kernel(
        body,
        [float_array(streams * (last - first), depth, rows)],
        [rhs, after],
        [ANY, ANY],
        scratch=[
            pltpu.VMEM((last - first, rows, count), jnp.float32),
            pltpu.SemaphoreType.DMA(()),
        ],
    )[0]


def turn_first(rhs, streams):
    rows, count = rhs.shape[2:]
    depth = count // streams

    def body(rhs_ref, *refs):
        outs, (held, sem) = refs[:-2], refs[-2:]
        copy = pltpu.make_async_copy(rhs_ref.at[0, 0], held, sem)
        copy.start()
        copy.wait()
        wide = jnp.transpose(held[...])
        for i in range(streams):
            outs[i][...] = wide[i * depth : (i + 1) * depth]

    return local_kernel(
        body,
        [float_array(depth, rows)] * streams,
        [rhs],
        [ANY],
        scratch=[pltpu.VMEM((rows, count), jnp.float32), pltpu.SemaphoreType.DMA(())],
    )


def turn_back(solved, after):
    flat = [value for streams in solved for value in streams]
    streams = len(solved[0])
    depth, rows = flat[0].shape

    def body(*refs):
        out, tie = refs[-2:]
        for index in range(len(solved)):
            wide = jnp.concatenate(
                [refs[index * streams + i][...] for i in range(streams)], axis=0
            )
            out[0, index] = jnp.transpose(wide)
        tie[...] = jnp.zeros(tie.shape, jnp.float32)

    return local_kernel(
        body,
        [float_array(1, len(solved), rows, depth * streams), float_array(8, 128)],
        [*flat, after],
        [VMEM] * len(flat) + [ANY],
    )


def leaf_exchange(packed):
    outer, inner = leaf_shape()
    part, width = packed[0].shape[1:]
    held = [packed[0]]
    if inner == 2:
        pairs = [(i, i ^ 1) for i in range(outer * inner)]
        held.append(lax.ppermute(packed[1], "leaf", pairs))

    def body(*refs):
        outside = lax.div(lax.axis_index("leaf"), inner)
        for distance in range(outer):
            target = partner(outside, -distance, outer) if distance else outside
            for i in range(inner):
                refs[inner + distance][i] = refs[i][target]

    portions = local_kernel(body, [float_array(inner, part, width)] * outer, held)
    return [portions[0]] + [
        swap(portions[distance], "leaf", distance, inner) for distance in range(outer - 1, 0, -1)
    ]


def share_out(received, rhs_turned, order, slots, tile_rows, after):
    members = lax.axis_size("grp")
    ancestors, part, rows = rhs_turned.shape
    inner = received[0].shape[0]
    block_count = ancestors * order // tile_rows
    width = order + (ancestors - 1) * rows

    def body(*refs):
        sources = refs[: len(received)]
        rhs_ref = refs[len(received)]
        outs = refs[len(received) + 2 : -1]
        share = refs[-1]
        me = lax.axis_index("grp")
        totals = [jnp.zeros((part, tile_rows), jnp.float32) for _ in range(block_count)]
        for source in sources:
            for i in range(inner):
                for m in range(slots):
                    tile = source[i, :, m * tile_rows : (m + 1) * tile_rows]
                    tag = source[i, :, slots * tile_rows + m : slots * tile_rows + m + 1]
                    tag = jnp.broadcast_to(tag, tile.shape)
                    for q in range(block_count):
                        totals[q] = totals[q] + jnp.where(tag == float(q), tile, 0.0)
        for q in range(block_count):
            share[:, q * tile_rows : (q + 1) * tile_rows] = -totals[q]
        for a in range(ancestors):
            for j in range(members):
                at = slice(a * order + j * rows, a * order + (j + 1) * rows)
                share[:, at] = share[:, at] + jnp.where(me == j, rhs_ref[a], 0.0)
        for distance in range(members):
            target = partner(me, -distance, members) if distance else me
            out = outs[distance]
            out[:, :order] = share[:, :order]
            for a in range(1, ancestors):
                value = jnp.zeros((part, rows), jnp.float32)
                for j in range(members):
                    at = slice(a * order + j * rows, a * order + (j + 1) * rows)
                    value = jnp.where(target == j, share[:, at], value)
                out[:, order + (a - 1) * rows : order + a * rows] = value

    return local_kernel(
        body,
        [float_array(part, width)] * members,
        [*received, rhs_turned, after],
        [VMEM] * (len(received) + 1) + [ANY],
        scratch=[pltpu.VMEM((part, ancestors * order), jnp.float32)],
    )


def split_factors(factors, after):
    count = len(factors)

    def body(*refs):
        for i in range(count):
            top, rest = high_low(refs[i][...])
            refs[count + 1 + 2 * i][...] = top
            refs[count + 2 + 2 * i][...] = rest

    outs = []
    for factor in factors:
        outs += [jax.ShapeDtypeStruct(factor.shape, jnp.bfloat16)] * 2
    return local_kernel(
        body,
        outs,
        [*factors, after],
        [VMEM] * count + [ANY],
        flops=4 * sum(f.size for f in factors),
    )


def solve_first(payloads, top, rest):
    part, width = payloads[0].shape
    rows, order = top.shape[1:]

    def body(*refs):
        sums = refs[: len(payloads)]
        top_ref, rest_ref, out, left = refs[len(payloads) :]
        total = sums[0][...]
        for ref in sums[1:]:
            total = total + ref[...]
        out[...] = split_product(total[:, :order], top_ref[0], rest_ref[0])
        left[...] = total[:, order:]

    return local_kernel(
        body,
        [float_array(part, rows), float_array(part, width - order)],
        [*payloads, top, rest],
        flops=6 * part * rows * order,
    )


def put_in_order(held, whole):
    me = lax.axis_index("grp")
    members = len(held)
    width = held[0].shape[1]
    for j in range(members):
        value = jnp.zeros(held[0].shape, jnp.float32)
        for distance in range(members):
            owner = partner(me, distance, members) if distance else me
            value = jnp.where(owner == j, held[distance], value)
        whole[:, j * width : (j + 1) * width] = value


def apply_split(pieces, top, rest, index, base=None, begin=0, others=None, far_first=True):
    members = lax.axis_size("grp")
    part, width = pieces[0].shape
    rows, order = top.shape[1:]
    extra = list(others or []) if base is None else [base]

    def body(*refs):
        top_ref, rest_ref = refs[members : members + 2]
        out, whole = refs[-2:]
        held = [refs[d][...] for d in range(members)]
        if far_first:
            held = held[:1] + held[-1:] + held[1:-1] if members > 2 else held
        put_in_order(held, whole)
        result = split_product(whole[...], top_ref[index], rest_ref[index])
        if others is not None:
            for i in range(len(others)):
                out[i] = refs[members + 2 + i][...]
            out[len(others)] = result
            return
        if base is not None:
            result = refs[members + 2][:, begin : begin + rows] - result
        out[...] = result

    shape = (part, rows) if others is None else (len(others) + 1, part, rows)
    return local_kernel(
        body,
        [float_array(*shape)],
        [*pieces, top, rest, *extra],
        flops=6 * part * rows * order,
        scratch=[pltpu.VMEM((part, order), jnp.float32)],
    )[0]


def on_device(
    rhs_local,
    diag_inv_local,
    sub_local,
    tiles,
    tile_block,
    tile_source,
    tile_count,
    rhs_anc,
    diag_inv_anc,
    sub_anc,
):
    supernodes, _, order = diag_inv_local.shape[1:]
    rhs_count = rhs_local.shape[-1]
    members = lax.axis_size("grp")
    rows = order // members
    slots, tile_rows = tiles.shape[2:4]

    streams = 2 if rhs_count % 16 == 0 else 1
    residuals = turn_first(rhs_local, streams)
    first = diag_inv_local[0, 0]
    rounded = lax.reduce_precision(first, 8, 7)
    first_top = rounded.astype(jnp.bfloat16)[None]
    first_rest = (first - rounded).astype(jnp.bfloat16)[None]
    solved = [[None] * streams for _ in range(supernodes)]
    gathered = [[None] * streams for _ in range(supernodes)]
    values = list(residuals)
    last = None
    for step in range(2 * supernodes):
        current = step // 2
        for i in range(streams):
            turn_taken = step > 0 and last is not None
            ties = [(1, last[0][2][1])] if step * streams + i > streams else []
            pieces = gather_rows(values[i], ties)
            if step == 1 and i == 0:
                later = turn(rhs_local, 1, supernodes, streams, pieces[1][1])
            if turn_taken:
                offset, piece = pieces[2]
                pieces[2] = (offset, lax.optimization_barrier((piece, last[1]))[0])
            if step == 0:
                owned = apply_split(
                    [p for _, p in pieces],
                    first_top,
                    first_rest,
                    0,
                    far_first=False,
                )
            else:
                whole = assemble(pieces, order)
                if step % 2 == 0:
                    owned = contract_last(whole, diag_inv_local[0, current])
                elif current + 1 < supernodes:
                    owned = later[current * streams + i] - contract_last(whole, sub_local[0, current])
            if step % 2 == 0:
                solved[current][i] = owned
            else:
                gathered[current][i] = whole
            values[i] = owned
            last = (pieces, owned)

    by_stream = [[values[i] for values in gathered] for i in range(streams)]
    done = [tile_terms(values, tiles[0, 0], tile_source) for values in by_stream[:-1]]
    packed = pack_terms(done, by_stream[-1], tiles[0, 0], tile_source, tile_block, tile_count)
    received = leaf_exchange(packed)
    solution_local, tie = turn_back(solved, packed[0])
    shares = share_out(
        received, jnp.swapaxes(rhs_anc, 1, 2), order, slots, tile_rows, tie
    )
    far_first = list(range(2, members)) + list(range(1, min(members, 2)))
    payloads = [shares[0]] + [send(shares[d], "grp", d) for d in far_first]
    inverse_top, inverse_rest, below_top, below_rest = split_factors(
        [diag_inv_anc, sub_anc], shares[0]
    )
    solution, left = solve_first(payloads, inverse_top, inverse_rest)
    solutions = [solution]
    ancestors = rhs_anc.shape[0]
    for ancestor in range(1, ancestors):
        pieces = gather_far_first(solutions[-1])
        residual = apply_split(
            pieces, below_top, below_rest, ancestor - 1, left, (ancestor - 1) * rows
        )
        pieces = gather_far_first(residual)
        others = solutions if ancestor + 1 == ancestors else None
        solved_now = apply_split(pieces, inverse_top, inverse_rest, ancestor, others=others)
        solutions.append(solved_now)
    solutions = solutions[-1] if ancestors > 1 else solutions[0][None]
    solutions = jnp.swapaxes(solutions, 1, 2)
    return (solution_local, solutions)


def solution(mesh):
    return jax.shard_map(
        on_device,
        mesh=mesh,
        in_specs=(
            P("leaf", None, "grp", None),
            P("leaf", None, "grp", None),
            P("leaf", None, "grp", None),
            P("leaf", "grp", None, None, None),
            P("leaf", "grp", None),
            P("leaf", "grp", None),
            P("leaf", "grp"),
            P(None, "grp", "leaf"),
            P(None, "grp", None),
            P(None, "grp", None),
        ),
        out_specs=(P("leaf", None, "grp", None), P(None, "grp", "leaf")),
        check_vma=False,
    )
```

```python
import jax
import jax.numpy as jnp
from jax import lax
from jax.experimental import pallas as pl
from jax.experimental.pallas import tpu as pltpu
from jax.sharding import PartitionSpec as P

high = lax.Precision.HIGH


def contract_last(left, right):
    return lax.dot_general(
        left,
        right,
        (((left.ndim - 1,), (right.ndim - 1,)), ((), ())),
        precision=high,
        preferred_element_type=jnp.float32,
    )


def partner(index, distance, count):
    if count & (count - 1):
        return lax.rem(index - distance + 2 * count, count)
    return index ^ abs(distance)


def send(value, axis, distance):
    count = lax.axis_size(axis)
    if count & (count - 1):
        pairs = [(i, (i + distance) % count) for i in range(count)]
    else:
        pairs = [(i, i ^ distance) for i in range(count)]
    return lax.ppermute(value, axis, pairs)


def gather_rows(value, ties=(), far_first=False):
    members = lax.axis_size("grp")
    me = lax.axis_index("grp")
    rows = value.shape[1]
    pieces = [(me * rows, value)]
    distances = list(range(1, members))
    if far_first:
        distances = distances[1:] + distances[:1]
    for distance in distances:
        owner = partner(me, distance, members)
        tied = value
        if distance in dict(ties):
            tied = lax.optimization_barrier((value, dict(ties)[distance]))[0]
        pieces.append((owner * rows, send(tied, "grp", distance)))
    return pieces


def gather_far_first(value):
    return [piece for _, piece in gather_rows(value, far_first=True)]


def assemble(pieces, order):
    whole = jnp.zeros((pieces[0][1].shape[0], order), jnp.float32)
    for offset, piece in pieces:
        whole = lax.dynamic_update_slice_in_dim(whole, piece, offset, 1)
    return whole


def apply_pieces(factor, index, pieces):
    total = None
    for offset, piece in pieces:
        size = (1, 1, factor.shape[2], piece.shape[1])
        columns = lax.dynamic_slice(factor, (0, index, 0, offset), size)[0, 0]
        term = contract_last(piece, columns)
        total = term if total is None else total + term
    return total


def swap(value, axis, distance, block):
    count = lax.axis_size(axis)
    outer = count // block
    if outer & (outer - 1):
        pairs = [(i, (i // block + distance) % outer * block + i % block) for i in range(count)]
    else:
        pairs = [(i, (i // block ^ distance) * block + i % block) for i in range(count)]
    return lax.ppermute(value, axis, pairs)


VMEM = pl.BlockSpec(memory_space=pltpu.VMEM)
SMEM = pl.BlockSpec(memory_space=pltpu.SMEM)
ANY = pl.BlockSpec(memory_space=pl.ANY)


def local_kernel(body, outs, operands, specs=None, flops=0, scratch=(), limit=None):
    size = sum(o.size * o.dtype.itemsize for o in list(outs) + list(operands))
    return pl.pallas_call(
        body,
        out_shape=list(outs),
        in_specs=specs or [VMEM] * len(operands),
        out_specs=[VMEM] * len(outs),
        scratch_shapes=list(scratch),
        cost_estimate=pl.CostEstimate(flops=flops, bytes_accessed=size, transcendentals=0),
        compiler_params=pltpu.CompilerParams(vmem_limit_bytes=limit or 2 * size + 2**21),
    )(*operands)


def float_array(*shape):
    return jax.ShapeDtypeStruct(shape, jnp.float32)


def high_low(value):
    top = value.astype(jnp.bfloat16)
    return top, (value - top.astype(jnp.float32)).astype(jnp.bfloat16)


def split_product(left, top, rest):
    def dot(x, y):
        return lax.dot_general(
            x, y, (((1,), (1,)), ((), ())), preferred_element_type=jnp.float32
        )

    count = left.shape[0]
    left_top, left_rest = high_low(left)
    both = dot(jnp.concatenate([left_top, left_rest], axis=0), top)
    return both[:count] + (dot(left_top, rest) + both[count:])


def leaf_shape():
    groups = lax.axis_size("leaf")
    inner = 2 if groups % 2 == 0 else 1
    return groups // inner, inner


def select_terms(sources_ref, gathered, tile_refs, store):
    for m in range(tile_refs.shape[0]):
        chosen = gathered[0][...]
        for index in range(1, len(gathered)):
            chosen = jnp.where(sources_ref[0, 0, m] == index, gathered[index][...], chosen)
        top, rest = high_low(tile_refs[m])
        store(m, split_product(chosen, top, rest))


def tile_terms(gathered, tiles, sources):
    slots, tile_rows, order = tiles.shape
    depth = gathered[0].shape[0]
    count = len(gathered)

    def body(*refs):
        out = refs[-1]

        def store(m, term):
            out[:, m * tile_rows : (m + 1) * tile_rows] = term

        select_terms(refs[count + 1], refs[:count], refs[count], store)

    return local_kernel(
        body,
        [float_array(depth, slots * tile_rows)],
        [*gathered, tiles, sources],
        [VMEM] * (count + 1) + [SMEM],
        flops=6 * depth * slots * tile_rows * order,
    )[0]


def pack_terms(done, gathered, tiles, sources, blocks, live):
    outer, inner = leaf_shape()
    slots, tile_rows, order = tiles.shape
    depth = gathered[0].shape[0]
    streams = len(done) + 1
    part = depth * streams // (outer * inner)
    width = (slots + 1) * tile_rows
    count = len(gathered)
    base = len(done)

    def body(*refs):
        source_ref, block_ref, live_ref = refs[base + count + 1 : base + count + 4]
        outs = refs[base + count + 4 : -1]
        terms = refs[-1]
        lanes = lax.broadcasted_iota(jnp.int32, (streams * depth, tile_rows), 1)
        tag = jnp.full((streams * depth, tile_rows), -1.0, jnp.float32)
        for m in range(slots):
            value = jnp.where(m < live_ref[0, 0], block_ref[0, 0, m], -1).astype(jnp.float32)
            tag = jnp.where(lanes == m, value, tag)
        terms[:, slots * tile_rows :] = tag
        for i in range(base):
            terms[i * depth : (i + 1) * depth, : slots * tile_rows] = refs[i][...]

        def store(m, term):
            terms[base * depth :, m * tile_rows : (m + 1) * tile_rows] = term

        select_terms(source_ref, refs[base : base + count], refs[base + count], store)
        inside = lax.rem(lax.axis_index("leaf"), inner)
        for o in range(outer):
            cut = [
                terms[(o * inner + i) * part : (o * inner + i + 1) * part, :]
                for i in range(inner)
            ]
            for i in range(inner):
                outs[i][o] = jnp.where(inside == 0, cut[i], cut[inner - 1 - i])

    return local_kernel(
        body,
        [float_array(outer, part, width)] * inner,
        [*done, *gathered, tiles, sources, blocks, live],
        [VMEM] * (base + count + 1) + [SMEM] * 3,
        flops=6 * depth * slots * tile_rows * order,
        scratch=[pltpu.VMEM((streams * depth, width), jnp.float32)],
    )


def turn(rhs, first, last, streams, after):
    rows, count = rhs.shape[2:]
    depth = count // streams

    def body(rhs_ref, after_ref, out, held, sem):
        copy = pltpu.make_async_copy(rhs_ref.at[0, first:last], held, sem)
        copy.start()
        copy.wait()
        for index in range(last - first):
            wide = jnp.transpose(held[index])
            for i in range(streams):
                out[index * streams + i] = wide[i * depth : (i + 1) * depth]

    return local_kernel(
        body,
        [float_array(streams * (last - first), depth, rows)],
        [rhs, after],
        [ANY, ANY],
        scratch=[
            pltpu.VMEM((last - first, rows, count), jnp.float32),
            pltpu.SemaphoreType.DMA(()),
        ],
    )[0]


def turn_first(rhs, streams):
    rows, count = rhs.shape[2:]
    depth = count // streams

    def body(rhs_ref, *refs):
        outs, (held, sem) = refs[:-2], refs[-2:]
        copy = pltpu.make_async_copy(rhs_ref.at[0, 0], held, sem)
        copy.start()
        copy.wait()
        wide = jnp.transpose(held[...])
        for i in range(streams):
            outs[i][...] = wide[i * depth : (i + 1) * depth]

    return local_kernel(
        body,
        [float_array(depth, rows)] * streams,
        [rhs],
        [ANY],
        scratch=[pltpu.VMEM((rows, count), jnp.float32), pltpu.SemaphoreType.DMA(())],
        limit=121 * 2**19,
    )


def turn_back(solved, after):
    flat = [value for streams in solved for value in streams]
    streams = len(solved[0])
    depth, rows = flat[0].shape

    def body(*refs):
        out, tie = refs[-2:]
        for index in range(len(solved)):
            wide = jnp.concatenate(
                [refs[index * streams + i][...] for i in range(streams)], axis=0
            )
            out[0, index] = jnp.transpose(wide)
        tie[...] = jnp.zeros(tie.shape, jnp.float32)

    return local_kernel(
        body,
        [float_array(1, len(solved), rows, depth * streams), float_array(8, 128)],
        [*flat, after],
        [VMEM] * len(flat) + [ANY],
    )


def leaf_exchange(packed):
    outer, inner = leaf_shape()
    part, width = packed[0].shape[1:]
    held = [packed[0]]
    if inner == 2:
        pairs = [(i, i ^ 1) for i in range(outer * inner)]
        held.append(lax.ppermute(packed[1], "leaf", pairs))

    def body(*refs):
        outside = lax.div(lax.axis_index("leaf"), inner)
        for distance in range(outer):
            target = partner(outside, -distance, outer) if distance else outside
            for i in range(inner):
                refs[inner + distance][i] = refs[i][target]

    portions = local_kernel(body, [float_array(inner, part, width)] * outer, held)
    return [portions[0]] + [
        swap(portions[distance], "leaf", distance, inner) for distance in range(outer - 1, 0, -1)
    ]


def share_out(received, rhs_turned, order, slots, tile_rows, after):
    members = lax.axis_size("grp")
    ancestors, part, rows = rhs_turned.shape
    inner = received[0].shape[0]
    block_count = ancestors * order // tile_rows
    width = (ancestors - 1) * rows

    def body(*refs):
        sources = refs[: len(received)]
        rhs_ref = refs[len(received)]
        outs = refs[len(received) + 2 : -1]
        share = refs[-1]
        me = lax.axis_index("grp")
        totals = [jnp.zeros((part, tile_rows), jnp.float32) for _ in range(block_count)]
        for source in sources:
            for i in range(inner):
                for m in range(slots):
                    tile = source[i, :, m * tile_rows : (m + 1) * tile_rows]
                    tag = source[i, :, slots * tile_rows + m : slots * tile_rows + m + 1]
                    tag = jnp.broadcast_to(tag, tile.shape)
                    for q in range(block_count):
                        totals[q] = totals[q] + jnp.where(tag == float(q), tile, 0.0)
        for q in range(block_count):
            share[:, q * tile_rows : (q + 1) * tile_rows] = -totals[q]
        for a in range(ancestors):
            for j in range(members):
                at = slice(a * order + j * rows, a * order + (j + 1) * rows)
                share[:, at] = share[:, at] + jnp.where(me == j, rhs_ref[a], 0.0)
        outs[0][...] = share[:, :order]
        for distance in range(members):
            target = partner(me, -distance, members) if distance else me
            out = outs[1 + distance]
            for a in range(1, ancestors):
                value = jnp.zeros((part, rows), jnp.float32)
                for j in range(members):
                    at = slice(a * order + j * rows, a * order + (j + 1) * rows)
                    value = jnp.where(target == j, share[:, at], value)
                out[:, (a - 1) * rows : a * rows] = value

    return local_kernel(
        body,
        [float_array(part, order)] + [float_array(part, width)] * members,
        [*received, rhs_turned, after],
        [VMEM] * (len(received) + 1) + [ANY],
        scratch=[pltpu.VMEM((part, ancestors * order), jnp.float32)],
    )


def split_factors(factors, after):
    count = len(factors)

    def body(*refs):
        for i in range(count):
            top, rest = high_low(refs[i][...])
            refs[count + 1 + 2 * i][...] = top
            refs[count + 2 + 2 * i][...] = rest

    outs = []
    for factor in factors:
        outs += [jax.ShapeDtypeStruct(factor.shape, jnp.bfloat16)] * 2
    return local_kernel(
        body,
        outs,
        [*factors, after],
        [VMEM] * count + [ANY],
        flops=4 * sum(f.size for f in factors),
    )


def solve_first(shares, others, top, rest):
    members = len(others)
    part, width = others[0].shape
    rows, order = top.shape[1:]

    def body(*refs):
        total = refs[0][...]
        for ref in refs[1:members]:
            total = total + ref[...]
        other_refs = refs[members : 2 * members]
        top_ref, rest_ref, out = refs[2 * members : 2 * members + 3]
        value = split_product(total, top_ref[0], rest_ref[0])
        out[...] = value
        for distance in range(1, members):
            message = refs[2 * members + 2 + distance]
            message[:, :rows] = value
            message[:, rows:] = other_refs[distance][...]

    return local_kernel(
        body,
        [float_array(part, rows)] + [float_array(part, rows + width)] * (members - 1),
        [*shares, *others, top, rest],
        flops=6 * part * rows * order,
    )


def take_messages(own, other, messages, top, rest):
    members = len(messages) + 1
    part, width = other.shape
    rows, order = top.shape[1:]

    def body(*refs):
        own_ref, other_ref = refs[:2]
        held = refs[2 : members + 1]
        top_ref, rest_ref, out, left, whole = refs[members + 1 :]
        total = other_ref[...]
        for ref in held:
            total = total + ref[:, rows:]
        left[...] = total
        pieces = [ref[:, :rows] for ref in held[-1:] + held[:-1]]
        put_in_order([own_ref[...]] + pieces, whole)
        out[...] = total[:, :rows] - split_product(whole[...], top_ref[0], rest_ref[0])

    return local_kernel(
        body,
        [float_array(part, rows), float_array(part, width)],
        [own, other, *messages, top, rest],
        flops=6 * part * rows * order,
        scratch=[pltpu.VMEM((part, order), jnp.float32)],
    )


def put_in_order(held, whole):
    me = lax.axis_index("grp")
    members = len(held)
    width = held[0].shape[1]
    for j in range(members):
        value = jnp.zeros(held[0].shape, jnp.float32)
        for distance in range(members):
            owner = partner(me, distance, members) if distance else me
            value = jnp.where(owner == j, held[distance], value)
        whole[:, j * width : (j + 1) * width] = value


def apply_split(pieces, top, rest, index, base=None, begin=0, others=None, far_first=True):
    members = lax.axis_size("grp")
    part, width = pieces[0].shape
    rows, order = top.shape[1:]
    extra = list(others or []) if base is None else [base]

    def body(*refs):
        top_ref, rest_ref = refs[members : members + 2]
        out, whole = refs[-2:]
        held = [refs[d][...] for d in range(members)]
        if far_first:
            held = held[:1] + held[-1:] + held[1:-1] if members > 2 else held
        put_in_order(held, whole)
        result = split_product(whole[...], top_ref[index], rest_ref[index])
        if others is not None:
            for i in range(len(others)):
                out[i] = refs[members + 2 + i][...]
            out[len(others)] = result
            return
        if base is not None:
            result = refs[members + 2][:, begin : begin + rows] - result
        out[...] = result

    shape = (part, rows) if others is None else (len(others) + 1, part, rows)
    return local_kernel(
        body,
        [float_array(*shape)],
        [*pieces, top, rest, *extra],
        flops=6 * part * rows * order,
        scratch=[pltpu.VMEM((part, order), jnp.float32)],
    )[0]


def on_device(
    rhs_local,
    diag_inv_local,
    sub_local,
    tiles,
    tile_block,
    tile_source,
    tile_count,
    rhs_anc,
    diag_inv_anc,
    sub_anc,
):
    supernodes, _, order = diag_inv_local.shape[1:]
    rhs_count = rhs_local.shape[-1]
    members = lax.axis_size("grp")
    rows = order // members
    slots, tile_rows = tiles.shape[2:4]

    streams = 2 if rhs_count % 16 == 0 else 1
    residuals = turn_first(rhs_local, streams)
    first = diag_inv_local[0, 0]
    rounded = lax.reduce_precision(first, 8, 7)
    first_top = rounded.astype(jnp.bfloat16)[None]
    first_rest = (first - rounded).astype(jnp.bfloat16)[None]
    solved = [[None] * streams for _ in range(supernodes)]
    gathered = [[None] * streams for _ in range(supernodes)]
    values = list(residuals)
    last = None
    for step in range(2 * supernodes):
        current = step // 2
        for i in range(streams):
            turn_taken = step > 0 and last is not None
            ties = [(1, last[0][2][1])] if step * streams + i > streams else []
            pieces = gather_rows(values[i], ties)
            if step == 1 and i == 0:
                later = turn(rhs_local, 1, supernodes, streams, pieces[1][1])
            if turn_taken:
                offset, piece = pieces[2]
                pieces[2] = (offset, lax.optimization_barrier((piece, last[1]))[0])
            if step == 0:
                owned = apply_split(
                    [p for _, p in pieces],
                    first_top,
                    first_rest,
                    0,
                    far_first=False,
                )
            else:
                whole = assemble(pieces, order)
                if step % 2 == 0:
                    owned = contract_last(whole, diag_inv_local[0, current])
                elif current + 1 < supernodes:
                    owned = later[current * streams + i] - contract_last(whole, sub_local[0, current])
            if step % 2 == 0:
                solved[current][i] = owned
            else:
                gathered[current][i] = whole
            values[i] = owned
            last = (pieces, owned)

    by_stream = [[values[i] for values in gathered] for i in range(streams)]
    done = [tile_terms(values, tiles[0, 0], tile_source) for values in by_stream[:-1]]
    packed = pack_terms(done, by_stream[-1], tiles[0, 0], tile_source, tile_block, tile_count)
    received = leaf_exchange(packed)
    solution_local, tie = turn_back(solved, packed[0])
    shares = share_out(
        received, jnp.swapaxes(rhs_anc, 1, 2), order, slots, tile_rows, tie
    )
    far_first = list(range(2, members)) + list(range(1, min(members, 2)))
    first_share, others = shares[0], shares[1:]
    sums = [first_share] + [send(first_share, "grp", d) for d in far_first]
    inverse_top, inverse_rest, below_top, below_rest = split_factors(
        [diag_inv_anc, sub_anc], first_share
    )
    solution, *messages = solve_first(sums, others, inverse_top, inverse_rest)
    solutions = [solution]
    ancestors = rhs_anc.shape[0]
    for ancestor in range(1, ancestors):
        if ancestor == 1:
            arrived = [send(messages[d - 1], "grp", d) for d in far_first]
            residual, left = take_messages(solution, others[0], arrived, below_top, below_rest)
        else:
            pieces = gather_far_first(solutions[-1])
            residual = apply_split(
                pieces, below_top, below_rest, ancestor - 1, left, (ancestor - 1) * rows
            )
        pieces = gather_far_first(residual)
        behind = solutions if ancestor + 1 == ancestors else None
        solved_now = apply_split(pieces, inverse_top, inverse_rest, ancestor, others=behind)
        solutions.append(solved_now)
    solutions = solutions[-1] if ancestors > 1 else solutions[0][None]
    solutions = jnp.swapaxes(solutions, 1, 2)
    return (solution_local, solutions)


def solution(mesh):
    return jax.shard_map(
        on_device,
        mesh=mesh,
        in_specs=(
            P("leaf", None, "grp", None),
            P("leaf", None, "grp", None),
            P("leaf", None, "grp", None),
            P("leaf", "grp", None, None, None),
            P("leaf", "grp", None),
            P("leaf", "grp", None),
            P("leaf", "grp"),
            P(None, "grp", "leaf"),
            P(None, "grp", None),
            P(None, "grp", None),
        ),
        out_specs=(P("leaf", None, "grp", None), P(None, "grp", "leaf")),
        check_vma=False,
    )
```

```python
import jax
import jax.numpy as jnp
from jax import lax
from jax.experimental import pallas as pl
from jax.experimental.pallas import tpu as pltpu
from jax.sharding import PartitionSpec as P

high = lax.Precision.HIGH


def contract_last(left, right):
    return lax.dot_general(
        left,
        right,
        (((left.ndim - 1,), (right.ndim - 1,)), ((), ())),
        precision=high,
        preferred_element_type=jnp.float32,
    )


def partner(index, distance, count):
    if count & (count - 1):
        return lax.rem(index - distance + 2 * count, count)
    return index ^ abs(distance)


def send(value, axis, distance):
    count = lax.axis_size(axis)
    if count & (count - 1):
        pairs = [(i, (i + distance) % count) for i in range(count)]
    else:
        pairs = [(i, i ^ distance) for i in range(count)]
    return lax.ppermute(value, axis, pairs)


def gather_rows(value, ties=(), far_first=False):
    members = lax.axis_size("grp")
    me = lax.axis_index("grp")
    rows = value.shape[1]
    pieces = [(me * rows, value)]
    distances = list(range(1, members))
    if far_first:
        distances = distances[1:] + distances[:1]
    for distance in distances:
        owner = partner(me, distance, members)
        tied = value
        if distance in dict(ties):
            tied = lax.optimization_barrier((value, dict(ties)[distance]))[0]
        pieces.append((owner * rows, send(tied, "grp", distance)))
    return pieces


def gather_far_first(value):
    return [piece for _, piece in gather_rows(value, far_first=True)]


def assemble(pieces, order):
    whole = jnp.zeros((pieces[0][1].shape[0], order), jnp.float32)
    for offset, piece in pieces:
        whole = lax.dynamic_update_slice_in_dim(whole, piece, offset, 1)
    return whole


def apply_pieces(factor, index, pieces):
    total = None
    for offset, piece in pieces:
        size = (1, 1, factor.shape[2], piece.shape[1])
        columns = lax.dynamic_slice(factor, (0, index, 0, offset), size)[0, 0]
        term = contract_last(piece, columns)
        total = term if total is None else total + term
    return total


def swap(value, axis, distance, block):
    count = lax.axis_size(axis)
    outer = count // block
    if outer & (outer - 1):
        pairs = [(i, (i // block + distance) % outer * block + i % block) for i in range(count)]
    else:
        pairs = [(i, (i // block ^ distance) * block + i % block) for i in range(count)]
    return lax.ppermute(value, axis, pairs)


VMEM = pl.BlockSpec(memory_space=pltpu.VMEM)
SMEM = pl.BlockSpec(memory_space=pltpu.SMEM)
ANY = pl.BlockSpec(memory_space=pl.ANY)


def local_kernel(body, outs, operands, specs=None, flops=0, scratch=(), limit=None):
    size = sum(o.size * o.dtype.itemsize for o in list(outs) + list(operands))
    return pl.pallas_call(
        body,
        out_shape=list(outs),
        in_specs=specs or [VMEM] * len(operands),
        out_specs=[VMEM] * len(outs),
        scratch_shapes=list(scratch),
        cost_estimate=pl.CostEstimate(flops=flops, bytes_accessed=size, transcendentals=0),
        compiler_params=pltpu.CompilerParams(vmem_limit_bytes=limit or 2 * size + 2**21),
    )(*operands)


def float_array(*shape):
    return jax.ShapeDtypeStruct(shape, jnp.float32)


def high_low(value):
    top = value.astype(jnp.bfloat16)
    return top, (value - top.astype(jnp.float32)).astype(jnp.bfloat16)


def split_product(left, top, rest):
    def dot(x, y):
        return lax.dot_general(
            x, y, (((1,), (1,)), ((), ())), preferred_element_type=jnp.float32
        )

    count = left.shape[0]
    left_top, left_rest = high_low(left)
    both = dot(jnp.concatenate([left_top, left_rest], axis=0), top)
    return both[:count] + (dot(left_top, rest) + both[count:])


def leaf_shape():
    groups = lax.axis_size("leaf")
    inner = 2 if groups % 2 == 0 else 1
    return groups // inner, inner


def select_terms(sources_ref, gathered, tile_refs, store):
    for m in range(tile_refs.shape[0]):
        chosen = gathered[0][...]
        for index in range(1, len(gathered)):
            chosen = jnp.where(sources_ref[0, 0, m] == index, gathered[index][...], chosen)
        top, rest = high_low(tile_refs[m])
        store(m, split_product(chosen, top, rest))


def tile_terms(gathered, tiles, sources):
    slots, tile_rows, order = tiles.shape
    depth = gathered[0].shape[0]
    count = len(gathered)

    def body(*refs):
        out = refs[-1]

        def store(m, term):
            out[:, m * tile_rows : (m + 1) * tile_rows] = term

        select_terms(refs[count + 1], refs[:count], refs[count], store)

    return local_kernel(
        body,
        [float_array(depth, slots * tile_rows)],
        [*gathered, tiles, sources],
        [VMEM] * (count + 1) + [SMEM],
        flops=6 * depth * slots * tile_rows * order,
    )[0]


def pack_terms(done, gathered, tiles, sources, blocks, live):
    outer, inner = leaf_shape()
    slots, tile_rows, order = tiles.shape
    depth = gathered[0].shape[0]
    streams = len(done) + 1
    part = depth * streams // (outer * inner)
    width = (slots + 1) * tile_rows
    count = len(gathered)
    base = len(done)

    def body(*refs):
        source_ref, block_ref, live_ref = refs[base + count + 1 : base + count + 4]
        outs = refs[base + count + 4 : -1]
        terms = refs[-1]
        lanes = lax.broadcasted_iota(jnp.int32, (streams * depth, tile_rows), 1)
        tag = jnp.full((streams * depth, tile_rows), -1.0, jnp.float32)
        for m in range(slots):
            value = jnp.where(m < live_ref[0, 0], block_ref[0, 0, m], -1).astype(jnp.float32)
            tag = jnp.where(lanes == m, value, tag)
        terms[:, slots * tile_rows :] = tag
        for i in range(base):
            terms[i * depth : (i + 1) * depth, : slots * tile_rows] = refs[i][...]

        def store(m, term):
            terms[base * depth :, m * tile_rows : (m + 1) * tile_rows] = term

        select_terms(source_ref, refs[base : base + count], refs[base + count], store)
        inside = lax.rem(lax.axis_index("leaf"), inner)
        for o in range(outer):
            cut = [
                terms[(o * inner + i) * part : (o * inner + i + 1) * part, :]
                for i in range(inner)
            ]
            for i in range(inner):
                outs[i][o] = jnp.where(inside == 0, cut[i], cut[inner - 1 - i])

    return local_kernel(
        body,
        [float_array(outer, part, width)] * inner,
        [*done, *gathered, tiles, sources, blocks, live],
        [VMEM] * (base + count + 1) + [SMEM] * 3,
        flops=6 * depth * slots * tile_rows * order,
        scratch=[pltpu.VMEM((streams * depth, width), jnp.float32)],
    )


def turn(rhs, first, last, streams, after):
    rows, count = rhs.shape[2:]
    depth = count // streams

    def body(rhs_ref, after_ref, out, held, sem):
        copy = pltpu.make_async_copy(rhs_ref.at[0, first:last], held, sem)
        copy.start()
        copy.wait()
        for index in range(last - first):
            wide = jnp.transpose(held[index])
            for i in range(streams):
                out[index * streams + i] = wide[i * depth : (i + 1) * depth]

    return local_kernel(
        body,
        [float_array(streams * (last - first), depth, rows)],
        [rhs, after],
        [ANY, ANY],
        scratch=[
            pltpu.VMEM((last - first, rows, count), jnp.float32),
            pltpu.SemaphoreType.DMA(()),
        ],
    )[0]


def turn_first(rhs, streams):
    rows, count = rhs.shape[2:]
    depth = count // streams

    def body(rhs_ref, *refs):
        outs, (held, sem) = refs[:-2], refs[-2:]
        copy = pltpu.make_async_copy(rhs_ref.at[0, 0], held, sem)
        copy.start()
        copy.wait()
        wide = jnp.transpose(held[...])
        for i in range(streams):
            outs[i][...] = wide[i * depth : (i + 1) * depth]

    return local_kernel(
        body,
        [float_array(depth, rows)] * streams,
        [rhs],
        [ANY],
        scratch=[pltpu.VMEM((rows, count), jnp.float32), pltpu.SemaphoreType.DMA(())],
    )


def turn_back(solved, after):
    flat = [value for streams in solved for value in streams]
    streams = len(solved[0])
    depth, rows = flat[0].shape

    def body(*refs):
        out, tie = refs[-2:]
        for index in range(len(solved)):
            wide = jnp.concatenate(
                [refs[index * streams + i][...] for i in range(streams)], axis=0
            )
            out[0, index] = jnp.transpose(wide)
        tie[...] = jnp.zeros(tie.shape, jnp.float32)

    return local_kernel(
        body,
        [float_array(1, len(solved), rows, depth * streams), float_array(8, 128)],
        [*flat, after],
        [VMEM] * len(flat) + [ANY],
    )


def leaf_exchange(packed):
    outer, inner = leaf_shape()
    part, width = packed[0].shape[1:]
    held = [packed[0]]
    if inner == 2:
        pairs = [(i, i ^ 1) for i in range(outer * inner)]
        held.append(lax.ppermute(packed[1], "leaf", pairs))

    def body(*refs):
        outside = lax.div(lax.axis_index("leaf"), inner)
        for distance in range(outer):
            target = partner(outside, -distance, outer) if distance else outside
            for i in range(inner):
                refs[inner + distance][i] = refs[i][target]

    portions = local_kernel(body, [float_array(inner, part, width)] * outer, held)
    return [portions[0]] + [
        swap(portions[distance], "leaf", distance, inner) for distance in range(outer - 1, 0, -1)
    ]


def share_out(received, rhs_turned, order, slots, tile_rows, after):
    members = lax.axis_size("grp")
    ancestors, part, rows = rhs_turned.shape
    inner = received[0].shape[0]
    block_count = ancestors * order // tile_rows
    width = (ancestors - 1) * rows

    def body(*refs):
        sources = refs[: len(received)]
        rhs_ref = refs[len(received)]
        outs = refs[len(received) + 2 : -1]
        share = refs[-1]
        me = lax.axis_index("grp")
        totals = [jnp.zeros((part, tile_rows), jnp.float32) for _ in range(block_count)]
        for source in sources:
            for i in range(inner):
                for m in range(slots):
                    tile = source[i, :, m * tile_rows : (m + 1) * tile_rows]
                    tag = source[i, :, slots * tile_rows + m : slots * tile_rows + m + 1]
                    tag = jnp.broadcast_to(tag, tile.shape)
                    for q in range(block_count):
                        totals[q] = totals[q] + jnp.where(tag == float(q), tile, 0.0)
        for q in range(block_count):
            share[:, q * tile_rows : (q + 1) * tile_rows] = -totals[q]
        for a in range(ancestors):
            for j in range(members):
                at = slice(a * order + j * rows, a * order + (j + 1) * rows)
                share[:, at] = share[:, at] + jnp.where(me == j, rhs_ref[a], 0.0)
        outs[0][...] = share[:, :order]
        for distance in range(members):
            target = partner(me, -distance, members) if distance else me
            out = outs[1 + distance]
            for a in range(1, ancestors):
                value = jnp.zeros((part, rows), jnp.float32)
                for j in range(members):
                    at = slice(a * order + j * rows, a * order + (j + 1) * rows)
                    value = jnp.where(target == j, share[:, at], value)
                out[:, (a - 1) * rows : a * rows] = value

    return local_kernel(
        body,
        [float_array(part, order)] + [float_array(part, width)] * members,
        [*received, rhs_turned, after],
        [VMEM] * (len(received) + 1) + [ANY],
        scratch=[pltpu.VMEM((part, ancestors * order), jnp.float32)],
    )


def split_factors(factors, after):
    count = len(factors)

    def body(*refs):
        for i in range(count):
            top, rest = high_low(refs[i][...])
            refs[count + 1 + 2 * i][...] = top
            refs[count + 2 + 2 * i][...] = rest

    outs = []
    for factor in factors:
        outs += [jax.ShapeDtypeStruct(factor.shape, jnp.bfloat16)] * 2
    return local_kernel(
        body,
        outs,
        [*factors, after],
        [VMEM] * count + [ANY],
        flops=4 * sum(f.size for f in factors),
    )


def solve_first(shares, others, top, rest):
    members = len(others)
    part, width = others[0].shape
    rows, order = top.shape[1:]

    def body(*refs):
        total = refs[0][...]
        for ref in refs[1:members]:
            total = total + ref[...]
        other_refs = refs[members : 2 * members]
        top_ref, rest_ref, out = refs[2 * members : 2 * members + 3]
        value = split_product(total, top_ref[0], rest_ref[0])
        out[...] = value
        for distance in range(1, members):
            message = refs[2 * members + 2 + distance]
            message[:, :rows] = value
            message[:, rows:] = other_refs[distance][...]

    return local_kernel(
        body,
        [float_array(part, rows)] + [float_array(part, rows + width)] * (members - 1),
        [*shares, *others, top, rest],
        flops=6 * part * rows * order,
    )


def take_messages(own, other, messages, top, rest):
    members = len(messages) + 1
    part, width = other.shape
    rows, order = top.shape[1:]

    def body(*refs):
        own_ref, other_ref = refs[:2]
        held = refs[2 : members + 1]
        top_ref, rest_ref, out = refs[members + 1 : members + 4]
        whole = refs[-1]
        total = other_ref[...]
        for ref in held:
            total = total + ref[:, rows:]
        if width > rows:
            refs[members + 4][...] = total
        pieces = [ref[:, :rows] for ref in held[-1:] + held[:-1]]
        put_in_order([own_ref[...]] + pieces, whole)
        out[...] = total[:, :rows] - split_product(whole[...], top_ref[0], rest_ref[0])

    return local_kernel(
        body,
        [float_array(part, rows)] + [float_array(part, width)] * (width > rows),
        [own, other, *messages, top, rest],
        flops=6 * part * rows * order,
        scratch=[pltpu.VMEM((part, order), jnp.float32)],
    )


def put_in_order(held, whole):
    me = lax.axis_index("grp")
    members = len(held)
    width = held[0].shape[1]
    for j in range(members):
        value = jnp.zeros(held[0].shape, jnp.float32)
        for distance in range(members):
            owner = partner(me, distance, members) if distance else me
            value = jnp.where(owner == j, held[distance], value)
        whole[:, j * width : (j + 1) * width] = value


def apply_split(pieces, top, rest, index, base=None, begin=0, others=None, far_first=True):
    members = lax.axis_size("grp")
    part, width = pieces[0].shape
    rows, order = top.shape[1:]
    extra = list(others or []) if base is None else [base]

    def body(*refs):
        top_ref, rest_ref = refs[members : members + 2]
        out, whole = refs[-2:]
        held = [refs[d][...] for d in range(members)]
        if far_first:
            held = held[:1] + held[-1:] + held[1:-1] if members > 2 else held
        put_in_order(held, whole)
        result = split_product(whole[...], top_ref[index], rest_ref[index])
        if others is not None:
            for i in range(len(others)):
                out[i] = refs[members + 2 + i][...]
            out[len(others)] = result
            return
        if base is not None:
            result = refs[members + 2][:, begin : begin + rows] - result
        out[...] = result

    shape = (part, rows) if others is None else (len(others) + 1, part, rows)
    return local_kernel(
        body,
        [float_array(*shape)],
        [*pieces, top, rest, *extra],
        flops=6 * part * rows * order,
        scratch=[pltpu.VMEM((part, order), jnp.float32)],
    )[0]


def on_device(
    rhs_local,
    diag_inv_local,
    sub_local,
    tiles,
    tile_block,
    tile_source,
    tile_count,
    rhs_anc,
    diag_inv_anc,
    sub_anc,
):
    supernodes, _, order = diag_inv_local.shape[1:]
    rhs_count = rhs_local.shape[-1]
    members = lax.axis_size("grp")
    rows = order // members
    slots, tile_rows = tiles.shape[2:4]

    streams = 2 if rhs_count % 16 == 0 else 1
    residuals = turn_first(rhs_local, streams)
    first = diag_inv_local[0, 0]
    rounded = lax.reduce_precision(first, 8, 7)
    first_top = rounded.astype(jnp.bfloat16)[None]
    first_rest = (first - rounded).astype(jnp.bfloat16)[None]
    solved = [[None] * streams for _ in range(supernodes)]
    gathered = [[None] * streams for _ in range(supernodes)]
    values = list(residuals)
    last = None
    for step in range(2 * supernodes):
        current = step // 2
        for i in range(streams):
            turn_taken = step > 0 and last is not None
            ties = [(1, last[0][2][1])] if step * streams + i > streams else []
            pieces = gather_rows(values[i], ties)
            if step == 1 and i == 0:
                later = turn(rhs_local, 1, supernodes, streams, pieces[1][1])
            if turn_taken:
                offset, piece = pieces[2]
                pieces[2] = (offset, lax.optimization_barrier((piece, last[1]))[0])
            if step == 0:
                owned = apply_split(
                    [p for _, p in pieces],
                    first_top,
                    first_rest,
                    0,
                    far_first=False,
                )
            else:
                whole = assemble(pieces, order)
                if step % 2 == 0:
                    owned = contract_last(whole, diag_inv_local[0, current])
                elif current + 1 < supernodes:
                    owned = later[current * streams + i] - contract_last(whole, sub_local[0, current])
            if step % 2 == 0:
                solved[current][i] = owned
            else:
                gathered[current][i] = whole
            values[i] = owned
            last = (pieces, owned)

    by_stream = [[values[i] for values in gathered] for i in range(streams)]
    done = [tile_terms(values, tiles[0, 0], tile_source) for values in by_stream[:-1]]
    packed = pack_terms(done, by_stream[-1], tiles[0, 0], tile_source, tile_block, tile_count)
    received = leaf_exchange(packed)
    solution_local, tie = turn_back(solved, packed[0])
    shares = share_out(
        received, jnp.swapaxes(rhs_anc, 1, 2), order, slots, tile_rows, tie
    )
    far_first = list(range(2, members)) + list(range(1, min(members, 2)))
    first_share, others = shares[0], shares[1:]
    sums = [first_share] + [send(first_share, "grp", d) for d in far_first]
    inverse_top, inverse_rest, below_top, below_rest = split_factors(
        [diag_inv_anc, sub_anc], first_share
    )
    solution, *messages = solve_first(sums, others, inverse_top, inverse_rest)
    solutions = [solution]
    ancestors = rhs_anc.shape[0]
    for ancestor in range(1, ancestors):
        if ancestor == 1:
            arrived = [send(messages[d - 1], "grp", d) for d in far_first]
            residual, *left = take_messages(solution, others[0], arrived, below_top, below_rest)
        else:
            pieces = gather_far_first(solutions[-1])
            residual = apply_split(
                pieces, below_top, below_rest, ancestor - 1, left[0], (ancestor - 1) * rows
            )
        pieces = gather_far_first(residual)
        behind = solutions if ancestor + 1 == ancestors else None
        solved_now = apply_split(pieces, inverse_top, inverse_rest, ancestor, others=behind)
        solutions.append(solved_now)
    solutions = solutions[-1] if ancestors > 1 else solutions[0][None]
    solutions = jnp.swapaxes(solutions, 1, 2)
    return (solution_local, solutions)


def solution(mesh):
    return jax.shard_map(
        on_device,
        mesh=mesh,
        in_specs=(
            P("leaf", None, "grp", None),
            P("leaf", None, "grp", None),
            P("leaf", None, "grp", None),
            P("leaf", "grp", None, None, None),
            P("leaf", "grp", None),
            P("leaf", "grp", None),
            P("leaf", "grp"),
            P(None, "grp", "leaf"),
            P(None, "grp", None),
            P(None, "grp", None),
        ),
        out_specs=(P("leaf", None, "grp", None), P(None, "grp", "leaf")),
        check_vma=False,
    )
```

```python
import jax
import jax.numpy as jnp
from jax import lax
from jax.experimental import pallas as pl
from jax.experimental.pallas import tpu as pltpu
from jax.sharding import PartitionSpec as P

high = lax.Precision.HIGH


def contract_last(left, right):
    return lax.dot_general(
        left,
        right,
        (((left.ndim - 1,), (right.ndim - 1,)), ((), ())),
        precision=high,
        preferred_element_type=jnp.float32,
    )


def partner(index, distance, count):
    if count & (count - 1):
        return lax.rem(index - distance + 2 * count, count)
    return index ^ abs(distance)


def send(value, axis, distance):
    count = lax.axis_size(axis)
    if count & (count - 1):
        pairs = [(i, (i + distance) % count) for i in range(count)]
    else:
        pairs = [(i, i ^ distance) for i in range(count)]
    return lax.ppermute(value, axis, pairs)


def gather_rows(value, ties=None, far_first=False):
    members = lax.axis_size("grp")
    me = lax.axis_index("grp")
    rows = value.shape[1]
    pieces = [(me * rows, value)]
    distances = list(range(1, members))
    if ties is not None:
        distances[1:] = distances[:0:-1]
    if far_first:
        distances = distances[1:] + distances[:1]
    for distance in distances:
        owner = partner(me, distance, members)
        tied = value
        if distance in dict(ties or ()):
            tied = lax.optimization_barrier((value, dict(ties)[distance]))[0]
        pieces.append((owner * rows, send(tied, "grp", distance)))
    return pieces


def gather_far_first(value):
    return [piece for _, piece in gather_rows(value, far_first=True)]


def assemble(pieces, order):
    whole = jnp.zeros((pieces[0][1].shape[0], order), jnp.float32)
    for offset, piece in pieces:
        whole = lax.dynamic_update_slice_in_dim(whole, piece, offset, 1)
    return whole


def apply_pieces(factor, index, pieces):
    total = None
    for offset, piece in pieces:
        size = (1, 1, factor.shape[2], piece.shape[1])
        columns = lax.dynamic_slice(factor, (0, index, 0, offset), size)[0, 0]
        term = contract_last(piece, columns)
        total = term if total is None else total + term
    return total


def swap(value, axis, distance, block):
    count = lax.axis_size(axis)
    outer = count // block
    if outer & (outer - 1):
        pairs = [(i, (i // block + distance) % outer * block + i % block) for i in range(count)]
    else:
        pairs = [(i, (i // block ^ distance) * block + i % block) for i in range(count)]
    return lax.ppermute(value, axis, pairs)


VMEM = pl.BlockSpec(memory_space=pltpu.VMEM)
SMEM = pl.BlockSpec(memory_space=pltpu.SMEM)
ANY = pl.BlockSpec(memory_space=pl.ANY)


def local_kernel(body, outs, operands, specs=None, flops=0, scratch=(), limit=None):
    size = sum(o.size * o.dtype.itemsize for o in list(outs) + list(operands))
    return pl.pallas_call(
        body,
        out_shape=list(outs),
        in_specs=specs or [VMEM] * len(operands),
        out_specs=[VMEM] * len(outs),
        scratch_shapes=list(scratch),
        cost_estimate=pl.CostEstimate(flops=flops, bytes_accessed=size, transcendentals=0),
        compiler_params=pltpu.CompilerParams(vmem_limit_bytes=limit or 2 * size + 2**21),
    )(*operands)


def float_array(*shape):
    return jax.ShapeDtypeStruct(shape, jnp.float32)


def high_low(value):
    top = value.astype(jnp.bfloat16)
    return top, (value - top.astype(jnp.float32)).astype(jnp.bfloat16)


def split_product(left, top, rest):
    def dot(x, y):
        return lax.dot_general(
            x, y, (((1,), (1,)), ((), ())), preferred_element_type=jnp.float32
        )

    count = left.shape[0]
    left_top, left_rest = high_low(left)
    both = dot(jnp.concatenate([left_top, left_rest], axis=0), top)
    return both[:count] + (dot(left_top, rest) + both[count:])


def leaf_shape():
    groups = lax.axis_size("leaf")
    inner = 2 if groups % 2 == 0 else 1
    return groups // inner, inner


def select_terms(sources_ref, gathered, tile_refs, store):
    for m in range(tile_refs.shape[0]):
        chosen = gathered[0][...]
        for index in range(1, len(gathered)):
            chosen = jnp.where(sources_ref[0, 0, m] == index, gathered[index][...], chosen)
        top, rest = high_low(tile_refs[m])
        store(m, split_product(chosen, top, rest))


def tile_terms(gathered, tiles, sources):
    slots, tile_rows, order = tiles.shape
    depth = gathered[0].shape[0]
    count = len(gathered)

    def body(*refs):
        out = refs[-1]

        def store(m, term):
            out[:, m * tile_rows : (m + 1) * tile_rows] = term

        select_terms(refs[count + 1], refs[:count], refs[count], store)

    return local_kernel(
        body,
        [float_array(depth, slots * tile_rows)],
        [*gathered, tiles, sources],
        [VMEM] * (count + 1) + [SMEM],
        flops=6 * depth * slots * tile_rows * order,
    )[0]


def pack_terms(done, gathered, tiles, sources, blocks, live):
    outer, inner = leaf_shape()
    slots, tile_rows, order = tiles.shape
    depth = gathered[0].shape[0]
    streams = len(done) + 1
    part = depth * streams // (outer * inner)
    width = (slots + 1) * tile_rows
    count = len(gathered)
    base = len(done)

    def body(*refs):
        source_ref, block_ref, live_ref = refs[base + count + 1 : base + count + 4]
        outs = refs[base + count + 4 : -1]
        terms = refs[-1]
        lanes = lax.broadcasted_iota(jnp.int32, (streams * depth, tile_rows), 1)
        tag = jnp.full((streams * depth, tile_rows), -1.0, jnp.float32)
        for m in range(slots):
            value = jnp.where(m < live_ref[0, 0], block_ref[0, 0, m], -1).astype(jnp.float32)
            tag = jnp.where(lanes == m, value, tag)
        terms[:, slots * tile_rows :] = tag
        for i in range(base):
            terms[i * depth : (i + 1) * depth, : slots * tile_rows] = refs[i][...]

        def store(m, term):
            terms[base * depth :, m * tile_rows : (m + 1) * tile_rows] = term

        select_terms(source_ref, refs[base : base + count], refs[base + count], store)
        inside = lax.rem(lax.axis_index("leaf"), inner)
        for o in range(outer):
            cut = [
                terms[(o * inner + i) * part : (o * inner + i + 1) * part, :]
                for i in range(inner)
            ]
            for i in range(inner):
                outs[i][o] = jnp.where(inside == 0, cut[i], cut[inner - 1 - i])

    return local_kernel(
        body,
        [float_array(outer, part, width)] * inner,
        [*done, *gathered, tiles, sources, blocks, live],
        [VMEM] * (base + count + 1) + [SMEM] * 3,
        flops=6 * depth * slots * tile_rows * order,
        scratch=[pltpu.VMEM((streams * depth, width), jnp.float32)],
    )


def turn(rhs, first, last, streams, after):
    rows, count = rhs.shape[2:]
    depth = count // streams

    def body(rhs_ref, after_ref, out, held, sem):
        copy = pltpu.make_async_copy(rhs_ref.at[0, first:last], held, sem)
        copy.start()
        copy.wait()
        for index in range(last - first):
            wide = jnp.transpose(held[index])
            for i in range(streams):
                out[index * streams + i] = wide[i * depth : (i + 1) * depth]

    return local_kernel(
        body,
        [float_array(streams * (last - first), depth, rows)],
        [rhs, after],
        [ANY, ANY],
        scratch=[
            pltpu.VMEM((last - first, rows, count), jnp.float32),
            pltpu.SemaphoreType.DMA(()),
        ],
    )[0]


def turn_first(rhs, streams):
    rows, count = rhs.shape[2:]
    depth = count // streams

    def body(rhs_ref, *refs):
        outs, (held, sem) = refs[:-2], refs[-2:]
        copy = pltpu.make_async_copy(rhs_ref.at[0, 0], held, sem)
        copy.start()
        copy.wait()
        wide = jnp.transpose(held[...])
        for i in range(streams):
            outs[i][...] = wide[i * depth : (i + 1) * depth]

    return local_kernel(
        body,
        [float_array(depth, rows)] * streams,
        [rhs],
        [ANY],
        scratch=[pltpu.VMEM((rows, count), jnp.float32), pltpu.SemaphoreType.DMA(())],
    )


def turn_back(solved, after):
    flat = [value for streams in solved for value in streams]
    streams = len(solved[0])
    depth, rows = flat[0].shape

    def body(*refs):
        out, tie = refs[-2:]
        for index in range(len(solved)):
            wide = jnp.concatenate(
                [refs[index * streams + i][...] for i in range(streams)], axis=0
            )
            out[0, index] = jnp.transpose(wide)
        tie[...] = jnp.zeros(tie.shape, jnp.float32)

    return local_kernel(
        body,
        [float_array(1, len(solved), rows, depth * streams), float_array(8, 128)],
        [*flat, after],
        [VMEM] * len(flat) + [ANY],
    )


def leaf_exchange(packed):
    outer, inner = leaf_shape()
    part, width = packed[0].shape[1:]
    held = [packed[0]]
    if inner == 2:
        pairs = [(i, i ^ 1) for i in range(outer * inner)]
        held.append(lax.ppermute(packed[1], "leaf", pairs))

    def body(*refs):
        outside = lax.div(lax.axis_index("leaf"), inner)
        for distance in range(outer):
            target = partner(outside, -distance, outer) if distance else outside
            for i in range(inner):
                refs[inner + distance][i] = refs[i][target]

    portions = local_kernel(body, [float_array(inner, part, width)] * outer, held)
    return [portions[0]] + [
        swap(portions[distance], "leaf", distance, inner) for distance in range(outer - 1, 0, -1)
    ]


def share_out(received, rhs_turned, order, slots, tile_rows, after):
    members = lax.axis_size("grp")
    ancestors, part, rows = rhs_turned.shape
    inner = received[0].shape[0]
    block_count = ancestors * order // tile_rows
    width = (ancestors - 1) * rows

    def body(*refs):
        sources = refs[: len(received)]
        rhs_ref = refs[len(received)]
        outs = refs[len(received) + 2 : -1]
        share = refs[-1]
        me = lax.axis_index("grp")
        totals = [jnp.zeros((part, tile_rows), jnp.float32) for _ in range(block_count)]
        for source in sources:
            for i in range(inner):
                for m in range(slots):
                    tile = source[i, :, m * tile_rows : (m + 1) * tile_rows]
                    tag = source[i, :, slots * tile_rows + m : slots * tile_rows + m + 1]
                    tag = jnp.broadcast_to(tag, tile.shape)
                    for q in range(block_count):
                        totals[q] = totals[q] + jnp.where(tag == float(q), tile, 0.0)
        for q in range(block_count):
            share[:, q * tile_rows : (q + 1) * tile_rows] = -totals[q]
        for a in range(ancestors):
            for j in range(members):
                at = slice(a * order + j * rows, a * order + (j + 1) * rows)
                share[:, at] = share[:, at] + jnp.where(me == j, rhs_ref[a], 0.0)
        outs[0][...] = share[:, :order]
        for distance in range(members):
            target = partner(me, -distance, members) if distance else me
            out = outs[1 + distance]
            for a in range(1, ancestors):
                value = jnp.zeros((part, rows), jnp.float32)
                for j in range(members):
                    at = slice(a * order + j * rows, a * order + (j + 1) * rows)
                    value = jnp.where(target == j, share[:, at], value)
                out[:, (a - 1) * rows : a * rows] = value

    return local_kernel(
        body,
        [float_array(part, order)] + [float_array(part, width)] * members,
        [*received, rhs_turned, after],
        [VMEM] * (len(received) + 1) + [ANY],
        scratch=[pltpu.VMEM((part, ancestors * order), jnp.float32)],
    )


def split_factors(factors, after):
    count = len(factors)

    def body(*refs):
        for i in range(count):
            top, rest = high_low(refs[i][...])
            refs[count + 1 + 2 * i][...] = top
            refs[count + 2 + 2 * i][...] = rest

    outs = []
    for factor in factors:
        outs += [jax.ShapeDtypeStruct(factor.shape, jnp.bfloat16)] * 2
    return local_kernel(
        body,
        outs,
        [*factors, after],
        [VMEM] * count + [ANY],
        flops=4 * sum(f.size for f in factors),
    )


def solve_first(shares, others, top, rest):
    members = len(others)
    part, width = others[0].shape
    rows, order = top.shape[1:]

    def body(*refs):
        total = refs[0][...]
        for ref in refs[1:members]:
            total = total + ref[...]
        other_refs = refs[members : 2 * members]
        top_ref, rest_ref, out = refs[2 * members : 2 * members + 3]
        value = split_product(total, top_ref[0], rest_ref[0])
        out[...] = value
        for distance in range(1, members):
            message = refs[2 * members + 2 + distance]
            message[:, :rows] = value
            message[:, rows:] = other_refs[distance][...]

    return local_kernel(
        body,
        [float_array(part, rows)] + [float_array(part, rows + width)] * (members - 1),
        [*shares, *others, top, rest],
        flops=6 * part * rows * order,
    )


def take_messages(own, other, messages, top, rest):
    members = len(messages) + 1
    part, width = other.shape
    rows, order = top.shape[1:]

    def body(*refs):
        own_ref, other_ref = refs[:2]
        held = refs[2 : members + 1]
        top_ref, rest_ref, out = refs[members + 1 : members + 4]
        whole = refs[-1]
        total = other_ref[...]
        for ref in held:
            total = total + ref[:, rows:]
        if width > rows:
            refs[members + 4][...] = total
        pieces = [ref[:, :rows] for ref in held[-1:] + held[:-1]]
        put_in_order([own_ref[...]] + pieces, whole)
        out[...] = total[:, :rows] - split_product(whole[...], top_ref[0], rest_ref[0])

    return local_kernel(
        body,
        [float_array(part, rows)] + [float_array(part, width)] * (width > rows),
        [own, other, *messages, top, rest],
        flops=6 * part * rows * order,
        scratch=[pltpu.VMEM((part, order), jnp.float32)],
    )


def put_in_order(held, whole):
    me = lax.axis_index("grp")
    members = len(held)
    width = held[0].shape[1]
    for j in range(members):
        value = jnp.zeros(held[0].shape, jnp.float32)
        for distance in range(members):
            owner = partner(me, distance, members) if distance else me
            value = jnp.where(owner == j, held[distance], value)
        whole[:, j * width : (j + 1) * width] = value


def apply_split(pieces, top, rest, index, base=None, begin=0, others=None, far_first=True):
    members = lax.axis_size("grp")
    part, width = pieces[0].shape
    rows, order = top.shape[1:]
    extra = list(others or []) if base is None else [base]

    def body(*refs):
        top_ref, rest_ref = refs[members : members + 2]
        out, whole = refs[-2:]
        held = [refs[d][...] for d in range(members)]
        if far_first:
            held = held[:1] + held[-1:] + held[1:-1] if members > 2 else held
        put_in_order(held, whole)
        result = split_product(whole[...], top_ref[index], rest_ref[index])
        if others is not None:
            for i in range(len(others)):
                out[i] = refs[members + 2 + i][...]
            out[len(others)] = result
            return
        if base is not None:
            result = refs[members + 2][:, begin : begin + rows] - result
        out[...] = result

    shape = (part, rows) if others is None else (len(others) + 1, part, rows)
    return local_kernel(
        body,
        [float_array(*shape)],
        [*pieces, top, rest, *extra],
        flops=6 * part * rows * order,
        scratch=[pltpu.VMEM((part, order), jnp.float32)],
    )[0]


def on_device(
    rhs_local,
    diag_inv_local,
    sub_local,
    tiles,
    tile_block,
    tile_source,
    tile_count,
    rhs_anc,
    diag_inv_anc,
    sub_anc,
):
    supernodes, _, order = diag_inv_local.shape[1:]
    rhs_count = rhs_local.shape[-1]
    members = lax.axis_size("grp")
    rows = order // members
    slots, tile_rows = tiles.shape[2:4]

    streams = 2 if rhs_count % 16 == 0 else 1
    residuals = turn_first(rhs_local, streams)
    first = diag_inv_local[0, 0]
    rounded = lax.reduce_precision(first, 8, 7)
    first_top = rounded.astype(jnp.bfloat16)[None]
    first_rest = (first - rounded).astype(jnp.bfloat16)[None]
    solved = [[None] * streams for _ in range(supernodes)]
    gathered = [[None] * streams for _ in range(supernodes)]
    values = list(residuals)
    last = None
    for step in range(2 * supernodes):
        current = step // 2
        for i in range(streams):
            turn_taken = step > 0 and last is not None
            ties = [(1, last[0][2][1])] if step * streams + i > streams else []
            pieces = gather_rows(values[i], ties)
            if step == 1 and i == 0:
                later = turn(rhs_local, 1, supernodes, streams, pieces[1][1])
            if turn_taken:
                offset, piece = pieces[2]
                pieces[2] = (offset, lax.optimization_barrier((piece, last[1]))[0])
            if step == 0:
                owned = apply_split(
                    [p for _, p in pieces[:2] + pieces[:1:-1]],
                    first_top,
                    first_rest,
                    0,
                    far_first=False,
                )
            else:
                whole = assemble(pieces, order)
                if step % 2 == 0:
                    owned = contract_last(whole, diag_inv_local[0, current])
                elif current + 1 < supernodes:
                    owned = later[current * streams + i] - contract_last(whole, sub_local[0, current])
            if step % 2 == 0:
                solved[current][i] = owned
            else:
                gathered[current][i] = whole
            values[i] = owned
            last = (pieces, owned)

    by_stream = [[values[i] for values in gathered] for i in range(streams)]
    done = [tile_terms(values, tiles[0, 0], tile_source) for values in by_stream[:-1]]
    packed = pack_terms(done, by_stream[-1], tiles[0, 0], tile_source, tile_block, tile_count)
    received = leaf_exchange(packed)
    solution_local, tie = turn_back(solved, packed[0])
    shares = share_out(
        received, jnp.swapaxes(rhs_anc, 1, 2), order, slots, tile_rows, tie
    )
    far_first = list(range(2, members)) + list(range(1, min(members, 2)))
    first_share, others = shares[0], shares[1:]
    sums = [first_share] + [send(first_share, "grp", d) for d in far_first]
    inverse_top, inverse_rest, below_top, below_rest = split_factors(
        [diag_inv_anc, sub_anc], first_share
    )
    solution, *messages = solve_first(sums, others, inverse_top, inverse_rest)
    solutions = [solution]
    ancestors = rhs_anc.shape[0]
    for ancestor in range(1, ancestors):
        if ancestor == 1:
            arrived = [send(messages[d - 1], "grp", d) for d in far_first]
            residual, *left = take_messages(solution, others[0], arrived, below_top, below_rest)
        else:
            pieces = gather_far_first(solutions[-1])
            residual = apply_split(
                pieces, below_top, below_rest, ancestor - 1, left[0], (ancestor - 1) * rows
            )
        pieces = gather_far_first(residual)
        behind = solutions if ancestor + 1 == ancestors else None
        solved_now = apply_split(pieces, inverse_top, inverse_rest, ancestor, others=behind)
        solutions.append(solved_now)
    solutions = solutions[-1] if ancestors > 1 else solutions[0][None]
    solutions = jnp.swapaxes(solutions, 1, 2)
    return (solution_local, solutions)


def solution(mesh):
    return jax.shard_map(
        on_device,
        mesh=mesh,
        in_specs=(
            P("leaf", None, "grp", None),
            P("leaf", None, "grp", None),
            P("leaf", None, "grp", None),
            P("leaf", "grp", None, None, None),
            P("leaf", "grp", None),
            P("leaf", "grp", None),
            P("leaf", "grp"),
            P(None, "grp", "leaf"),
            P(None, "grp", None),
            P(None, "grp", None),
        ),
        out_specs=(P("leaf", None, "grp", None), P(None, "grp", "leaf")),
        check_vma=False,
    )
```

```python
import jax
import jax.numpy as jnp
from jax import lax
from jax.experimental import pallas as pl
from jax.experimental.pallas import tpu as pltpu
from jax.sharding import PartitionSpec as P

high = lax.Precision.HIGH


def contract_last(left, right):
    return lax.dot_general(
        left,
        right,
        (((left.ndim - 1,), (right.ndim - 1,)), ((), ())),
        precision=high,
        preferred_element_type=jnp.float32,
    )


def partner(index, distance, count):
    if count & (count - 1):
        return lax.rem(index - distance + 2 * count, count)
    return index ^ abs(distance)


def send(value, axis, distance):
    count = lax.axis_size(axis)
    if count & (count - 1):
        pairs = [(i, (i + distance) % count) for i in range(count)]
    else:
        pairs = [(i, i ^ distance) for i in range(count)]
    return lax.ppermute(value, axis, pairs)


def gather_rows(value, ties=(), swapped=False, far_first=False):
    members = lax.axis_size("grp")
    me = lax.axis_index("grp")
    rows = value.shape[1]
    pieces = [(me * rows, value)]
    distances = list(range(1, members))
    if swapped:
        distances[1:] = distances[:0:-1]
    if far_first:
        distances = distances[1:] + distances[:1]
    for distance in distances:
        owner = partner(me, distance, members)
        tied = value
        if distance in dict(ties):
            tied = lax.optimization_barrier((value, dict(ties)[distance]))[0]
        pieces.append((owner * rows, send(tied, "grp", distance)))
    return pieces


def gather_far_first(value):
    return [piece for _, piece in gather_rows(value, far_first=True)]


def assemble(pieces, order):
    whole = jnp.zeros((pieces[0][1].shape[0], order), jnp.float32)
    for offset, piece in pieces:
        whole = lax.dynamic_update_slice_in_dim(whole, piece, offset, 1)
    return whole


def apply_pieces(factor, index, pieces):
    total = None
    for offset, piece in pieces:
        size = (1, 1, factor.shape[2], piece.shape[1])
        columns = lax.dynamic_slice(factor, (0, index, 0, offset), size)[0, 0]
        term = contract_last(piece, columns)
        total = term if total is None else total + term
    return total


def swap(value, axis, distance, block):
    count = lax.axis_size(axis)
    outer = count // block
    if outer & (outer - 1):
        pairs = [(i, (i // block + distance) % outer * block + i % block) for i in range(count)]
    else:
        pairs = [(i, (i // block ^ distance) * block + i % block) for i in range(count)]
    return lax.ppermute(value, axis, pairs)


VMEM = pl.BlockSpec(memory_space=pltpu.VMEM)
SMEM = pl.BlockSpec(memory_space=pltpu.SMEM)
ANY = pl.BlockSpec(memory_space=pl.ANY)


def local_kernel(body, outs, operands, specs=None, flops=0, scratch=(), limit=None):
    size = sum(o.size * o.dtype.itemsize for o in list(outs) + list(operands))
    return pl.pallas_call(
        body,
        out_shape=list(outs),
        in_specs=specs or [VMEM] * len(operands),
        out_specs=[VMEM] * len(outs),
        scratch_shapes=list(scratch),
        cost_estimate=pl.CostEstimate(flops=flops, bytes_accessed=size, transcendentals=0),
        compiler_params=pltpu.CompilerParams(vmem_limit_bytes=limit or 2 * size + 2**21),
    )(*operands)


def float_array(*shape):
    return jax.ShapeDtypeStruct(shape, jnp.float32)


def high_low(value):
    top = value.astype(jnp.bfloat16)
    return top, (value - top.astype(jnp.float32)).astype(jnp.bfloat16)


def split_product(left, top, rest):
    def dot(x, y):
        return lax.dot_general(
            x, y, (((1,), (1,)), ((), ())), preferred_element_type=jnp.float32
        )

    count = left.shape[0]
    left_top, left_rest = high_low(left)
    both = dot(jnp.concatenate([left_top, left_rest], axis=0), top)
    return both[:count] + (dot(left_top, rest) + both[count:])


def leaf_shape():
    groups = lax.axis_size("leaf")
    inner = 2 if groups % 2 == 0 else 1
    return groups // inner, inner


def select_terms(sources_ref, gathered, tile_refs, store):
    for m in range(tile_refs.shape[0]):
        chosen = gathered[0][...]
        for index in range(1, len(gathered)):
            chosen = jnp.where(sources_ref[0, 0, m] == index, gathered[index][...], chosen)
        top, rest = high_low(tile_refs[m])
        store(m, split_product(chosen, top, rest))


def tile_terms(gathered, tiles, sources):
    slots, tile_rows, order = tiles.shape
    depth = gathered[0].shape[0]
    count = len(gathered)

    def body(*refs):
        out = refs[-1]

        def store(m, term):
            out[:, m * tile_rows : (m + 1) * tile_rows] = term

        select_terms(refs[count + 1], refs[:count], refs[count], store)

    return local_kernel(
        body,
        [float_array(depth, slots * tile_rows)],
        [*gathered, tiles, sources],
        [VMEM] * (count + 1) + [SMEM],
        flops=6 * depth * slots * tile_rows * order,
    )[0]


def pack_terms(done, gathered, tiles, sources, blocks, live):
    outer, inner = leaf_shape()
    slots, tile_rows, order = tiles.shape
    depth = gathered[0].shape[0]
    streams = len(done) + 1
    part = depth * streams // (outer * inner)
    width = (slots + 1) * tile_rows
    count = len(gathered)
    base = len(done)

    def body(*refs):
        source_ref, block_ref, live_ref = refs[base + count + 1 : base + count + 4]
        outs = refs[base + count + 4 : -1]
        terms = refs[-1]
        lanes = lax.broadcasted_iota(jnp.int32, (streams * depth, tile_rows), 1)
        tag = jnp.full((streams * depth, tile_rows), -1.0, jnp.float32)
        for m in range(slots):
            value = jnp.where(m < live_ref[0, 0], block_ref[0, 0, m], -1).astype(jnp.float32)
            tag = jnp.where(lanes == m, value, tag)
        terms[:, slots * tile_rows :] = tag
        for i in range(base):
            terms[i * depth : (i + 1) * depth, : slots * tile_rows] = refs[i][...]

        def store(m, term):
            terms[base * depth :, m * tile_rows : (m + 1) * tile_rows] = term

        select_terms(source_ref, refs[base : base + count], refs[base + count], store)
        inside = lax.rem(lax.axis_index("leaf"), inner)
        for o in range(outer):
            cut = [
                terms[(o * inner + i) * part : (o * inner + i + 1) * part, :]
                for i in range(inner)
            ]
            for i in range(inner):
                outs[i][o] = jnp.where(inside == 0, cut[i], cut[inner - 1 - i])

    return local_kernel(
        body,
        [float_array(outer, part, width)] * inner,
        [*done, *gathered, tiles, sources, blocks, live],
        [VMEM] * (base + count + 1) + [SMEM] * 3,
        flops=6 * depth * slots * tile_rows * order,
        scratch=[pltpu.VMEM((streams * depth, width), jnp.float32)],
    )


def turn(rhs, first, last, streams, after):
    rows, count = rhs.shape[2:]
    depth = count // streams

    def body(rhs_ref, after_ref, out, held, sem):
        copy = pltpu.make_async_copy(rhs_ref.at[0, first:last], held, sem)
        copy.start()
        copy.wait()
        for index in range(last - first):
            wide = jnp.transpose(held[index])
            for i in range(streams):
                out[index * streams + i] = wide[i * depth : (i + 1) * depth]

    return local_kernel(
        body,
        [float_array(streams * (last - first), depth, rows)],
        [rhs, after],
        [ANY, ANY],
        scratch=[
            pltpu.VMEM((last - first, rows, count), jnp.float32),
            pltpu.SemaphoreType.DMA(()),
        ],
    )[0]


def turn_first(rhs, streams):
    rows, count = rhs.shape[2:]
    depth = count // streams

    def body(rhs_ref, *refs):
        outs, (held, sem) = refs[:-2], refs[-2:]
        copy = pltpu.make_async_copy(rhs_ref.at[0, 0], held, sem)
        copy.start()
        copy.wait()
        wide = jnp.transpose(held[...])
        for i in range(streams):
            outs[i][...] = wide[i * depth : (i + 1) * depth]

    return local_kernel(
        body,
        [float_array(depth, rows)] * streams,
        [rhs],
        [ANY],
        scratch=[pltpu.VMEM((rows, count), jnp.float32), pltpu.SemaphoreType.DMA(())],
    )


def turn_back(solved, after):
    flat = [value for streams in solved for value in streams]
    streams = len(solved[0])
    depth, rows = flat[0].shape

    def body(*refs):
        out, tie = refs[-2:]
        for index in range(len(solved)):
            wide = jnp.concatenate(
                [refs[index * streams + i][...] for i in range(streams)], axis=0
            )
            out[0, index] = jnp.transpose(wide)
        tie[...] = jnp.zeros(tie.shape, jnp.float32)

    return local_kernel(
        body,
        [float_array(1, len(solved), rows, depth * streams), float_array(8, 128)],
        [*flat, after],
        [VMEM] * len(flat) + [ANY],
    )


def leaf_exchange(packed):
    outer, inner = leaf_shape()
    part, width = packed[0].shape[1:]
    held = [packed[0]]
    if inner == 2:
        pairs = [(i, i ^ 1) for i in range(outer * inner)]
        held.append(lax.ppermute(packed[1], "leaf", pairs))

    def body(*refs):
        outside = lax.div(lax.axis_index("leaf"), inner)
        for distance in range(outer):
            target = partner(outside, -distance, outer) if distance else outside
            for i in range(inner):
                refs[inner + distance][i] = refs[i][target]

    portions = local_kernel(body, [float_array(inner, part, width)] * outer, held)
    return [portions[0]] + [
        swap(portions[distance], "leaf", distance, inner) for distance in range(outer - 1, 0, -1)
    ]


def share_out(received, rhs_turned, order, slots, tile_rows, after):
    members = lax.axis_size("grp")
    ancestors, part, rows = rhs_turned.shape
    inner = received[0].shape[0]
    block_count = ancestors * order // tile_rows
    width = (ancestors - 1) * rows

    def body(*refs):
        sources = refs[: len(received)]
        rhs_ref = refs[len(received)]
        outs = refs[len(received) + 2 : -1]
        share = refs[-1]
        me = lax.axis_index("grp")
        totals = [jnp.zeros((part, tile_rows), jnp.float32) for _ in range(block_count)]
        for source in sources:
            for i in range(inner):
                for m in range(slots):
                    tile = source[i, :, m * tile_rows : (m + 1) * tile_rows]
                    tag = source[i, :, slots * tile_rows + m : slots * tile_rows + m + 1]
                    tag = jnp.broadcast_to(tag, tile.shape)
                    for q in range(block_count):
                        totals[q] = totals[q] + jnp.where(tag == float(q), tile, 0.0)
        for q in range(block_count):
            share[:, q * tile_rows : (q + 1) * tile_rows] = -totals[q]
        for a in range(ancestors):
            for j in range(members):
                at = slice(a * order + j * rows, a * order + (j + 1) * rows)
                share[:, at] = share[:, at] + jnp.where(me == j, rhs_ref[a], 0.0)
        outs[0][...] = share[:, :order]
        for distance in range(members):
            target = partner(me, -distance, members) if distance else me
            out = outs[1 + distance]
            for a in range(1, ancestors):
                value = jnp.zeros((part, rows), jnp.float32)
                for j in range(members):
                    at = slice(a * order + j * rows, a * order + (j + 1) * rows)
                    value = jnp.where(target == j, share[:, at], value)
                out[:, (a - 1) * rows : a * rows] = value

    return local_kernel(
        body,
        [float_array(part, order)] + [float_array(part, width)] * members,
        [*received, rhs_turned, after],
        [VMEM] * (len(received) + 1) + [ANY],
        scratch=[pltpu.VMEM((part, ancestors * order), jnp.float32)],
    )


def split_factors(factors, after):
    count = len(factors)

    def body(*refs):
        for i in range(count):
            top, rest = high_low(refs[i][...])
            refs[count + 1 + 2 * i][...] = top
            refs[count + 2 + 2 * i][...] = rest

    outs = []
    for factor in factors:
        outs += [jax.ShapeDtypeStruct(factor.shape, jnp.bfloat16)] * 2
    return local_kernel(
        body,
        outs,
        [*factors, after],
        [VMEM] * count + [ANY],
        flops=4 * sum(f.size for f in factors),
    )


def solve_first(shares, others, top, rest):
    members = len(others)
    part, width = others[0].shape
    rows, order = top.shape[1:]

    def body(*refs):
        total = refs[0][...]
        for ref in refs[1:members]:
            total = total + ref[...]
        other_refs = refs[members : 2 * members]
        top_ref, rest_ref, out = refs[2 * members : 2 * members + 3]
        value = split_product(total, top_ref[0], rest_ref[0])
        out[...] = value
        for distance in range(1, members):
            message = refs[2 * members + 2 + distance]
            message[:, :rows] = value
            message[:, rows:] = other_refs[distance][...]

    return local_kernel(
        body,
        [float_array(part, rows)] + [float_array(part, rows + width)] * (members - 1),
        [*shares, *others, top, rest],
        flops=6 * part * rows * order,
    )


def take_messages(own, other, messages, top, rest):
    members = len(messages) + 1
    part, width = other.shape
    rows, order = top.shape[1:]

    def body(*refs):
        own_ref, other_ref = refs[:2]
        held = refs[2 : members + 1]
        top_ref, rest_ref, out = refs[members + 1 : members + 4]
        whole = refs[-1]
        total = other_ref[...]
        for ref in held:
            total = total + ref[:, rows:]
        if width > rows:
            refs[members + 4][...] = total
        pieces = [ref[:, :rows] for ref in held[-1:] + held[:-1]]
        put_in_order([own_ref[...]] + pieces, whole)
        out[...] = total[:, :rows] - split_product(whole[...], top_ref[0], rest_ref[0])

    return local_kernel(
        body,
        [float_array(part, rows)] + [float_array(part, width)] * (width > rows),
        [own, other, *messages, top, rest],
        flops=6 * part * rows * order,
        scratch=[pltpu.VMEM((part, order), jnp.float32)],
    )


def put_in_order(held, whole):
    me = lax.axis_index("grp")
    members = len(held)
    width = held[0].shape[1]
    for j in range(members):
        value = jnp.zeros(held[0].shape, jnp.float32)
        for distance in range(members):
            owner = partner(me, distance, members) if distance else me
            value = jnp.where(owner == j, held[distance], value)
        whole[:, j * width : (j + 1) * width] = value


def apply_split(pieces, top, rest, index, base=None, begin=0, others=None, far_first=True):
    members = lax.axis_size("grp")
    part, width = pieces[0].shape
    rows, order = top.shape[1:]
    extra = list(others or []) if base is None else [base]

    def body(*refs):
        top_ref, rest_ref = refs[members : members + 2]
        out, whole = refs[-2:]
        held = [refs[d][...] for d in range(members)]
        if far_first:
            held = held[:1] + held[-1:] + held[1:-1] if members > 2 else held
        put_in_order(held, whole)
        result = split_product(whole[...], top_ref[index], rest_ref[index])
        if others is not None:
            for i in range(len(others)):
                out[i] = refs[members + 2 + i][...]
            out[len(others)] = result
            return
        if base is not None:
            result = refs[members + 2][:, begin : begin + rows] - result
        out[...] = result

    shape = (part, rows) if others is None else (len(others) + 1, part, rows)
    return local_kernel(
        body,
        [float_array(*shape)],
        [*pieces, top, rest, *extra],
        flops=6 * part * rows * order,
        scratch=[pltpu.VMEM((part, order), jnp.float32)],
    )[0]


def on_device(
    rhs_local,
    diag_inv_local,
    sub_local,
    tiles,
    tile_block,
    tile_source,
    tile_count,
    rhs_anc,
    diag_inv_anc,
    sub_anc,
):
    supernodes, _, order = diag_inv_local.shape[1:]
    rhs_count = rhs_local.shape[-1]
    members = lax.axis_size("grp")
    rows = order // members
    slots, tile_rows = tiles.shape[2:4]

    streams = 2 if rhs_count % 16 == 0 else 1
    residuals = turn_first(rhs_local, streams)
    first = diag_inv_local[0, 0]
    rounded = lax.reduce_precision(first, 8, 7)
    first_top = rounded.astype(jnp.bfloat16)[None]
    first_rest = (first - rounded).astype(jnp.bfloat16)[None]
    solved = [[None] * streams for _ in range(supernodes)]
    gathered = [[None] * streams for _ in range(supernodes)]
    values = list(residuals)
    last = None
    for step in range(2 * supernodes):
        current = step // 2
        for i in range(streams):
            turn_taken = step > 0 and last is not None
            ties = [(1, last[0][2][1])] if step * streams + i > streams else []
            pieces = gather_rows(values[i], ties, i % 2 == 1 and step + 1 < 2 * supernodes)
            if step == 1 and i == 0:
                later = turn(rhs_local, 1, supernodes, streams, pieces[1][1])
            if turn_taken:
                offset, piece = pieces[2]
                pieces[2] = (offset, lax.optimization_barrier((piece, last[1]))[0])
            if step == 0:
                in_turn = pieces[:2] + pieces[:1:-1] if i % 2 else pieces
                owned = apply_split(
                    [p for _, p in in_turn],
                    first_top,
                    first_rest,
                    0,
                    far_first=False,
                )
            else:
                whole = assemble(pieces, order)
                if step % 2 == 0:
                    owned = contract_last(whole, diag_inv_local[0, current])
                elif current + 1 < supernodes:
                    owned = later[current * streams + i] - contract_last(whole, sub_local[0, current])
            if step % 2 == 0:
                solved[current][i] = owned
            else:
                gathered[current][i] = whole
            values[i] = owned
            last = (pieces, owned)

    by_stream = [[values[i] for values in gathered] for i in range(streams)]
    done = [tile_terms(values, tiles[0, 0], tile_source) for values in by_stream[:-1]]
    packed = pack_terms(done, by_stream[-1], tiles[0, 0], tile_source, tile_block, tile_count)
    received = leaf_exchange(packed)
    solution_local, tie = turn_back(solved, packed[0])
    shares = share_out(
        received, jnp.swapaxes(rhs_anc, 1, 2), order, slots, tile_rows, tie
    )
    far_first = list(range(2, members)) + list(range(1, min(members, 2)))
    first_share, others = shares[0], shares[1:]
    sums = [first_share] + [send(first_share, "grp", d) for d in far_first]
    inverse_top, inverse_rest, below_top, below_rest = split_factors(
        [diag_inv_anc, sub_anc], first_share
    )
    solution, *messages = solve_first(sums, others, inverse_top, inverse_rest)
    solutions = [solution]
    ancestors = rhs_anc.shape[0]
    for ancestor in range(1, ancestors):
        if ancestor == 1:
            arrived = [send(messages[d - 1], "grp", d) for d in far_first]
            residual, *left = take_messages(solution, others[0], arrived, below_top, below_rest)
        else:
            pieces = gather_far_first(solutions[-1])
            residual = apply_split(
                pieces, below_top, below_rest, ancestor - 1, left[0], (ancestor - 1) * rows
            )
        pieces = gather_far_first(residual)
        behind = solutions if ancestor + 1 == ancestors else None
        solved_now = apply_split(pieces, inverse_top, inverse_rest, ancestor, others=behind)
        solutions.append(solved_now)
    solutions = solutions[-1] if ancestors > 1 else solutions[0][None]
    solutions = jnp.swapaxes(solutions, 1, 2)
    return (solution_local, solutions)


def solution(mesh):
    return jax.shard_map(
        on_device,
        mesh=mesh,
        in_specs=(
            P("leaf", None, "grp", None),
            P("leaf", None, "grp", None),
            P("leaf", None, "grp", None),
            P("leaf", "grp", None, None, None),
            P("leaf", "grp", None),
            P("leaf", "grp", None),
            P("leaf", "grp"),
            P(None, "grp", "leaf"),
            P(None, "grp", None),
            P(None, "grp", None),
        ),
        out_specs=(P("leaf", None, "grp", None), P(None, "grp", "leaf")),
        check_vma=False,
    )
```

```python
import jax
import jax.numpy as jnp
from jax import lax
from jax.experimental import pallas as pl
from jax.experimental.pallas import tpu as pltpu
from jax.sharding import PartitionSpec as P

high = lax.Precision.HIGH


def contract_last(left, right):
    return lax.dot_general(
        left,
        right,
        (((left.ndim - 1,), (right.ndim - 1,)), ((), ())),
        precision=high,
        preferred_element_type=jnp.float32,
    )


def partner(index, distance, count):
    if count & (count - 1):
        return lax.rem(index - distance + 2 * count, count)
    return index ^ abs(distance)


def send(value, axis, distance):
    count = lax.axis_size(axis)
    if count & (count - 1):
        pairs = [(i, (i + distance) % count) for i in range(count)]
    else:
        pairs = [(i, i ^ distance) for i in range(count)]
    return lax.ppermute(value, axis, pairs)


def gather_rows(value, ties=(), far_first=False):
    members = lax.axis_size("grp")
    me = lax.axis_index("grp")
    rows = value.shape[1]
    pieces = [(me * rows, value)]
    distances = list(range(1, members))
    if far_first:
        distances = distances[1:] + distances[:1]
    for distance in distances:
        owner = partner(me, distance, members)
        tied = value
        if distance in dict(ties):
            tied = lax.optimization_barrier((value, dict(ties)[distance]))[0]
        pieces.append((owner * rows, send(tied, "grp", distance)))
    return pieces


def gather_far_first(value):
    return [piece for _, piece in gather_rows(value, far_first=True)]


def assemble(pieces, order):
    whole = jnp.zeros((pieces[0][1].shape[0], order), jnp.float32)
    for offset, piece in pieces:
        whole = lax.dynamic_update_slice_in_dim(whole, piece, offset, 1)
    return whole


def apply_pieces(factor, index, pieces):
    total = None
    for offset, piece in pieces:
        size = (1, 1, factor.shape[2], piece.shape[1])
        columns = lax.dynamic_slice(factor, (0, index, 0, offset), size)[0, 0]
        term = contract_last(piece, columns)
        total = term if total is None else total + term
    return total


def swap(value, axis, distance, block):
    count = lax.axis_size(axis)
    outer = count // block
    if outer & (outer - 1):
        pairs = [(i, (i // block + distance) % outer * block + i % block) for i in range(count)]
    else:
        pairs = [(i, (i // block ^ distance) * block + i % block) for i in range(count)]
    return lax.ppermute(value, axis, pairs)


VMEM = pl.BlockSpec(memory_space=pltpu.VMEM)
SMEM = pl.BlockSpec(memory_space=pltpu.SMEM)
ANY = pl.BlockSpec(memory_space=pl.ANY)


def local_kernel(body, outs, operands, specs=None, flops=0, scratch=(), limit=None):
    size = sum(o.size * o.dtype.itemsize for o in list(outs) + list(operands))
    return pl.pallas_call(
        body,
        out_shape=list(outs),
        in_specs=specs or [VMEM] * len(operands),
        out_specs=[VMEM] * len(outs),
        scratch_shapes=list(scratch),
        cost_estimate=pl.CostEstimate(flops=flops, bytes_accessed=size, transcendentals=0),
        compiler_params=pltpu.CompilerParams(vmem_limit_bytes=limit or 2 * size + 2**21),
    )(*operands)


def float_array(*shape):
    return jax.ShapeDtypeStruct(shape, jnp.float32)


def high_low(value):
    top = value.astype(jnp.bfloat16)
    return top, (value - top.astype(jnp.float32)).astype(jnp.bfloat16)


def split_product(left, top, rest):
    def dot(x, y):
        return lax.dot_general(
            x, y, (((1,), (1,)), ((), ())), preferred_element_type=jnp.float32
        )

    count = left.shape[0]
    left_top, left_rest = high_low(left)
    both = dot(jnp.concatenate([left_top, left_rest], axis=0), top)
    return both[:count] + (dot(left_top, rest) + both[count:])


def leaf_shape():
    groups = lax.axis_size("leaf")
    inner = 2 if groups % 2 == 0 else 1
    return groups // inner, inner


def select_terms(sources_ref, gathered, tile_refs, store):
    for m in range(tile_refs.shape[0]):
        chosen = gathered[0][...]
        for index in range(1, len(gathered)):
            chosen = jnp.where(sources_ref[0, 0, m] == index, gathered[index][...], chosen)
        top, rest = high_low(tile_refs[m])
        store(m, split_product(chosen, top, rest))


def tile_terms(gathered, tiles, sources):
    slots, tile_rows, order = tiles.shape
    depth = gathered[0].shape[0]
    count = len(gathered)

    def body(*refs):
        out = refs[-1]

        def store(m, term):
            out[:, m * tile_rows : (m + 1) * tile_rows] = term

        select_terms(refs[count + 1], refs[:count], refs[count], store)

    return local_kernel(
        body,
        [float_array(depth, slots * tile_rows)],
        [*gathered, tiles, sources],
        [VMEM] * (count + 1) + [SMEM],
        flops=6 * depth * slots * tile_rows * order,
    )[0]


def pack_terms(done, gathered, tiles, sources, blocks, live):
    outer, inner = leaf_shape()
    slots, tile_rows, order = tiles.shape
    depth = gathered[0].shape[0]
    streams = len(done) + 1
    part = depth * streams // (outer * inner)
    width = (slots + 1) * tile_rows
    count = len(gathered)
    base = len(done)

    def body(*refs):
        source_ref, block_ref, live_ref = refs[base + count + 1 : base + count + 4]
        outs = refs[base + count + 4 : -1]
        terms = refs[-1]
        lanes = lax.broadcasted_iota(jnp.int32, (streams * depth, tile_rows), 1)
        tag = jnp.full((streams * depth, tile_rows), -1.0, jnp.float32)
        for m in range(slots):
            value = jnp.where(m < live_ref[0, 0], block_ref[0, 0, m], -1).astype(jnp.float32)
            tag = jnp.where(lanes == m, value, tag)
        terms[:, slots * tile_rows :] = tag
        for i in range(base):
            terms[i * depth : (i + 1) * depth, : slots * tile_rows] = refs[i][...]

        def store(m, term):
            terms[base * depth :, m * tile_rows : (m + 1) * tile_rows] = term

        select_terms(source_ref, refs[base : base + count], refs[base + count], store)
        inside = lax.rem(lax.axis_index("leaf"), inner)
        for o in range(outer):
            cut = [
                terms[(o * inner + i) * part : (o * inner + i + 1) * part, :]
                for i in range(inner)
            ]
            for i in range(inner):
                outs[i][o] = jnp.where(inside == 0, cut[i], cut[inner - 1 - i])

    return local_kernel(
        body,
        [float_array(outer, part, width)] * inner,
        [*done, *gathered, tiles, sources, blocks, live],
        [VMEM] * (base + count + 1) + [SMEM] * 3,
        flops=6 * depth * slots * tile_rows * order,
        scratch=[pltpu.VMEM((streams * depth, width), jnp.float32)],
    )


def turn(rhs, first, last, streams, after):
    rows, count = rhs.shape[2:]
    depth = count // streams

    def body(rhs_ref, after_ref, out, held, sem):
        copy = pltpu.make_async_copy(rhs_ref.at[0, first:last], held, sem)
        copy.start()
        copy.wait()
        for index in range(last - first):
            wide = jnp.transpose(held[index])
            for i in range(streams):
                out[index * streams + i] = wide[i * depth : (i + 1) * depth]

    return local_kernel(
        body,
        [float_array(streams * (last - first), depth, rows)],
        [rhs, after],
        [ANY, ANY],
        scratch=[
            pltpu.VMEM((last - first, rows, count), jnp.float32),
            pltpu.SemaphoreType.DMA(()),
        ],
    )[0]


def turn_first(rhs, streams):
    rows, count = rhs.shape[2:]
    depth = count // streams

    def body(rhs_ref, *refs):
        outs, (held, sem) = refs[:-2], refs[-2:]
        copy = pltpu.make_async_copy(rhs_ref.at[0, 0], held, sem)
        copy.start()
        copy.wait()
        wide = jnp.transpose(held[...])
        for i in range(streams):
            outs[i][...] = wide[i * depth : (i + 1) * depth]

    return local_kernel(
        body,
        [float_array(depth, rows)] * streams,
        [rhs],
        [ANY],
        scratch=[pltpu.VMEM((rows, count), jnp.float32), pltpu.SemaphoreType.DMA(())],
    )


def turn_back(solved, after):
    flat = [value for streams in solved for value in streams]
    streams = len(solved[0])
    depth, rows = flat[0].shape

    def body(*refs):
        out, tie = refs[-2:]
        for index in range(len(solved)):
            wide = jnp.concatenate(
                [refs[index * streams + i][...] for i in range(streams)], axis=0
            )
            out[0, index] = jnp.transpose(wide)
        tie[...] = jnp.zeros(tie.shape, jnp.float32)

    return local_kernel(
        body,
        [float_array(1, len(solved), rows, depth * streams), float_array(8, 128)],
        [*flat, after],
        [VMEM] * len(flat) + [ANY],
    )


def leaf_exchange(packed):
    outer, inner = leaf_shape()
    part, width = packed[0].shape[1:]
    held = [packed[0]]
    if inner == 2:
        pairs = [(i, i ^ 1) for i in range(outer * inner)]
        held.append(lax.ppermute(packed[1], "leaf", pairs))

    def body(*refs):
        outside = lax.div(lax.axis_index("leaf"), inner)
        for distance in range(outer):
            target = partner(outside, -distance, outer) if distance else outside
            for i in range(inner):
                refs[inner + distance][i] = refs[i][target]

    portions = local_kernel(body, [float_array(inner, part, width)] * outer, held)
    return [portions[0]] + [
        swap(portions[distance], "leaf", distance, inner) for distance in range(outer - 1, 0, -1)
    ]


def share_out(received, rhs_turned, order, slots, tile_rows, after):
    members = lax.axis_size("grp")
    ancestors, part, rows = rhs_turned.shape
    inner = received[0].shape[0]
    block_count = ancestors * order // tile_rows
    width = (ancestors - 1) * rows

    def body(*refs):
        sources = refs[: len(received)]
        rhs_ref = refs[len(received)]
        outs = refs[len(received) + 2 : -1]
        share = refs[-1]
        me = lax.axis_index("grp")
        totals = [jnp.zeros((part, tile_rows), jnp.float32) for _ in range(block_count)]
        for source in sources:
            for i in range(inner):
                for m in range(slots):
                    tile = source[i, :, m * tile_rows : (m + 1) * tile_rows]
                    tag = source[i, :, slots * tile_rows + m : slots * tile_rows + m + 1]
                    tag = jnp.broadcast_to(tag, tile.shape)
                    for q in range(block_count):
                        totals[q] = totals[q] + jnp.where(tag == float(q), tile, 0.0)
        for q in range(block_count):
            share[:, q * tile_rows : (q + 1) * tile_rows] = -totals[q]
        for a in range(ancestors):
            for j in range(members):
                at = slice(a * order + j * rows, a * order + (j + 1) * rows)
                share[:, at] = share[:, at] + jnp.where(me == j, rhs_ref[a], 0.0)
        outs[0][...] = share[:, :order]
        for distance in range(members):
            target = partner(me, -distance, members) if distance else me
            out = outs[1 + distance]
            for a in range(1, ancestors):
                value = jnp.zeros((part, rows), jnp.float32)
                for j in range(members):
                    at = slice(a * order + j * rows, a * order + (j + 1) * rows)
                    value = jnp.where(target == j, share[:, at], value)
                out[:, (a - 1) * rows : a * rows] = value

    return local_kernel(
        body,
        [float_array(part, order)] + [float_array(part, width)] * members,
        [*received, rhs_turned, after],
        [VMEM] * (len(received) + 1) + [ANY],
        scratch=[pltpu.VMEM((part, ancestors * order), jnp.float32)],
    )


def split_factors(factors, after):
    count = len(factors)

    def body(*refs):
        for i in range(count):
            top, rest = high_low(refs[i][...])
            refs[count + 1 + 2 * i][...] = top
            refs[count + 2 + 2 * i][...] = rest

    outs = []
    for factor in factors:
        outs += [jax.ShapeDtypeStruct(factor.shape, jnp.bfloat16)] * 2
    return local_kernel(
        body,
        outs,
        [*factors, after],
        [VMEM] * count + [ANY],
        flops=4 * sum(f.size for f in factors),
    )


def solve_first(shares, others, top, rest):
    members = len(others)
    part, width = others[0].shape
    rows, order = top.shape[1:]

    def body(*refs):
        total = refs[0][...]
        for ref in refs[1:members]:
            total = total + ref[...]
        other_refs = refs[members : 2 * members]
        top_ref, rest_ref, out = refs[2 * members : 2 * members + 3]
        value = split_product(total, top_ref[0], rest_ref[0])
        out[...] = value
        for distance in range(1, members):
            message = refs[2 * members + 2 + distance]
            message[:, :rows] = value
            message[:, rows:] = other_refs[distance][...]

    return local_kernel(
        body,
        [float_array(part, rows)] + [float_array(part, rows + width)] * (members - 1),
        [*shares, *others, top, rest],
        flops=6 * part * rows * order,
    )


def take_messages(own, other, messages, top, rest):
    members = len(messages) + 1
    part, width = other.shape
    rows, order = top.shape[1:]

    def body(*refs):
        own_ref, other_ref = refs[:2]
        held = refs[2 : members + 1]
        top_ref, rest_ref, out = refs[members + 1 : members + 4]
        whole = refs[-1]
        total = other_ref[...]
        for ref in held:
            total = total + ref[:, rows:]
        if width > rows:
            refs[members + 4][...] = total
        pieces = [ref[:, :rows] for ref in held[-1:] + held[:-1]]
        put_in_order([own_ref[...]] + pieces, whole)
        out[...] = total[:, :rows] - split_product(whole[...], top_ref[0], rest_ref[0])

    return local_kernel(
        body,
        [float_array(part, rows)] + [float_array(part, width)] * (width > rows),
        [own, other, *messages, top, rest],
        flops=6 * part * rows * order,
        scratch=[pltpu.VMEM((part, order), jnp.float32)],
    )


def put_in_order(held, whole):
    me = lax.axis_index("grp")
    members = len(held)
    width = held[0].shape[1]
    for j in range(members):
        value = jnp.zeros(held[0].shape, jnp.float32)
        for distance in range(members):
            owner = partner(me, distance, members) if distance else me
            value = jnp.where(owner == j, held[distance], value)
        whole[:, j * width : (j + 1) * width] = value


def apply_split(pieces, top, rest, index, base=None, begin=0, others=None, far_first=True):
    members = lax.axis_size("grp")
    part, width = pieces[0].shape
    rows, order = top.shape[1:]
    extra = list(others or []) if base is None else [base]

    def body(*refs):
        top_ref, rest_ref = refs[members : members + 2]
        out, whole = refs[-2:]
        held = [refs[d][...] for d in range(members)]
        if far_first:
            held = held[:1] + held[-1:] + held[1:-1] if members > 2 else held
        put_in_order(held, whole)
        result = split_product(whole[...], top_ref[index], rest_ref[index])
        if others is not None:
            for i in range(len(others)):
                out[i] = refs[members + 2 + i][...]
            out[len(others)] = result
            return
        if base is not None:
            result = refs[members + 2][:, begin : begin + rows] - result
        out[...] = result

    shape = (part, rows) if others is None else (len(others) + 1, part, rows)
    return local_kernel(
        body,
        [float_array(*shape)],
        [*pieces, top, rest, *extra],
        flops=6 * part * rows * order,
        scratch=[pltpu.VMEM((part, order), jnp.float32)],
    )[0]


def on_device(
    rhs_local,
    diag_inv_local,
    sub_local,
    tiles,
    tile_block,
    tile_source,
    tile_count,
    rhs_anc,
    diag_inv_anc,
    sub_anc,
):
    supernodes, _, order = diag_inv_local.shape[1:]
    rhs_count = rhs_local.shape[-1]
    members = lax.axis_size("grp")
    rows = order // members
    slots, tile_rows = tiles.shape[2:4]

    streams = 2 if rhs_count % 16 == 0 else 1
    residuals = turn_first(rhs_local, streams)
    first = diag_inv_local[0, 0]
    rounded = lax.reduce_precision(first, 8, 7)
    first_top = rounded.astype(jnp.bfloat16)[None]
    first_rest = (first - rounded).astype(jnp.bfloat16)[None]
    solved = [[None] * streams for _ in range(supernodes)]
    gathered = [[None] * streams for _ in range(supernodes)]
    values = list(residuals)
    last = None
    for step in range(2 * supernodes):
        current = step // 2
        for i in range(streams):
            turn_taken = step > 0 and last is not None
            ties = [(1, last[0][2][1])] if step * streams + i > streams else []
            pieces = gather_rows(values[i], ties, step == 0)
            if step == 1 and i == 0:
                later = turn(rhs_local, 1, supernodes, streams, pieces[1][1])
            if turn_taken:
                offset, piece = pieces[2]
                pieces[2] = (offset, lax.optimization_barrier((piece, last[1]))[0])
            if step == 0:
                far_first, pieces = pieces, pieces[:1] + pieces[-1:] + pieces[1:-1]
                owned = apply_split(
                    [p for _, p in far_first],
                    first_top,
                    first_rest,
                    0,
                )
            else:
                whole = assemble(pieces, order)
                if step % 2 == 0:
                    owned = contract_last(whole, diag_inv_local[0, current])
                elif current + 1 < supernodes:
                    owned = later[current * streams + i] - contract_last(whole, sub_local[0, current])
            if step % 2 == 0:
                solved[current][i] = owned
            else:
                gathered[current][i] = whole
            values[i] = owned
            last = (pieces, owned)

    by_stream = [[values[i] for values in gathered] for i in range(streams)]
    done = [tile_terms(values, tiles[0, 0], tile_source) for values in by_stream[:-1]]
    packed = pack_terms(done, by_stream[-1], tiles[0, 0], tile_source, tile_block, tile_count)
    received = leaf_exchange(packed)
    solution_local, tie = turn_back(solved, packed[0])
    shares = share_out(
        received, jnp.swapaxes(rhs_anc, 1, 2), order, slots, tile_rows, tie
    )
    far_first = list(range(2, members)) + list(range(1, min(members, 2)))
    first_share, others = shares[0], shares[1:]
    sums = [first_share] + [send(first_share, "grp", d) for d in far_first]
    inverse_top, inverse_rest, below_top, below_rest = split_factors(
        [diag_inv_anc, sub_anc], first_share
    )
    solution, *messages = solve_first(sums, others, inverse_top, inverse_rest)
    solutions = [solution]
    ancestors = rhs_anc.shape[0]
    for ancestor in range(1, ancestors):
        if ancestor == 1:
            arrived = [send(messages[d - 1], "grp", d) for d in far_first]
            residual, *left = take_messages(solution, others[0], arrived, below_top, below_rest)
        else:
            pieces = gather_far_first(solutions[-1])
            residual = apply_split(
                pieces, below_top, below_rest, ancestor - 1, left[0], (ancestor - 1) * rows
            )
        pieces = gather_far_first(residual)
        behind = solutions if ancestor + 1 == ancestors else None
        solved_now = apply_split(pieces, inverse_top, inverse_rest, ancestor, others=behind)
        solutions.append(solved_now)
    solutions = solutions[-1] if ancestors > 1 else solutions[0][None]
    solutions = jnp.swapaxes(solutions, 1, 2)
    return (solution_local, solutions)


def solution(mesh):
    return jax.shard_map(
        on_device,
        mesh=mesh,
        in_specs=(
            P("leaf", None, "grp", None),
            P("leaf", None, "grp", None),
            P("leaf", None, "grp", None),
            P("leaf", "grp", None, None, None),
            P("leaf", "grp", None),
            P("leaf", "grp", None),
            P("leaf", "grp"),
            P(None, "grp", "leaf"),
            P(None, "grp", None),
            P(None, "grp", None),
        ),
        out_specs=(P("leaf", None, "grp", None), P(None, "grp", "leaf")),
        check_vma=False,
    )
```

```python
import jax
import jax.numpy as jnp
from jax import lax
from jax.experimental import pallas as pl
from jax.experimental.pallas import tpu as pltpu
from jax.sharding import PartitionSpec as P

high = lax.Precision.HIGH


def contract_last(left, right):
    return lax.dot_general(
        left,
        right,
        (((left.ndim - 1,), (right.ndim - 1,)), ((), ())),
        precision=high,
        preferred_element_type=jnp.float32,
    )


def partner(index, distance, count):
    if count & (count - 1):
        return lax.rem(index - distance + 2 * count, count)
    return index ^ abs(distance)


def send(value, axis, distance):
    count = lax.axis_size(axis)
    if count & (count - 1):
        pairs = [(i, (i + distance) % count) for i in range(count)]
    else:
        pairs = [(i, i ^ distance) for i in range(count)]
    return lax.ppermute(value, axis, pairs)


def gather_rows(value, ties=(), far_first=False):
    members = lax.axis_size("grp")
    me = lax.axis_index("grp")
    rows = value.shape[1]
    pieces = [(me * rows, value)]
    distances = list(range(1, members))
    if far_first:
        distances = distances[1:] + distances[:1]
    for distance in distances:
        owner = partner(me, distance, members)
        tied = value
        if distance in dict(ties):
            tied = lax.optimization_barrier((value, dict(ties)[distance]))[0]
        pieces.append((owner * rows, send(tied, "grp", distance)))
    return pieces


def gather_far_first(value):
    return [piece for _, piece in gather_rows(value, far_first=True)]


def assemble(pieces, order):
    whole = jnp.zeros((pieces[0][1].shape[0], order), jnp.float32)
    for offset, piece in pieces:
        whole = lax.dynamic_update_slice_in_dim(whole, piece, offset, 1)
    return whole


def apply_pieces(factor, index, pieces):
    total = None
    for offset, piece in pieces:
        size = (1, 1, factor.shape[2], piece.shape[1])
        columns = lax.dynamic_slice(factor, (0, index, 0, offset), size)[0, 0]
        term = contract_last(piece, columns)
        total = term if total is None else total + term
    return total


def swap(value, axis, distance, block):
    count = lax.axis_size(axis)
    outer = count // block
    if outer & (outer - 1):
        pairs = [(i, (i // block + distance) % outer * block + i % block) for i in range(count)]
    else:
        pairs = [(i, (i // block ^ distance) * block + i % block) for i in range(count)]
    return lax.ppermute(value, axis, pairs)


VMEM = pl.BlockSpec(memory_space=pltpu.VMEM)
SMEM = pl.BlockSpec(memory_space=pltpu.SMEM)
ANY = pl.BlockSpec(memory_space=pl.ANY)


def local_kernel(body, outs, operands, specs=None, flops=0, scratch=(), limit=None):
    size = sum(o.size * o.dtype.itemsize for o in list(outs) + list(operands))
    return pl.pallas_call(
        body,
        out_shape=list(outs),
        in_specs=specs or [VMEM] * len(operands),
        out_specs=[VMEM] * len(outs),
        scratch_shapes=list(scratch),
        cost_estimate=pl.CostEstimate(flops=flops, bytes_accessed=size, transcendentals=0),
        compiler_params=pltpu.CompilerParams(vmem_limit_bytes=limit or 2 * size + 2**21),
    )(*operands)


def float_array(*shape):
    return jax.ShapeDtypeStruct(shape, jnp.float32)


def high_low(value):
    top = value.astype(jnp.bfloat16)
    return top, (value - top.astype(jnp.float32)).astype(jnp.bfloat16)


def split_product(left, top, rest):
    def dot(x, y):
        return lax.dot_general(
            x, y, (((1,), (1,)), ((), ())), preferred_element_type=jnp.float32
        )

    count = left.shape[0]
    left_top, left_rest = high_low(left)
    both = dot(jnp.concatenate([left_top, left_rest], axis=0), top)
    return both[:count] + (dot(left_top, rest) + both[count:])


def leaf_shape():
    groups = lax.axis_size("leaf")
    inner = 2 if groups % 2 == 0 else 1
    return groups // inner, inner


def select_terms(sources_ref, gathered, tile_refs, store):
    for m in range(tile_refs.shape[0]):
        chosen = gathered[0][...]
        for index in range(1, len(gathered)):
            chosen = jnp.where(sources_ref[0, 0, m] == index, gathered[index][...], chosen)
        top, rest = high_low(tile_refs[m])
        store(m, split_product(chosen, top, rest))


def tile_terms(gathered, tiles, sources):
    slots, tile_rows, order = tiles.shape
    depth = gathered[0].shape[0]
    count = len(gathered)

    def body(*refs):
        out = refs[-1]

        def store(m, term):
            out[:, m * tile_rows : (m + 1) * tile_rows] = term

        select_terms(refs[count + 1], refs[:count], refs[count], store)

    return local_kernel(
        body,
        [float_array(depth, slots * tile_rows)],
        [*gathered, tiles, sources],
        [VMEM] * (count + 1) + [SMEM],
        flops=6 * depth * slots * tile_rows * order,
    )[0]


def pack_terms(done, gathered, tiles, sources, blocks, live):
    outer, inner = leaf_shape()
    slots, tile_rows, order = tiles.shape
    depth = gathered[0].shape[0]
    streams = len(done) + 1
    part = depth * streams // (outer * inner)
    width = (slots + 1) * tile_rows
    count = len(gathered)
    base = len(done)

    def body(*refs):
        source_ref, block_ref, live_ref = refs[base + count + 1 : base + count + 4]
        outs = refs[base + count + 4 : -1]
        terms = refs[-1]
        lanes = lax.broadcasted_iota(jnp.int32, (streams * depth, tile_rows), 1)
        tag = jnp.full((streams * depth, tile_rows), -1.0, jnp.float32)
        for m in range(slots):
            value = jnp.where(m < live_ref[0, 0], block_ref[0, 0, m], -1).astype(jnp.float32)
            tag = jnp.where(lanes == m, value, tag)
        terms[:, slots * tile_rows :] = tag
        for i in range(base):
            terms[i * depth : (i + 1) * depth, : slots * tile_rows] = refs[i][...]

        def store(m, term):
            terms[base * depth :, m * tile_rows : (m + 1) * tile_rows] = term

        select_terms(source_ref, refs[base : base + count], refs[base + count], store)
        inside = lax.rem(lax.axis_index("leaf"), inner)
        for o in range(outer):
            cut = [
                terms[(o * inner + i) * part : (o * inner + i + 1) * part, :]
                for i in range(inner)
            ]
            for i in range(inner):
                outs[i][o] = jnp.where(inside == 0, cut[i], cut[inner - 1 - i])

    return local_kernel(
        body,
        [float_array(outer, part, width)] * inner,
        [*done, *gathered, tiles, sources, blocks, live],
        [VMEM] * (base + count + 1) + [SMEM] * 3,
        flops=6 * depth * slots * tile_rows * order,
        scratch=[pltpu.VMEM((streams * depth, width), jnp.float32)],
    )


def turn(rhs, first, last, streams, after):
    rows, count = rhs.shape[2:]
    depth = count // streams

    def body(rhs_ref, after_ref, out, held, sem):
        copy = pltpu.make_async_copy(rhs_ref.at[0, first:last], held, sem)
        copy.start()
        copy.wait()
        for index in range(last - first):
            wide = jnp.transpose(held[index])
            for i in range(streams):
                out[index * streams + i] = wide[i * depth : (i + 1) * depth]

    return local_kernel(
        body,
        [float_array(streams * (last - first), depth, rows)],
        [rhs, after],
        [ANY, ANY],
        scratch=[
            pltpu.VMEM((last - first, rows, count), jnp.float32),
            pltpu.SemaphoreType.DMA(()),
        ],
    )[0]


def turn_first(rhs, streams):
    rows, count = rhs.shape[2:]
    depth = count // streams

    def body(rhs_ref, *refs):
        outs, (held, sem) = refs[:-2], refs[-2:]
        copy = pltpu.make_async_copy(rhs_ref.at[0, 0], held, sem)
        copy.start()
        copy.wait()
        wide = jnp.transpose(held[...])
        for i in range(streams):
            outs[i][...] = wide[i * depth : (i + 1) * depth]

    return local_kernel(
        body,
        [float_array(depth, rows)] * streams,
        [rhs],
        [ANY],
        scratch=[pltpu.VMEM((rows, count), jnp.float32), pltpu.SemaphoreType.DMA(())],
    )


def turn_back(solved, after):
    flat = [value for streams in solved for value in streams]
    streams = len(solved[0])
    depth, rows = flat[0].shape

    def body(*refs):
        out, tie = refs[-2:]
        for index in range(len(solved)):
            wide = jnp.concatenate(
                [refs[index * streams + i][...] for i in range(streams)], axis=0
            )
            out[0, index] = jnp.transpose(wide)
        tie[...] = jnp.zeros(tie.shape, jnp.float32)

    return local_kernel(
        body,
        [float_array(1, len(solved), rows, depth * streams), float_array(8, 128)],
        [*flat, after],
        [VMEM] * len(flat) + [ANY],
    )


def leaf_exchange(packed):
    outer, inner = leaf_shape()
    part, width = packed[0].shape[1:]
    held = [packed[0]]
    if inner == 2:
        pairs = [(i, i ^ 1) for i in range(outer * inner)]
        held.append(lax.ppermute(packed[1], "leaf", pairs))

    def body(*refs):
        outside = lax.div(lax.axis_index("leaf"), inner)
        for distance in range(outer):
            target = partner(outside, -distance, outer) if distance else outside
            for i in range(inner):
                refs[inner + distance][i] = refs[i][target]

    portions = local_kernel(body, [float_array(inner, part, width)] * outer, held)
    return [portions[0]] + [
        swap(portions[distance], "leaf", distance, inner) for distance in range(outer - 1, 0, -1)
    ]


def share_out(received, rhs_turned, order, slots, tile_rows, after):
    members = lax.axis_size("grp")
    ancestors, part, rows = rhs_turned.shape
    inner = received[0].shape[0]
    block_count = ancestors * order // tile_rows
    width = (ancestors - 1) * rows

    def body(*refs):
        sources = refs[: len(received)]
        rhs_ref = refs[len(received)]
        outs = refs[len(received) + 2 : -1]
        share = refs[-1]
        me = lax.axis_index("grp")
        totals = [jnp.zeros((part, tile_rows), jnp.float32) for _ in range(block_count)]
        for source in sources:
            for i in range(inner):
                for m in range(slots):
                    tile = source[i, :, m * tile_rows : (m + 1) * tile_rows]
                    tag = source[i, :, slots * tile_rows + m : slots * tile_rows + m + 1]
                    tag = jnp.broadcast_to(tag, tile.shape)
                    for q in range(block_count):
                        totals[q] = totals[q] + jnp.where(tag == float(q), tile, 0.0)
        for q in range(block_count):
            share[:, q * tile_rows : (q + 1) * tile_rows] = -totals[q]
        for a in range(ancestors):
            for j in range(members):
                at = slice(a * order + j * rows, a * order + (j + 1) * rows)
                share[:, at] = share[:, at] + jnp.where(me == j, rhs_ref[a], 0.0)
        outs[0][...] = share[:, :order]
        for distance in range(members):
            target = partner(me, -distance, members) if distance else me
            out = outs[1 + distance]
            for a in range(1, ancestors):
                value = jnp.zeros((part, rows), jnp.float32)
                for j in range(members):
                    at = slice(a * order + j * rows, a * order + (j + 1) * rows)
                    value = jnp.where(target == j, share[:, at], value)
                out[:, (a - 1) * rows : a * rows] = value

    return local_kernel(
        body,
        [float_array(part, order)] + [float_array(part, width)] * members,
        [*received, rhs_turned, after],
        [VMEM] * (len(received) + 1) + [ANY],
        scratch=[pltpu.VMEM((part, ancestors * order), jnp.float32)],
    )


def split_factors(factors, after):
    count = len(factors)

    def body(*refs):
        for i in range(count):
            top, rest = high_low(refs[i][...])
            refs[count + 1 + 2 * i][...] = top
            refs[count + 2 + 2 * i][...] = rest

    outs = []
    for factor in factors:
        outs += [jax.ShapeDtypeStruct(factor.shape, jnp.bfloat16)] * 2
    return local_kernel(
        body,
        outs,
        [*factors, after],
        [VMEM] * count + [ANY],
        flops=4 * sum(f.size for f in factors),
    )


def solve_first(shares, others, top, rest):
    members = len(others)
    part, width = others[0].shape
    rows, order = top.shape[1:]

    def body(*refs):
        total = refs[0][...]
        for ref in refs[1:members]:
            total = total + ref[...]
        other_refs = refs[members : 2 * members]
        top_ref, rest_ref, out = refs[2 * members : 2 * members + 3]
        value = split_product(total, top_ref[0], rest_ref[0])
        out[...] = value
        for distance in range(1, members):
            message = refs[2 * members + 2 + distance]
            message[:, :rows] = value
            message[:, rows:] = other_refs[distance][...]

    return local_kernel(
        body,
        [float_array(part, rows)] + [float_array(part, rows + width)] * (members - 1),
        [*shares, *others, top, rest],
        flops=6 * part * rows * order,
    )


def take_messages(own, other, messages, top, rest):
    members = len(messages) + 1
    part, width = other.shape
    rows, order = top.shape[1:]

    def body(*refs):
        own_ref, other_ref = refs[:2]
        held = refs[2 : members + 1]
        top_ref, rest_ref, out = refs[members + 1 : members + 4]
        whole = refs[-1]
        total = other_ref[...]
        for ref in held:
            total = total + ref[:, rows:]
        if width > rows:
            refs[members + 4][...] = total
        pieces = [ref[:, :rows] for ref in held[-1:] + held[:-1]]
        put_in_order([own_ref[...]] + pieces, whole)
        out[...] = total[:, :rows] - split_product(whole[...], top_ref[0], rest_ref[0])

    return local_kernel(
        body,
        [float_array(part, rows)] + [float_array(part, width)] * (width > rows),
        [own, other, *messages, top, rest],
        flops=6 * part * rows * order,
        scratch=[pltpu.VMEM((part, order), jnp.float32)],
    )


def put_in_order(held, whole):
    me = lax.axis_index("grp")
    members = len(held)
    width = held[0].shape[1]
    for j in range(members):
        value = jnp.zeros(held[0].shape, jnp.float32)
        for distance in range(members):
            owner = partner(me, distance, members) if distance else me
            value = jnp.where(owner == j, held[distance], value)
        whole[:, j * width : (j + 1) * width] = value


def apply_split(pieces, top, rest, index, base=None, begin=0, others=None, far_first=True):
    members = lax.axis_size("grp")
    part, width = pieces[0].shape
    rows, order = top.shape[1:]
    extra = list(others or []) if base is None else [base]

    def body(*refs):
        top_ref, rest_ref = refs[members : members + 2]
        out, whole = refs[-2:]
        held = [refs[d][...] for d in range(members)]
        if far_first:
            held = held[:1] + held[-1:] + held[1:-1] if members > 2 else held
        put_in_order(held, whole)
        result = split_product(whole[...], top_ref[index], rest_ref[index])
        if others is not None:
            for i in range(len(others)):
                out[i] = refs[members + 2 + i][...]
            out[len(others)] = result
            return
        if base is not None:
            result = refs[members + 2][:, begin : begin + rows] - result
        out[...] = result

    shape = (part, rows) if others is None else (len(others) + 1, part, rows)
    return local_kernel(
        body,
        [float_array(*shape)],
        [*pieces, top, rest, *extra],
        flops=6 * part * rows * order,
        scratch=[pltpu.VMEM((part, order), jnp.float32)],
    )[0]


def on_device(
    rhs_local,
    diag_inv_local,
    sub_local,
    tiles,
    tile_block,
    tile_source,
    tile_count,
    rhs_anc,
    diag_inv_anc,
    sub_anc,
):
    supernodes, _, order = diag_inv_local.shape[1:]
    rhs_count = rhs_local.shape[-1]
    members = lax.axis_size("grp")
    rows = order // members
    slots, tile_rows = tiles.shape[2:4]

    streams = 2 if rhs_count % 16 == 0 else 1
    residuals = turn_first(rhs_local, streams)
    first = diag_inv_local[0, 0]
    rounded = lax.reduce_precision(first, 8, 7)
    first_top = rounded.astype(jnp.bfloat16)[None]
    first_rest = (first - rounded).astype(jnp.bfloat16)[None]
    solved = [[None] * streams for _ in range(supernodes)]
    gathered = [[None] * streams for _ in range(supernodes)]
    values = list(residuals)
    last = None
    for step in range(2 * supernodes):
        current = step // 2
        for i in range(streams):
            turn_taken = step > 0 and last is not None
            ties = [(1, last[0][2][1])] if step * streams + i > streams else []
            early = step == 1 and i == 0
            pieces = gather_rows(values[i], ties, early)
            if step == 1 and i == 0:
                later = turn(rhs_local, 1, supernodes, streams, pieces[1][1])
            if turn_taken:
                offset, piece = pieces[2]
                pieces[2] = (offset, lax.optimization_barrier((piece, last[1]))[0])
            if step == 0:
                owned = apply_split(
                    [p for _, p in pieces],
                    first_top,
                    first_rest,
                    0,
                    far_first=False,
                )
            else:
                whole = assemble(pieces, order)
                if step % 2 == 0:
                    owned = contract_last(whole, diag_inv_local[0, current])
                elif current + 1 < supernodes:
                    owned = later[current * streams + i] - contract_last(whole, sub_local[0, current])
            if step % 2 == 0:
                solved[current][i] = owned
            else:
                gathered[current][i] = whole
            values[i] = owned
            last = (pieces, owned)

    by_stream = [[values[i] for values in gathered] for i in range(streams)]
    done = [tile_terms(values, tiles[0, 0], tile_source) for values in by_stream[:-1]]
    packed = pack_terms(done, by_stream[-1], tiles[0, 0], tile_source, tile_block, tile_count)
    received = leaf_exchange(packed)
    solution_local, tie = turn_back(solved, packed[0])
    shares = share_out(
        received, jnp.swapaxes(rhs_anc, 1, 2), order, slots, tile_rows, tie
    )
    far_first = list(range(2, members)) + list(range(1, min(members, 2)))
    first_share, others = shares[0], shares[1:]
    sums = [first_share] + [send(first_share, "grp", d) for d in far_first]
    inverse_top, inverse_rest, below_top, below_rest = split_factors(
        [diag_inv_anc, sub_anc], first_share
    )
    solution, *messages = solve_first(sums, others, inverse_top, inverse_rest)
    solutions = [solution]
    ancestors = rhs_anc.shape[0]
    for ancestor in range(1, ancestors):
        if ancestor == 1:
            arrived = [send(messages[d - 1], "grp", d) for d in far_first]
            residual, *left = take_messages(solution, others[0], arrived, below_top, below_rest)
        else:
            pieces = gather_far_first(solutions[-1])
            residual = apply_split(
                pieces, below_top, below_rest, ancestor - 1, left[0], (ancestor - 1) * rows
            )
        pieces = gather_far_first(residual)
        behind = solutions if ancestor + 1 == ancestors else None
        solved_now = apply_split(pieces, inverse_top, inverse_rest, ancestor, others=behind)
        solutions.append(solved_now)
    solutions = solutions[-1] if ancestors > 1 else solutions[0][None]
    solutions = jnp.swapaxes(solutions, 1, 2)
    return (solution_local, solutions)


def solution(mesh):
    return jax.shard_map(
        on_device,
        mesh=mesh,
        in_specs=(
            P("leaf", None, "grp", None),
            P("leaf", None, "grp", None),
            P("leaf", None, "grp", None),
            P("leaf", "grp", None, None, None),
            P("leaf", "grp", None),
            P("leaf", "grp", None),
            P("leaf", "grp"),
            P(None, "grp", "leaf"),
            P(None, "grp", None),
            P(None, "grp", None),
        ),
        out_specs=(P("leaf", None, "grp", None), P(None, "grp", "leaf")),
        check_vma=False,
    )
```

```python
import jax
import jax.numpy as jnp
from jax import lax
from jax.experimental import pallas as pl
from jax.experimental.pallas import tpu as pltpu
from jax.sharding import PartitionSpec as P

high = lax.Precision.HIGH


def contract_last(left, right):
    return lax.dot_general(
        left,
        right,
        (((left.ndim - 1,), (right.ndim - 1,)), ((), ())),
        precision=high,
        preferred_element_type=jnp.float32,
    )


def partner(index, distance, count):
    if count & (count - 1):
        return lax.rem(index - distance + 2 * count, count)
    return index ^ abs(distance)


def send(value, axis, distance):
    count = lax.axis_size(axis)
    if count & (count - 1):
        pairs = [(i, (i + distance) % count) for i in range(count)]
    else:
        pairs = [(i, i ^ distance) for i in range(count)]
    return lax.ppermute(value, axis, pairs)


def gather_rows(value, ties=(), far_first=False):
    members = lax.axis_size("grp")
    me = lax.axis_index("grp")
    rows = value.shape[1]
    pieces = [(me * rows, value)]
    distances = list(range(1, members))
    if far_first:
        distances = distances[::-1]
    for distance in distances:
        owner = partner(me, distance, members)
        tied = value
        if distance in dict(ties):
            tied = lax.optimization_barrier((value, dict(ties)[distance]))[0]
        pieces.append((owner * rows, send(tied, "grp", distance)))
    return pieces


def gather_far_first(value):
    return [piece for _, piece in gather_rows(value, far_first=True)]


def assemble(pieces, order):
    whole = jnp.zeros((pieces[0][1].shape[0], order), jnp.float32)
    for offset, piece in pieces:
        whole = lax.dynamic_update_slice_in_dim(whole, piece, offset, 1)
    return whole


def apply_pieces(factor, index, pieces):
    total = None
    for offset, piece in pieces:
        size = (1, 1, factor.shape[2], piece.shape[1])
        columns = lax.dynamic_slice(factor, (0, index, 0, offset), size)[0, 0]
        term = contract_last(piece, columns)
        total = term if total is None else total + term
    return total


def swap(value, axis, distance, block):
    count = lax.axis_size(axis)
    outer = count // block
    if outer & (outer - 1):
        pairs = [(i, (i // block + distance) % outer * block + i % block) for i in range(count)]
    else:
        pairs = [(i, (i // block ^ distance) * block + i % block) for i in range(count)]
    return lax.ppermute(value, axis, pairs)


VMEM = pl.BlockSpec(memory_space=pltpu.VMEM)
SMEM = pl.BlockSpec(memory_space=pltpu.SMEM)
ANY = pl.BlockSpec(memory_space=pl.ANY)


def local_kernel(body, outs, operands, specs=None, flops=0, scratch=(), limit=None):
    size = sum(o.size * o.dtype.itemsize for o in list(outs) + list(operands))
    return pl.pallas_call(
        body,
        out_shape=list(outs),
        in_specs=specs or [VMEM] * len(operands),
        out_specs=[VMEM] * len(outs),
        scratch_shapes=list(scratch),
        cost_estimate=pl.CostEstimate(flops=flops, bytes_accessed=size, transcendentals=0),
        compiler_params=pltpu.CompilerParams(vmem_limit_bytes=limit or 2 * size + 2**21),
    )(*operands)


def float_array(*shape):
    return jax.ShapeDtypeStruct(shape, jnp.float32)


def high_low(value):
    top = value.astype(jnp.bfloat16)
    return top, (value - top.astype(jnp.float32)).astype(jnp.bfloat16)


def split_product(left, top, rest):
    def dot(x, y):
        return lax.dot_general(
            x, y, (((1,), (1,)), ((), ())), preferred_element_type=jnp.float32
        )

    count = left.shape[0]
    left_top, left_rest = high_low(left)
    both = dot(jnp.concatenate([left_top, left_rest], axis=0), top)
    return both[:count] + (dot(left_top, rest) + both[count:])


def leaf_shape():
    groups = lax.axis_size("leaf")
    inner = 2 if groups % 2 == 0 else 1
    return groups // inner, inner


def select_terms(sources_ref, gathered, tile_refs, store):
    for m in range(tile_refs.shape[0]):
        chosen = gathered[0][...]
        for index in range(1, len(gathered)):
            chosen = jnp.where(sources_ref[0, 0, m] == index, gathered[index][...], chosen)
        top, rest = high_low(tile_refs[m])
        store(m, split_product(chosen, top, rest))


def tile_terms(gathered, tiles, sources):
    slots, tile_rows, order = tiles.shape
    depth = gathered[0].shape[0]
    count = len(gathered)

    def body(*refs):
        out = refs[-1]

        def store(m, term):
            out[:, m * tile_rows : (m + 1) * tile_rows] = term

        select_terms(refs[count + 1], refs[:count], refs[count], store)

    return local_kernel(
        body,
        [float_array(depth, slots * tile_rows)],
        [*gathered, tiles, sources],
        [VMEM] * (count + 1) + [SMEM],
        flops=6 * depth * slots * tile_rows * order,
    )[0]


def pack_terms(done, gathered, tiles, sources, blocks, live):
    outer, inner = leaf_shape()
    slots, tile_rows, order = tiles.shape
    depth = gathered[0].shape[0]
    streams = len(done) + 1
    part = depth * streams // (outer * inner)
    width = (slots + 1) * tile_rows
    count = len(gathered)
    base = len(done)

    def body(*refs):
        source_ref, block_ref, live_ref = refs[base + count + 1 : base + count + 4]
        outs = refs[base + count + 4 : -1]
        terms = refs[-1]
        lanes = lax.broadcasted_iota(jnp.int32, (streams * depth, tile_rows), 1)
        tag = jnp.full((streams * depth, tile_rows), -1.0, jnp.float32)
        for m in range(slots):
            value = jnp.where(m < live_ref[0, 0], block_ref[0, 0, m], -1).astype(jnp.float32)
            tag = jnp.where(lanes == m, value, tag)
        terms[:, slots * tile_rows :] = tag
        for i in range(base):
            terms[i * depth : (i + 1) * depth, : slots * tile_rows] = refs[i][...]

        def store(m, term):
            terms[base * depth :, m * tile_rows : (m + 1) * tile_rows] = term

        select_terms(source_ref, refs[base : base + count], refs[base + count], store)
        inside = lax.rem(lax.axis_index("leaf"), inner)
        for o in range(outer):
            cut = [
                terms[(o * inner + i) * part : (o * inner + i + 1) * part, :]
                for i in range(inner)
            ]
            for i in range(inner):
                outs[i][o] = jnp.where(inside == 0, cut[i], cut[inner - 1 - i])

    return local_kernel(
        body,
        [float_array(outer, part, width)] * inner,
        [*done, *gathered, tiles, sources, blocks, live],
        [VMEM] * (base + count + 1) + [SMEM] * 3,
        flops=6 * depth * slots * tile_rows * order,
        scratch=[pltpu.VMEM((streams * depth, width), jnp.float32)],
    )


def turn(rhs, first, last, streams, after):
    rows, count = rhs.shape[2:]
    depth = count // streams

    def body(rhs_ref, after_ref, out, held, sem):
        copy = pltpu.make_async_copy(rhs_ref.at[0, first:last], held, sem)
        copy.start()
        copy.wait()
        for index in range(last - first):
            wide = jnp.transpose(held[index])
            for i in range(streams):
                out[index * streams + i] = wide[i * depth : (i + 1) * depth]

    return local_kernel(
        body,
        [float_array(streams * (last - first), depth, rows)],
        [rhs, after],
        [ANY, ANY],
        scratch=[
            pltpu.VMEM((last - first, rows, count), jnp.float32),
            pltpu.SemaphoreType.DMA(()),
        ],
    )[0]


def turn_first(rhs, streams):
    rows, count = rhs.shape[2:]
    depth = count // streams

    def body(rhs_ref, *refs):
        outs, (held, sem) = refs[:-2], refs[-2:]
        copy = pltpu.make_async_copy(rhs_ref.at[0, 0], held, sem)
        copy.start()
        copy.wait()
        wide = jnp.transpose(held[...])
        for i in range(streams):
            outs[i][...] = wide[i * depth : (i + 1) * depth]

    return local_kernel(
        body,
        [float_array(depth, rows)] * streams,
        [rhs],
        [ANY],
        scratch=[pltpu.VMEM((rows, count), jnp.float32), pltpu.SemaphoreType.DMA(())],
    )


def turn_back(solved, after):
    flat = [value for streams in solved for value in streams]
    streams = len(solved[0])
    depth, rows = flat[0].shape

    def body(*refs):
        out, tie = refs[-2:]
        for index in range(len(solved)):
            wide = jnp.concatenate(
                [refs[index * streams + i][...] for i in range(streams)], axis=0
            )
            out[0, index] = jnp.transpose(wide)
        tie[...] = jnp.zeros(tie.shape, jnp.float32)

    return local_kernel(
        body,
        [float_array(1, len(solved), rows, depth * streams), float_array(8, 128)],
        [*flat, after],
        [VMEM] * len(flat) + [ANY],
    )


def leaf_exchange(packed):
    outer, inner = leaf_shape()
    part, width = packed[0].shape[1:]
    held = [packed[0]]
    if inner == 2:
        pairs = [(i, i ^ 1) for i in range(outer * inner)]
        held.append(lax.ppermute(packed[1], "leaf", pairs))

    def body(*refs):
        outside = lax.div(lax.axis_index("leaf"), inner)
        for distance in range(outer):
            target = partner(outside, -distance, outer) if distance else outside
            for i in range(inner):
                refs[inner + distance][i] = refs[i][target]

    portions = local_kernel(body, [float_array(inner, part, width)] * outer, held)
    return [portions[0]] + [
        swap(portions[distance], "leaf", distance, inner) for distance in range(outer - 1, 0, -1)
    ]


def share_out(received, rhs_turned, order, slots, tile_rows, after):
    members = lax.axis_size("grp")
    ancestors, part, rows = rhs_turned.shape
    inner = received[0].shape[0]
    block_count = ancestors * order // tile_rows
    width = (ancestors - 1) * rows

    def body(*refs):
        sources = refs[: len(received)]
        rhs_ref = refs[len(received)]
        outs = refs[len(received) + 2 : -1]
        share = refs[-1]
        me = lax.axis_index("grp")
        totals = [jnp.zeros((part, tile_rows), jnp.float32) for _ in range(block_count)]
        for source in sources:
            for i in range(inner):
                for m in range(slots):
                    tile = source[i, :, m * tile_rows : (m + 1) * tile_rows]
                    tag = source[i, :, slots * tile_rows + m : slots * tile_rows + m + 1]
                    tag = jnp.broadcast_to(tag, tile.shape)
                    for q in range(block_count):
                        totals[q] = totals[q] + jnp.where(tag == float(q), tile, 0.0)
        for q in range(block_count):
            share[:, q * tile_rows : (q + 1) * tile_rows] = -totals[q]
        for a in range(ancestors):
            for j in range(members):
                at = slice(a * order + j * rows, a * order + (j + 1) * rows)
                share[:, at] = share[:, at] + jnp.where(me == j, rhs_ref[a], 0.0)
        outs[0][...] = share[:, :order]
        for distance in range(members):
            target = partner(me, -distance, members) if distance else me
            out = outs[1 + distance]
            for a in range(1, ancestors):
                value = jnp.zeros((part, rows), jnp.float32)
                for j in range(members):
                    at = slice(a * order + j * rows, a * order + (j + 1) * rows)
                    value = jnp.where(target == j, share[:, at], value)
                out[:, (a - 1) * rows : a * rows] = value

    return local_kernel(
        body,
        [float_array(part, order)] + [float_array(part, width)] * members,
        [*received, rhs_turned, after],
        [VMEM] * (len(received) + 1) + [ANY],
        scratch=[pltpu.VMEM((part, ancestors * order), jnp.float32)],
    )


def split_factors(factors, after):
    count = len(factors)

    def body(*refs):
        for i in range(count):
            top, rest = high_low(refs[i][...])
            refs[count + 1 + 2 * i][...] = top
            refs[count + 2 + 2 * i][...] = rest

    outs = []
    for factor in factors:
        outs += [jax.ShapeDtypeStruct(factor.shape, jnp.bfloat16)] * 2
    return local_kernel(
        body,
        outs,
        [*factors, after],
        [VMEM] * count + [ANY],
        flops=4 * sum(f.size for f in factors),
    )


def solve_first(shares, others, top, rest):
    members = len(others)
    part, width = others[0].shape
    rows, order = top.shape[1:]

    def body(*refs):
        total = refs[0][...]
        for ref in refs[1:members]:
            total = total + ref[...]
        other_refs = refs[members : 2 * members]
        top_ref, rest_ref, out = refs[2 * members : 2 * members + 3]
        value = split_product(total, top_ref[0], rest_ref[0])
        out[...] = value
        for distance in range(1, members):
            message = refs[2 * members + 2 + distance]
            message[:, :rows] = value
            message[:, rows:] = other_refs[distance][...]

    return local_kernel(
        body,
        [float_array(part, rows)] + [float_array(part, rows + width)] * (members - 1),
        [*shares, *others, top, rest],
        flops=6 * part * rows * order,
    )


def take_messages(own, other, messages, top, rest):
    members = len(messages) + 1
    part, width = other.shape
    rows, order = top.shape[1:]

    def body(*refs):
        own_ref, other_ref = refs[:2]
        held = refs[2 : members + 1]
        top_ref, rest_ref, out = refs[members + 1 : members + 4]
        whole = refs[-1]
        total = other_ref[...]
        for ref in held:
            total = total + ref[:, rows:]
        if width > rows:
            refs[members + 4][...] = total
        pieces = [ref[:, :rows] for ref in held[::-1]]
        put_in_order([own_ref[...]] + pieces, whole)
        out[...] = total[:, :rows] - split_product(whole[...], top_ref[0], rest_ref[0])

    return local_kernel(
        body,
        [float_array(part, rows)] + [float_array(part, width)] * (width > rows),
        [own, other, *messages, top, rest],
        flops=6 * part * rows * order,
        scratch=[pltpu.VMEM((part, order), jnp.float32)],
    )


def put_in_order(held, whole):
    me = lax.axis_index("grp")
    members = len(held)
    width = held[0].shape[1]
    for j in range(members):
        value = jnp.zeros(held[0].shape, jnp.float32)
        for distance in range(members):
            owner = partner(me, distance, members) if distance else me
            value = jnp.where(owner == j, held[distance], value)
        whole[:, j * width : (j + 1) * width] = value


def apply_split(pieces, top, rest, index, base=None, begin=0, others=None, far_first=True):
    members = lax.axis_size("grp")
    part, width = pieces[0].shape
    rows, order = top.shape[1:]
    extra = list(others or []) if base is None else [base]

    def body(*refs):
        top_ref, rest_ref = refs[members : members + 2]
        out, whole = refs[-2:]
        held = [refs[d][...] for d in range(members)]
        if far_first:
            held = held[:1] + held[:0:-1]
        put_in_order(held, whole)
        result = split_product(whole[...], top_ref[index], rest_ref[index])
        if others is not None:
            for i in range(len(others)):
                out[i] = refs[members + 2 + i][...]
            out[len(others)] = result
            return
        if base is not None:
            result = refs[members + 2][:, begin : begin + rows] - result
        out[...] = result

    shape = (part, rows) if others is None else (len(others) + 1, part, rows)
    return local_kernel(
        body,
        [float_array(*shape)],
        [*pieces, top, rest, *extra],
        flops=6 * part * rows * order,
        scratch=[pltpu.VMEM((part, order), jnp.float32)],
    )[0]


def on_device(
    rhs_local,
    diag_inv_local,
    sub_local,
    tiles,
    tile_block,
    tile_source,
    tile_count,
    rhs_anc,
    diag_inv_anc,
    sub_anc,
):
    supernodes, _, order = diag_inv_local.shape[1:]
    rhs_count = rhs_local.shape[-1]
    members = lax.axis_size("grp")
    rows = order // members
    slots, tile_rows = tiles.shape[2:4]

    streams = 2 if rhs_count % 16 == 0 else 1
    residuals = turn_first(rhs_local, streams)
    first = diag_inv_local[0, 0]
    rounded = lax.reduce_precision(first, 8, 7)
    first_top = rounded.astype(jnp.bfloat16)[None]
    first_rest = (first - rounded).astype(jnp.bfloat16)[None]
    solved = [[None] * streams for _ in range(supernodes)]
    gathered = [[None] * streams for _ in range(supernodes)]
    values = list(residuals)
    last = None
    for step in range(2 * supernodes):
        current = step // 2
        for i in range(streams):
            turn_taken = step > 0 and last is not None
            ties = [(1, last[0][2][1])] if step * streams + i > streams else []
            pieces = gather_rows(values[i], ties)
            if step == 1 and i == 0:
                later = turn(rhs_local, 1, supernodes, streams, pieces[1][1])
            if turn_taken:
                offset, piece = pieces[2]
                pieces[2] = (offset, lax.optimization_barrier((piece, last[1]))[0])
            if step == 0:
                owned = apply_split(
                    [p for _, p in pieces],
                    first_top,
                    first_rest,
                    0,
                    far_first=False,
                )
            else:
                whole = assemble(pieces, order)
                if step % 2 == 0:
                    owned = contract_last(whole, diag_inv_local[0, current])
                elif current + 1 < supernodes:
                    owned = later[current * streams + i] - contract_last(whole, sub_local[0, current])
            if step % 2 == 0:
                solved[current][i] = owned
            else:
                gathered[current][i] = whole
            values[i] = owned
            last = (pieces, owned)

    by_stream = [[values[i] for values in gathered] for i in range(streams)]
    done = [tile_terms(values, tiles[0, 0], tile_source) for values in by_stream[:-1]]
    packed = pack_terms(done, by_stream[-1], tiles[0, 0], tile_source, tile_block, tile_count)
    received = leaf_exchange(packed)
    solution_local, tie = turn_back(solved, packed[0])
    shares = share_out(
        received, jnp.swapaxes(rhs_anc, 1, 2), order, slots, tile_rows, tie
    )
    far_first = list(range(members - 1, 0, -1))
    first_share, others = shares[0], shares[1:]
    sums = [first_share] + [send(first_share, "grp", d) for d in far_first]
    inverse_top, inverse_rest, below_top, below_rest = split_factors(
        [diag_inv_anc, sub_anc], first_share
    )
    solution, *messages = solve_first(sums, others, inverse_top, inverse_rest)
    solutions = [solution]
    ancestors = rhs_anc.shape[0]
    for ancestor in range(1, ancestors):
        if ancestor == 1:
            arrived = [send(messages[d - 1], "grp", d) for d in far_first]
            residual, *left = take_messages(solution, others[0], arrived, below_top, below_rest)
        else:
            pieces = gather_far_first(solutions[-1])
            residual = apply_split(
                pieces, below_top, below_rest, ancestor - 1, left[0], (ancestor - 1) * rows
            )
        pieces = gather_far_first(residual)
        behind = solutions if ancestor + 1 == ancestors else None
        solved_now = apply_split(pieces, inverse_top, inverse_rest, ancestor, others=behind)
        solutions.append(solved_now)
    solutions = solutions[-1] if ancestors > 1 else solutions[0][None]
    solutions = jnp.swapaxes(solutions, 1, 2)
    return (solution_local, solutions)


def solution(mesh):
    return jax.shard_map(
        on_device,
        mesh=mesh,
        in_specs=(
            P("leaf", None, "grp", None),
            P("leaf", None, "grp", None),
            P("leaf", None, "grp", None),
            P("leaf", "grp", None, None, None),
            P("leaf", "grp", None),
            P("leaf", "grp", None),
            P("leaf", "grp"),
            P(None, "grp", "leaf"),
            P(None, "grp", None),
            P(None, "grp", None),
        ),
        out_specs=(P("leaf", None, "grp", None), P(None, "grp", "leaf")),
        check_vma=False,
    )
```
